32 devices in a mesh: dp: 16 (over z, y, x), tensor: 2 (over core).
Axes of the slice: x: 2, y: 2, z: 4, core: 2. Of those that a mesh axis runs over, the one named last changes fastest.
Arguments:
- tokens: bfloat16 [32, 680, 1024], P('dp', 'tensor'), may hold values from -40 to 40
- condition: bfloat16 [32, 1024], P('dp'), may hold values from -6 to 6
- scale_index: int32 [32, 680], P('dp'), may hold values from 0 to 9, never falling along the last dimension, each value on 1 to 256 neighbouring positions
- ada_weight: bfloat16 [1024, 6, 1024], P('tensor', None, 'dp'), may hold values from -0.1875 to 0.1875
- ada_bias: bfloat16 [6, 16, 64], P(None, 'tensor', 'dp'), may hold values from -3 to 3
- qkv_weight: bfloat16 [3, 1024, 1024], P(None, 'dp', 'tensor'), may hold values from -0.1875 to 0.1875
- query_bias: bfloat16 [16, 64], P('tensor', 'dp'), may hold values from -3 to 3
- value_bias: bfloat16 [16, 64], P('tensor', 'dp'), may hold values from -3 to 3
- head_scale: float32 [16], P('tensor'), may hold values from 2 to 3.2
- proj_weight: bfloat16 [1024, 1024], P('tensor', 'dp'), may hold values from -0.375 to 0.375
- proj_bias: bfloat16 [16, 64], P('tensor', 'dp'), may hold values from -2 to 2
- up_weight: bfloat16 [1024, 4096], P('dp', 'tensor'), may hold values from -0.1875 to 0.1875
- up_bias: bfloat16 [16, 256], P('tensor', 'dp'), may hold values from -3 to 3
- down_weight: bfloat16 [4096, 1024], P('tensor', 'dp'), may hold values from -0.09375 to 0.09375
- down_bias: bfloat16 [16, 64], P('tensor', 'dp'), may hold values from -2 to 2
- out_grad: bfloat16 [32, 680, 1024], P('dp', 'tensor'), may hold values from -6 to 6
Outputs:
- output: float32 [32, 680, 1024], P('dp', 'tensor')
- grad_tokens: float32 [32, 680, 1024], P('dp', 'tensor')
- grad_condition: float32 [32, 1024], P('dp', 'tensor')
- grad_ada_weight: float32 [1024, 6, 1024], P('tensor', None, 'dp')
- grad_ada_bias: float32 [6, 16, 64], P(None, 'tensor', 'dp')
- grad_qkv_weight: float32 [3, 1024, 1024], P(None, 'dp', 'tensor')
- grad_query_bias: float32 [16, 64], P('tensor', 'dp')
- grad_value_bias: float32 [16, 64], P('tensor', 'dp')
- grad_head_scale: float32 [16], P('tensor')
- grad_proj_weight: float32 [1024, 1024], P('tensor', 'dp')
- grad_proj_bias: float32 [16, 64], P('tensor', 'dp')
- grad_up_weight: float32 [1024, 4096], P('dp', 'tensor')
- grad_up_bias: float32 [16, 256], P('tensor', 'dp')
- grad_down_weight: float32 [4096, 1024], P('tensor', 'dp')
- grad_down_bias: float32 [16, 64], P('tensor', 'dp')
The draws below stay inside these ranges and needn't reach their ends.
Inputs may be any that keep to these rules, and one draw needn't show every extreme that they name: `scale_index`: in each sequence the scale of a token never falls along its positions; each of the 10 scales has 1 to 256 tokens.
All inputs are finite; a program needn't handle non-finite values.
Results may differ from the reference program's by a relative error of at most 0.025.
Values may be sent and summed in bfloat16 or wider, within the bound.
A program may use at most 384 MiB of HBM per device.

```python
import math
import jax
import jax.numpy as jnp
import numpy as np
from jax import lax

D = 1024
HEADS = 16
HEAD_DIM = 64
FF = 4096
SEQ_LEN = 680
SCALES = 10
SCALE_MAX = 256
MICRO = 2
SEQS = 32


def draw_tokens(key, part):
    base_key, row_key, col_key = jax.random.split(key, 3)
    row_scale = jnp.exp(jax.random.uniform(row_key, (SEQS, SEQ_LEN, 1), jnp.float32, math.log(0.3), math.log(3.0)))
    col_scale = jnp.exp(jax.random.uniform(col_key, (1, 1, D), jnp.float32, math.log(0.3), math.log(3.0)))
    base_draw = jnp.clip(jax.random.normal(base_key, (SEQS, SEQ_LEN, D), jnp.float32), -4.0, 4.0)
    values = base_draw * row_scale * col_scale
    return values.astype(jnp.bfloat16)


def level_of(key, dims, shards, low, largest):
    def one(axis_at, parts):
        heights = jax.random.uniform(jax.random.fold_in(jax.random.fold_in(key, 6), axis_at), (parts,), jnp.float32, low / len(shards), largest / len(shards))
        return jnp.repeat(jnp.exp(heights), dims[axis_at] // parts).reshape((-1,) + (1,) * (len(dims) - axis_at - 1))

    level = one(*shards[0])
    for cut in shards[1:]:
        level = level * one(*cut)
    return level


def profile(count, total, bound, skew):
    weights = [(1 << 20) // math.isqrt(rank ** skew) + 1 for rank in range(2, count + 1)]
    surplus, counts = total - bound - (count - 1), [1] * (count - 1)
    while surplus > 0:
        movable = [i for i in range(count - 1) if counts[i] < bound]
        whole, budget = sum([weights[i] for i in movable]), surplus
        for i in movable:
            more = min(bound - counts[i], max(1, budget * weights[i] // whole), surplus)
            counts[i] = counts[i] + more
            surplus = surplus - more
    return np.array([bound] + counts)


def uneven_parts(own_key, number_of, total, limit, lean):
    if number_of == 2:
        one = jax.random.randint(own_key, (), max(1, total - limit), min(limit, total - 1) + 1)
        return jnp.stack([one, total - one])
    lengths = jnp.asarray(profile(number_of, total, limit, lean), jnp.int32)
    twos = (number_of - 1) // 2
    source_of, taker = lengths[1:1 + 2 * twos:2], lengths[2:2 + 2 * twos:2]
    room = jnp.minimum(source_of - 1, limit - taker)
    moved = jax.random.randint(jax.random.fold_in(own_key, 1), (twos,), 0, 1 << 20) % (room + 1)
    lengths = lengths.at[1:1 + 2 * twos:2].set(source_of - moved).at[2:2 + 2 * twos:2].set(taker + moved)
    return lengths[jax.random.permutation(jax.random.fold_in(own_key, 2), number_of)]


def scatter_about(stream_key, shape, scale, reach, pieces=(), dtype=jnp.bfloat16):
    entries = jax.random.normal(stream_key, shape, jnp.float32) * scale
    if len(pieces) > 0:
        entries = level_of(stream_key, shape, pieces, -0.22, 0.18) * entries
    return jnp.clip(entries, min=-reach, max=reach).astype(dtype)


def setup_inputs(seed: int = 0) -> dict:
    seeds = jax.random.split(jax.random.key(seed), 17)
    tokens = draw_tokens(jax.random.fold_in(seeds[16], 71), 0)
    condition = scatter_about(seeds[1], (SEQS, D), 1.0, 6.0, ((0, 16),))
    scale_index = jax.vmap(lambda own: jnp.searchsorted(jnp.cumsum(uneven_parts(own, SCALES, SEQ_LEN, SCALE_MAX, 0)), jnp.arange(SEQ_LEN), side="right"))(jax.random.split(seeds[2], SEQS)).reshape((SEQS, SEQ_LEN)).astype(jnp.int32)
    ada_weight = scatter_about(seeds[3], (D, 6, D), D ** -0.5, 0.1875, ((0, 2), (2, 16)))
    ada_bias = scatter_about(seeds[4], (6, HEADS, HEAD_DIM), 0.5, 3.0, ((1, 2), (2, 16)))
    qkv_weight = scatter_about(seeds[5], (3, D, D), D ** -0.5, 0.1875, ((1, 16), (2, 2)))
    query_bias = scatter_about(seeds[6], (HEADS, HEAD_DIM), 0.5, 3.0, ((0, 2), (1, 16)))
    value_bias = scatter_about(seeds[7], (HEADS, HEAD_DIM), 0.5, 3.0, ((0, 2), (1, 16)))
    head_scale = jnp.clip(2.0 + 1.2 * jax.random.uniform(seeds[8], (HEADS,), jnp.float32) ** level_of(seeds[8], (HEADS,), ((0, 2),), -0.2, 0.2), 2.0, 3.2)
    proj_weight = scatter_about(seeds[9], (D, D), (D // 4) ** -0.5, 0.375, ((0, 2), (1, 16)))
    proj_bias = scatter_about(seeds[10], (HEADS, HEAD_DIM), 0.3, 2.0, ((0, 2), (1, 16)))
    up_weight = scatter_about(seeds[11], (D, FF), D ** -0.5, 0.1875, ((0, 16), (1, 2)))
    up_bias = scatter_about(seeds[12], (HEADS, FF // HEADS), 0.5, 3.0, ((0, 2), (1, 16)))
    down_weight = scatter_about(seeds[13], (FF, D), FF ** -0.5, 0.09375, ((0, 2), (1, 16)))
    down_bias = scatter_about(seeds[14], (HEADS, HEAD_DIM), 0.3, 2.0, ((0, 2), (1, 16)))
    out_grad = scatter_about(seeds[15], (SEQS, SEQ_LEN, D), 1.0, 6.0, ((0, 16), (1, 2)))
    return dict(tokens=tokens, condition=condition, scale_index=scale_index, ada_weight=ada_weight, ada_bias=ada_bias, qkv_weight=qkv_weight, query_bias=query_bias, value_bias=value_bias, head_scale=head_scale, proj_weight=proj_weight, proj_bias=proj_bias, up_weight=up_weight, up_bias=up_bias, down_weight=down_weight, down_bias=down_bias, out_grad=out_grad)


@jax.custom_vjp
def low(v):
    return lax.optimization_barrier(v.astype(jnp.bfloat16)).astype(jnp.float32)

@jax.custom_vjp
def low_back(v):
    return v

def low_keep(v):
    return (low(v), None)

def low_pass(kept, grad):
    return (grad,)

def back_keep(v):
    return (v, None)

def back_low(kept, grad):
    return (low(grad),)
low.defvjp(low_keep, low_pass)
low_back.defvjp(back_keep, back_low)
HIGHEST = lax.Precision.HIGHEST
NORM_EPS = 1e-06
HEAD_EPS = 1e-06

def layer_norm(values):
    centred = values - lax.optimization_barrier(jnp.mean(values, axis=-1, keepdims=True))
    spread = lax.optimization_barrier(jnp.mean(centred * centred, axis=-1, keepdims=True))
    return centred * lax.rsqrt(spread + NORM_EPS)

def unit_rows(values):
    return values * lax.rsqrt(lax.optimization_barrier(jnp.sum(values * values, axis=-1, keepdims=True)) + HEAD_EPS)

def attend(block_item):
    queries, keys_in, values_in, scale_row = block_item
    scores = low_back(jnp.einsum('qhe,khe->hqk', queries, keys_in, precision=HIGHEST))
    allowed = scale_row[None, :] <= scale_row[:, None]
    scores = jnp.where(allowed[None, :, :], scores, -1e+30)
    row_max = lax.optimization_barrier(jnp.max(scores, axis=-1, keepdims=True))
    weights_exp = jnp.exp(scores - row_max)
    attn_prob = weights_exp / lax.optimization_barrier(jnp.sum(weights_exp, axis=-1, keepdims=True))
    return jnp.einsum('hqk,khe->qhe', low(attn_prob), values_in, precision=HIGHEST)

def layer_block(params, tokens, condition, scale_index):
    ada_weight, ada_bias, qkv_weight, query_bias, value_bias, head_scale, proj_weight, proj_bias, up_weight, up_bias, down_weight, down_bias = params
    group_size = tokens.shape[0]
    silu_cond = low(jax.nn.silu(condition))
    modulation = low_back(jnp.einsum('gd,djc->gjc', silu_cond, ada_weight, precision=HIGHEST)) + ada_bias.reshape(6, D)
    gamma_attn = modulation[:, 0][:, None, :]
    gamma_mlp = modulation[:, 1][:, None, :]
    scale_attn = modulation[:, 2][:, None, :]
    scale_mlp = modulation[:, 3][:, None, :]
    shift_attn = modulation[:, 4][:, None, :]
    shift_mlp = modulation[:, 5][:, None, :]
    mixed_attn = low(layer_norm(tokens) * (1.0 + scale_attn) + shift_attn)
    projected = low_back(jnp.einsum('gld,jdc->jglc', mixed_attn, qkv_weight, precision=HIGHEST))
    queries = (projected[0] + query_bias.reshape(D)).reshape(group_size, SEQ_LEN, HEADS, HEAD_DIM)
    keys_raw = projected[1].reshape(group_size, SEQ_LEN, HEADS, HEAD_DIM)
    values_low = low((projected[2] + value_bias.reshape(D)).reshape(group_size, SEQ_LEN, HEADS, HEAD_DIM))
    query_scaled = low(unit_rows(queries) * jnp.exp(head_scale)[:, None])
    key_low = low(unit_rows(keys_raw))
    attended = lax.map(jax.checkpoint(attend), (query_scaled, key_low, values_low, scale_index))
    attended = low(low_back(attended.reshape(group_size, SEQ_LEN, D)))
    branch_attn = low_back(jnp.einsum('gld,de->gle', attended, proj_weight, precision=HIGHEST)) + proj_bias.reshape(D)
    middle = tokens + gamma_attn * branch_attn
    mixed_mlp = low(layer_norm(middle) * (1.0 + scale_mlp) + shift_mlp)
    hidden = low_back(jnp.einsum('gld,df->glf', mixed_mlp, up_weight, precision=HIGHEST)) + up_bias.reshape(FF)
    activated = low(jax.nn.gelu(hidden, approximate=True))
    branch_mlp = low_back(jnp.einsum('glf,fd->gld', activated, down_weight, precision=HIGHEST)) + down_bias.reshape(D)
    return middle + gamma_mlp * branch_mlp

def reference(tokens, condition, scale_index, ada_weight, ada_bias, qkv_weight, query_bias, value_bias, head_scale, proj_weight, proj_bias, up_weight, up_bias, down_weight, down_bias, out_grad):
    params = tuple((parameter.astype(jnp.float32) for parameter in (ada_weight, ada_bias, qkv_weight, query_bias, value_bias, head_scale, proj_weight, proj_bias, up_weight, up_bias, down_weight, down_bias)))
    groups = SEQS // MICRO
    token_groups = tokens.astype(jnp.float32).reshape(groups, MICRO, SEQ_LEN, D)
    cond_groups = condition.astype(jnp.float32).reshape(groups, MICRO, D)
    scale_groups = scale_index.reshape(groups, MICRO, SEQ_LEN)
    grad_groups = out_grad.astype(jnp.float32).reshape(groups, MICRO, SEQ_LEN, D)

    def one_group(totals, group_item):
        token_block, cond_block, scale_block, grad_block = group_item

        def forward(param_set, token_in, cond_in):
            return layer_block(param_set, token_in, cond_in, scale_block)
        output, pullback = jax.vjp(forward, params, token_block, cond_block)
        grad_params, grad_token_block, grad_cond_block = pullback(grad_block)
        totals = jax.tree.map(lambda running, increment: running + increment, totals, grad_params)
        return (totals, (output, grad_token_block, grad_cond_block))
    zero_set = tuple((jnp.zeros_like(parameter) for parameter in params))
    totals, (outputs, grad_tokens, grad_condition) = lax.scan(one_group, zero_set, (token_groups, cond_groups, scale_groups, grad_groups))
    return (outputs.reshape(SEQS, SEQ_LEN, D), grad_tokens.reshape(SEQS, SEQ_LEN, D), grad_condition.reshape(SEQS, D), totals[0], totals[1], totals[2], totals[3], totals[4], totals[5], totals[6], totals[7], totals[8], totals[9], totals[10], totals[11])
```

```python
import functools

import jax
import jax.numpy as jnp
from jax import lax
from jax.experimental import pallas as pl
from jax.experimental.pallas import tpu as pltpu
from jax.sharding import PartitionSpec as P

NORM_EPS = 1e-06
HEAD_EPS = 1e-06
GELU_COEF = 0.7978845608028654
GELU_CUBE = 0.044715


def normalize(values):
    centred = values - jnp.mean(values, axis=-1, keepdims=True)
    inverse = lax.rsqrt(jnp.mean(centred * centred, axis=-1, keepdims=True) + NORM_EPS)
    return (centred * inverse, inverse)


def norm_back(grad_normed, normed, inverse):
    return inverse * (
        grad_normed
        - jnp.mean(grad_normed, axis=-1, keepdims=True)
        - normed * jnp.mean(grad_normed * normed, axis=-1, keepdims=True)
    )


def gelu_slope(hidden):
    inner = jnp.tanh(GELU_COEF * (hidden + GELU_CUBE * hidden * hidden * hidden))
    return 0.5 * (1.0 + inner) + 0.5 * hidden * (1.0 - inner * inner) * GELU_COEF * (
        1.0 + 3.0 * GELU_CUBE * hidden * hidden
    )


def masked_scores(query_unit, key_unit, scale_factor, scale_row):
    query_low = (query_unit * scale_factor).astype(jnp.bfloat16)
    key_low = key_unit.astype(jnp.bfloat16)
    scores = jnp.einsum("qhe,khe->hqk", query_low, key_low, preferred_element_type=jnp.float32)
    allowed = scale_row[None, :] <= scale_row[:, None]
    return (jnp.where(allowed[None, :, :], scores, -1e30), query_low, key_low)


def attention_core(mixed_all, qkv_full, query_bias_part, value_bias_part, head_scale, scale_row):
    part_width = qkv_full.shape[2]
    part_heads = head_scale.shape[0]
    head_dim = part_width // part_heads
    seq_len = scale_row.shape[0]
    projected = jnp.einsum("ld,jdc->jlc", mixed_all, qkv_full, preferred_element_type=jnp.float32)
    queries = (projected[0] + query_bias_part.reshape(part_width).astype(jnp.float32)).reshape(
        seq_len, part_heads, head_dim
    )
    keys_raw = projected[1].reshape(seq_len, part_heads, head_dim)
    values_low = (projected[2] + value_bias_part.reshape(part_width).astype(jnp.float32)).astype(
        jnp.bfloat16
    )
    values_low = values_low.reshape(seq_len, part_heads, head_dim)
    query_inverse = lax.rsqrt(jnp.sum(queries * queries, axis=-1, keepdims=True) + HEAD_EPS)
    key_inverse = lax.rsqrt(jnp.sum(keys_raw * keys_raw, axis=-1, keepdims=True) + HEAD_EPS)
    query_unit = queries * query_inverse
    key_unit = keys_raw * key_inverse
    scale_factor = jnp.exp(head_scale)[:, None]
    scores, query_low, key_low = masked_scores(query_unit, key_unit, scale_factor, scale_row)
    row_max = jnp.max(scores, axis=-1, keepdims=True)
    weights_exp = jnp.exp(scores - row_max)
    row_total = jnp.sum(weights_exp, axis=-1, keepdims=True)
    attn_prob = weights_exp / row_total
    log_norm = row_max + jnp.log(row_total)
    attended = jnp.einsum(
        "hqk,khe->qhe",
        attn_prob.astype(jnp.bfloat16),
        values_low,
        preferred_element_type=jnp.float32,
    )
    attended = attended.reshape(seq_len, part_width).astype(jnp.bfloat16)
    return (attended, (query_unit, key_unit, query_inverse, key_inverse, values_low, log_norm))


def forward_step(weights, token_rows, condition_row, scale_row, head_scale):
    (
        ada_full,
        ada_bias_part,
        qkv_full,
        query_bias_part,
        value_bias_part,
        proj_full,
        proj_bias_part,
        up_full,
        up_bias_part,
        down_full,
        down_bias_part,
    ) = weights
    width = token_rows.shape[1]
    part_width = qkv_full.shape[2]
    col_start = lax.axis_index("tensor") * part_width
    cond_rows = lax.dynamic_slice_in_dim(
        condition_row.astype(jnp.float32), col_start, part_width, 0
    )
    silu_rows = jax.nn.silu(cond_rows).astype(jnp.bfloat16)
    mod_terms = jnp.einsum("r,rjc->jc", silu_rows, ada_full, preferred_element_type=jnp.float32)
    own_cols = jnp.concatenate(
        [
            ada_bias_part.reshape(6, part_width),
            proj_bias_part.reshape(1, part_width),
            down_bias_part.reshape(1, part_width),
        ],
        axis=0,
    ).astype(jnp.float32)
    placed = lax.dynamic_update_slice(jnp.zeros((8, width), jnp.float32), own_cols, (0, col_start))
    local_mod = placed + jnp.concatenate([mod_terms, jnp.zeros((2, width), jnp.float32)], axis=0)
    modulation = lax.psum(local_mod, "tensor")
    inputs = token_rows.astype(jnp.float32)
    normed_attn, inverse_attn = normalize(inputs)
    mixed_attn = (normed_attn * (1.0 + modulation[2]) + modulation[4]).astype(jnp.bfloat16)
    mixed_all = lax.all_gather(mixed_attn, "tensor", axis=0, tiled=True)
    attended, attn_kept = attention_core(
        mixed_all, qkv_full, query_bias_part, value_bias_part, head_scale, scale_row
    )
    branch_attn = (
        lax.psum_scatter(
            jnp.dot(attended, proj_full, preferred_element_type=jnp.float32).astype(jnp.bfloat16),
            "tensor",
            scatter_dimension=0,
            tiled=True,
        ).astype(jnp.float32)
        + modulation[6]
    )
    middle = inputs + modulation[0] * branch_attn
    normed_mlp, inverse_mlp = normalize(middle)
    mixed_mlp = (normed_mlp * (1.0 + modulation[3]) + modulation[5]).astype(jnp.bfloat16)
    mlp_all = lax.all_gather(mixed_mlp, "tensor", axis=0, tiled=True)
    hidden = jnp.dot(mlp_all, up_full, preferred_element_type=jnp.float32) + up_bias_part.reshape(
        -1
    ).astype(jnp.float32)
    activated = jax.nn.gelu(hidden, approximate=True).astype(jnp.bfloat16)
    branch_mlp = (
        lax.psum_scatter(
            jnp.dot(activated, down_full, preferred_element_type=jnp.float32).astype(jnp.bfloat16),
            "tensor",
            scatter_dimension=0,
            tiled=True,
        ).astype(jnp.float32)
        + modulation[7]
    )
    output = middle + modulation[1] * branch_mlp
    query_unit, key_unit, query_inverse, key_inverse, values_low, log_norm = attn_kept
    kept = (
        modulation,
        normed_attn,
        inverse_attn,
        mixed_all,
        query_unit,
        key_unit,
        query_inverse,
        key_inverse,
        values_low,
        log_norm,
        attended,
        branch_attn,
        normed_mlp,
        inverse_mlp,
        mlp_all,
        hidden,
        activated,
        branch_mlp,
    )
    return (output, kept)


def backward_step(weights, kept, token_grad, condition_row, scale_row, head_scale):
    (
        ada_full,
        ada_bias_part,
        qkv_full,
        query_bias_part,
        value_bias_part,
        proj_full,
        proj_bias_part,
        up_full,
        up_bias_part,
        down_full,
        down_bias_part,
    ) = weights
    (
        modulation,
        normed_attn,
        inverse_attn,
        mixed_all,
        query_unit,
        key_unit,
        query_inverse,
        key_inverse,
        values_low,
        log_norm,
        attended,
        branch_attn,
        normed_mlp,
        inverse_mlp,
        mlp_all,
        hidden,
        activated,
        branch_mlp,
    ) = kept
    part_width = qkv_full.shape[2]
    part_heads = head_scale.shape[0]
    head_dim = part_width // part_heads
    seq_len = scale_row.shape[0]
    scale_factor = jnp.exp(head_scale)[:, None]
    grad_rows = token_grad.astype(jnp.float32)
    grad_branch_mlp = grad_rows * modulation[1]
    grad_gamma_mlp = jnp.sum(grad_rows * branch_mlp, axis=0)
    grad_down_bias = jnp.sum(grad_branch_mlp, axis=0)
    grad_mlp_all = lax.all_gather(
        grad_branch_mlp.astype(jnp.bfloat16), "tensor", axis=0, tiled=True
    )
    grad_down = jnp.einsum("lf,ld->fd", activated, grad_mlp_all, preferred_element_type=jnp.float32)
    grad_act = jnp.einsum("ld,fd->lf", grad_mlp_all, down_full, preferred_element_type=jnp.float32)
    grad_hidden = grad_act * gelu_slope(hidden)
    grad_up_bias = jnp.sum(grad_hidden, axis=0)
    hidden_low = grad_hidden.astype(jnp.bfloat16)
    grad_up = jnp.einsum("ld,lf->df", mlp_all, hidden_low, preferred_element_type=jnp.float32)
    grad_mixed_mlp = lax.psum_scatter(
        jnp.einsum("lf,df->ld", hidden_low, up_full, preferred_element_type=jnp.float32).astype(
            jnp.bfloat16
        ),
        "tensor",
        scatter_dimension=0,
        tiled=True,
    ).astype(jnp.float32)
    grad_scale_mlp = jnp.sum(grad_mixed_mlp * normed_mlp, axis=0)
    grad_shift_mlp = jnp.sum(grad_mixed_mlp, axis=0)
    grad_middle = grad_rows + norm_back(
        grad_mixed_mlp * (1.0 + modulation[3]), normed_mlp, inverse_mlp
    )
    grad_branch_attn = grad_middle * modulation[0]
    grad_gamma_attn = jnp.sum(grad_middle * branch_attn, axis=0)
    grad_proj_bias = jnp.sum(grad_branch_attn, axis=0)
    grad_attn_all = lax.all_gather(
        grad_branch_attn.astype(jnp.bfloat16), "tensor", axis=0, tiled=True
    )
    grad_proj = jnp.einsum("lc,ld->cd", attended, grad_attn_all, preferred_element_type=jnp.float32)
    grad_attended = jnp.einsum(
        "ld,cd->lc", grad_attn_all, proj_full, preferred_element_type=jnp.float32
    )
    grad_attended = grad_attended.astype(jnp.bfloat16).reshape(seq_len, part_heads, head_dim)
    scores, query_low, key_low = masked_scores(query_unit, key_unit, scale_factor, scale_row)
    attn_prob = jnp.exp(scores - log_norm)
    grad_prob = jnp.einsum(
        "qhe,khe->hqk", grad_attended, values_low, preferred_element_type=jnp.float32
    )
    row_dot = jnp.sum(attn_prob * grad_prob, axis=-1, keepdims=True)
    grad_scores = (attn_prob * (grad_prob - row_dot)).astype(jnp.bfloat16)
    grad_values = jnp.einsum(
        "hqk,qhe->khe",
        attn_prob.astype(jnp.bfloat16),
        grad_attended,
        preferred_element_type=jnp.float32,
    )
    grad_query_scaled = jnp.einsum(
        "hqk,khe->qhe", grad_scores, key_low, preferred_element_type=jnp.float32
    )
    grad_key_unit = jnp.einsum(
        "hqk,qhe->khe", grad_scores, query_low, preferred_element_type=jnp.float32
    )
    grad_head_scale = jnp.sum(grad_query_scaled * query_unit, axis=(0, 2)) * jnp.exp(head_scale)
    grad_query_unit = grad_query_scaled * scale_factor
    grad_queries = query_inverse * (
        grad_query_unit - query_unit * jnp.sum(grad_query_unit * query_unit, axis=-1, keepdims=True)
    )
    grad_keys = key_inverse * (
        grad_key_unit - key_unit * jnp.sum(grad_key_unit * key_unit, axis=-1, keepdims=True)
    )
    grad_query_bias = jnp.sum(grad_queries, axis=0)
    grad_value_bias = jnp.sum(grad_values, axis=0)
    grad_projected = (
        jnp.stack([grad_queries, grad_keys, grad_values])
        .reshape(3, seq_len, part_width)
        .astype(jnp.bfloat16)
    )
    grad_qkv = jnp.einsum(
        "ld,jlc->jdc", mixed_all, grad_projected, preferred_element_type=jnp.float32
    )
    grad_mixed_attn = lax.psum_scatter(
        jnp.einsum(
            "jlc,jdc->ld", grad_projected, qkv_full, preferred_element_type=jnp.float32
        ).astype(jnp.bfloat16),
        "tensor",
        scatter_dimension=0,
        tiled=True,
    ).astype(jnp.float32)
    grad_scale_attn = jnp.sum(grad_mixed_attn * normed_attn, axis=0)
    grad_shift_attn = jnp.sum(grad_mixed_attn, axis=0)
    grad_inputs = grad_middle + norm_back(
        grad_mixed_attn * (1.0 + modulation[2]), normed_attn, inverse_attn
    )
    mod_rows = jnp.stack(
        [
            grad_gamma_attn,
            grad_gamma_mlp,
            grad_scale_attn,
            grad_scale_mlp,
            grad_shift_attn,
            grad_shift_mlp,
            grad_proj_bias,
            grad_down_bias,
        ]
    )
    grad_modulation = lax.psum(mod_rows.astype(jnp.bfloat16), "tensor").astype(jnp.float32)
    col_start = lax.axis_index("tensor") * part_width
    cond_rows = lax.dynamic_slice_in_dim(
        condition_row.astype(jnp.float32), col_start, part_width, 0
    )
    silu_rows = jax.nn.silu(cond_rows).astype(jnp.bfloat16)
    mod_low = grad_modulation[:6].astype(jnp.bfloat16)
    grad_ada = jnp.einsum("r,jc->rjc", silu_rows, mod_low, preferred_element_type=jnp.float32)
    grad_silu = jnp.einsum("jc,rjc->r", mod_low, ada_full, preferred_element_type=jnp.float32)
    sigmoid_rows = jax.nn.sigmoid(cond_rows)
    grad_condition = grad_silu * sigmoid_rows * (1.0 + cond_rows * (1.0 - sigmoid_rows))
    own_cols = lax.dynamic_slice_in_dim(grad_modulation, col_start, part_width, 1)
    increments = (
        grad_ada,
        own_cols[:6].reshape(6, part_heads, head_dim),
        grad_qkv,
        grad_query_bias,
        grad_value_bias,
        grad_head_scale,
        grad_proj,
        own_cols[6].reshape(part_heads, head_dim),
        grad_up,
        grad_up_bias.reshape(part_heads, -1),
        grad_down,
        own_cols[7].reshape(part_heads, head_dim),
    )
    return (increments, grad_inputs, grad_condition)


def on_device(
    tokens,
    condition,
    scale_index,
    ada_weight,
    ada_bias,
    qkv_weight,
    query_bias,
    value_bias,
    head_scale,
    proj_weight,
    proj_bias,
    up_weight,
    up_bias,
    down_weight,
    down_bias,
    out_grad,
):

    def fetch_weights():
        return (
            lax.all_gather(ada_weight, "dp", axis=2, tiled=True),
            lax.all_gather(ada_bias, "dp", axis=2, tiled=True),
            lax.all_gather(qkv_weight, "dp", axis=1, tiled=True),
            lax.all_gather(query_bias, "dp", axis=1, tiled=True),
            lax.all_gather(value_bias, "dp", axis=1, tiled=True),
            lax.all_gather(proj_weight, "dp", axis=1, tiled=True),
            lax.all_gather(proj_bias, "dp", axis=1, tiled=True),
            lax.all_gather(up_weight, "dp", axis=0, tiled=True),
            lax.all_gather(up_bias, "dp", axis=1, tiled=True),
            lax.all_gather(down_weight, "dp", axis=1, tiled=True),
            lax.all_gather(down_bias, "dp", axis=1, tiled=True),
        )

    def forward_scan(carried, step_in):
        token_rows, condition_row, scale_row = step_in
        weights_now = fetch_weights()
        output, kept = forward_step(weights_now, token_rows, condition_row, scale_row, head_scale)
        return (carried, (output, kept))

    unused_carry, (outputs, kept_all) = lax.scan(
        forward_scan, jnp.zeros((), jnp.int32), (tokens, condition, scale_index)
    )
    width = tokens.shape[2]
    part_width = qkv_weight.shape[2]
    part_heads = head_scale.shape[0]
    head_dim = part_width // part_heads
    part_ff = up_weight.shape[1]
    zero_grads = (
        jnp.zeros((part_width, 6, width), jnp.float32),
        jnp.zeros((6, part_heads, head_dim), jnp.float32),
        jnp.zeros((3, width, part_width), jnp.float32),
        jnp.zeros((part_heads, head_dim), jnp.float32),
        jnp.zeros((part_heads, head_dim), jnp.float32),
        jnp.zeros((part_heads,), jnp.float32),
        jnp.zeros((part_width, width), jnp.float32),
        jnp.zeros((part_heads, head_dim), jnp.float32),
        jnp.zeros((width, part_ff), jnp.float32),
        jnp.zeros((part_heads, part_ff // part_heads), jnp.float32),
        jnp.zeros((part_ff, width), jnp.float32),
        jnp.zeros((part_heads, head_dim), jnp.float32),
    )

    def backward_scan(totals, step_in):
        kept, token_grad, condition_row, scale_row = step_in
        weights_now = fetch_weights()
        increments, grad_inputs, grad_condition = backward_step(
            weights_now, kept, token_grad, condition_row, scale_row, head_scale
        )
        totals = tuple((running + increment for running, increment in zip(totals, increments)))
        return (totals, (grad_inputs, grad_condition))

    totals, (grad_tokens, grad_condition) = lax.scan(
        backward_scan, zero_grads, (kept_all, out_grad, condition, scale_index), reverse=True
    )
    scale_total = lax.psum(totals[5], "dp")
    reduced = (
        lax.psum_scatter(
            totals[0].astype(jnp.bfloat16), "dp", scatter_dimension=2, tiled=True
        ).astype(jnp.float32),
        lax.psum_scatter(
            totals[1].astype(jnp.bfloat16), "dp", scatter_dimension=2, tiled=True
        ).astype(jnp.float32),
        lax.psum_scatter(
            totals[2].astype(jnp.bfloat16), "dp", scatter_dimension=1, tiled=True
        ).astype(jnp.float32),
        lax.psum_scatter(
            totals[3].astype(jnp.bfloat16), "dp", scatter_dimension=1, tiled=True
        ).astype(jnp.float32),
        lax.psum_scatter(
            totals[4].astype(jnp.bfloat16), "dp", scatter_dimension=1, tiled=True
        ).astype(jnp.float32),
        lax.psum_scatter(
            totals[6].astype(jnp.bfloat16), "dp", scatter_dimension=1, tiled=True
        ).astype(jnp.float32),
        lax.psum_scatter(
            totals[7].astype(jnp.bfloat16), "dp", scatter_dimension=1, tiled=True
        ).astype(jnp.float32),
        lax.psum_scatter(
            totals[8].astype(jnp.bfloat16), "dp", scatter_dimension=0, tiled=True
        ).astype(jnp.float32),
        lax.psum_scatter(
            totals[9].astype(jnp.bfloat16), "dp", scatter_dimension=1, tiled=True
        ).astype(jnp.float32),
        lax.psum_scatter(
            totals[10].astype(jnp.bfloat16), "dp", scatter_dimension=1, tiled=True
        ).astype(jnp.float32),
        lax.psum_scatter(
            totals[11].astype(jnp.bfloat16), "dp", scatter_dimension=1, tiled=True
        ).astype(jnp.float32),
    )
    return (
        outputs,
        grad_tokens,
        grad_condition,
        reduced[0],
        reduced[1],
        reduced[2],
        reduced[3],
        reduced[4],
        scale_total,
        reduced[5],
        reduced[6],
        reduced[7],
        reduced[8],
        reduced[9],
        reduced[10],
    )


GRIDS = {(16, 2): (4, 2, 2)}
MESH_ID = pl.DeviceIdType.MESH
ANY = pl.ANY
F32 = jnp.float32
BF16 = jnp.bfloat16


def place():
    return (lax.axis_index("dp"), lax.axis_index("tensor"))


def coords(grid):
    chip, core = place()
    nz, ny, nx = grid
    return (chip // (ny * nx), (chip // nx) % ny, chip % nx, core)


def greet_all(count):
    chip, core = place()
    me = chip * 2 + core
    barrier = pltpu.get_barrier_semaphore()
    for k in range(1, count):
        peer = (me + k) % count
        pl.semaphore_signal(barrier, inc=1, device_id=(peer // 2, peer % 2), device_id_type=MESH_ID)
    pl.semaphore_wait(barrier, count - 1)


def remote(src, dst, send_sem, recv_sem, device):
    return pltpu.make_async_remote_copy(
        src_ref=src,
        dst_ref=dst,
        send_sem=send_sem,
        recv_sem=recv_sem,
        device_id=device,
        device_id_type=MESH_ID,
    )


def swap_kernel(count, to_all, src_ref, dst_ref, local_sem, send_sem, recv_sem):
    chip, core = place()
    me = chip * 2 + core
    greet_all(count)
    own = pltpu.make_async_copy(src_ref if to_all else src_ref.at[me], dst_ref.at[me], local_sem)
    own.start()
    copies = []
    for k in range(1, count):
        peer = (me + k) % count
        copy = remote(
            src_ref if to_all else src_ref.at[peer],
            dst_ref.at[me],
            send_sem.at[k - 1],
            recv_sem.at[k - 1],
            (peer // 2, peer % 2),
        )
        copy.start()
        copies.append(copy)
    own.wait()
    for copy in copies:
        copy.wait()


def swap(values, count, to_all, collective_id, name):
    block = values.shape if to_all else values.shape[1:]
    return pl.pallas_call(
        functools.partial(swap_kernel, count, to_all),
        out_shape=jax.ShapeDtypeStruct((count,) + block, values.dtype),
        in_specs=[pl.BlockSpec(memory_space=pltpu.VMEM)],
        out_specs=pl.BlockSpec(memory_space=pltpu.VMEM),
        scratch_shapes=[
            pltpu.SemaphoreType.DMA,
            pltpu.SemaphoreType.DMA((count - 1,)),
            pltpu.SemaphoreType.DMA((count - 1,)),
        ],
        compiler_params=pltpu.CompilerParams(collective_id=collective_id, has_side_effects=True),
        name=name,
    )(values)


def gather_kernel(
    grid, chunks, shard_ref, tok_ref, grad_ref, full_ref, tok_out, grad_out, local_sem, z_send, z_recv, p_send, p_recv, t_send, t_recv
):
    nz, ny, nx = grid
    half = nz // 2
    z, y, x, core = coords(grid)

    def dev(z_at, y_at, x_at):
        return ((z_at * ny + y_at) * nx + x_at, core)

    x_peer = dev(z, y, 1 - x)
    y_peer = dev(z, 1 - y, x)
    sibling = (place()[0], 1 - core)
    greet_all(nz * ny * nx * 2)
    swaps = []
    for i, (src, dst) in enumerate(((tok_ref, tok_out), (grad_ref, grad_out))):
        own = pltpu.make_async_copy(src, dst.at[core], local_sem.at[chunks + i])
        own.start()
        copy = remote(src, dst.at[core], t_send.at[i], t_recv.at[i], sibling)
        copy.start()
        swaps += [own, copy]

    def own_copy(c):
        return pltpu.make_async_copy(shard_ref.at[c], full_ref.at[c, z, y, x], local_sem.at[c])

    def z_copies(c):
        return [
            remote(
                shard_ref.at[c],
                full_ref.at[c, z, y, x],
                z_send.at[c, k - 1],
                z_recv.at[c, k - 1],
                dev((z + k) % nz, y, x),
            )
            for k in range(1, nz)
        ]

    def first_copies(c):
        low = full_ref.at[c, pl.ds(0, half), y, x]
        high = full_ref.at[c, pl.ds(half, half), y, x]
        return [
            remote(low, low, p_send.at[c, 0], p_recv.at[c, 0], x_peer),
            remote(high, high, p_send.at[c, 1], p_recv.at[c, 1], y_peer),
        ]

    def second_copies(c):
        low = full_ref.at[c, pl.ds(0, half), y]
        high = full_ref.at[c, pl.ds(half, half), :, x]
        return [
            remote(low, low, p_send.at[c, 2], p_recv.at[c, 2], y_peer),
            remote(high, high, p_send.at[c, 3], p_recv.at[c, 3], x_peer),
        ]

    ahead = 2
    for t in range(-ahead, chunks + 2):
        if 0 <= t + ahead < chunks:
            c = t + ahead
            own_copy(c).start()
            for copy in z_copies(c):
                copy.start()
        if 0 <= t < chunks:
            own_copy(t).wait()
            for copy in z_copies(t):
                copy.wait_recv()
            for copy in first_copies(t):
                copy.start()
        if 0 <= t - 1 < chunks:
            for copy in first_copies(t - 1):
                copy.wait_recv()
            for copy in second_copies(t - 1):
                copy.start()
        if 0 <= t - 2 < chunks:
            for copy in second_copies(t - 2):
                copy.wait_recv()
    for c in range(chunks):
        for copy in z_copies(c) + first_copies(c) + second_copies(c):
            copy.wait_send()
    for copy in swaps:
        copy.wait()


def gather_weights(grid, shard, tok, grad, collective_id):
    nz, ny, nx = grid
    chunks = shard.shape[0]
    return pl.pallas_call(
        functools.partial(gather_kernel, grid, chunks),
        out_shape=[
            jax.ShapeDtypeStruct((chunks, nz, ny, nx) + shard.shape[1:], shard.dtype),
            jax.ShapeDtypeStruct((2,) + tok.shape, tok.dtype),
            jax.ShapeDtypeStruct((2,) + grad.shape, grad.dtype),
        ],
        in_specs=[pl.BlockSpec(memory_space=ANY)] * 3,
        out_specs=[pl.BlockSpec(memory_space=ANY)] * 3,
        scratch_shapes=[
            pltpu.SemaphoreType.DMA((chunks + 2,)),
            pltpu.SemaphoreType.DMA((chunks, nz - 1)),
            pltpu.SemaphoreType.DMA((chunks, nz - 1)),
            pltpu.SemaphoreType.DMA((chunks, 4)),
            pltpu.SemaphoreType.DMA((chunks, 4)),
            pltpu.SemaphoreType.DMA((2,)),
            pltpu.SemaphoreType.DMA((2,)),
        ],
        compiler_params=pltpu.CompilerParams(collective_id=collective_id, has_side_effects=True),
        name="gather_weights",
    )(shard, tok, grad)


def reduce_kernel(
    grid,
    chunks,
    full_ref,
    out_ref,
    keep_low,
    keep_high,
    got_low,
    got_high,
    next_low,
    next_high,
    column,
    got_z,
    local_sem,
    p_send,
    p_recv,
    z_send,
    z_recv,
):
    nz, ny, nx = grid
    half = nz // 2
    z, y, x, core = coords(grid)

    def dev(z_at, y_at, x_at):
        return ((z_at * ny + y_at) * nx + x_at, core)

    x_peer = dev(z, y, 1 - x)
    y_peer = dev(z, 1 - y, x)
    greet_all(nz * ny * nx * 2)

    def own_copies(c):
        return [
            pltpu.make_async_copy(full_ref.at[c, pl.ds(0, half), y], keep_low.at[c], local_sem.at[c, 0]),
            pltpu.make_async_copy(
                full_ref.at[c, pl.ds(half, half), :, x], keep_high.at[c], local_sem.at[c, 1]
            ),
        ]

    def first_copies(c):
        return [
            remote(
                full_ref.at[c, pl.ds(0, half), 1 - y], got_low.at[c], p_send.at[c, 0], p_recv.at[c, 0], y_peer
            ),
            remote(
                full_ref.at[c, pl.ds(half, half), :, 1 - x],
                got_high.at[c],
                p_send.at[c, 1],
                p_recv.at[c, 1],
                x_peer,
            ),
        ]

    def second_copies(c):
        return [
            remote(keep_low.at[c, :, 1 - x], next_low.at[c], p_send.at[c, 2], p_recv.at[c, 2], x_peer),
            remote(keep_high.at[c, :, 1 - y], next_high.at[c], p_send.at[c, 3], p_recv.at[c, 3], y_peer),
        ]

    def z_copies(c):
        return [
            remote(
                column.at[c, (z + k) % nz],
                got_z.at[c, k - 1],
                z_send.at[c, k - 1],
                z_recv.at[c, k - 1],
                dev((z + k) % nz, y, x),
            )
            for k in range(1, nz)
        ]

    def add(a, b):
        return (a.astype(F32) + b.astype(F32)).astype(BF16)

    ahead = 2
    for t in range(-ahead, chunks + 2):
        if 0 <= t + ahead < chunks:
            c = t + ahead
            for copy in first_copies(c) + own_copies(c):
                copy.start()
        if 0 <= t < chunks:
            for copy in own_copies(t):
                copy.wait()
            for copy in first_copies(t):
                copy.wait_recv()
            keep_low[t] = add(keep_low[t], got_low[t])
            keep_high[t] = add(keep_high[t], got_high[t])
            for copy in second_copies(t):
                copy.start()
        if 0 <= t - 1 < chunks:
            c = t - 1
            for copy in second_copies(c):
                copy.wait_recv()
            column[c, 0:half] = add(keep_low[c, :, x], next_low[c])
            column[c, half:nz] = add(keep_high[c, :, y], next_high[c])
            for copy in z_copies(c):
                copy.start()
        if 0 <= t - 2 < chunks:
            c = t - 2
            for copy in z_copies(c):
                copy.wait_recv()
            total = column[c, z].astype(F32)
            for k in range(nz - 1):
                total = total + got_z[c, k].astype(F32)
            out_ref[c] = total
    for c in range(chunks):
        for copy in first_copies(c) + second_copies(c) + z_copies(c):
            copy.wait_send()


def reduce_weights(grid, full, collective_id):
    nz, ny, nx = grid
    half = nz // 2
    chunks = full.shape[0]
    block = full.shape[4:]
    return pl.pallas_call(
        functools.partial(reduce_kernel, grid, chunks),
        out_shape=jax.ShapeDtypeStruct((chunks,) + block, F32),
        in_specs=[pl.BlockSpec(memory_space=ANY)],
        out_specs=pl.BlockSpec(memory_space=pltpu.VMEM),
        scratch_shapes=[
            pltpu.VMEM((chunks, half, nx) + block, BF16),
            pltpu.VMEM((chunks, half, ny) + block, BF16),
            pltpu.VMEM((chunks, half, nx) + block, BF16),
            pltpu.VMEM((chunks, half, ny) + block, BF16),
            pltpu.VMEM((chunks, half) + block, BF16),
            pltpu.VMEM((chunks, half) + block, BF16),
            pltpu.VMEM((chunks, nz) + block, BF16),
            pltpu.VMEM((chunks, nz - 1) + block, BF16),
            pltpu.SemaphoreType.DMA((chunks, 2)),
            pltpu.SemaphoreType.DMA((chunks, 4)),
            pltpu.SemaphoreType.DMA((chunks, 4)),
            pltpu.SemaphoreType.DMA((chunks, nz - 1)),
            pltpu.SemaphoreType.DMA((chunks, nz - 1)),
        ],
        compiler_params=pltpu.CompilerParams(
            collective_id=collective_id, has_side_effects=True, vmem_limit_bytes=48 * 2**20
        ),
        name="reduce_weights",
    )(full)


def sibling_swap(values):
    return lax.ppermute(values, "tensor", [(0, 1), (1, 0)])


def pad_rows(values, rows):
    count, length = values.shape
    return jnp.pad(values, ((0, 0), (0, rows * 128 - length))).reshape(count, rows, 128)


def fast_device(
    grid,
    tokens,
    condition,
    scale_index,
    ada_weight,
    ada_bias,
    qkv_weight,
    query_bias,
    value_bias,
    head_scale,
    proj_weight,
    proj_bias,
    up_weight,
    up_bias,
    down_weight,
    down_bias,
    out_grad,
):
    nz, ny, nx = grid
    dp = nz * ny * nx
    count = dp * 2
    seqs, own_len, width = tokens.shape
    seq_len = own_len * 2
    part = qkv_weight.shape[2]
    heads = head_scale.shape[0]
    head_dim = part // heads
    own_rows = qkv_weight.shape[1]
    ff_chunks = up_weight.shape[1] // part
    chip, core = place()

    shard = jnp.concatenate(
        [
            qkv_weight,
            proj_weight.T[None],
            up_weight.reshape(own_rows, ff_chunks, part).transpose(1, 0, 2),
            down_weight.T.reshape(own_rows, ff_chunks, part).transpose(1, 0, 2),
        ],
        axis=0,
    )
    full, tok_all, grad_all = gather_weights(
        grid, shard, tokens.transpose(1, 0, 2), out_grad.transpose(1, 0, 2), 0
    )
    full = full.reshape(-1, width, part)
    inputs = tok_all.reshape(seq_len, seqs, width).transpose(1, 0, 2).astype(F32)
    grad_rows = grad_all.reshape(seq_len, seqs, width).transpose(1, 0, 2).astype(F32)

    pieces = [condition, ada_bias, query_bias, value_bias, proj_bias, up_bias, down_bias]
    small = jnp.concatenate([piece.reshape(1, -1) for piece in pieces], axis=1)
    small_rows = -(-small.shape[1] // (16 * 128)) * 16
    every = swap(pad_rows(small, small_rows)[0], count, True, 1, "gather_small")
    every = every.reshape(dp, 2, small_rows * 128)
    parts, at = [], 0
    for piece in pieces:
        parts.append(every[:, :, at : at + piece.size].reshape((dp, 2) + piece.shape).astype(F32))
        at += piece.size
    cond_all = parts[0][:, 0].reshape(dp * seqs, width)
    own_of = lambda values: lax.dynamic_index_in_dim(values, core, 1, keepdims=False)
    spread = lambda values: values.transpose(1, 0, 2).reshape(-1)
    both = lambda values: values.transpose(1, 2, 0, 3).reshape(-1)
    ada_bias_full = parts[1].transpose(2, 1, 3, 0, 4).reshape(6, width)
    query_bias_own = spread(own_of(parts[2]))
    value_bias_own = spread(own_of(parts[3]))
    proj_bias_full = both(parts[4])
    up_bias_own = spread(own_of(parts[5]))
    down_bias_full = both(parts[6])

    cond_half = lax.dynamic_slice_in_dim(cond_all, core * part, part, 1)
    silu_half = jax.nn.silu(cond_half).astype(BF16)
    mod_part = jnp.einsum("sr,rjc->sjc", silu_half, ada_weight, preferred_element_type=F32)
    cols = mod_part.shape[2]
    mod_send = jnp.repeat(pad_rows(mod_part.reshape(dp, seqs * 6 * cols), 8), 2, axis=0)
    mod_got = swap(mod_send, count, False, 2, "swap_modulation")
    mod_got = mod_got.reshape(dp, 2, -1)[:, :, : seqs * 6 * cols].sum(axis=1)
    modulation = mod_got.reshape(dp, seqs, 6, cols).transpose(1, 2, 0, 3).reshape(seqs, 6, width)
    modulation = modulation + ada_bias_full
    mod = [modulation[:, j][:, None, :] for j in range(6)]

    normed_attn, inverse_attn = normalize(inputs)
    mixed_attn = (normed_attn * (1.0 + mod[2]) + mod[4]).astype(BF16)
    projected = jnp.einsum("sld,jdc->jslc", mixed_attn, full[:3], preferred_element_type=F32)
    split = lambda values: values.reshape(seqs, seq_len, heads, head_dim)
    queries = split(projected[0] + query_bias_own)
    keys_raw = split(projected[1])
    values_low = split((projected[2] + value_bias_own).astype(BF16))
    query_inverse = lax.rsqrt(jnp.sum(queries * queries, axis=-1, keepdims=True) + HEAD_EPS)
    key_inverse = lax.rsqrt(jnp.sum(keys_raw * keys_raw, axis=-1, keepdims=True) + HEAD_EPS)
    query_unit = queries * query_inverse
    key_unit = keys_raw * key_inverse
    scale_factor = jnp.exp(head_scale)[:, None]
    query_low = (query_unit * scale_factor).astype(BF16)
    key_low = key_unit.astype(BF16)
    scores = jnp.einsum("sqhe,skhe->shqk", query_low, key_low, preferred_element_type=F32)
    allowed = (scale_index[:, None, :] <= scale_index[:, :, None])[:, None]
    scores = jnp.where(allowed, scores, -1e30)
    row_max = jnp.max(scores, axis=-1, keepdims=True)
    weights_exp = jnp.exp(scores - row_max)
    attn_prob = weights_exp / jnp.sum(weights_exp, axis=-1, keepdims=True)
    prob_low = attn_prob.astype(BF16)
    attended = jnp.einsum("shqk,skhe->sqhe", prob_low, values_low, preferred_element_type=F32)
    attended = attended.reshape(seqs, seq_len, part).astype(BF16)
    branch_part = jnp.einsum("slc,dc->sld", attended, full[3], preferred_element_type=F32).astype(BF16)
    branch_attn = branch_part.astype(F32) + sibling_swap(branch_part).astype(F32) + proj_bias_full
    middle = inputs + mod[0] * branch_attn
    normed_mlp, inverse_mlp = normalize(middle)
    mixed_mlp = (normed_mlp * (1.0 + mod[3]) + mod[5]).astype(BF16)
    up = full[4 : 4 + ff_chunks]
    down = full[4 + ff_chunks :]
    hidden = jnp.einsum("sld,jdf->jslf", mixed_mlp, up, preferred_element_type=F32)
    hidden = hidden + up_bias_own.reshape(ff_chunks, 1, 1, part)
    activated = jax.nn.gelu(hidden, approximate=True).astype(BF16)
    mlp_part = jnp.einsum("jslf,jdf->sld", activated, down, preferred_element_type=F32).astype(BF16)
    branch_mlp = mlp_part.astype(F32) + sibling_swap(mlp_part).astype(F32) + down_bias_full
    output = middle + mod[1] * branch_mlp

    grad_gamma_mlp = jnp.sum(grad_rows * branch_mlp, axis=1)
    grad_branch_mlp = grad_rows * mod[1]
    grad_down_bias = jnp.sum(grad_branch_mlp, axis=(0, 1))
    dm_low = grad_branch_mlp.astype(BF16)
    grad_down = jnp.einsum("sld,jslf->jdf", dm_low, activated, preferred_element_type=F32).astype(BF16)
    grad_act = jnp.einsum("sld,jdf->jslf", dm_low, down, preferred_element_type=F32)
    grad_hidden = grad_act * gelu_slope(hidden)
    grad_up_bias = jnp.sum(grad_hidden, axis=(1, 2)).reshape(-1)
    hidden_low = grad_hidden.astype(BF16)
    grad_up = jnp.einsum("sld,jslf->jdf", mixed_mlp, hidden_low, preferred_element_type=F32).astype(BF16)
    gm_part = jnp.einsum("jslf,jdf->sld", hidden_low, up, preferred_element_type=F32).astype(BF16)
    grad_mixed_mlp = gm_part.astype(F32) + sibling_swap(gm_part).astype(F32)
    grad_scale_mlp = jnp.sum(grad_mixed_mlp * normed_mlp, axis=1)
    grad_shift_mlp = jnp.sum(grad_mixed_mlp, axis=1)
    grad_middle = grad_rows + norm_back(grad_mixed_mlp * (1.0 + mod[3]), normed_mlp, inverse_mlp)
    grad_gamma_attn = jnp.sum(grad_middle * branch_attn, axis=1)
    grad_branch_attn = grad_middle * mod[0]
    grad_proj_bias = jnp.sum(grad_branch_attn, axis=(0, 1))
    da_low = grad_branch_attn.astype(BF16)
    grad_proj = jnp.einsum("sld,slc->dc", da_low, attended, preferred_element_type=F32).astype(BF16)
    grad_attended = split(
        jnp.einsum("sld,dc->slc", da_low, full[3], preferred_element_type=F32).astype(BF16)
    )
    grad_prob = jnp.einsum("sqhe,skhe->shqk", grad_attended, values_low, preferred_element_type=F32)
    row_dot = jnp.sum(attn_prob * grad_prob, axis=-1, keepdims=True)
    grad_scores = (attn_prob * (grad_prob - row_dot)).astype(BF16)
    grad_values = jnp.einsum("shqk,sqhe->skhe", prob_low, grad_attended, preferred_element_type=F32)
    grad_query_scaled = jnp.einsum("shqk,skhe->sqhe", grad_scores, key_low, preferred_element_type=F32)
    grad_key_unit = jnp.einsum("shqk,sqhe->skhe", grad_scores, query_low, preferred_element_type=F32)
    grad_head_scale = jnp.sum(grad_query_scaled * query_unit, axis=(0, 1, 3)) * jnp.exp(head_scale)
    grad_query_unit = grad_query_scaled * scale_factor
    grad_queries = query_inverse * (
        grad_query_unit - query_unit * jnp.sum(grad_query_unit * query_unit, axis=-1, keepdims=True)
    )
    grad_keys = key_inverse * (
        grad_key_unit - key_unit * jnp.sum(grad_key_unit * key_unit, axis=-1, keepdims=True)
    )
    grad_query_bias = jnp.sum(grad_queries, axis=(0, 1)).reshape(-1)
    grad_value_bias = jnp.sum(grad_values, axis=(0, 1)).reshape(-1)
    qkv_low = jnp.stack([grad_queries, grad_keys, grad_values]).reshape(3, seqs, seq_len, part)
    qkv_low = qkv_low.astype(BF16)
    grad_qkv = jnp.einsum("sld,jslc->jdc", mixed_attn, qkv_low, preferred_element_type=F32).astype(BF16)
    ga_part = jnp.einsum("jslc,jdc->sld", qkv_low, full[:3], preferred_element_type=F32).astype(BF16)
    grad_mixed_attn = ga_part.astype(F32) + sibling_swap(ga_part).astype(F32)
    grad_scale_attn = jnp.sum(grad_mixed_attn * normed_attn, axis=1)
    grad_shift_attn = jnp.sum(grad_mixed_attn, axis=1)
    grad_inputs = grad_middle + norm_back(
        grad_mixed_attn * (1.0 + mod[2]), normed_attn, inverse_attn
    )

    grad_mod = jnp.stack(
        [
            grad_gamma_attn,
            grad_gamma_mlp,
            grad_scale_attn,
            grad_scale_mlp,
            grad_shift_attn,
            grad_shift_mlp,
        ],
        axis=1,
    )
    twice = lambda values: jnp.repeat(values[:, None], 2, axis=1)
    to_owner = lambda values: values.reshape(heads, dp, -1).transpose(1, 0, 2).reshape(dp, -1)
    to_both = lambda values: (
        values.reshape(2, heads, dp, -1).transpose(2, 0, 1, 3).reshape(dp, 2, -1)
    )
    send = jnp.concatenate(
        [
            twice(grad_mod.reshape(seqs, 6, dp, cols).transpose(2, 0, 1, 3).reshape(dp, -1)),
            twice(to_owner(grad_query_bias)),
            twice(to_owner(grad_value_bias)),
            twice(to_owner(grad_up_bias)),
            to_both(grad_proj_bias),
            to_both(grad_down_bias),
            jnp.broadcast_to(grad_head_scale, (dp, 2, heads)),
        ],
        axis=2,
    )
    rows = -(-send.shape[2] // (8 * 128)) * 8
    got = swap(pad_rows(send.reshape(count, -1), rows), count, False, 3, "swap_grads")
    got = own_of(got.reshape(dp, 2, -1))
    n_mod = seqs * 6 * cols
    mod_low = got[:, :n_mod].reshape(dp * seqs, 6, cols)
    grad_ada_bias_cols = jnp.sum(mod_low, axis=0)
    mod_low = mod_low.astype(BF16)
    sums = jnp.sum(got[:, n_mod:], axis=0)
    owned, at = [], 0
    for shape in (query_bias.shape, value_bias.shape, up_bias.shape, proj_bias.shape, down_bias.shape):
        size = shape[0] * shape[1]
        owned.append(sums[at : at + size].reshape(shape))
        at += size
    scale_total = sums[at : at + heads]
    grad_ada = jnp.einsum("sr,sjc->rjc", silu_half, mod_low, preferred_element_type=F32)
    cond_part = jnp.einsum("sjc,rjc->sr", mod_low, ada_weight, preferred_element_type=F32)
    return_send = jnp.repeat(cond_part.reshape(dp, seqs * part // 128, 128), 2, axis=0)
    ada_bias_send = jnp.broadcast_to(
        jnp.pad(grad_ada_bias_cols.reshape(1, -1), ((0, 0), (0, 1024 - 6 * cols))).reshape(1, 8, 128),
        (count, 8, 128),
    )
    last = swap(
        jnp.concatenate([return_send, ada_bias_send], axis=1), count, False, 4, "swap_condition"
    )
    last = own_of(last.reshape(dp, 2, -1))
    grad_silu = jnp.sum(last[:, : seqs * part], axis=0).reshape(seqs, part)
    cond_own = lax.dynamic_slice_in_dim(condition.astype(F32), core * part, part, 1)
    sigmoid = jax.nn.sigmoid(cond_own)
    grad_condition = grad_silu * sigmoid * (1.0 + cond_own * (1.0 - sigmoid))
    ada_cols = last[:, seqs * part : seqs * part + 6 * cols].reshape(dp, 6, cols)
    ada_rows = lax.dynamic_slice_in_dim(ada_cols, core * heads, heads, 0).transpose(1, 0, 2)
    grad_ada_bias = lax.dynamic_slice_in_dim(ada_rows, chip * ada_bias.shape[2], ada_bias.shape[2], 2)

    reduced = reduce_weights(
        grid,
        jnp.concatenate([grad_qkv, grad_proj[None], grad_up, grad_down], axis=0).reshape(
            (-1,) + grid + (own_rows, part)
        ),
        5,
    )
    wide = lambda values: values.transpose(1, 0, 2).reshape(own_rows, -1)
    own_half = lambda values: lax.dynamic_slice_in_dim(values, core * own_len, own_len, 1)
    return (
        own_half(output),
        own_half(grad_inputs),
        grad_condition,
        grad_ada,
        grad_ada_bias,
        reduced[:3],
        owned[0],
        owned[1],
        scale_total,
        reduced[3].T,
        owned[3],
        wide(reduced[4 : 4 + ff_chunks]),
        owned[2],
        wide(reduced[4 + ff_chunks :]).T,
        owned[4],
    )


def solution(mesh):
    in_specs = (
        P("dp", "tensor", None),
        P("dp", None),
        P("dp", None),
        P("tensor", None, "dp"),
        P(None, "tensor", "dp"),
        P(None, "dp", "tensor"),
        P("tensor", "dp"),
        P("tensor", "dp"),
        P("tensor"),
        P("tensor", "dp"),
        P("tensor", "dp"),
        P("dp", "tensor"),
        P("tensor", "dp"),
        P("tensor", "dp"),
        P("tensor", "dp"),
        P("dp", "tensor", None),
    )
    out_specs = (
        P("dp", "tensor", None),
        P("dp", "tensor", None),
        P("dp", "tensor"),
        P("tensor", None, "dp"),
        P(None, "tensor", "dp"),
        P(None, "dp", "tensor"),
        P("tensor", "dp"),
        P("tensor", "dp"),
        P("tensor"),
        P("tensor", "dp"),
        P("tensor", "dp"),
        P("dp", "tensor"),
        P("tensor", "dp"),
        P("tensor", "dp"),
        P("tensor", "dp"),
    )
    grid = GRIDS.get((mesh.shape["dp"], mesh.shape["tensor"]))
    body = on_device if grid is None else functools.partial(fast_device, grid)
    return jax.shard_map(
        body, mesh=mesh, in_specs=in_specs, out_specs=out_specs, check_vma=False
    )
```

```python
import functools

import jax
import jax.numpy as jnp
from jax import lax
from jax.experimental import pallas as pl
from jax.experimental.pallas import tpu as pltpu
from jax.sharding import PartitionSpec as P

NORM_EPS = 1e-06
HEAD_EPS = 1e-06
GELU_COEF = 0.7978845608028654
GELU_CUBE = 0.044715


def normalize(values):
    centred = values - jnp.mean(values, axis=-1, keepdims=True)
    inverse = lax.rsqrt(jnp.mean(centred * centred, axis=-1, keepdims=True) + NORM_EPS)
    return (centred * inverse, inverse)


def norm_back(grad_normed, normed, inverse):
    return inverse * (
        grad_normed
        - jnp.mean(grad_normed, axis=-1, keepdims=True)
        - normed * jnp.mean(grad_normed * normed, axis=-1, keepdims=True)
    )


def gelu_slope(hidden):
    inner = jnp.tanh(GELU_COEF * (hidden + GELU_CUBE * hidden * hidden * hidden))
    return 0.5 * (1.0 + inner) + 0.5 * hidden * (1.0 - inner * inner) * GELU_COEF * (
        1.0 + 3.0 * GELU_CUBE * hidden * hidden
    )


def masked_scores(query_unit, key_unit, scale_factor, scale_row):
    query_low = (query_unit * scale_factor).astype(jnp.bfloat16)
    key_low = key_unit.astype(jnp.bfloat16)
    scores = jnp.einsum("qhe,khe->hqk", query_low, key_low, preferred_element_type=jnp.float32)
    allowed = scale_row[None, :] <= scale_row[:, None]
    return (jnp.where(allowed[None, :, :], scores, -1e30), query_low, key_low)


def attention_core(mixed_all, qkv_full, query_bias_part, value_bias_part, head_scale, scale_row):
    part_width = qkv_full.shape[2]
    part_heads = head_scale.shape[0]
    head_dim = part_width // part_heads
    seq_len = scale_row.shape[0]
    projected = jnp.einsum("ld,jdc->jlc", mixed_all, qkv_full, preferred_element_type=jnp.float32)
    queries = (projected[0] + query_bias_part.reshape(part_width).astype(jnp.float32)).reshape(
        seq_len, part_heads, head_dim
    )
    keys_raw = projected[1].reshape(seq_len, part_heads, head_dim)
    values_low = (projected[2] + value_bias_part.reshape(part_width).astype(jnp.float32)).astype(
        jnp.bfloat16
    )
    values_low = values_low.reshape(seq_len, part_heads, head_dim)
    query_inverse = lax.rsqrt(jnp.sum(queries * queries, axis=-1, keepdims=True) + HEAD_EPS)
    key_inverse = lax.rsqrt(jnp.sum(keys_raw * keys_raw, axis=-1, keepdims=True) + HEAD_EPS)
    query_unit = queries * query_inverse
    key_unit = keys_raw * key_inverse
    scale_factor = jnp.exp(head_scale)[:, None]
    scores, query_low, key_low = masked_scores(query_unit, key_unit, scale_factor, scale_row)
    row_max = jnp.max(scores, axis=-1, keepdims=True)
    weights_exp = jnp.exp(scores - row_max)
    row_total = jnp.sum(weights_exp, axis=-1, keepdims=True)
    attn_prob = weights_exp / row_total
    log_norm = row_max + jnp.log(row_total)
    attended = jnp.einsum(
        "hqk,khe->qhe",
        attn_prob.astype(jnp.bfloat16),
        values_low,
        preferred_element_type=jnp.float32,
    )
    attended = attended.reshape(seq_len, part_width).astype(jnp.bfloat16)
    return (attended, (query_unit, key_unit, query_inverse, key_inverse, values_low, log_norm))


def forward_step(weights, token_rows, condition_row, scale_row, head_scale):
    (
        ada_full,
        ada_bias_part,
        qkv_full,
        query_bias_part,
        value_bias_part,
        proj_full,
        proj_bias_part,
        up_full,
        up_bias_part,
        down_full,
        down_bias_part,
    ) = weights
    width = token_rows.shape[1]
    part_width = qkv_full.shape[2]
    col_start = lax.axis_index("tensor") * part_width
    cond_rows = lax.dynamic_slice_in_dim(
        condition_row.astype(jnp.float32), col_start, part_width, 0
    )
    silu_rows = jax.nn.silu(cond_rows).astype(jnp.bfloat16)
    mod_terms = jnp.einsum("r,rjc->jc", silu_rows, ada_full, preferred_element_type=jnp.float32)
    own_cols = jnp.concatenate(
        [
            ada_bias_part.reshape(6, part_width),
            proj_bias_part.reshape(1, part_width),
            down_bias_part.reshape(1, part_width),
        ],
        axis=0,
    ).astype(jnp.float32)
    placed = lax.dynamic_update_slice(jnp.zeros((8, width), jnp.float32), own_cols, (0, col_start))
    local_mod = placed + jnp.concatenate([mod_terms, jnp.zeros((2, width), jnp.float32)], axis=0)
    modulation = lax.psum(local_mod, "tensor")
    inputs = token_rows.astype(jnp.float32)
    normed_attn, inverse_attn = normalize(inputs)
    mixed_attn = (normed_attn * (1.0 + modulation[2]) + modulation[4]).astype(jnp.bfloat16)
    mixed_all = lax.all_gather(mixed_attn, "tensor", axis=0, tiled=True)
    attended, attn_kept = attention_core(
        mixed_all, qkv_full, query_bias_part, value_bias_part, head_scale, scale_row
    )
    branch_attn = (
        lax.psum_scatter(
            jnp.dot(attended, proj_full, preferred_element_type=jnp.float32).astype(jnp.bfloat16),
            "tensor",
            scatter_dimension=0,
            tiled=True,
        ).astype(jnp.float32)
        + modulation[6]
    )
    middle = inputs + modulation[0] * branch_attn
    normed_mlp, inverse_mlp = normalize(middle)
    mixed_mlp = (normed_mlp * (1.0 + modulation[3]) + modulation[5]).astype(jnp.bfloat16)
    mlp_all = lax.all_gather(mixed_mlp, "tensor", axis=0, tiled=True)
    hidden = jnp.dot(mlp_all, up_full, preferred_element_type=jnp.float32) + up_bias_part.reshape(
        -1
    ).astype(jnp.float32)
    activated = jax.nn.gelu(hidden, approximate=True).astype(jnp.bfloat16)
    branch_mlp = (
        lax.psum_scatter(
            jnp.dot(activated, down_full, preferred_element_type=jnp.float32).astype(jnp.bfloat16),
            "tensor",
            scatter_dimension=0,
            tiled=True,
        ).astype(jnp.float32)
        + modulation[7]
    )
    output = middle + modulation[1] * branch_mlp
    query_unit, key_unit, query_inverse, key_inverse, values_low, log_norm = attn_kept
    kept = (
        modulation,
        normed_attn,
        inverse_attn,
        mixed_all,
        query_unit,
        key_unit,
        query_inverse,
        key_inverse,
        values_low,
        log_norm,
        attended,
        branch_attn,
        normed_mlp,
        inverse_mlp,
        mlp_all,
        hidden,
        activated,
        branch_mlp,
    )
    return (output, kept)


def backward_step(weights, kept, token_grad, condition_row, scale_row, head_scale):
    (
        ada_full,
        ada_bias_part,
        qkv_full,
        query_bias_part,
        value_bias_part,
        proj_full,
        proj_bias_part,
        up_full,
        up_bias_part,
        down_full,
        down_bias_part,
    ) = weights
    (
        modulation,
        normed_attn,
        inverse_attn,
        mixed_all,
        query_unit,
        key_unit,
        query_inverse,
        key_inverse,
        values_low,
        log_norm,
        attended,
        branch_attn,
        normed_mlp,
        inverse_mlp,
        mlp_all,
        hidden,
        activated,
        branch_mlp,
    ) = kept
    part_width = qkv_full.shape[2]
    part_heads = head_scale.shape[0]
    head_dim = part_width // part_heads
    seq_len = scale_row.shape[0]
    scale_factor = jnp.exp(head_scale)[:, None]
    grad_rows = token_grad.astype(jnp.float32)
    grad_branch_mlp = grad_rows * modulation[1]
    grad_gamma_mlp = jnp.sum(grad_rows * branch_mlp, axis=0)
    grad_down_bias = jnp.sum(grad_branch_mlp, axis=0)
    grad_mlp_all = lax.all_gather(
        grad_branch_mlp.astype(jnp.bfloat16), "tensor", axis=0, tiled=True
    )
    grad_down = jnp.einsum("lf,ld->fd", activated, grad_mlp_all, preferred_element_type=jnp.float32)
    grad_act = jnp.einsum("ld,fd->lf", grad_mlp_all, down_full, preferred_element_type=jnp.float32)
    grad_hidden = grad_act * gelu_slope(hidden)
    grad_up_bias = jnp.sum(grad_hidden, axis=0)
    hidden_low = grad_hidden.astype(jnp.bfloat16)
    grad_up = jnp.einsum("ld,lf->df", mlp_all, hidden_low, preferred_element_type=jnp.float32)
    grad_mixed_mlp = lax.psum_scatter(
        jnp.einsum("lf,df->ld", hidden_low, up_full, preferred_element_type=jnp.float32).astype(
            jnp.bfloat16
        ),
        "tensor",
        scatter_dimension=0,
        tiled=True,
    ).astype(jnp.float32)
    grad_scale_mlp = jnp.sum(grad_mixed_mlp * normed_mlp, axis=0)
    grad_shift_mlp = jnp.sum(grad_mixed_mlp, axis=0)
    grad_middle = grad_rows + norm_back(
        grad_mixed_mlp * (1.0 + modulation[3]), normed_mlp, inverse_mlp
    )
    grad_branch_attn = grad_middle * modulation[0]
    grad_gamma_attn = jnp.sum(grad_middle * branch_attn, axis=0)
    grad_proj_bias = jnp.sum(grad_branch_attn, axis=0)
    grad_attn_all = lax.all_gather(
        grad_branch_attn.astype(jnp.bfloat16), "tensor", axis=0, tiled=True
    )
    grad_proj = jnp.einsum("lc,ld->cd", attended, grad_attn_all, preferred_element_type=jnp.float32)
    grad_attended = jnp.einsum(
        "ld,cd->lc", grad_attn_all, proj_full, preferred_element_type=jnp.float32
    )
    grad_attended = grad_attended.astype(jnp.bfloat16).reshape(seq_len, part_heads, head_dim)
    scores, query_low, key_low = masked_scores(query_unit, key_unit, scale_factor, scale_row)
    attn_prob = jnp.exp(scores - log_norm)
    grad_prob = jnp.einsum(
        "qhe,khe->hqk", grad_attended, values_low, preferred_element_type=jnp.float32
    )
    row_dot = jnp.sum(attn_prob * grad_prob, axis=-1, keepdims=True)
    grad_scores = (attn_prob * (grad_prob - row_dot)).astype(jnp.bfloat16)
    grad_values = jnp.einsum(
        "hqk,qhe->khe",
        attn_prob.astype(jnp.bfloat16),
        grad_attended,
        preferred_element_type=jnp.float32,
    )
    grad_query_scaled = jnp.einsum(
        "hqk,khe->qhe", grad_scores, key_low, preferred_element_type=jnp.float32
    )
    grad_key_unit = jnp.einsum(
        "hqk,qhe->khe", grad_scores, query_low, preferred_element_type=jnp.float32
    )
    grad_head_scale = jnp.sum(grad_query_scaled * query_unit, axis=(0, 2)) * jnp.exp(head_scale)
    grad_query_unit = grad_query_scaled * scale_factor
    grad_queries = query_inverse * (
        grad_query_unit - query_unit * jnp.sum(grad_query_unit * query_unit, axis=-1, keepdims=True)
    )
    grad_keys = key_inverse * (
        grad_key_unit - key_unit * jnp.sum(grad_key_unit * key_unit, axis=-1, keepdims=True)
    )
    grad_query_bias = jnp.sum(grad_queries, axis=0)
    grad_value_bias = jnp.sum(grad_values, axis=0)
    grad_projected = (
        jnp.stack([grad_queries, grad_keys, grad_values])
        .reshape(3, seq_len, part_width)
        .astype(jnp.bfloat16)
    )
    grad_qkv = jnp.einsum(
        "ld,jlc->jdc", mixed_all, grad_projected, preferred_element_type=jnp.float32
    )
    grad_mixed_attn = lax.psum_scatter(
        jnp.einsum(
            "jlc,jdc->ld", grad_projected, qkv_full, preferred_element_type=jnp.float32
        ).astype(jnp.bfloat16),
        "tensor",
        scatter_dimension=0,
        tiled=True,
    ).astype(jnp.float32)
    grad_scale_attn = jnp.sum(grad_mixed_attn * normed_attn, axis=0)
    grad_shift_attn = jnp.sum(grad_mixed_attn, axis=0)
    grad_inputs = grad_middle + norm_back(
        grad_mixed_attn * (1.0 + modulation[2]), normed_attn, inverse_attn
    )
    mod_rows = jnp.stack(
        [
            grad_gamma_attn,
            grad_gamma_mlp,
            grad_scale_attn,
            grad_scale_mlp,
            grad_shift_attn,
            grad_shift_mlp,
            grad_proj_bias,
            grad_down_bias,
        ]
    )
    grad_modulation = lax.psum(mod_rows.astype(jnp.bfloat16), "tensor").astype(jnp.float32)
    col_start = lax.axis_index("tensor") * part_width
    cond_rows = lax.dynamic_slice_in_dim(
        condition_row.astype(jnp.float32), col_start, part_width, 0
    )
    silu_rows = jax.nn.silu(cond_rows).astype(jnp.bfloat16)
    mod_low = grad_modulation[:6].astype(jnp.bfloat16)
    grad_ada = jnp.einsum("r,jc->rjc", silu_rows, mod_low, preferred_element_type=jnp.float32)
    grad_silu = jnp.einsum("jc,rjc->r", mod_low, ada_full, preferred_element_type=jnp.float32)
    sigmoid_rows = jax.nn.sigmoid(cond_rows)
    grad_condition = grad_silu * sigmoid_rows * (1.0 + cond_rows * (1.0 - sigmoid_rows))
    own_cols = lax.dynamic_slice_in_dim(grad_modulation, col_start, part_width, 1)
    increments = (
        grad_ada,
        own_cols[:6].reshape(6, part_heads, head_dim),
        grad_qkv,
        grad_query_bias,
        grad_value_bias,
        grad_head_scale,
        grad_proj,
        own_cols[6].reshape(part_heads, head_dim),
        grad_up,
        grad_up_bias.reshape(part_heads, -1),
        grad_down,
        own_cols[7].reshape(part_heads, head_dim),
    )
    return (increments, grad_inputs, grad_condition)


def on_device(
    tokens,
    condition,
    scale_index,
    ada_weight,
    ada_bias,
    qkv_weight,
    query_bias,
    value_bias,
    head_scale,
    proj_weight,
    proj_bias,
    up_weight,
    up_bias,
    down_weight,
    down_bias,
    out_grad,
):

    def fetch_weights():
        return (
            lax.all_gather(ada_weight, "dp", axis=2, tiled=True),
            lax.all_gather(ada_bias, "dp", axis=2, tiled=True),
            lax.all_gather(qkv_weight, "dp", axis=1, tiled=True),
            lax.all_gather(query_bias, "dp", axis=1, tiled=True),
            lax.all_gather(value_bias, "dp", axis=1, tiled=True),
            lax.all_gather(proj_weight, "dp", axis=1, tiled=True),
            lax.all_gather(proj_bias, "dp", axis=1, tiled=True),
            lax.all_gather(up_weight, "dp", axis=0, tiled=True),
            lax.all_gather(up_bias, "dp", axis=1, tiled=True),
            lax.all_gather(down_weight, "dp", axis=1, tiled=True),
            lax.all_gather(down_bias, "dp", axis=1, tiled=True),
        )

    def forward_scan(carried, step_in):
        token_rows, condition_row, scale_row = step_in
        weights_now = fetch_weights()
        output, kept = forward_step(weights_now, token_rows, condition_row, scale_row, head_scale)
        return (carried, (output, kept))

    unused_carry, (outputs, kept_all) = lax.scan(
        forward_scan, jnp.zeros((), jnp.int32), (tokens, condition, scale_index)
    )
    width = tokens.shape[2]
    part_width = qkv_weight.shape[2]
    part_heads = head_scale.shape[0]
    head_dim = part_width // part_heads
    part_ff = up_weight.shape[1]
    zero_grads = (
        jnp.zeros((part_width, 6, width), jnp.float32),
        jnp.zeros((6, part_heads, head_dim), jnp.float32),
        jnp.zeros((3, width, part_width), jnp.float32),
        jnp.zeros((part_heads, head_dim), jnp.float32),
        jnp.zeros((part_heads, head_dim), jnp.float32),
        jnp.zeros((part_heads,), jnp.float32),
        jnp.zeros((part_width, width), jnp.float32),
        jnp.zeros((part_heads, head_dim), jnp.float32),
        jnp.zeros((width, part_ff), jnp.float32),
        jnp.zeros((part_heads, part_ff // part_heads), jnp.float32),
        jnp.zeros((part_ff, width), jnp.float32),
        jnp.zeros((part_heads, head_dim), jnp.float32),
    )

    def backward_scan(totals, step_in):
        kept, token_grad, condition_row, scale_row = step_in
        weights_now = fetch_weights()
        increments, grad_inputs, grad_condition = backward_step(
            weights_now, kept, token_grad, condition_row, scale_row, head_scale
        )
        totals = tuple((running + increment for running, increment in zip(totals, increments)))
        return (totals, (grad_inputs, grad_condition))

    totals, (grad_tokens, grad_condition) = lax.scan(
        backward_scan, zero_grads, (kept_all, out_grad, condition, scale_index), reverse=True
    )
    scale_total = lax.psum(totals[5], "dp")
    reduced = (
        lax.psum_scatter(
            totals[0].astype(jnp.bfloat16), "dp", scatter_dimension=2, tiled=True
        ).astype(jnp.float32),
        lax.psum_scatter(
            totals[1].astype(jnp.bfloat16), "dp", scatter_dimension=2, tiled=True
        ).astype(jnp.float32),
        lax.psum_scatter(
            totals[2].astype(jnp.bfloat16), "dp", scatter_dimension=1, tiled=True
        ).astype(jnp.float32),
        lax.psum_scatter(
            totals[3].astype(jnp.bfloat16), "dp", scatter_dimension=1, tiled=True
        ).astype(jnp.float32),
        lax.psum_scatter(
            totals[4].astype(jnp.bfloat16), "dp", scatter_dimension=1, tiled=True
        ).astype(jnp.float32),
        lax.psum_scatter(
            totals[6].astype(jnp.bfloat16), "dp", scatter_dimension=1, tiled=True
        ).astype(jnp.float32),
        lax.psum_scatter(
            totals[7].astype(jnp.bfloat16), "dp", scatter_dimension=1, tiled=True
        ).astype(jnp.float32),
        lax.psum_scatter(
            totals[8].astype(jnp.bfloat16), "dp", scatter_dimension=0, tiled=True
        ).astype(jnp.float32),
        lax.psum_scatter(
            totals[9].astype(jnp.bfloat16), "dp", scatter_dimension=1, tiled=True
        ).astype(jnp.float32),
        lax.psum_scatter(
            totals[10].astype(jnp.bfloat16), "dp", scatter_dimension=1, tiled=True
        ).astype(jnp.float32),
        lax.psum_scatter(
            totals[11].astype(jnp.bfloat16), "dp", scatter_dimension=1, tiled=True
        ).astype(jnp.float32),
    )
    return (
        outputs,
        grad_tokens,
        grad_condition,
        reduced[0],
        reduced[1],
        reduced[2],
        reduced[3],
        reduced[4],
        scale_total,
        reduced[5],
        reduced[6],
        reduced[7],
        reduced[8],
        reduced[9],
        reduced[10],
    )


GRIDS = {(16, 2): (4, 2, 2)}
MESH_ID = pl.DeviceIdType.MESH
ANY = pl.ANY
F32 = jnp.float32
BF16 = jnp.bfloat16
SCALES = 10
MASK = -16384.0


def place():
    return (lax.axis_index("dp"), lax.axis_index("tensor"))


def coords(grid):
    chip, core = place()
    nz, ny, nx = grid
    return (chip // (ny * nx), (chip // nx) % ny, chip % nx, core)


def greet_all(count):
    chip, core = place()
    me = chip * 2 + core
    barrier = pltpu.get_barrier_semaphore()
    for k in range(1, count):
        peer = (me + k) % count
        pl.semaphore_signal(barrier, inc=1, device_id=(peer // 2, peer % 2), device_id_type=MESH_ID)
    pl.semaphore_wait(barrier, count - 1)


def remote(src, dst, send_sem, recv_sem, device):
    return pltpu.make_async_remote_copy(
        src_ref=src,
        dst_ref=dst,
        send_sem=send_sem,
        recv_sem=recv_sem,
        device_id=device,
        device_id_type=MESH_ID,
    )


def swap_kernel(count, to_all, src_ref, dst_ref, local_sem, send_sem, recv_sem):
    chip, core = place()
    me = chip * 2 + core
    greet_all(count)
    own = pltpu.make_async_copy(src_ref if to_all else src_ref.at[me], dst_ref.at[me], local_sem)
    own.start()
    copies = []
    for k in range(1, count):
        peer = (me + k) % count
        copy = remote(
            src_ref if to_all else src_ref.at[peer],
            dst_ref.at[me],
            send_sem.at[k - 1],
            recv_sem.at[k - 1],
            (peer // 2, peer % 2),
        )
        copy.start()
        copies.append(copy)
    own.wait()
    for copy in copies:
        copy.wait()


def swap(values, count, to_all, collective_id, name):
    block = values.shape if to_all else values.shape[1:]
    return pl.pallas_call(
        functools.partial(swap_kernel, count, to_all),
        out_shape=jax.ShapeDtypeStruct((count,) + block, values.dtype),
        in_specs=[pl.BlockSpec(memory_space=pltpu.VMEM)],
        out_specs=pl.BlockSpec(memory_space=pltpu.VMEM),
        scratch_shapes=[
            pltpu.SemaphoreType.DMA,
            pltpu.SemaphoreType.DMA((count - 1,)),
            pltpu.SemaphoreType.DMA((count - 1,)),
        ],
        compiler_params=pltpu.CompilerParams(collective_id=collective_id, has_side_effects=True),
        name=name,
    )(values)


def gather_kernel(
    grid, chunks, shard_ref, tok_ref, grad_ref, full_ref, tok_out, grad_out, local_sem, z_send, z_recv, p_send, p_recv, t_send, t_recv
):
    nz, ny, nx = grid
    half = nz // 2
    z, y, x, core = coords(grid)

    def dev(z_at, y_at, x_at):
        return ((z_at * ny + y_at) * nx + x_at, core)

    x_peer = dev(z, y, 1 - x)
    y_peer = dev(z, 1 - y, x)
    sibling = (place()[0], 1 - core)
    greet_all(nz * ny * nx * 2)
    swaps = []
    for i, (src, dst) in enumerate(((tok_ref, tok_out), (grad_ref, grad_out))):
        own = pltpu.make_async_copy(src, dst.at[:, core], local_sem.at[chunks + i])
        own.start()
        copy = remote(src, dst.at[:, core], t_send.at[i], t_recv.at[i], sibling)
        copy.start()
        swaps += [own, copy]

    def own_copy(c):
        return pltpu.make_async_copy(shard_ref.at[c], full_ref.at[c, z, y, x], local_sem.at[c])

    def z_copies(c):
        return [
            remote(
                shard_ref.at[c],
                full_ref.at[c, z, y, x],
                z_send.at[c, k - 1],
                z_recv.at[c, k - 1],
                dev((z + k) % nz, y, x),
            )
            for k in range(1, nz)
        ]

    def first_copies(c):
        low = full_ref.at[c, pl.ds(0, half), y, x]
        high = full_ref.at[c, pl.ds(half, half), y, x]
        return [
            remote(low, low, p_send.at[c, 0], p_recv.at[c, 0], x_peer),
            remote(high, high, p_send.at[c, 1], p_recv.at[c, 1], y_peer),
        ]

    def second_copies(c):
        low = full_ref.at[c, pl.ds(0, half), y]
        high = full_ref.at[c, pl.ds(half, half), :, x]
        return [
            remote(low, low, p_send.at[c, 2], p_recv.at[c, 2], y_peer),
            remote(high, high, p_send.at[c, 3], p_recv.at[c, 3], x_peer),
        ]

    ahead = 2
    for t in range(-ahead, chunks + 2):
        if 0 <= t + ahead < chunks:
            c = t + ahead
            own_copy(c).start()
            for copy in z_copies(c):
                copy.start()
        if 0 <= t < chunks:
            own_copy(t).wait()
            for copy in z_copies(t):
                copy.wait_recv()
            for copy in first_copies(t):
                copy.start()
        if 0 <= t - 1 < chunks:
            for copy in first_copies(t - 1):
                copy.wait_recv()
            for copy in second_copies(t - 1):
                copy.start()
        if 0 <= t - 2 < chunks:
            for copy in second_copies(t - 2):
                copy.wait_recv()
    for c in range(chunks):
        for copy in z_copies(c) + first_copies(c) + second_copies(c):
            copy.wait_send()
    for copy in swaps:
        copy.wait()


def gather_weights(grid, shard, tok, grad, collective_id):
    nz, ny, nx = grid
    chunks = shard.shape[0]
    return pl.pallas_call(
        functools.partial(gather_kernel, grid, chunks),
        out_shape=[
            jax.ShapeDtypeStruct((chunks, nz, ny, nx) + shard.shape[1:], shard.dtype),
            jax.ShapeDtypeStruct((tok.shape[0], 2) + tok.shape[1:], tok.dtype),
            jax.ShapeDtypeStruct((grad.shape[0], 2) + grad.shape[1:], grad.dtype),
        ],
        in_specs=[pl.BlockSpec(memory_space=ANY)] + [pl.BlockSpec(memory_space=pltpu.VMEM)] * 2,
        out_specs=[pl.BlockSpec(memory_space=ANY)] * 3,
        scratch_shapes=[
            pltpu.SemaphoreType.DMA((chunks + 2,)),
            pltpu.SemaphoreType.DMA((chunks, nz - 1)),
            pltpu.SemaphoreType.DMA((chunks, nz - 1)),
            pltpu.SemaphoreType.DMA((chunks, 4)),
            pltpu.SemaphoreType.DMA((chunks, 4)),
            pltpu.SemaphoreType.DMA((2,)),
            pltpu.SemaphoreType.DMA((2,)),
        ],
        compiler_params=pltpu.CompilerParams(collective_id=collective_id, has_side_effects=True),
        name="gather_weights",
    )(shard, tok, grad)


def reduce_kernel(
    grid,
    chunks,
    full_ref,
    out_ref,
    keep_low,
    keep_high,
    got_low,
    got_high,
    next_low,
    next_high,
    column,
    got_z,
    local_sem,
    p_send,
    p_recv,
    z_send,
    z_recv,
):
    nz, ny, nx = grid
    half = nz // 2
    z, y, x, core = coords(grid)

    def dev(z_at, y_at, x_at):
        return ((z_at * ny + y_at) * nx + x_at, core)

    x_peer = dev(z, y, 1 - x)
    y_peer = dev(z, 1 - y, x)
    greet_all(nz * ny * nx * 2)

    def own_copies(c):
        return [
            pltpu.make_async_copy(full_ref.at[c, pl.ds(0, half), y], keep_low.at[c], local_sem.at[c, 0]),
            pltpu.make_async_copy(
                full_ref.at[c, pl.ds(half, half), :, x], keep_high.at[c], local_sem.at[c, 1]
            ),
        ]

    def first_copies(c):
        return [
            remote(
                full_ref.at[c, pl.ds(0, half), 1 - y], got_low.at[c], p_send.at[c, 0], p_recv.at[c, 0], y_peer
            ),
            remote(
                full_ref.at[c, pl.ds(half, half), :, 1 - x],
                got_high.at[c],
                p_send.at[c, 1],
                p_recv.at[c, 1],
                x_peer,
            ),
        ]

    def second_copies(c):
        return [
            remote(keep_low.at[c, :, 1 - x], next_low.at[c], p_send.at[c, 2], p_recv.at[c, 2], x_peer),
            remote(keep_high.at[c, :, 1 - y], next_high.at[c], p_send.at[c, 3], p_recv.at[c, 3], y_peer),
        ]

    def z_copies(c):
        return [
            remote(
                column.at[c, (z + k) % nz],
                got_z.at[c, k - 1],
                z_send.at[c, k - 1],
                z_recv.at[c, k - 1],
                dev((z + k) % nz, y, x),
            )
            for k in range(1, nz)
        ]

    def add(a, b):
        return (a.astype(F32) + b.astype(F32)).astype(BF16)

    ahead = 2
    for t in range(-ahead, chunks + 2):
        if 0 <= t + ahead < chunks:
            c = t + ahead
            for copy in first_copies(c) + own_copies(c):
                copy.start()
        if 0 <= t < chunks:
            for copy in own_copies(t):
                copy.wait()
            for copy in first_copies(t):
                copy.wait_recv()
            keep_low[t] = add(keep_low[t], got_low[t])
            keep_high[t] = add(keep_high[t], got_high[t])
            for copy in second_copies(t):
                copy.start()
        if 0 <= t - 1 < chunks:
            c = t - 1
            for copy in second_copies(c):
                copy.wait_recv()
            column[c, 0:half] = add(keep_low[c, :, x], next_low[c])
            column[c, half:nz] = add(keep_high[c, :, y], next_high[c])
            for copy in z_copies(c):
                copy.start()
        if 0 <= t - 2 < chunks:
            c = t - 2
            for copy in z_copies(c):
                copy.wait_recv()
            total = column[c, z].astype(F32)
            for k in range(nz - 1):
                total = total + got_z[c, k].astype(F32)
            out_ref[c] = total
    for c in range(chunks):
        for copy in first_copies(c) + second_copies(c) + z_copies(c):
            copy.wait_send()


def reduce_weights(grid, full, collective_id):
    nz, ny, nx = grid
    half = nz // 2
    chunks = full.shape[0]
    block = full.shape[4:]
    return pl.pallas_call(
        functools.partial(reduce_kernel, grid, chunks),
        out_shape=jax.ShapeDtypeStruct((chunks,) + block, F32),
        in_specs=[pl.BlockSpec(memory_space=ANY)],
        out_specs=pl.BlockSpec(memory_space=pltpu.VMEM),
        scratch_shapes=[
            pltpu.VMEM((chunks, half, nx) + block, BF16),
            pltpu.VMEM((chunks, half, ny) + block, BF16),
            pltpu.VMEM((chunks, half, nx) + block, BF16),
            pltpu.VMEM((chunks, half, ny) + block, BF16),
            pltpu.VMEM((chunks, half) + block, BF16),
            pltpu.VMEM((chunks, half) + block, BF16),
            pltpu.VMEM((chunks, nz) + block, BF16),
            pltpu.VMEM((chunks, nz - 1) + block, BF16),
            pltpu.SemaphoreType.DMA((chunks, 2)),
            pltpu.SemaphoreType.DMA((chunks, 4)),
            pltpu.SemaphoreType.DMA((chunks, 4)),
            pltpu.SemaphoreType.DMA((chunks, nz - 1)),
            pltpu.SemaphoreType.DMA((chunks, nz - 1)),
        ],
        compiler_params=pltpu.CompilerParams(
            collective_id=collective_id, has_side_effects=True, vmem_limit_bytes=48 * 2**20
        ),
        name="reduce_weights",
    )(full)


def dot(a, b):
    return jnp.dot(a, b, preferred_element_type=F32)


def dot_nt(a, b):
    return lax.dot_general(a, b, (((1,), (1,)), ((), ())), preferred_element_type=F32)


def dot_tn(a, b):
    return lax.dot_general(a, b, (((0,), (0,)), ((), ())), preferred_element_type=F32)


def lane_code(rows):
    lane = lax.broadcasted_iota(jnp.int32, (rows, 128), 1)
    return lane < 64, lane & 63


def both_heads(pair, spare):
    first, unused = lane_code(pair.shape[0])
    pair = pair.astype(F32)
    if not isinstance(spare, float):
        spare = spare.astype(F32)
    return (
        jnp.where(first, pair, spare).astype(BF16),
        jnp.where(first, spare, pair).astype(BF16),
    )


def column_sum(values):
    return jnp.sum(values, axis=0, keepdims=True)


def transpose_into(dst, src):
    def step(i, carry):
        at = pl.multiple_of(i * 128, 128)
        dst[:, pl.ds(at, 128)] = src[pl.ds(at, 128), :].T
        return carry

    lax.fori_loop(0, src.shape[0] // 128, step, 0)


def for_blocks(count, rows, body):
    def step(a, carry):
        body(a, pl.ds(pl.multiple_of(a * rows, 16), rows))
        return carry

    lax.fori_loop(0, count, step, 0)


def split_kernel(tok_ref, grad_ref, tok_out, grad_out):
    length = tok_ref.shape[0]
    for src, dst in ((tok_ref, tok_out), (grad_ref, grad_out)):
        dst[...] = jnp.zeros_like(dst)
        for s in range(src.shape[1]):
            dst[s, 0:length] = src[:, s, :].astype(F32).astype(BF16)


def attn_forward(sizes, x, mod, scale, w, query_bias, value_bias, key_scale, ones, mixed, qaug, keys, values_low, key_spare, rq, rk, att, part):
    seqs, pad = sizes
    width = x.shape[1]
    pairs = att.shape[1] // 128

    def project(a, rows):
        s = a // 2
        normed, unused = normalize(x[rows, :].astype(F32))
        m = (normed * (1.0 + mod[s, 2:3, :]) + mod[s, 4:5, :]).astype(BF16)
        mixed[rows, :] = m
        first, code = lane_code(pad)
        level = scale[rows, :]
        q_spare = jnp.where(code == level, 1.0, 0.0)
        k_spare = jnp.where(
            code < SCALES, jnp.where(level > code, MASK, 0.0), jnp.where(code < SCALES + 3, 1.0, 0.0)
        )
        key_spare[rows, :] = k_spare.astype(BF16)
        values = dot(m, w[0]) + query_bias[...]
        inv = lax.rsqrt(dot((values * values).astype(BF16), ones[...]) + HEAD_EPS)
        rq[rows, :] = inv.astype(BF16)
        values = values * inv * key_scale[...]
        for p in range(pairs):
            piece = values[:, p * 128 : p * 128 + 128]
            qaug[2 * p, rows, :] = jnp.where(first, piece, q_spare).astype(BF16)
            qaug[2 * p + 1, rows, :] = jnp.where(first, q_spare, piece).astype(BF16)
        values = dot(m, w[1])
        inv = lax.rsqrt(dot((values * values).astype(BF16), ones[...]) + HEAD_EPS)
        rk[rows, :] = inv.astype(BF16)
        keys[rows, :] = (values * inv).astype(BF16)
        values_low[rows, :] = (dot(m, w[2]) + value_bias[...]).astype(BF16)

    for_blocks(seqs * 2, pad, project)

    def attend(i, carry):
        p = i // (seqs * 2)
        block = i % (seqs * 2)
        s = block // 2
        rows = pl.ds(pl.multiple_of(block * pad, 16), pad)
        all_rows = pl.ds(pl.multiple_of(s * 2 * pad, 16), 2 * pad)
        lanes = pl.ds(pl.multiple_of(p * 128, 128), 128)
        first, code = lane_code(pad)
        k_sides = both_heads(keys[all_rows, lanes], key_spare[all_rows, :])
        v_sides = both_heads(values_low[all_rows, lanes], 1.0)
        outs = []
        for side in range(2):
            h = 2 * p + side
            q = qaug[h, rows, :]
            prob = jnp.exp2(dot_nt(q, k_sides[side])).astype(BF16)
            o = dot(prob, v_sides[side])
            outs.append(o / pltpu.roll(o, 64, 1))
            norm = -jnp.log2(o)
            high = norm.astype(BF16)
            rest = norm - high.astype(F32)
            middle = rest.astype(BF16)
            low = (rest - middle.astype(F32)).astype(BF16)
            spare = jnp.logical_not(first) if side == 0 else first
            q = q.astype(F32)
            for at, piece in enumerate((high, middle, low)):
                q = jnp.where(spare & (code == SCALES + at), piece.astype(F32), q)
            qaug[h, rows, :] = q.astype(BF16)
        att[rows, lanes] = jnp.where(first, outs[0], outs[1]).astype(BF16)
        return carry

    lax.fori_loop(0, pairs * seqs * 2, attend, 0)

    def out_project(a, rows):
        part[rows, :] = dot_nt(att[rows, :], w[3]).astype(BF16)

    for_blocks(seqs * 2, pad, out_project)


def mlp_forward(sizes, x, part, part_other, grad, mod, up, up_bias, down, branch, mlp, slope, mlp_part, dm, grad_down, act, turned):
    seqs, pad = sizes
    chunks = up.shape[0]

    def mix(a, rows):
        s = a // 2
        b = part[rows, :].astype(F32) + part_other[rows, :].astype(F32) + mod[s, 6:7, :]
        branch[rows, :] = b.astype(BF16)
        normed, unused = normalize(x[rows, :].astype(F32) + mod[s, 0:1, :] * b)
        mlp[rows, :] = (normed * (1.0 + mod[s, 3:4, :]) + mod[s, 5:6, :]).astype(BF16)
        dm[rows, :] = (grad[rows, :].astype(F32) * mod[s, 1:2, :]).astype(BF16)

    for_blocks(seqs * 2, pad, mix)
    transpose_into(turned, dm)
    for c in range(chunks):

        def raise_rows(a, rows):
            h = dot(mlp[rows, :], up[c]) + up_bias[c]
            square = h * h
            t = jnp.tanh(h * (GELU_COEF + GELU_COEF * GELU_CUBE * square))
            act[c, rows, :] = (0.5 * h * (1.0 + t)).astype(BF16)
            slope[c, rows, :] = (
                0.5 * (1.0 + t)
                + h * (1.0 - t * t) * (0.5 * GELU_COEF + 1.5 * GELU_COEF * GELU_CUBE * square)
            ).astype(BF16)

        for_blocks(seqs * 2, pad, raise_rows)
        grad_down[c] = dot(turned[...], act[c]).astype(BF16)

    def lower(a, rows):
        total = dot_nt(act[0, rows, :], down[0])
        for c in range(1, chunks):
            total = total + dot_nt(act[c, rows, :], down[c])
        mlp_part[rows, :] = total.astype(BF16)

    for_blocks(seqs * 2, pad, lower)


def mlp_backward(sizes, dm, down, slope, mlp, up, grad_part, grad_up, bias_sum, turned, low):
    seqs, pad = sizes
    chunks = up.shape[0]
    transpose_into(turned, mlp)
    bias_sum[...] = jnp.zeros_like(bias_sum)
    for c in range(chunks):

        def back(a, rows):
            gh = dot(dm[rows, :], down[c]) * slope[c, rows, :].astype(F32)
            bias_sum[c] += column_sum(gh)
            low[c, rows, :] = gh.astype(BF16)

        for_blocks(seqs * 2, pad, back)
        grad_up[c] = dot(turned[...], low[c]).astype(BF16)

    def gather(a, rows):
        total = dot_nt(low[0, rows, :], up[0])
        for c in range(1, chunks):
            total = total + dot_nt(low[c, rows, :], up[c])
        grad_part[rows, :] = total.astype(BF16)

    for_blocks(seqs * 2, pad, gather)


def middle_backward(sizes, x, grad, branch, grad_part, grad_other, mod, proj, att, grad_mid, grad_att, grad_proj, stats, da, turned):
    seqs, pad = sizes
    stats[...] = jnp.zeros_like(stats)

    def back(a, rows):
        s = a // 2
        b = branch[rows, :].astype(F32)
        gm = grad_part[rows, :].astype(F32) + grad_other[rows, :].astype(F32)
        normed, inverse = normalize(x[rows, :].astype(F32) + mod[s, 0:1, :] * b)
        stats[s, 1:2, :] += 0.5 * column_sum(gm * normed)
        stats[s, 2:3, :] += 0.5 * column_sum(gm)
        mid = grad[rows, :].astype(F32) + norm_back(gm * (1.0 + mod[s, 3:4, :]), normed, inverse)
        grad_mid[rows, :] = mid.astype(BF16)
        stats[s, 0:1, :] += 0.5 * column_sum(mid * b)
        branch_grad = mid * mod[s, 0:1, :]
        stats[s, 3:4, :] += 0.5 * column_sum(branch_grad)
        low = branch_grad.astype(BF16)
        da[rows, :] = low
        grad_att[rows, :] = dot(low, proj[...]).astype(BF16)

    for_blocks(seqs * 2, pad, back)
    transpose_into(turned, da)
    grad_proj[...] = dot(turned[...], att[...]).astype(BF16)


def attn_backward(
    sizes, mixed, w, qaug, keys, values_low, key_spare, grad_att, rq, rk, key_scale, ones, grad_qkv, grad_part, bias_sum, low, turned
):
    seqs, pad = sizes
    pairs = rq.shape[1] // 128
    bias_sum[...] = jnp.zeros_like(bias_sum)
    transpose_into(turned, mixed)
    ln2 = 0.6931471805599453

    def attend(i, carry):
        p = i // seqs
        s = i % seqs
        start = pl.multiple_of(s * 2 * pad, 16)
        all_rows = pl.ds(start, 2 * pad)
        lanes = pl.ds(pl.multiple_of(p * 128, 128), 128)
        first, code = lane_code(pad)
        first_all, unused = lane_code(2 * pad)
        k_sides = both_heads(keys[all_rows, lanes], key_spare[all_rows, :])
        v_sides = both_heads(values_low[all_rows, lanes], 0.0)
        g_sides = both_heads(grad_att[all_rows, lanes], 0.0)
        grads_k, grads_v, grads_q = [], [], [[], []]
        for side in range(2):
            h = 2 * p + side
            k = k_sides[side]
            v = v_sides[side]
            sum_k = sum_v = None
            for t in range(2):
                rows = pl.ds(pl.multiple_of(start + t * pad, 16), pad)
                q = qaug[h, rows, :]
                g = g_sides[side][t * pad : t * pad + pad]
                prob = jnp.exp2(dot_nt(k, q))
                grad_prob = dot_nt(v, g)
                ds = (prob * (grad_prob - column_sum(prob * grad_prob))).astype(BF16)
                gv = dot(prob.astype(BF16), g)
                gk = dot(ds, q)
                sum_v = gv if t == 0 else sum_v + gv
                sum_k = gk if t == 0 else sum_k + gk
                grads_q[t].append(dot_tn(ds, k))
            grads_k.append(sum_k)
            grads_v.append(sum_v)
        for t in range(2):
            rows = pl.ds(pl.multiple_of(start + t * pad, 16), pad)
            gq = jnp.where(first, grads_q[t][0], grads_q[t][1])
            q = jnp.where(first, qaug[2 * p, rows, :].astype(F32), qaug[2 * p + 1, rows, :].astype(F32))
            bias_sum[2:3, lanes] += ln2 * column_sum(gq * q)
            low[0, rows, lanes] = gq.astype(BF16)
        low[1, all_rows, lanes] = (ln2 * jnp.where(first_all, grads_k[0], grads_k[1])).astype(BF16)
        low[2, all_rows, lanes] = jnp.where(first_all, grads_v[0], grads_v[1]).astype(BF16)
        return carry

    lax.fori_loop(0, pairs * seqs, attend, 0)

    def finish(a, rows):
        first, code = lane_code(pad)

        scale = key_scale[...]
        unit = jnp.concatenate(
            [
                jnp.where(first, qaug[2 * p, rows, :].astype(F32), qaug[2 * p + 1, rows, :].astype(F32))
                for p in range(pairs)
            ],
            axis=1,
        )
        unit = unit / scale
        f = low[0, rows, :].astype(F32) * (scale * ln2)
        product = f * unit
        gq = rq[rows, :].astype(F32) * (f - unit * dot(product.astype(BF16), ones[...]))
        bias_sum[0:1, :] += column_sum(gq)
        low[0, rows, :] = gq.astype(BF16)
        unit = keys[rows, :].astype(F32)
        f = low[1, rows, :].astype(F32)
        gk = rk[rows, :].astype(F32) * (f - unit * dot((f * unit).astype(BF16), ones[...]))
        low[1, rows, :] = gk.astype(BF16)
        bias_sum[1:2, :] += column_sum(low[2, rows, :].astype(F32))
        total = dot_nt(low[0, rows, :], w[0])
        for j in range(1, 3):
            total = total + dot_nt(low[j, rows, :], w[j])
        grad_part[rows, :] = total.astype(BF16)

    for_blocks(seqs * 2, pad, finish)
    for j in range(3):
        grad_qkv[j] = dot(turned[...], low[j]).astype(BF16)


def finish_rows(sizes, x, grad, branch, mlp_part, mlp_other, grad_mid, grad_part, grad_other, mod, output, grad_tokens, stats):
    seqs, pad = sizes
    core = lax.axis_index("tensor")
    length = output.shape[0]
    for s in range(seqs):
        rows = pl.ds(pl.multiple_of((s * 2 + core) * pad, 16), pad)
        b = mlp_part[rows, :].astype(F32) + mlp_other[rows, :].astype(F32) + mod[s, 7:8, :]
        g = grad[rows, :].astype(F32)
        xs = x[rows, :].astype(F32)
        middle = xs + mod[s, 0:1, :] * branch[rows, :].astype(F32)
        out = middle + mod[s, 1:2, :] * b
        output[:, s, :] = out[0:length]
        stats[s, 0:1, :] = column_sum(g * b)
        stats[s, 1:2, :] = column_sum(g * mod[s, 1:2, :])
        normed, inverse = normalize(xs)
        gm = grad_part[rows, :].astype(F32) + grad_other[rows, :].astype(F32)
        stats[s, 2:3, :] = column_sum(gm * normed)
        stats[s, 3:4, :] = column_sum(gm)
        gt = grad_mid[rows, :].astype(F32) + norm_back(gm * (1.0 + mod[s, 2:3, :]), normed, inverse)
        grad_tokens[:, s, :] = gt[0:length]
        stats[s, 4:8, :] = jnp.zeros_like(stats[s, 4:8, :])


def run(body, sizes, operands, outs, scratch=(), name=None):
    def kernel(*refs):
        body(sizes, *refs)

    return pl.pallas_call(
        kernel,
        out_shape=[jax.ShapeDtypeStruct(shape, dtype) for shape, dtype in outs],
        in_specs=[pl.BlockSpec(memory_space=pltpu.VMEM)] * len(operands),
        out_specs=[pl.BlockSpec(memory_space=pltpu.VMEM)] * len(outs),
        scratch_shapes=[pltpu.VMEM(shape, dtype) for shape, dtype in scratch],
        compiler_params=pltpu.CompilerParams(vmem_limit_bytes=60 * 2**20),
        name=name,
    )(*operands)


def sibling_swap(values):
    return lax.ppermute(values, "tensor", [(0, 1), (1, 0)])


def pad_rows(values, rows):
    count, length = values.shape
    return jnp.pad(values, ((0, 0), (0, rows * 128 - length))).reshape(count, rows, 128)


def fast_device(
    grid,
    tokens,
    condition,
    scale_index,
    ada_weight,
    ada_bias,
    qkv_weight,
    query_bias,
    value_bias,
    head_scale,
    proj_weight,
    proj_bias,
    up_weight,
    up_bias,
    down_weight,
    down_bias,
    out_grad,
):
    nz, ny, nx = grid
    dp = nz * ny * nx
    count = dp * 2
    seqs, own_len, width = tokens.shape
    seq_len = own_len * 2
    part = qkv_weight.shape[2]
    heads = head_scale.shape[0]
    head_dim = part // heads
    own_rows = qkv_weight.shape[1]
    ff_chunks = up_weight.shape[1] // part
    chip, core = place()

    shard = jnp.concatenate(
        [
            qkv_weight,
            proj_weight.T[None],
            up_weight.reshape(own_rows, ff_chunks, part).transpose(1, 0, 2),
            down_weight.T.reshape(own_rows, ff_chunks, part).transpose(1, 0, 2),
        ],
        axis=0,
    )
    pad = -(-own_len // 16) * 16
    total = seqs * 2 * pad
    sizes = (seqs, pad)
    tok_own, grad_own = run(
        lambda unused, *refs: split_kernel(*refs),
        sizes,
        (tokens.transpose(1, 0, 2), out_grad.transpose(1, 0, 2)),
        [((seqs, pad, width), BF16)] * 2,
        name="split_rows",
    )
    full, x, grad = gather_weights(grid, shard, tok_own, grad_own, 0)
    full = full.reshape(-1, width, part)
    x = x.reshape(total, width)
    grad = grad.reshape(total, width)

    pieces = [condition, ada_bias, query_bias, value_bias, proj_bias, up_bias, down_bias]
    small = jnp.concatenate([piece.reshape(1, -1) for piece in pieces], axis=1)
    small_rows = -(-small.shape[1] // (16 * 128)) * 16
    every = swap(pad_rows(small, small_rows)[0], count, True, 1, "gather_small")
    every = every.reshape(dp, 2, small_rows * 128)
    parts, at = [], 0
    for piece in pieces:
        parts.append(every[:, :, at : at + piece.size].reshape((dp, 2) + piece.shape).astype(F32))
        at += piece.size
    cond_all = parts[0][:, 0].reshape(dp * seqs, width)
    own_of = lambda values: lax.dynamic_index_in_dim(values, core, 1, keepdims=False)
    spread = lambda values: values.transpose(1, 0, 2).reshape(-1)
    both = lambda values: values.transpose(1, 2, 0, 3).reshape(-1)
    ada_bias_full = parts[1].transpose(2, 1, 3, 0, 4).reshape(6, width)
    query_bias_own = spread(own_of(parts[2]))
    value_bias_own = spread(own_of(parts[3]))
    proj_bias_full = both(parts[4])
    up_bias_own = spread(own_of(parts[5]))
    down_bias_full = both(parts[6])

    cond_half = lax.dynamic_slice_in_dim(cond_all, core * part, part, 1)
    silu_half = jax.nn.silu(cond_half).astype(BF16)
    mod_part = jnp.einsum("sr,rjc->sjc", silu_half, ada_weight, preferred_element_type=F32)
    cols = mod_part.shape[2]
    mod_send = jnp.repeat(pad_rows(mod_part.reshape(dp, seqs * 6 * cols), 8), 2, axis=0)
    mod_got = swap(mod_send, count, False, 2, "swap_modulation")
    mod_got = mod_got.reshape(dp, 2, -1)[:, :, : seqs * 6 * cols].sum(axis=1)
    modulation = mod_got.reshape(dp, seqs, 6, cols).transpose(1, 2, 0, 3).reshape(seqs, 6, width)
    modulation = modulation + ada_bias_full
    ends = jnp.stack([proj_bias_full, down_bias_full])
    mod = jnp.concatenate([modulation, jnp.broadcast_to(ends, (seqs,) + ends.shape)], axis=1)

    level = jnp.pad(
        scale_index.reshape(seqs, 2, own_len), ((0, 0), (0, 0), (0, pad - own_len)), constant_values=100
    ).reshape(total, 1)
    key_scale = jnp.repeat(jnp.exp(head_scale) * 1.4426950408889634, head_dim).reshape(1, part)
    head_at = jnp.arange(part) // head_dim
    ones = (head_at[:, None] == head_at[None, :]).astype(BF16)
    wide_rows = ((total, width), BF16)
    part_rows = ((total, part), BF16)
    head_rows = ((heads, total, 2 * head_dim), BF16)
    up = full[4 : 4 + ff_chunks]
    down = full[4 + ff_chunks :]
    ff_rows = ((ff_chunks, total, part), BF16)
    weight_rows = ((width, part), BF16)
    turned = ((width, total), BF16)

    mixed, qaug, keys, values_low, key_spare, rq, rk, att, attn_part = run(
        attn_forward,
        sizes,
        (x, mod, level, full[:4], query_bias_own[None], value_bias_own[None], key_scale, ones),
        [wide_rows, head_rows, part_rows, part_rows, ((total, 128), BF16), part_rows, part_rows, part_rows, wide_rows],
        name="attn_forward",
    )
    branch, mlp, slope, mlp_part, dm, grad_down = run(
        mlp_forward,
        sizes,
        (x, attn_part, sibling_swap(attn_part), grad, mod, up, up_bias_own.reshape(ff_chunks, 1, part), down),
        [wide_rows, wide_rows, ff_rows, wide_rows, wide_rows, ((ff_chunks, width, part), BF16)],
        [ff_rows, turned],
        name="mlp_forward",
    )
    mlp_other = sibling_swap(mlp_part)
    gm_part, grad_up, up_sum = run(
        mlp_backward,
        sizes,
        (dm, down, slope, mlp, up),
        [wide_rows, ((ff_chunks, width, part), BF16), ((ff_chunks, 1, part), F32)],
        [turned, ff_rows],
        name="mlp_backward",
    )
    grad_mid, grad_att, grad_proj, mid_stats = run(
        middle_backward,
        sizes,
        (x, grad, branch, gm_part, sibling_swap(gm_part), mod, full[3], att),
        [wide_rows, part_rows, weight_rows, ((seqs, 4, width), F32)],
        [wide_rows, turned],
        name="middle_backward",
    )
    grad_qkv, ga_part, qkv_sum = run(
        attn_backward,
        sizes,
        (mixed, full[:3], qaug, keys, values_low, key_spare, grad_att, rq, rk, key_scale, ones),
        [((3, width, part), BF16), wide_rows, ((8, part), F32)],
        [((3, total, part), BF16), turned],
        name="attn_backward",
    )
    output, grad_inputs, end_stats = run(
        finish_rows,
        sizes,
        (x, grad, branch, mlp_part, mlp_other, grad_mid, ga_part, sibling_swap(ga_part), mod),
        [((own_len, seqs, width), F32), ((own_len, seqs, width), F32), ((seqs, 8, width), F32)],
        name="finish_rows",
    )
    grad_head_scale = jnp.sum(qkv_sum[2].reshape(heads, head_dim), axis=1)

    grad_mod = jnp.stack(
        [
            mid_stats[:, 0],
            end_stats[:, 0],
            end_stats[:, 2],
            mid_stats[:, 1],
            end_stats[:, 3],
            mid_stats[:, 2],
        ],
        axis=1,
    )
    grad_proj_bias = jnp.sum(mid_stats[:, 3], axis=0)
    grad_down_bias = jnp.sum(end_stats[:, 1], axis=0)
    twice = lambda values: jnp.repeat(values[:, None], 2, axis=1)
    to_owner = lambda values: values.reshape(heads, dp, -1).transpose(1, 0, 2).reshape(dp, -1)
    to_both = lambda values: (
        values.reshape(2, heads, dp, -1).transpose(2, 0, 1, 3).reshape(dp, 2, -1)
    )
    send = jnp.concatenate(
        [
            twice(grad_mod.reshape(seqs, 6, dp, cols).transpose(2, 0, 1, 3).reshape(dp, -1)),
            twice(to_owner(qkv_sum[0])),
            twice(to_owner(qkv_sum[1])),
            twice(to_owner(up_sum)),
            jnp.broadcast_to(grad_head_scale, (dp, 2, heads)),
            to_both(grad_proj_bias),
            to_both(grad_down_bias),
        ],
        axis=2,
    )
    rows = -(-send.shape[2] // (8 * 128)) * 8
    got = swap(pad_rows(send.reshape(count, -1), rows), count, False, 3, "swap_grads")
    got = got.reshape(dp, 2, -1)
    n_mod = seqs * 6 * cols
    mod_low = jnp.sum(got[:, :, :n_mod], axis=1).reshape(dp * seqs, 6, cols)
    grad_ada_bias_cols = jnp.sum(mod_low, axis=0)
    mod_low = mod_low.astype(BF16)
    own_sums = jnp.sum(own_of(got), axis=0)
    all_sums = jnp.sum(got, axis=(0, 1))
    owned, at = [], n_mod
    for piece, sums in (
        (query_bias, own_sums),
        (value_bias, own_sums),
        (up_bias, own_sums),
        (head_scale, own_sums),
        (proj_bias, all_sums),
        (down_bias, all_sums),
    ):
        owned.append(sums[at : at + piece.size].reshape(piece.shape))
        at += piece.size
    grad_ada = jnp.einsum("sr,sjc->rjc", silu_half, mod_low, preferred_element_type=F32)
    cond_part = jnp.einsum("sjc,rjc->sr", mod_low, ada_weight, preferred_element_type=F32)
    return_send = jnp.repeat(cond_part.reshape(dp, seqs * part // 128, 128), 2, axis=0)
    ada_bias_send = jnp.broadcast_to(
        jnp.pad(grad_ada_bias_cols.reshape(1, -1), ((0, 0), (0, 1024 - 6 * cols))).reshape(1, 8, 128),
        (count, 8, 128),
    )
    last = swap(
        jnp.concatenate([return_send, ada_bias_send], axis=1), count, False, 4, "swap_condition"
    )
    last = own_of(last.reshape(dp, 2, -1))
    grad_silu = jnp.sum(last[:, : seqs * part], axis=0).reshape(seqs, part)
    cond_own = lax.dynamic_slice_in_dim(condition.astype(F32), core * part, part, 1)
    sigmoid = jax.nn.sigmoid(cond_own)
    grad_condition = grad_silu * sigmoid * (1.0 + cond_own * (1.0 - sigmoid))
    ada_cols = last[:, seqs * part : seqs * part + 6 * cols].reshape(dp, 6, cols)
    ada_rows = lax.dynamic_slice_in_dim(ada_cols, core * heads, heads, 0).transpose(1, 0, 2)
    grad_ada_bias = lax.dynamic_slice_in_dim(ada_rows, chip * ada_bias.shape[2], ada_bias.shape[2], 2)

    reduced = reduce_weights(
        grid,
        jnp.concatenate([grad_qkv, grad_proj[None], grad_up, grad_down], axis=0).reshape(
            (-1,) + grid + (own_rows, part)
        ),
        5,
    )
    wide = lambda values: values.transpose(1, 0, 2).reshape(own_rows, -1)
    return (
        output.transpose(1, 0, 2),
        grad_inputs.transpose(1, 0, 2),
        grad_condition,
        grad_ada,
        grad_ada_bias,
        reduced[:3],
        owned[0],
        owned[1],
        owned[3],
        reduced[3].T,
        owned[4],
        wide(reduced[4 : 4 + ff_chunks]),
        owned[2],
        wide(reduced[4 + ff_chunks :]).T,
        owned[5],
    )


def solution(mesh):
    in_specs = (
        P("dp", "tensor", None),
        P("dp", None),
        P("dp", None),
        P("tensor", None, "dp"),
        P(None, "tensor", "dp"),
        P(None, "dp", "tensor"),
        P("tensor", "dp"),
        P("tensor", "dp"),
        P("tensor"),
        P("tensor", "dp"),
        P("tensor", "dp"),
        P("dp", "tensor"),
        P("tensor", "dp"),
        P("tensor", "dp"),
        P("tensor", "dp"),
        P("dp", "tensor", None),
    )
    out_specs = (
        P("dp", "tensor", None),
        P("dp", "tensor", None),
        P("dp", "tensor"),
        P("tensor", None, "dp"),
        P(None, "tensor", "dp"),
        P(None, "dp", "tensor"),
        P("tensor", "dp"),
        P("tensor", "dp"),
        P("tensor"),
        P("tensor", "dp"),
        P("tensor", "dp"),
        P("dp", "tensor"),
        P("tensor", "dp"),
        P("tensor", "dp"),
        P("tensor", "dp"),
    )
    grid = GRIDS.get((mesh.shape["dp"], mesh.shape["tensor"]))
    body = on_device if grid is None else functools.partial(fast_device, grid)
    return jax.shard_map(
        body, mesh=mesh, in_specs=in_specs, out_specs=out_specs, check_vma=False
    )
```

```python
import functools

import jax
import jax.numpy as jnp
from jax import lax
from jax.experimental import pallas as pl
from jax.experimental.pallas import tpu as pltpu
from jax.sharding import PartitionSpec as P

NORM_EPS = 1e-06
HEAD_EPS = 1e-06
GELU_COEF = 0.7978845608028654
GELU_CUBE = 0.044715


def normalize(values):
    centred = values - jnp.mean(values, axis=-1, keepdims=True)
    inverse = lax.rsqrt(jnp.mean(centred * centred, axis=-1, keepdims=True) + NORM_EPS)
    return (centred * inverse, inverse)


def norm_back(grad_normed, normed, inverse):
    return inverse * (
        grad_normed
        - jnp.mean(grad_normed, axis=-1, keepdims=True)
        - normed * jnp.mean(grad_normed * normed, axis=-1, keepdims=True)
    )


def gelu_slope(hidden):
    inner = jnp.tanh(GELU_COEF * (hidden + GELU_CUBE * hidden * hidden * hidden))
    return 0.5 * (1.0 + inner) + 0.5 * hidden * (1.0 - inner * inner) * GELU_COEF * (
        1.0 + 3.0 * GELU_CUBE * hidden * hidden
    )


def masked_scores(query_unit, key_unit, scale_factor, scale_row):
    query_low = (query_unit * scale_factor).astype(jnp.bfloat16)
    key_low = key_unit.astype(jnp.bfloat16)
    scores = jnp.einsum("qhe,khe->hqk", query_low, key_low, preferred_element_type=jnp.float32)
    allowed = scale_row[None, :] <= scale_row[:, None]
    return (jnp.where(allowed[None, :, :], scores, -1e30), query_low, key_low)


def attention_core(mixed_all, qkv_full, query_bias_part, value_bias_part, head_scale, scale_row):
    part_width = qkv_full.shape[2]
    part_heads = head_scale.shape[0]
    head_dim = part_width // part_heads
    seq_len = scale_row.shape[0]
    projected = jnp.einsum("ld,jdc->jlc", mixed_all, qkv_full, preferred_element_type=jnp.float32)
    queries = (projected[0] + query_bias_part.reshape(part_width).astype(jnp.float32)).reshape(
        seq_len, part_heads, head_dim
    )
    keys_raw = projected[1].reshape(seq_len, part_heads, head_dim)
    values_low = (projected[2] + value_bias_part.reshape(part_width).astype(jnp.float32)).astype(
        jnp.bfloat16
    )
    values_low = values_low.reshape(seq_len, part_heads, head_dim)
    query_inverse = lax.rsqrt(jnp.sum(queries * queries, axis=-1, keepdims=True) + HEAD_EPS)
    key_inverse = lax.rsqrt(jnp.sum(keys_raw * keys_raw, axis=-1, keepdims=True) + HEAD_EPS)
    query_unit = queries * query_inverse
    key_unit = keys_raw * key_inverse
    scale_factor = jnp.exp(head_scale)[:, None]
    scores, query_low, key_low = masked_scores(query_unit, key_unit, scale_factor, scale_row)
    row_max = jnp.max(scores, axis=-1, keepdims=True)
    weights_exp = jnp.exp(scores - row_max)
    row_total = jnp.sum(weights_exp, axis=-1, keepdims=True)
    attn_prob = weights_exp / row_total
    log_norm = row_max + jnp.log(row_total)
    attended = jnp.einsum(
        "hqk,khe->qhe",
        attn_prob.astype(jnp.bfloat16),
        values_low,
        preferred_element_type=jnp.float32,
    )
    attended = attended.reshape(seq_len, part_width).astype(jnp.bfloat16)
    return (attended, (query_unit, key_unit, query_inverse, key_inverse, values_low, log_norm))


def forward_step(weights, token_rows, condition_row, scale_row, head_scale):
    (
        ada_full,
        ada_bias_part,
        qkv_full,
        query_bias_part,
        value_bias_part,
        proj_full,
        proj_bias_part,
        up_full,
        up_bias_part,
        down_full,
        down_bias_part,
    ) = weights
    width = token_rows.shape[1]
    part_width = qkv_full.shape[2]
    col_start = lax.axis_index("tensor") * part_width
    cond_rows = lax.dynamic_slice_in_dim(
        condition_row.astype(jnp.float32), col_start, part_width, 0
    )
    silu_rows = jax.nn.silu(cond_rows).astype(jnp.bfloat16)
    mod_terms = jnp.einsum("r,rjc->jc", silu_rows, ada_full, preferred_element_type=jnp.float32)
    own_cols = jnp.concatenate(
        [
            ada_bias_part.reshape(6, part_width),
            proj_bias_part.reshape(1, part_width),
            down_bias_part.reshape(1, part_width),
        ],
        axis=0,
    ).astype(jnp.float32)
    placed = lax.dynamic_update_slice(jnp.zeros((8, width), jnp.float32), own_cols, (0, col_start))
    local_mod = placed + jnp.concatenate([mod_terms, jnp.zeros((2, width), jnp.float32)], axis=0)
    modulation = lax.psum(local_mod, "tensor")
    inputs = token_rows.astype(jnp.float32)
    normed_attn, inverse_attn = normalize(inputs)
    mixed_attn = (normed_attn * (1.0 + modulation[2]) + modulation[4]).astype(jnp.bfloat16)
    mixed_all = lax.all_gather(mixed_attn, "tensor", axis=0, tiled=True)
    attended, attn_kept = attention_core(
        mixed_all, qkv_full, query_bias_part, value_bias_part, head_scale, scale_row
    )
    branch_attn = (
        lax.psum_scatter(
            jnp.dot(attended, proj_full, preferred_element_type=jnp.float32).astype(jnp.bfloat16),
            "tensor",
            scatter_dimension=0,
            tiled=True,
        ).astype(jnp.float32)
        + modulation[6]
    )
    middle = inputs + modulation[0] * branch_attn
    normed_mlp, inverse_mlp = normalize(middle)
    mixed_mlp = (normed_mlp * (1.0 + modulation[3]) + modulation[5]).astype(jnp.bfloat16)
    mlp_all = lax.all_gather(mixed_mlp, "tensor", axis=0, tiled=True)
    hidden = jnp.dot(mlp_all, up_full, preferred_element_type=jnp.float32) + up_bias_part.reshape(
        -1
    ).astype(jnp.float32)
    activated = jax.nn.gelu(hidden, approximate=True).astype(jnp.bfloat16)
    branch_mlp = (
        lax.psum_scatter(
            jnp.dot(activated, down_full, preferred_element_type=jnp.float32).astype(jnp.bfloat16),
            "tensor",
            scatter_dimension=0,
            tiled=True,
        ).astype(jnp.float32)
        + modulation[7]
    )
    output = middle + modulation[1] * branch_mlp
    query_unit, key_unit, query_inverse, key_inverse, values_low, log_norm = attn_kept
    kept = (
        modulation,
        normed_attn,
        inverse_attn,
        mixed_all,
        query_unit,
        key_unit,
        query_inverse,
        key_inverse,
        values_low,
        log_norm,
        attended,
        branch_attn,
        normed_mlp,
        inverse_mlp,
        mlp_all,
        hidden,
        activated,
        branch_mlp,
    )
    return (output, kept)


def backward_step(weights, kept, token_grad, condition_row, scale_row, head_scale):
    (
        ada_full,
        ada_bias_part,
        qkv_full,
        query_bias_part,
        value_bias_part,
        proj_full,
        proj_bias_part,
        up_full,
        up_bias_part,
        down_full,
        down_bias_part,
    ) = weights
    (
        modulation,
        normed_attn,
        inverse_attn,
        mixed_all,
        query_unit,
        key_unit,
        query_inverse,
        key_inverse,
        values_low,
        log_norm,
        attended,
        branch_attn,
        normed_mlp,
        inverse_mlp,
        mlp_all,
        hidden,
        activated,
        branch_mlp,
    ) = kept
    part_width = qkv_full.shape[2]
    part_heads = head_scale.shape[0]
    head_dim = part_width // part_heads
    seq_len = scale_row.shape[0]
    scale_factor = jnp.exp(head_scale)[:, None]
    grad_rows = token_grad.astype(jnp.float32)
    grad_branch_mlp = grad_rows * modulation[1]
    grad_gamma_mlp = jnp.sum(grad_rows * branch_mlp, axis=0)
    grad_down_bias = jnp.sum(grad_branch_mlp, axis=0)
    grad_mlp_all = lax.all_gather(
        grad_branch_mlp.astype(jnp.bfloat16), "tensor", axis=0, tiled=True
    )
    grad_down = jnp.einsum("lf,ld->fd", activated, grad_mlp_all, preferred_element_type=jnp.float32)
    grad_act = jnp.einsum("ld,fd->lf", grad_mlp_all, down_full, preferred_element_type=jnp.float32)
    grad_hidden = grad_act * gelu_slope(hidden)
    grad_up_bias = jnp.sum(grad_hidden, axis=0)
    hidden_low = grad_hidden.astype(jnp.bfloat16)
    grad_up = jnp.einsum("ld,lf->df", mlp_all, hidden_low, preferred_element_type=jnp.float32)
    grad_mixed_mlp = lax.psum_scatter(
        jnp.einsum("lf,df->ld", hidden_low, up_full, preferred_element_type=jnp.float32).astype(
            jnp.bfloat16
        ),
        "tensor",
        scatter_dimension=0,
        tiled=True,
    ).astype(jnp.float32)
    grad_scale_mlp = jnp.sum(grad_mixed_mlp * normed_mlp, axis=0)
    grad_shift_mlp = jnp.sum(grad_mixed_mlp, axis=0)
    grad_middle = grad_rows + norm_back(
        grad_mixed_mlp * (1.0 + modulation[3]), normed_mlp, inverse_mlp
    )
    grad_branch_attn = grad_middle * modulation[0]
    grad_gamma_attn = jnp.sum(grad_middle * branch_attn, axis=0)
    grad_proj_bias = jnp.sum(grad_branch_attn, axis=0)
    grad_attn_all = lax.all_gather(
        grad_branch_attn.astype(jnp.bfloat16), "tensor", axis=0, tiled=True
    )
    grad_proj = jnp.einsum("lc,ld->cd", attended, grad_attn_all, preferred_element_type=jnp.float32)
    grad_attended = jnp.einsum(
        "ld,cd->lc", grad_attn_all, proj_full, preferred_element_type=jnp.float32
    )
    grad_attended = grad_attended.astype(jnp.bfloat16).reshape(seq_len, part_heads, head_dim)
    scores, query_low, key_low = masked_scores(query_unit, key_unit, scale_factor, scale_row)
    attn_prob = jnp.exp(scores - log_norm)
    grad_prob = jnp.einsum(
        "qhe,khe->hqk", grad_attended, values_low, preferred_element_type=jnp.float32
    )
    row_dot = jnp.sum(attn_prob * grad_prob, axis=-1, keepdims=True)
    grad_scores = (attn_prob * (grad_prob - row_dot)).astype(jnp.bfloat16)
    grad_values = jnp.einsum(
        "hqk,qhe->khe",
        attn_prob.astype(jnp.bfloat16),
        grad_attended,
        preferred_element_type=jnp.float32,
    )
    grad_query_scaled = jnp.einsum(
        "hqk,khe->qhe", grad_scores, key_low, preferred_element_type=jnp.float32
    )
    grad_key_unit = jnp.einsum(
        "hqk,qhe->khe", grad_scores, query_low, preferred_element_type=jnp.float32
    )
    grad_head_scale = jnp.sum(grad_query_scaled * query_unit, axis=(0, 2)) * jnp.exp(head_scale)
    grad_query_unit = grad_query_scaled * scale_factor
    grad_queries = query_inverse * (
        grad_query_unit - query_unit * jnp.sum(grad_query_unit * query_unit, axis=-1, keepdims=True)
    )
    grad_keys = key_inverse * (
        grad_key_unit - key_unit * jnp.sum(grad_key_unit * key_unit, axis=-1, keepdims=True)
    )
    grad_query_bias = jnp.sum(grad_queries, axis=0)
    grad_value_bias = jnp.sum(grad_values, axis=0)
    grad_projected = (
        jnp.stack([grad_queries, grad_keys, grad_values])
        .reshape(3, seq_len, part_width)
        .astype(jnp.bfloat16)
    )
    grad_qkv = jnp.einsum(
        "ld,jlc->jdc", mixed_all, grad_projected, preferred_element_type=jnp.float32
    )
    grad_mixed_attn = lax.psum_scatter(
        jnp.einsum(
            "jlc,jdc->ld", grad_projected, qkv_full, preferred_element_type=jnp.float32
        ).astype(jnp.bfloat16),
        "tensor",
        scatter_dimension=0,
        tiled=True,
    ).astype(jnp.float32)
    grad_scale_attn = jnp.sum(grad_mixed_attn * normed_attn, axis=0)
    grad_shift_attn = jnp.sum(grad_mixed_attn, axis=0)
    grad_inputs = grad_middle + norm_back(
        grad_mixed_attn * (1.0 + modulation[2]), normed_attn, inverse_attn
    )
    mod_rows = jnp.stack(
        [
            grad_gamma_attn,
            grad_gamma_mlp,
            grad_scale_attn,
            grad_scale_mlp,
            grad_shift_attn,
            grad_shift_mlp,
            grad_proj_bias,
            grad_down_bias,
        ]
    )
    grad_modulation = lax.psum(mod_rows.astype(jnp.bfloat16), "tensor").astype(jnp.float32)
    col_start = lax.axis_index("tensor") * part_width
    cond_rows = lax.dynamic_slice_in_dim(
        condition_row.astype(jnp.float32), col_start, part_width, 0
    )
    silu_rows = jax.nn.silu(cond_rows).astype(jnp.bfloat16)
    mod_low = grad_modulation[:6].astype(jnp.bfloat16)
    grad_ada = jnp.einsum("r,jc->rjc", silu_rows, mod_low, preferred_element_type=jnp.float32)
    grad_silu = jnp.einsum("jc,rjc->r", mod_low, ada_full, preferred_element_type=jnp.float32)
    sigmoid_rows = jax.nn.sigmoid(cond_rows)
    grad_condition = grad_silu * sigmoid_rows * (1.0 + cond_rows * (1.0 - sigmoid_rows))
    own_cols = lax.dynamic_slice_in_dim(grad_modulation, col_start, part_width, 1)
    increments = (
        grad_ada,
        own_cols[:6].reshape(6, part_heads, head_dim),
        grad_qkv,
        grad_query_bias,
        grad_value_bias,
        grad_head_scale,
        grad_proj,
        own_cols[6].reshape(part_heads, head_dim),
        grad_up,
        grad_up_bias.reshape(part_heads, -1),
        grad_down,
        own_cols[7].reshape(part_heads, head_dim),
    )
    return (increments, grad_inputs, grad_condition)


def on_device(
    tokens,
    condition,
    scale_index,
    ada_weight,
    ada_bias,
    qkv_weight,
    query_bias,
    value_bias,
    head_scale,
    proj_weight,
    proj_bias,
    up_weight,
    up_bias,
    down_weight,
    down_bias,
    out_grad,
):

    def fetch_weights():
        return (
            lax.all_gather(ada_weight, "dp", axis=2, tiled=True),
            lax.all_gather(ada_bias, "dp", axis=2, tiled=True),
            lax.all_gather(qkv_weight, "dp", axis=1, tiled=True),
            lax.all_gather(query_bias, "dp", axis=1, tiled=True),
            lax.all_gather(value_bias, "dp", axis=1, tiled=True),
            lax.all_gather(proj_weight, "dp", axis=1, tiled=True),
            lax.all_gather(proj_bias, "dp", axis=1, tiled=True),
            lax.all_gather(up_weight, "dp", axis=0, tiled=True),
            lax.all_gather(up_bias, "dp", axis=1, tiled=True),
            lax.all_gather(down_weight, "dp", axis=1, tiled=True),
            lax.all_gather(down_bias, "dp", axis=1, tiled=True),
        )

    def forward_scan(carried, step_in):
        token_rows, condition_row, scale_row = step_in
        weights_now = fetch_weights()
        output, kept = forward_step(weights_now, token_rows, condition_row, scale_row, head_scale)
        return (carried, (output, kept))

    unused_carry, (outputs, kept_all) = lax.scan(
        forward_scan, jnp.zeros((), jnp.int32), (tokens, condition, scale_index)
    )
    width = tokens.shape[2]
    part_width = qkv_weight.shape[2]
    part_heads = head_scale.shape[0]
    head_dim = part_width // part_heads
    part_ff = up_weight.shape[1]
    zero_grads = (
        jnp.zeros((part_width, 6, width), jnp.float32),
        jnp.zeros((6, part_heads, head_dim), jnp.float32),
        jnp.zeros((3, width, part_width), jnp.float32),
        jnp.zeros((part_heads, head_dim), jnp.float32),
        jnp.zeros((part_heads, head_dim), jnp.float32),
        jnp.zeros((part_heads,), jnp.float32),
        jnp.zeros((part_width, width), jnp.float32),
        jnp.zeros((part_heads, head_dim), jnp.float32),
        jnp.zeros((width, part_ff), jnp.float32),
        jnp.zeros((part_heads, part_ff // part_heads), jnp.float32),
        jnp.zeros((part_ff, width), jnp.float32),
        jnp.zeros((part_heads, head_dim), jnp.float32),
    )

    def backward_scan(totals, step_in):
        kept, token_grad, condition_row, scale_row = step_in
        weights_now = fetch_weights()
        increments, grad_inputs, grad_condition = backward_step(
            weights_now, kept, token_grad, condition_row, scale_row, head_scale
        )
        totals = tuple((running + increment for running, increment in zip(totals, increments)))
        return (totals, (grad_inputs, grad_condition))

    totals, (grad_tokens, grad_condition) = lax.scan(
        backward_scan, zero_grads, (kept_all, out_grad, condition, scale_index), reverse=True
    )
    scale_total = lax.psum(totals[5], "dp")
    reduced = (
        lax.psum_scatter(
            totals[0].astype(jnp.bfloat16), "dp", scatter_dimension=2, tiled=True
        ).astype(jnp.float32),
        lax.psum_scatter(
            totals[1].astype(jnp.bfloat16), "dp", scatter_dimension=2, tiled=True
        ).astype(jnp.float32),
        lax.psum_scatter(
            totals[2].astype(jnp.bfloat16), "dp", scatter_dimension=1, tiled=True
        ).astype(jnp.float32),
        lax.psum_scatter(
            totals[3].astype(jnp.bfloat16), "dp", scatter_dimension=1, tiled=True
        ).astype(jnp.float32),
        lax.psum_scatter(
            totals[4].astype(jnp.bfloat16), "dp", scatter_dimension=1, tiled=True
        ).astype(jnp.float32),
        lax.psum_scatter(
            totals[6].astype(jnp.bfloat16), "dp", scatter_dimension=1, tiled=True
        ).astype(jnp.float32),
        lax.psum_scatter(
            totals[7].astype(jnp.bfloat16), "dp", scatter_dimension=1, tiled=True
        ).astype(jnp.float32),
        lax.psum_scatter(
            totals[8].astype(jnp.bfloat16), "dp", scatter_dimension=0, tiled=True
        ).astype(jnp.float32),
        lax.psum_scatter(
            totals[9].astype(jnp.bfloat16), "dp", scatter_dimension=1, tiled=True
        ).astype(jnp.float32),
        lax.psum_scatter(
            totals[10].astype(jnp.bfloat16), "dp", scatter_dimension=1, tiled=True
        ).astype(jnp.float32),
        lax.psum_scatter(
            totals[11].astype(jnp.bfloat16), "dp", scatter_dimension=1, tiled=True
        ).astype(jnp.float32),
    )
    return (
        outputs,
        grad_tokens,
        grad_condition,
        reduced[0],
        reduced[1],
        reduced[2],
        reduced[3],
        reduced[4],
        scale_total,
        reduced[5],
        reduced[6],
        reduced[7],
        reduced[8],
        reduced[9],
        reduced[10],
    )


GRIDS = {(16, 2): (4, 2, 2)}
MESH_ID = pl.DeviceIdType.MESH
ANY = pl.ANY
F32 = jnp.float32
BF16 = jnp.bfloat16
SCALES = 10
MASK = -16384.0


def place():
    return (lax.axis_index("dp"), lax.axis_index("tensor"))


def coords(grid):
    chip, core = place()
    nz, ny, nx = grid
    return (chip // (ny * nx), (chip // nx) % ny, chip % nx, core)


def greet_all(count):
    chip, core = place()
    me = chip * 2 + core
    barrier = pltpu.get_barrier_semaphore()
    for k in range(1, count):
        peer = (me + k) % count
        pl.semaphore_signal(barrier, inc=1, device_id=(peer // 2, peer % 2), device_id_type=MESH_ID)
    pl.semaphore_wait(barrier, count - 1)


def remote(src, dst, send_sem, recv_sem, device):
    return pltpu.make_async_remote_copy(
        src_ref=src,
        dst_ref=dst,
        send_sem=send_sem,
        recv_sem=recv_sem,
        device_id=device,
        device_id_type=MESH_ID,
    )


def swap_kernel(count, to_all, src_ref, dst_ref, local_sem, send_sem, recv_sem):
    chip, core = place()
    me = chip * 2 + core
    greet_all(count)
    own = pltpu.make_async_copy(src_ref if to_all else src_ref.at[me], dst_ref.at[me], local_sem)
    own.start()
    copies = []
    for k in range(1, count):
        peer = (me + k) % count
        copy = remote(
            src_ref if to_all else src_ref.at[peer],
            dst_ref.at[me],
            send_sem.at[k - 1],
            recv_sem.at[k - 1],
            (peer // 2, peer % 2),
        )
        copy.start()
        copies.append(copy)
    own.wait()
    for copy in copies:
        copy.wait()


def swap(values, count, to_all, collective_id, name):
    block = values.shape if to_all else values.shape[1:]
    return pl.pallas_call(
        functools.partial(swap_kernel, count, to_all),
        out_shape=jax.ShapeDtypeStruct((count,) + block, values.dtype),
        in_specs=[pl.BlockSpec(memory_space=pltpu.VMEM)],
        out_specs=pl.BlockSpec(memory_space=pltpu.VMEM),
        scratch_shapes=[
            pltpu.SemaphoreType.DMA,
            pltpu.SemaphoreType.DMA((count - 1,)),
            pltpu.SemaphoreType.DMA((count - 1,)),
        ],
        compiler_params=pltpu.CompilerParams(collective_id=collective_id, has_side_effects=True),
        name=name,
    )(values)

def greet(peers):
    barrier = pltpu.get_barrier_semaphore()
    for peer in peers:
        pl.semaphore_signal(barrier, inc=1, device_id=peer, device_id_type=MESH_ID)
    pl.semaphore_wait(barrier, len(peers))


def forward_kernel(
    grid,
    sizes,
    chunk_counts,
    shard,
    tok,
    grad_in,
    mod,
    query_spare,
    key_spare,
    query_bias,
    value_bias,
    key_scale,
    up_bias,
    ones,
    full,
    x_out,
    grad_out,
    mixed_out,
    qaug_out,
    kv_out,
    inverse_out,
    att_out,
    branch_out,
    mlp_out,
    slope_out,
    dm_out,
    grad_down_out,
    mlp_own,
    mlp_other,
    x,
    dm,
    mixed,
    part,
    other,
    turned,
    qaug,
    kv,
    inverses,
    att,
    w,
    slope,
    act,
    grad_down,
    local_sem,
    z_send,
    z_recv,
    p_send,
    p_recv,
    t_send,
    t_recv,
    load_sem,
    save_sem,
):
    nz, ny, nx = grid
    half = nz // 2
    seqs, pad = sizes
    chunks = shard.shape[0]
    ff_chunks = chunk_counts
    z, y, x_at, core = coords(grid)
    width = x.shape[1]
    part_width = att.shape[1]
    pairs = part_width // 128
    blocks = seqs * 2
    length = tok.shape[0]

    def dev(z_to, y_to, x_to):
        return ((z_to * ny + y_to) * nx + x_to, core)

    x_peer = dev(z, y, 1 - x_at)
    y_peer = dev(z, 1 - y, x_at)
    sibling = (place()[0], 1 - core)
    greet([x_peer, y_peer, sibling] + [dev((z + k) % nz, y, x_at) for k in range(1, nz)])

    def own_copy(c):
        return pltpu.make_async_copy(shard.at[c], full.at[c, z, y, x_at], local_sem.at[c])

    def z_copies(c):
        return [
            remote(
                shard.at[c],
                full.at[c, z, y, x_at],
                z_send.at[c, k - 1],
                z_recv.at[c, k - 1],
                dev((z + k) % nz, y, x_at),
            )
            for k in range(1, nz)
        ]

    def first_copies(c):
        low = full.at[c, pl.ds(0, half), y, x_at]
        high = full.at[c, pl.ds(half, half), y, x_at]
        return [
            remote(low, low, p_send.at[c, 0], p_recv.at[c, 0], x_peer),
            remote(high, high, p_send.at[c, 1], p_recv.at[c, 1], y_peer),
        ]

    def second_copies(c):
        low = full.at[c, pl.ds(0, half), y]
        high = full.at[c, pl.ds(half, half), :, x_at]
        return [
            remote(low, low, p_send.at[c, 2], p_recv.at[c, 2], y_peer),
            remote(high, high, p_send.at[c, 3], p_recv.at[c, 3], x_peer),
        ]

    ahead = 2
    progress = [-ahead]

    def advance(upto):
        while progress[0] <= upto:
            t = progress[0]
            if 0 <= t + ahead < chunks:
                own_copy(t + ahead).start()
                for copy in z_copies(t + ahead):
                    copy.start()
            if 0 <= t < chunks:
                own_copy(t).wait()
                for copy in z_copies(t):
                    copy.wait_recv()
                for copy in first_copies(t):
                    copy.start()
            if 0 <= t - 1 < chunks:
                for copy in first_copies(t - 1):
                    copy.wait_recv()
                for copy in second_copies(t - 1):
                    copy.start()
            if 0 <= t - 2 < chunks:
                for copy in second_copies(t - 2):
                    copy.wait_recv()
            progress[0] += 1

    def load(c):
        return pltpu.make_async_copy(full.at[c], w.at[c % 4], load_sem.at[c])

    def weight(c):
        return w[c % 4].reshape(width, part_width)

    saves = []

    def save(src, dst):
        copy = pltpu.make_async_copy(src, dst, save_sem.at[len(saves)])
        copy.start()
        saves.append(copy)
        return copy

    def block_rows(a):
        return pl.ds(pl.multiple_of(a * pad, 16), pad)

    advance(-1)

    def own_rows(s, which):
        return block_rows(s * 2 + which)

    swaps = []
    for i, (src, dst) in enumerate(((tok, x), (grad_in, dm))):
        for s in range(seqs):
            values = src[:, s, :].astype(F32).astype(BF16)
            start = pl.multiple_of((s * 2 + core) * pad, 16)
            dst[pl.ds(start + length // 16 * 16, pad - length // 16 * 16), :] = jnp.zeros(
                (pad - length // 16 * 16, width), BF16
            )
            dst[pl.ds(start, length), :] = values
            piece = dst.at[own_rows(s, core), :]
            copy = remote(piece, piece, t_send.at[i * seqs + s], t_recv.at[i * seqs + s], sibling)
            copy.start()
            swaps.append(copy)
    for copy in swaps[:seqs]:
        copy.wait()
    save(x, x_out)

    def mix_attn(a, rows):
        s = a // 2
        normed, unused = normalize(x[rows, :].astype(F32))
        mixed[rows, :] = (normed * (1.0 + mod[s, 2:3, :]) + mod[s, 4:5, :]).astype(BF16)

    for_blocks(blocks, pad, mix_attn)
    mixed_saved = save(mixed, mixed_out)
    advance(0)
    for copy in swaps[seqs:]:
        copy.wait()
    grad_saved = save(dm, grad_out)
    advance(1)
    grad_saved.wait()

    def scale_grad(a, rows):
        dm[rows, :] = (dm[rows, :].astype(F32) * mod[a // 2, 1:2, :]).astype(BF16)

    for_blocks(blocks, pad, scale_grad)
    save(dm, dm_out)
    advance(2)
    load(0).start()
    transpose_into(turned, dm)
    advance(3)
    load(1).start()

    load(0).wait()

    def project_q(a, rows):
        first, unused = lane_code(pad)
        q_spare = query_spare[rows, :].astype(F32)
        values = dot(mixed[rows, :], weight(0)) + query_bias[...]
        inv = lax.rsqrt(dot((values * values).astype(BF16), ones[...]) + HEAD_EPS)
        inverses[rows, 0:part_width] = inv.astype(BF16)
        values = values * inv * key_scale[...]
        for p in range(pairs):
            piece = values[:, p * 128 : p * 128 + 128]
            qaug[2 * p, rows, :] = jnp.where(first, piece, q_spare).astype(BF16)
            qaug[2 * p + 1, rows, :] = jnp.where(first, q_spare, piece).astype(BF16)

    for_blocks(blocks, pad, project_q)
    advance(4)
    load(2).start()
    load(1).wait()

    def project_k(a, rows):
        values = dot(mixed[rows, :], weight(1))
        inv = lax.rsqrt(dot((values * values).astype(BF16), ones[...]) + HEAD_EPS)
        inverses[rows, part_width : 2 * part_width] = inv.astype(BF16)
        kv[rows, 0:part_width] = (values * inv).astype(BF16)

    for_blocks(blocks, pad, project_k)
    save(inverses, inverse_out)
    load(2).wait()

    def project_v(a, rows):
        kv[rows, part_width : 2 * part_width] = (
            dot(mixed[rows, :], weight(2)) + value_bias[...]
        ).astype(BF16)

    for_blocks(blocks, pad, project_v)
    save(kv, kv_out)
    advance(5)
    load(3).start()

    def attend(i, carry):
        p = i // blocks
        block = i % blocks
        rows = block_rows(block)
        all_rows = pl.ds(pl.multiple_of((block // 2) * 2 * pad, 16), 2 * pad)
        at = pl.multiple_of(p * 128, 128)
        first, code = lane_code(pad)
        k_sides = both_heads(kv[all_rows, pl.ds(at, 128)], key_spare[all_rows, :])
        v_sides = both_heads(kv[all_rows, pl.ds(at + part_width, 128)], 1.0)
        outs = []
        for side in range(2):
            h = 2 * p + side
            q = qaug[h, rows, :]
            prob = jnp.exp2(dot_nt(q, k_sides[side])).astype(BF16)
            o = dot(prob, v_sides[side])
            outs.append(o / pltpu.roll(o, 64, 1))
            norm = -jnp.log2(o)
            high = norm.astype(BF16)
            rest = norm - high.astype(F32)
            middle = rest.astype(BF16)
            low = (rest - middle.astype(F32)).astype(BF16)
            spare = jnp.logical_not(first) if side == 0 else first
            q = q.astype(F32)
            for where, piece in enumerate((high, middle, low)):
                q = jnp.where(spare & (code == SCALES + where), piece.astype(F32), q)
            qaug[h, rows, :] = q.astype(BF16)
        att[rows, pl.ds(at, 128)] = jnp.where(first, outs[0], outs[1]).astype(BF16)
        return carry

    count = pairs * blocks
    for quarter in range(2):
        lax.fori_loop(quarter * count // 2, (quarter + 1) * count // 2, attend, 0)
        advance(6 + quarter)
        load(4 + quarter).start()
    save(qaug, qaug_out)
    save(att, att_out)
    load(3).wait()
    part_copies = []
    for a in range(blocks):
        rows = block_rows(a)
        part[rows, :] = dot_nt(att[rows, :], weight(3)).astype(BF16)
        copy = remote(
            part.at[rows, :], other.at[rows, :], t_send.at[2 * seqs + a], t_recv.at[2 * seqs + a], sibling
        )
        copy.start()
        part_copies.append(copy)
    mixed_saved.wait()
    mlp = mixed
    for a in range(blocks):
        rows = block_rows(a)
        s = a // 2
        part_copies[a].wait()
        b = part[rows, :].astype(F32) + other[rows, :].astype(F32) + mod[s, 6:7, :]
        other[rows, :] = b.astype(BF16)
        normed, unused = normalize(x[rows, :].astype(F32) + mod[s, 0:1, :] * b)
        mlp[rows, :] = (normed * (1.0 + mod[s, 3:4, :]) + mod[s, 5:6, :]).astype(BF16)
    save(other, branch_out)
    save(mlp, mlp_out)
    for c in range(ff_chunks):
        advance(6 + c)
        if c >= 2:
            load(4 + c).start()
        load(4 + c).wait()

        def raise_rows(a, rows):
            h = dot(mlp[rows, :], weight(4 + c)) + up_bias[c]
            square = h * h
            t = jnp.tanh(h * (GELU_COEF + GELU_COEF * GELU_CUBE * square))
            act[c, rows, :] = (0.5 * h * (1.0 + t)).astype(BF16)
            slope[c, rows, :] = (
                0.5 * (1.0 + t)
                + h * (1.0 - t * t) * (0.5 * GELU_COEF + 1.5 * GELU_COEF * GELU_CUBE * square)
            ).astype(BF16)

        for_blocks(blocks, pad, raise_rows)
        save(slope.at[c], slope_out.at[c])
    down_saved = []
    for c in range(ff_chunks):
        advance(10 + c)
        load(8 + c).start()
        if c >= 2:
            down_saved[c - 2].wait()
        grad_down[c % 2] = dot(turned[...], act[c]).astype(BF16).reshape(grad_down.shape[1:])
        down_saved.append(save(grad_down.at[c % 2], grad_down_out.at[c]))
    for c in range(ff_chunks):
        load(8 + c).wait()
    end_copies = []
    for step in range(blocks):
        s = step % seqs
        which = 1 - core if step < seqs else core
        rows = own_rows(s, which)
        total = dot_nt(act[0, rows, :], weight(8))
        for c in range(1, ff_chunks):
            total = total + dot_nt(act[c, rows, :], weight(8 + c))
        part[rows, :] = total.astype(BF16)
        if step < seqs:
            copy = remote(
                part.at[rows, :],
                mlp_other.at[s],
                t_send.at[2 * seqs + blocks + s],
                t_recv.at[2 * seqs + blocks + s],
                sibling,
            )
            copy.start()
            end_copies.append(copy)
        else:
            save(part.at[rows, :], mlp_own.at[s])
    for copy in end_copies:
        copy.wait()
    done = [mixed_saved, grad_saved] + down_saved[:-2]
    for copy in saves:
        if all(copy is not other_copy for other_copy in done):
            copy.wait()
    for c in range(chunks):
        for copy in z_copies(c) + first_copies(c) + second_copies(c):
            copy.wait_send()


def forward_pass(grid, sizes, shard, tok, grad_in, mod, query_spare, key_spare, query_bias, value_bias, key_scale, up_bias, ones, collective_id):
    nz, ny, nx = grid
    seqs, pad = sizes
    chunks, own_rows, part = shard.shape
    ff_chunks = up_bias.shape[0]
    width = tok.shape[2]
    total = seqs * 2 * pad
    heads = part // 64
    wide = ((total, width), BF16)
    narrow = ((total, part), BF16)
    chunk = (nz, ny, nx, own_rows, part)
    outs = [
        ((chunks,) + chunk, BF16),
        wide,
        wide,
        wide,
        ((heads, total, 128), BF16),
        wide,
        wide,
        narrow,
        wide,
        wide,
        ((ff_chunks, total, part), BF16),
        wide,
        ((ff_chunks,) + chunk, BF16),
        ((seqs, pad, width), BF16),
        ((seqs, pad, width), BF16),
    ]
    scratch = [
        wide,
        wide,
        wide,
        wide,
        wide,
        ((width, total), BF16),
        ((heads, total, 128), BF16),
        wide,
        wide,
        narrow,
        ((4,) + chunk, BF16),
        ((ff_chunks, total, part), BF16),
        ((ff_chunks, total, part), BF16),
        ((2,) + chunk, BF16),
    ]
    swaps = 3 * seqs + seqs * 2
    vmem = pl.BlockSpec(memory_space=pltpu.VMEM)
    hbm = pl.BlockSpec(memory_space=ANY)
    return pl.pallas_call(
        functools.partial(forward_kernel, grid, sizes, ff_chunks),
        out_shape=[jax.ShapeDtypeStruct(shape, dtype) for shape, dtype in outs],
        in_specs=[hbm] + [vmem] * 10,
        out_specs=[hbm] * len(outs),
        scratch_shapes=[pltpu.VMEM(shape, dtype) for shape, dtype in scratch]
        + [
            pltpu.SemaphoreType.DMA((chunks,)),
            pltpu.SemaphoreType.DMA((chunks, nz - 1)),
            pltpu.SemaphoreType.DMA((chunks, nz - 1)),
            pltpu.SemaphoreType.DMA((chunks, 4)),
            pltpu.SemaphoreType.DMA((chunks, 4)),
            pltpu.SemaphoreType.DMA((swaps,)),
            pltpu.SemaphoreType.DMA((swaps,)),
            pltpu.SemaphoreType.DMA((chunks,)),
            pltpu.SemaphoreType.DMA((24,)),
        ],
        compiler_params=pltpu.CompilerParams(
            collective_id=collective_id, has_side_effects=True, vmem_limit_bytes=60 * 2**20
        ),
        name="forward_pass",
    )(shard, tok, grad_in, mod, query_spare, key_spare, query_bias, value_bias, key_scale, up_bias, ones)


def reduce_kernel(
    grid,
    chunks,
    full_ref,
    out_ref,
    keep_low,
    keep_high,
    got_low,
    got_high,
    next_low,
    next_high,
    column,
    got_z,
    local_sem,
    p_send,
    p_recv,
    z_send,
    z_recv,
):
    nz, ny, nx = grid
    half = nz // 2
    z, y, x, core = coords(grid)

    def dev(z_at, y_at, x_at):
        return ((z_at * ny + y_at) * nx + x_at, core)

    x_peer = dev(z, y, 1 - x)
    y_peer = dev(z, 1 - y, x)
    greet_all(nz * ny * nx * 2)

    def own_copies(c):
        return [
            pltpu.make_async_copy(full_ref.at[c, pl.ds(0, half), y], keep_low.at[c], local_sem.at[c, 0]),
            pltpu.make_async_copy(
                full_ref.at[c, pl.ds(half, half), :, x], keep_high.at[c], local_sem.at[c, 1]
            ),
        ]

    def first_copies(c):
        return [
            remote(
                full_ref.at[c, pl.ds(0, half), 1 - y], got_low.at[c], p_send.at[c, 0], p_recv.at[c, 0], y_peer
            ),
            remote(
                full_ref.at[c, pl.ds(half, half), :, 1 - x],
                got_high.at[c],
                p_send.at[c, 1],
                p_recv.at[c, 1],
                x_peer,
            ),
        ]

    def second_copies(c):
        return [
            remote(keep_low.at[c, :, 1 - x], next_low.at[c], p_send.at[c, 2], p_recv.at[c, 2], x_peer),
            remote(keep_high.at[c, :, 1 - y], next_high.at[c], p_send.at[c, 3], p_recv.at[c, 3], y_peer),
        ]

    def z_copies(c):
        return [
            remote(
                column.at[c, (z + k) % nz],
                got_z.at[c, k - 1],
                z_send.at[c, k - 1],
                z_recv.at[c, k - 1],
                dev((z + k) % nz, y, x),
            )
            for k in range(1, nz)
        ]

    def add(a, b):
        return (a.astype(F32) + b.astype(F32)).astype(BF16)

    ahead = 2
    for t in range(-ahead, chunks + 2):
        if 0 <= t + ahead < chunks:
            c = t + ahead
            for copy in first_copies(c) + own_copies(c):
                copy.start()
        if 0 <= t < chunks:
            for copy in own_copies(t):
                copy.wait()
            for copy in first_copies(t):
                copy.wait_recv()
            keep_low[t] = add(keep_low[t], got_low[t])
            keep_high[t] = add(keep_high[t], got_high[t])
            for copy in second_copies(t):
                copy.start()
        if 0 <= t - 1 < chunks:
            c = t - 1
            for copy in second_copies(c):
                copy.wait_recv()
            column[c, 0:half] = add(keep_low[c, :, x], next_low[c])
            column[c, half:nz] = add(keep_high[c, :, y], next_high[c])
            for copy in z_copies(c):
                copy.start()
        if 0 <= t - 2 < chunks:
            c = t - 2
            for copy in z_copies(c):
                copy.wait_recv()
            total = column[c, z].astype(F32)
            for k in range(nz - 1):
                total = total + got_z[c, k].astype(F32)
            out_ref[c] = total
    for c in range(chunks):
        for copy in first_copies(c) + second_copies(c) + z_copies(c):
            copy.wait_send()


def reduce_weights(grid, full, collective_id):
    nz, ny, nx = grid
    half = nz // 2
    chunks = full.shape[0]
    block = full.shape[4:]
    return pl.pallas_call(
        functools.partial(reduce_kernel, grid, chunks),
        out_shape=jax.ShapeDtypeStruct((chunks,) + block, F32),
        in_specs=[pl.BlockSpec(memory_space=ANY)],
        out_specs=pl.BlockSpec(memory_space=pltpu.VMEM),
        scratch_shapes=[
            pltpu.VMEM((chunks, half, nx) + block, BF16),
            pltpu.VMEM((chunks, half, ny) + block, BF16),
            pltpu.VMEM((chunks, half, nx) + block, BF16),
            pltpu.VMEM((chunks, half, ny) + block, BF16),
            pltpu.VMEM((chunks, half) + block, BF16),
            pltpu.VMEM((chunks, half) + block, BF16),
            pltpu.VMEM((chunks, nz) + block, BF16),
            pltpu.VMEM((chunks, nz - 1) + block, BF16),
            pltpu.SemaphoreType.DMA((chunks, 2)),
            pltpu.SemaphoreType.DMA((chunks, 4)),
            pltpu.SemaphoreType.DMA((chunks, 4)),
            pltpu.SemaphoreType.DMA((chunks, nz - 1)),
            pltpu.SemaphoreType.DMA((chunks, nz - 1)),
        ],
        compiler_params=pltpu.CompilerParams(
            collective_id=collective_id, has_side_effects=True, vmem_limit_bytes=48 * 2**20
        ),
        name="reduce_weights",
    )(full)


def dot(a, b):
    return jnp.dot(a, b, preferred_element_type=F32)


def dot_nt(a, b):
    return lax.dot_general(a, b, (((1,), (1,)), ((), ())), preferred_element_type=F32)


def dot_tn(a, b):
    return lax.dot_general(a, b, (((0,), (0,)), ((), ())), preferred_element_type=F32)


def lane_code(rows):
    lane = lax.broadcasted_iota(jnp.int32, (rows, 128), 1)
    return lane < 64, lane & 63


def both_heads(pair, spare):
    first, unused = lane_code(pair.shape[0])
    pair = pair.astype(F32)
    if not isinstance(spare, float):
        spare = spare.astype(F32)
    return (
        jnp.where(first, pair, spare).astype(BF16),
        jnp.where(first, spare, pair).astype(BF16),
    )


def column_sum(values):
    return jnp.sum(values, axis=0, keepdims=True)


def transpose_into(dst, src):
    def step(i, carry):
        at = pl.multiple_of(i * 128, 128)
        dst[:, pl.ds(at, 128)] = src[pl.ds(at, 128), :].T
        return carry

    lax.fori_loop(0, src.shape[0] // 128, step, 0)


def for_blocks(count, rows, body):
    def step(a, carry):
        body(a, pl.ds(pl.multiple_of(a * rows, 16), rows))
        return carry

    lax.fori_loop(0, count, step, 0)


def mlp_backward(sizes, dm, down, slope, mlp, up, grad_part, grad_up, bias_sum, turned, low):
    seqs, pad = sizes
    chunks = up.shape[0]
    transpose_into(turned, mlp)
    bias_sum[...] = jnp.zeros_like(bias_sum)
    for c in range(chunks):

        def back(a, rows):
            gh = dot(dm[rows, :], down[c]) * slope[c, rows, :].astype(F32)
            bias_sum[c] += column_sum(gh)
            low[c, rows, :] = gh.astype(BF16)

        for_blocks(seqs * 2, pad, back)
        grad_up[c] = dot(turned[...], low[c]).astype(BF16)

    def gather(a, rows):
        total = dot_nt(low[0, rows, :], up[0])
        for c in range(1, chunks):
            total = total + dot_nt(low[c, rows, :], up[c])
        grad_part[rows, :] = total.astype(BF16)

    for_blocks(seqs * 2, pad, gather)


def middle_backward(sizes, x, grad, branch, grad_part, grad_other, mod, proj, att, grad_mid, grad_att, grad_proj, stats, da, turned):
    seqs, pad = sizes
    stats[...] = jnp.zeros_like(stats)

    def back(a, rows):
        s = a // 2
        b = branch[rows, :].astype(F32)
        gm = grad_part[rows, :].astype(F32) + grad_other[rows, :].astype(F32)
        normed, inverse = normalize(x[rows, :].astype(F32) + mod[s, 0:1, :] * b)
        stats[s, 1:2, :] += 0.5 * column_sum(gm * normed)
        stats[s, 2:3, :] += 0.5 * column_sum(gm)
        mid = grad[rows, :].astype(F32) + norm_back(gm * (1.0 + mod[s, 3:4, :]), normed, inverse)
        grad_mid[rows, :] = mid.astype(BF16)
        stats[s, 0:1, :] += 0.5 * column_sum(mid * b)
        branch_grad = mid * mod[s, 0:1, :]
        stats[s, 3:4, :] += 0.5 * column_sum(branch_grad)
        low = branch_grad.astype(BF16)
        da[rows, :] = low
        grad_att[rows, :] = dot(low, proj[...]).astype(BF16)

    for_blocks(seqs * 2, pad, back)
    transpose_into(turned, da)
    grad_proj[...] = dot(turned[...], att[...]).astype(BF16)


def attn_backward(
    sizes, mixed, w, qaug, kv, key_spare, grad_att, inverses, key_scale, ones, grad_qkv, grad_part, bias_sum, low, turned
):
    seqs, pad = sizes
    part_width = grad_att.shape[1]
    pairs = part_width // 128
    bias_sum[...] = jnp.zeros_like(bias_sum)
    transpose_into(turned, mixed)
    ln2 = 0.6931471805599453

    def attend(i, carry):
        p = i // seqs
        s = i % seqs
        start = pl.multiple_of(s * 2 * pad, 16)
        all_rows = pl.ds(start, 2 * pad)
        at = pl.multiple_of(p * 128, 128)
        lanes = pl.ds(at, 128)
        first, code = lane_code(pad)
        first_all, unused = lane_code(2 * pad)
        k_sides = both_heads(kv[all_rows, lanes], key_spare[all_rows, :])
        v_sides = both_heads(kv[all_rows, pl.ds(at + part_width, 128)], 0.0)
        g_sides = both_heads(grad_att[all_rows, lanes], 0.0)
        grads_k, grads_v, grads_q = [], [], [[], []]
        for side in range(2):
            h = 2 * p + side
            k = k_sides[side]
            v = v_sides[side]
            sum_k = sum_v = None
            for t in range(2):
                rows = pl.ds(pl.multiple_of(start + t * pad, 16), pad)
                q = qaug[h, rows, :]
                g = g_sides[side][t * pad : t * pad + pad]
                prob = jnp.exp2(dot_nt(k, q))
                grad_prob = dot_nt(v, g)
                ds = (prob * (grad_prob - column_sum(prob * grad_prob))).astype(BF16)
                gv = dot(prob.astype(BF16), g)
                gk = dot(ds, q)
                sum_v = gv if t == 0 else sum_v + gv
                sum_k = gk if t == 0 else sum_k + gk
                grads_q[t].append(dot_tn(ds, k))
            grads_k.append(sum_k)
            grads_v.append(sum_v)
        for t in range(2):
            rows = pl.ds(pl.multiple_of(start + t * pad, 16), pad)
            gq = jnp.where(first, grads_q[t][0], grads_q[t][1])
            q = jnp.where(first, qaug[2 * p, rows, :].astype(F32), qaug[2 * p + 1, rows, :].astype(F32))
            bias_sum[2:3, lanes] += ln2 * column_sum(gq * q)
            low[0, rows, lanes] = gq.astype(BF16)
        low[1, all_rows, lanes] = (ln2 * jnp.where(first_all, grads_k[0], grads_k[1])).astype(BF16)
        low[2, all_rows, lanes] = jnp.where(first_all, grads_v[0], grads_v[1]).astype(BF16)
        return carry

    lax.fori_loop(0, pairs * seqs, attend, 0)

    def finish(a, rows):
        first, code = lane_code(pad)

        scale = key_scale[...]
        unit = jnp.concatenate(
            [
                jnp.where(first, qaug[2 * p, rows, :].astype(F32), qaug[2 * p + 1, rows, :].astype(F32))
                for p in range(pairs)
            ],
            axis=1,
        )
        unit = unit / scale
        f = low[0, rows, :].astype(F32) * (scale * ln2)
        product = f * unit
        gq = inverses[rows, 0:part_width].astype(F32) * (f - unit * dot(product.astype(BF16), ones[...]))
        bias_sum[0:1, :] += column_sum(gq)
        low[0, rows, :] = gq.astype(BF16)
        unit = kv[rows, 0:part_width].astype(F32)
        f = low[1, rows, :].astype(F32)
        gk = inverses[rows, part_width : 2 * part_width].astype(F32) * (f - unit * dot((f * unit).astype(BF16), ones[...]))
        low[1, rows, :] = gk.astype(BF16)
        bias_sum[1:2, :] += column_sum(low[2, rows, :].astype(F32))
        total = dot_nt(low[0, rows, :], w[0])
        for j in range(1, 3):
            total = total + dot_nt(low[j, rows, :], w[j])
        grad_part[rows, :] = total.astype(BF16)

    for_blocks(seqs * 2, pad, finish)
    for j in range(3):
        grad_qkv[j] = dot(turned[...], low[j]).astype(BF16)


def finish_rows(sizes, x, grad, branch, mlp_part, mlp_other, grad_mid, grad_part, grad_other, mod, output, grad_tokens, stats):
    seqs, pad = sizes
    core = lax.axis_index("tensor")
    length = output.shape[0]
    for s in range(seqs):
        rows = pl.ds(pl.multiple_of((s * 2 + core) * pad, 16), pad)
        b = mlp_part[s].astype(F32) + mlp_other[s].astype(F32) + mod[s, 7:8, :]
        g = grad[rows, :].astype(F32)
        xs = x[rows, :].astype(F32)
        middle = xs + mod[s, 0:1, :] * branch[rows, :].astype(F32)
        out = middle + mod[s, 1:2, :] * b
        output[:, s, :] = out[0:length]
        stats[s, 0:1, :] = column_sum(g * b)
        stats[s, 1:2, :] = column_sum(g * mod[s, 1:2, :])
        normed, inverse = normalize(xs)
        gm = grad_part[rows, :].astype(F32) + grad_other[rows, :].astype(F32)
        stats[s, 2:3, :] = column_sum(gm * normed)
        stats[s, 3:4, :] = column_sum(gm)
        gt = grad_mid[rows, :].astype(F32) + norm_back(gm * (1.0 + mod[s, 2:3, :]), normed, inverse)
        grad_tokens[:, s, :] = gt[0:length]
        stats[s, 4:8, :] = jnp.zeros_like(stats[s, 4:8, :])


def run(body, sizes, operands, outs, scratch=(), name=None):
    def kernel(*refs):
        body(sizes, *refs)

    return pl.pallas_call(
        kernel,
        out_shape=[jax.ShapeDtypeStruct(shape, dtype) for shape, dtype in outs],
        in_specs=[pl.BlockSpec(memory_space=pltpu.VMEM)] * len(operands),
        out_specs=[pl.BlockSpec(memory_space=pltpu.VMEM)] * len(outs),
        scratch_shapes=[pltpu.VMEM(shape, dtype) for shape, dtype in scratch],
        compiler_params=pltpu.CompilerParams(vmem_limit_bytes=60 * 2**20),
        name=name,
    )(*operands)


def sibling_swap(values):
    return lax.ppermute(values, "tensor", [(0, 1), (1, 0)])


def pad_rows(values, rows):
    count, length = values.shape
    return jnp.pad(values, ((0, 0), (0, rows * 128 - length))).reshape(count, rows, 128)


def fast_device(
    grid,
    tokens,
    condition,
    scale_index,
    ada_weight,
    ada_bias,
    qkv_weight,
    query_bias,
    value_bias,
    head_scale,
    proj_weight,
    proj_bias,
    up_weight,
    up_bias,
    down_weight,
    down_bias,
    out_grad,
):
    nz, ny, nx = grid
    dp = nz * ny * nx
    count = dp * 2
    seqs, own_len, width = tokens.shape
    seq_len = own_len * 2
    part = qkv_weight.shape[2]
    heads = head_scale.shape[0]
    head_dim = part // heads
    own_rows = qkv_weight.shape[1]
    ff_chunks = up_weight.shape[1] // part
    chip, core = place()

    shard = jnp.concatenate(
        [
            qkv_weight,
            proj_weight.T[None],
            up_weight.reshape(own_rows, ff_chunks, part).transpose(1, 0, 2),
            down_weight.T.reshape(own_rows, ff_chunks, part).transpose(1, 0, 2),
        ],
        axis=0,
    )
    pad = -(-own_len // 16) * 16
    total = seqs * 2 * pad
    sizes = (seqs, pad)
    pieces = [condition, ada_bias, query_bias, value_bias, proj_bias, up_bias, down_bias]
    small = jnp.concatenate([piece.reshape(1, -1) for piece in pieces], axis=1)
    small_rows = -(-small.shape[1] // (16 * 128)) * 16
    every = swap(pad_rows(small, small_rows)[0], count, True, 1, "gather_small")
    every = every.reshape(dp, 2, small_rows * 128)
    parts, at = [], 0
    for piece in pieces:
        parts.append(every[:, :, at : at + piece.size].reshape((dp, 2) + piece.shape).astype(F32))
        at += piece.size
    cond_all = parts[0][:, 0].reshape(dp * seqs, width)
    own_of = lambda values: lax.dynamic_index_in_dim(values, core, 1, keepdims=False)
    spread = lambda values: values.transpose(1, 0, 2).reshape(-1)
    both = lambda values: values.transpose(1, 2, 0, 3).reshape(-1)
    ada_bias_full = parts[1].transpose(2, 1, 3, 0, 4).reshape(6, width)
    query_bias_own = spread(own_of(parts[2]))
    value_bias_own = spread(own_of(parts[3]))
    proj_bias_full = both(parts[4])
    up_bias_own = spread(own_of(parts[5]))
    down_bias_full = both(parts[6])

    cond_half = lax.dynamic_slice_in_dim(cond_all, core * part, part, 1)
    silu_half = jax.nn.silu(cond_half).astype(BF16)
    mod_part = jnp.einsum("sr,rjc->sjc", silu_half, ada_weight, preferred_element_type=F32)
    cols = mod_part.shape[2]
    mod_send = jnp.repeat(pad_rows(mod_part.reshape(dp, seqs * 6 * cols), 8), 2, axis=0)
    mod_got = swap(mod_send, count, False, 2, "swap_modulation")
    mod_got = mod_got.reshape(dp, 2, -1)[:, :, : seqs * 6 * cols].sum(axis=1)
    modulation = mod_got.reshape(dp, seqs, 6, cols).transpose(1, 2, 0, 3).reshape(seqs, 6, width)
    modulation = modulation + ada_bias_full
    ends = jnp.stack([proj_bias_full, down_bias_full])
    mod = jnp.concatenate([modulation, jnp.broadcast_to(ends, (seqs,) + ends.shape)], axis=1)

    level = jnp.pad(
        scale_index.reshape(seqs, 2, own_len), ((0, 0), (0, 0), (0, pad - own_len)), constant_values=100
    ).reshape(total, 1)
    code = jnp.arange(128)[None] % 64
    query_spare = jnp.where(code == level, 1.0, 0.0).astype(BF16)
    key_spare = jnp.where(
        code < SCALES, jnp.where(level > code, MASK, 0.0), jnp.where(code < SCALES + 3, 1.0, 0.0)
    ).astype(BF16)
    key_scale = jnp.repeat(jnp.exp(head_scale) * 1.4426950408889634, head_dim).reshape(1, part)
    head_at = jnp.arange(part) // head_dim
    ones = (head_at[:, None] == head_at[None, :]).astype(BF16)
    wide_rows = ((total, width), BF16)
    part_rows = ((total, part), BF16)
    head_rows = ((heads, total, 2 * head_dim), BF16)
    ff_rows = ((ff_chunks, total, part), BF16)
    weight_rows = ((width, part), BF16)
    turned = ((width, total), BF16)

    (
        full,
        x,
        grad,
        mixed,
        qaug,
        kv,
        inverses,
        att,
        branch,
        mlp,
        slope,
        dm,
        grad_down,
        mlp_part,
        mlp_other,
    ) = forward_pass(
        grid,
        sizes,
        shard,
        tokens.transpose(1, 0, 2),
        out_grad.transpose(1, 0, 2),
        mod,
        query_spare,
        key_spare,
        query_bias_own[None],
        value_bias_own[None],
        key_scale,
        up_bias_own.reshape(ff_chunks, 1, part),
        ones,
        0,
    )
    full = full.reshape(-1, width, part)
    grad_down = grad_down.reshape(-1, width, part)
    up = full[4 : 4 + ff_chunks]
    down = full[4 + ff_chunks :]
    gm_part, grad_up, up_sum = run(
        mlp_backward,
        sizes,
        (dm, down, slope, mlp, up),
        [wide_rows, ((ff_chunks, width, part), BF16), ((ff_chunks, 1, part), F32)],
        [turned, ff_rows],
        name="mlp_backward",
    )
    grad_mid, grad_att, grad_proj, mid_stats = run(
        middle_backward,
        sizes,
        (x, grad, branch, gm_part, sibling_swap(gm_part), mod, full[3], att),
        [wide_rows, part_rows, weight_rows, ((seqs, 4, width), F32)],
        [wide_rows, turned],
        name="middle_backward",
    )
    grad_qkv, ga_part, qkv_sum = run(
        attn_backward,
        sizes,
        (mixed, full[:3], qaug, kv, key_spare, grad_att, inverses, key_scale, ones),
        [((3, width, part), BF16), wide_rows, ((8, part), F32)],
        [((3, total, part), BF16), turned],
        name="attn_backward",
    )
    output, grad_inputs, end_stats = run(
        finish_rows,
        sizes,
        (x, grad, branch, mlp_part, mlp_other, grad_mid, ga_part, sibling_swap(ga_part), mod),
        [((own_len, seqs, width), F32), ((own_len, seqs, width), F32), ((seqs, 8, width), F32)],
        name="finish_rows",
    )
    grad_head_scale = jnp.sum(qkv_sum[2].reshape(heads, head_dim), axis=1)

    grad_mod = jnp.stack(
        [
            mid_stats[:, 0],
            end_stats[:, 0],
            end_stats[:, 2],
            mid_stats[:, 1],
            end_stats[:, 3],
            mid_stats[:, 2],
        ],
        axis=1,
    )
    grad_proj_bias = jnp.sum(mid_stats[:, 3], axis=0)
    grad_down_bias = jnp.sum(end_stats[:, 1], axis=0)
    twice = lambda values: jnp.repeat(values[:, None], 2, axis=1)
    to_owner = lambda values: values.reshape(heads, dp, -1).transpose(1, 0, 2).reshape(dp, -1)
    to_both = lambda values: (
        values.reshape(2, heads, dp, -1).transpose(2, 0, 1, 3).reshape(dp, 2, -1)
    )
    send = jnp.concatenate(
        [
            twice(grad_mod.reshape(seqs, 6, dp, cols).transpose(2, 0, 1, 3).reshape(dp, -1)),
            twice(to_owner(qkv_sum[0])),
            twice(to_owner(qkv_sum[1])),
            twice(to_owner(up_sum)),
            jnp.broadcast_to(grad_head_scale, (dp, 2, heads)),
            to_both(grad_proj_bias),
            to_both(grad_down_bias),
        ],
        axis=2,
    )
    rows = -(-send.shape[2] // (8 * 128)) * 8
    got = swap(pad_rows(send.reshape(count, -1), rows), count, False, 3, "swap_grads")
    got = got.reshape(dp, 2, -1)
    n_mod = seqs * 6 * cols
    mod_low = jnp.sum(got[:, :, :n_mod], axis=1).reshape(dp * seqs, 6, cols)
    grad_ada_bias_cols = jnp.sum(mod_low, axis=0)
    mod_low = mod_low.astype(BF16)
    own_sums = jnp.sum(own_of(got), axis=0)
    all_sums = jnp.sum(got, axis=(0, 1))
    owned, at = [], n_mod
    for piece, sums in (
        (query_bias, own_sums),
        (value_bias, own_sums),
        (up_bias, own_sums),
        (head_scale, own_sums),
        (proj_bias, all_sums),
        (down_bias, all_sums),
    ):
        owned.append(sums[at : at + piece.size].reshape(piece.shape))
        at += piece.size
    grad_ada = jnp.einsum("sr,sjc->rjc", silu_half, mod_low, preferred_element_type=F32)
    cond_part = jnp.einsum("sjc,rjc->sr", mod_low, ada_weight, preferred_element_type=F32)
    return_send = jnp.repeat(cond_part.reshape(dp, seqs * part // 128, 128), 2, axis=0)
    ada_bias_send = jnp.broadcast_to(
        jnp.pad(grad_ada_bias_cols.reshape(1, -1), ((0, 0), (0, 1024 - 6 * cols))).reshape(1, 8, 128),
        (count, 8, 128),
    )
    last = swap(
        jnp.concatenate([return_send, ada_bias_send], axis=1), count, False, 4, "swap_condition"
    )
    last = own_of(last.reshape(dp, 2, -1))
    grad_silu = jnp.sum(last[:, : seqs * part], axis=0).reshape(seqs, part)
    cond_own = lax.dynamic_slice_in_dim(condition.astype(F32), core * part, part, 1)
    sigmoid = jax.nn.sigmoid(cond_own)
    grad_condition = grad_silu * sigmoid * (1.0 + cond_own * (1.0 - sigmoid))
    ada_cols = last[:, seqs * part : seqs * part + 6 * cols].reshape(dp, 6, cols)
    ada_rows = lax.dynamic_slice_in_dim(ada_cols, core * heads, heads, 0).transpose(1, 0, 2)
    grad_ada_bias = lax.dynamic_slice_in_dim(ada_rows, chip * ada_bias.shape[2], ada_bias.shape[2], 2)

    reduced = reduce_weights(
        grid,
        jnp.concatenate([grad_qkv, grad_proj[None], grad_up, grad_down], axis=0).reshape(
            (-1,) + grid + (own_rows, part)
        ),
        5,
    )
    wide = lambda values: values.transpose(1, 0, 2).reshape(own_rows, -1)
    return (
        output.transpose(1, 0, 2),
        grad_inputs.transpose(1, 0, 2),
        grad_condition,
        grad_ada,
        grad_ada_bias,
        reduced[:3],
        owned[0],
        owned[1],
        owned[3],
        reduced[3].T,
        owned[4],
        wide(reduced[4 : 4 + ff_chunks]),
        owned[2],
        wide(reduced[4 + ff_chunks :]).T,
        owned[5],
    )


def solution(mesh):
    in_specs = (
        P("dp", "tensor", None),
        P("dp", None),
        P("dp", None),
        P("tensor", None, "dp"),
        P(None, "tensor", "dp"),
        P(None, "dp", "tensor"),
        P("tensor", "dp"),
        P("tensor", "dp"),
        P("tensor"),
        P("tensor", "dp"),
        P("tensor", "dp"),
        P("dp", "tensor"),
        P("tensor", "dp"),
        P("tensor", "dp"),
        P("tensor", "dp"),
        P("dp", "tensor", None),
    )
    out_specs = (
        P("dp", "tensor", None),
        P("dp", "tensor", None),
        P("dp", "tensor"),
        P("tensor", None, "dp"),
        P(None, "tensor", "dp"),
        P(None, "dp", "tensor"),
        P("tensor", "dp"),
        P("tensor", "dp"),
        P("tensor"),
        P("tensor", "dp"),
        P("tensor", "dp"),
        P("dp", "tensor"),
        P("tensor", "dp"),
        P("tensor", "dp"),
        P("tensor", "dp"),
    )
    grid = GRIDS.get((mesh.shape["dp"], mesh.shape["tensor"]))
    body = on_device if grid is None else functools.partial(fast_device, grid)
    return jax.shard_map(
        body, mesh=mesh, in_specs=in_specs, out_specs=out_specs, check_vma=False
    )
```

```python
import functools

import jax
import jax.numpy as jnp
from jax import lax
from jax.experimental import pallas as pl
from jax.experimental.pallas import tpu as pltpu
from jax.sharding import PartitionSpec as P

NORM_EPS = 1e-06
HEAD_EPS = 1e-06
GELU_COEF = 0.7978845608028654
GELU_CUBE = 0.044715


def normalize(values):
    centred = values - jnp.mean(values, axis=-1, keepdims=True)
    inverse = lax.rsqrt(jnp.mean(centred * centred, axis=-1, keepdims=True) + NORM_EPS)
    return (centred * inverse, inverse)


def norm_back(grad_normed, normed, inverse):
    return inverse * (
        grad_normed
        - jnp.mean(grad_normed, axis=-1, keepdims=True)
        - normed * jnp.mean(grad_normed * normed, axis=-1, keepdims=True)
    )


def gelu_slope(hidden):
    inner = jnp.tanh(GELU_COEF * (hidden + GELU_CUBE * hidden * hidden * hidden))
    return 0.5 * (1.0 + inner) + 0.5 * hidden * (1.0 - inner * inner) * GELU_COEF * (
        1.0 + 3.0 * GELU_CUBE * hidden * hidden
    )


def masked_scores(query_unit, key_unit, scale_factor, scale_row):
    query_low = (query_unit * scale_factor).astype(jnp.bfloat16)
    key_low = key_unit.astype(jnp.bfloat16)
    scores = jnp.einsum("qhe,khe->hqk", query_low, key_low, preferred_element_type=jnp.float32)
    allowed = scale_row[None, :] <= scale_row[:, None]
    return (jnp.where(allowed[None, :, :], scores, -1e30), query_low, key_low)


def attention_core(mixed_all, qkv_full, query_bias_part, value_bias_part, head_scale, scale_row):
    part_width = qkv_full.shape[2]
    part_heads = head_scale.shape[0]
    head_dim = part_width // part_heads
    seq_len = scale_row.shape[0]
    projected = jnp.einsum("ld,jdc->jlc", mixed_all, qkv_full, preferred_element_type=jnp.float32)
    queries = (projected[0] + query_bias_part.reshape(part_width).astype(jnp.float32)).reshape(
        seq_len, part_heads, head_dim
    )
    keys_raw = projected[1].reshape(seq_len, part_heads, head_dim)
    values_low = (projected[2] + value_bias_part.reshape(part_width).astype(jnp.float32)).astype(
        jnp.bfloat16
    )
    values_low = values_low.reshape(seq_len, part_heads, head_dim)
    query_inverse = lax.rsqrt(jnp.sum(queries * queries, axis=-1, keepdims=True) + HEAD_EPS)
    key_inverse = lax.rsqrt(jnp.sum(keys_raw * keys_raw, axis=-1, keepdims=True) + HEAD_EPS)
    query_unit = queries * query_inverse
    key_unit = keys_raw * key_inverse
    scale_factor = jnp.exp(head_scale)[:, None]
    scores, query_low, key_low = masked_scores(query_unit, key_unit, scale_factor, scale_row)
    row_max = jnp.max(scores, axis=-1, keepdims=True)
    weights_exp = jnp.exp(scores - row_max)
    row_total = jnp.sum(weights_exp, axis=-1, keepdims=True)
    attn_prob = weights_exp / row_total
    log_norm = row_max + jnp.log(row_total)
    attended = jnp.einsum(
        "hqk,khe->qhe",
        attn_prob.astype(jnp.bfloat16),
        values_low,
        preferred_element_type=jnp.float32,
    )
    attended = attended.reshape(seq_len, part_width).astype(jnp.bfloat16)
    return (attended, (query_unit, key_unit, query_inverse, key_inverse, values_low, log_norm))


def forward_step(weights, token_rows, condition_row, scale_row, head_scale):
    (
        ada_full,
        ada_bias_part,
        qkv_full,
        query_bias_part,
        value_bias_part,
        proj_full,
        proj_bias_part,
        up_full,
        up_bias_part,
        down_full,
        down_bias_part,
    ) = weights
    width = token_rows.shape[1]
    part_width = qkv_full.shape[2]
    col_start = lax.axis_index("tensor") * part_width
    cond_rows = lax.dynamic_slice_in_dim(
        condition_row.astype(jnp.float32), col_start, part_width, 0
    )
    silu_rows = jax.nn.silu(cond_rows).astype(jnp.bfloat16)
    mod_terms = jnp.einsum("r,rjc->jc", silu_rows, ada_full, preferred_element_type=jnp.float32)
    own_cols = jnp.concatenate(
        [
            ada_bias_part.reshape(6, part_width),
            proj_bias_part.reshape(1, part_width),
            down_bias_part.reshape(1, part_width),
        ],
        axis=0,
    ).astype(jnp.float32)
    placed = lax.dynamic_update_slice(jnp.zeros((8, width), jnp.float32), own_cols, (0, col_start))
    local_mod = placed + jnp.concatenate([mod_terms, jnp.zeros((2, width), jnp.float32)], axis=0)
    modulation = lax.psum(local_mod, "tensor")
    inputs = token_rows.astype(jnp.float32)
    normed_attn, inverse_attn = normalize(inputs)
    mixed_attn = (normed_attn * (1.0 + modulation[2]) + modulation[4]).astype(jnp.bfloat16)
    mixed_all = lax.all_gather(mixed_attn, "tensor", axis=0, tiled=True)
    attended, attn_kept = attention_core(
        mixed_all, qkv_full, query_bias_part, value_bias_part, head_scale, scale_row
    )
    branch_attn = (
        lax.psum_scatter(
            jnp.dot(attended, proj_full, preferred_element_type=jnp.float32).astype(jnp.bfloat16),
            "tensor",
            scatter_dimension=0,
            tiled=True,
        ).astype(jnp.float32)
        + modulation[6]
    )
    middle = inputs + modulation[0] * branch_attn
    normed_mlp, inverse_mlp = normalize(middle)
    mixed_mlp = (normed_mlp * (1.0 + modulation[3]) + modulation[5]).astype(jnp.bfloat16)
    mlp_all = lax.all_gather(mixed_mlp, "tensor", axis=0, tiled=True)
    hidden = jnp.dot(mlp_all, up_full, preferred_element_type=jnp.float32) + up_bias_part.reshape(
        -1
    ).astype(jnp.float32)
    activated = jax.nn.gelu(hidden, approximate=True).astype(jnp.bfloat16)
    branch_mlp = (
        lax.psum_scatter(
            jnp.dot(activated, down_full, preferred_element_type=jnp.float32).astype(jnp.bfloat16),
            "tensor",
            scatter_dimension=0,
            tiled=True,
        ).astype(jnp.float32)
        + modulation[7]
    )
    output = middle + modulation[1] * branch_mlp
    query_unit, key_unit, query_inverse, key_inverse, values_low, log_norm = attn_kept
    kept = (
        modulation,
        normed_attn,
        inverse_attn,
        mixed_all,
        query_unit,
        key_unit,
        query_inverse,
        key_inverse,
        values_low,
        log_norm,
        attended,
        branch_attn,
        normed_mlp,
        inverse_mlp,
        mlp_all,
        hidden,
        activated,
        branch_mlp,
    )
    return (output, kept)


def backward_step(weights, kept, token_grad, condition_row, scale_row, head_scale):
    (
        ada_full,
        ada_bias_part,
        qkv_full,
        query_bias_part,
        value_bias_part,
        proj_full,
        proj_bias_part,
        up_full,
        up_bias_part,
        down_full,
        down_bias_part,
    ) = weights
    (
        modulation,
        normed_attn,
        inverse_attn,
        mixed_all,
        query_unit,
        key_unit,
        query_inverse,
        key_inverse,
        values_low,
        log_norm,
        attended,
        branch_attn,
        normed_mlp,
        inverse_mlp,
        mlp_all,
        hidden,
        activated,
        branch_mlp,
    ) = kept
    part_width = qkv_full.shape[2]
    part_heads = head_scale.shape[0]
    head_dim = part_width // part_heads
    seq_len = scale_row.shape[0]
    scale_factor = jnp.exp(head_scale)[:, None]
    grad_rows = token_grad.astype(jnp.float32)
    grad_branch_mlp = grad_rows * modulation[1]
    grad_gamma_mlp = jnp.sum(grad_rows * branch_mlp, axis=0)
    grad_down_bias = jnp.sum(grad_branch_mlp, axis=0)
    grad_mlp_all = lax.all_gather(
        grad_branch_mlp.astype(jnp.bfloat16), "tensor", axis=0, tiled=True
    )
    grad_down = jnp.einsum("lf,ld->fd", activated, grad_mlp_all, preferred_element_type=jnp.float32)
    grad_act = jnp.einsum("ld,fd->lf", grad_mlp_all, down_full, preferred_element_type=jnp.float32)
    grad_hidden = grad_act * gelu_slope(hidden)
    grad_up_bias = jnp.sum(grad_hidden, axis=0)
    hidden_low = grad_hidden.astype(jnp.bfloat16)
    grad_up = jnp.einsum("ld,lf->df", mlp_all, hidden_low, preferred_element_type=jnp.float32)
    grad_mixed_mlp = lax.psum_scatter(
        jnp.einsum("lf,df->ld", hidden_low, up_full, preferred_element_type=jnp.float32).astype(
            jnp.bfloat16
        ),
        "tensor",
        scatter_dimension=0,
        tiled=True,
    ).astype(jnp.float32)
    grad_scale_mlp = jnp.sum(grad_mixed_mlp * normed_mlp, axis=0)
    grad_shift_mlp = jnp.sum(grad_mixed_mlp, axis=0)
    grad_middle = grad_rows + norm_back(
        grad_mixed_mlp * (1.0 + modulation[3]), normed_mlp, inverse_mlp
    )
    grad_branch_attn = grad_middle * modulation[0]
    grad_gamma_attn = jnp.sum(grad_middle * branch_attn, axis=0)
    grad_proj_bias = jnp.sum(grad_branch_attn, axis=0)
    grad_attn_all = lax.all_gather(
        grad_branch_attn.astype(jnp.bfloat16), "tensor", axis=0, tiled=True
    )
    grad_proj = jnp.einsum("lc,ld->cd", attended, grad_attn_all, preferred_element_type=jnp.float32)
    grad_attended = jnp.einsum(
        "ld,cd->lc", grad_attn_all, proj_full, preferred_element_type=jnp.float32
    )
    grad_attended = grad_attended.astype(jnp.bfloat16).reshape(seq_len, part_heads, head_dim)
    scores, query_low, key_low = masked_scores(query_unit, key_unit, scale_factor, scale_row)
    attn_prob = jnp.exp(scores - log_norm)
    grad_prob = jnp.einsum(
        "qhe,khe->hqk", grad_attended, values_low, preferred_element_type=jnp.float32
    )
    row_dot = jnp.sum(attn_prob * grad_prob, axis=-1, keepdims=True)
    grad_scores = (attn_prob * (grad_prob - row_dot)).astype(jnp.bfloat16)
    grad_values = jnp.einsum(
        "hqk,qhe->khe",
        attn_prob.astype(jnp.bfloat16),
        grad_attended,
        preferred_element_type=jnp.float32,
    )
    grad_query_scaled = jnp.einsum(
        "hqk,khe->qhe", grad_scores, key_low, preferred_element_type=jnp.float32
    )
    grad_key_unit = jnp.einsum(
        "hqk,qhe->khe", grad_scores, query_low, preferred_element_type=jnp.float32
    )
    grad_head_scale = jnp.sum(grad_query_scaled * query_unit, axis=(0, 2)) * jnp.exp(head_scale)
    grad_query_unit = grad_query_scaled * scale_factor
    grad_queries = query_inverse * (
        grad_query_unit - query_unit * jnp.sum(grad_query_unit * query_unit, axis=-1, keepdims=True)
    )
    grad_keys = key_inverse * (
        grad_key_unit - key_unit * jnp.sum(grad_key_unit * key_unit, axis=-1, keepdims=True)
    )
    grad_query_bias = jnp.sum(grad_queries, axis=0)
    grad_value_bias = jnp.sum(grad_values, axis=0)
    grad_projected = (
        jnp.stack([grad_queries, grad_keys, grad_values])
        .reshape(3, seq_len, part_width)
        .astype(jnp.bfloat16)
    )
    grad_qkv = jnp.einsum(
        "ld,jlc->jdc", mixed_all, grad_projected, preferred_element_type=jnp.float32
    )
    grad_mixed_attn = lax.psum_scatter(
        jnp.einsum(
            "jlc,jdc->ld", grad_projected, qkv_full, preferred_element_type=jnp.float32
        ).astype(jnp.bfloat16),
        "tensor",
        scatter_dimension=0,
        tiled=True,
    ).astype(jnp.float32)
    grad_scale_attn = jnp.sum(grad_mixed_attn * normed_attn, axis=0)
    grad_shift_attn = jnp.sum(grad_mixed_attn, axis=0)
    grad_inputs = grad_middle + norm_back(
        grad_mixed_attn * (1.0 + modulation[2]), normed_attn, inverse_attn
    )
    mod_rows = jnp.stack(
        [
            grad_gamma_attn,
            grad_gamma_mlp,
            grad_scale_attn,
            grad_scale_mlp,
            grad_shift_attn,
            grad_shift_mlp,
            grad_proj_bias,
            grad_down_bias,
        ]
    )
    grad_modulation = lax.psum(mod_rows.astype(jnp.bfloat16), "tensor").astype(jnp.float32)
    col_start = lax.axis_index("tensor") * part_width
    cond_rows = lax.dynamic_slice_in_dim(
        condition_row.astype(jnp.float32), col_start, part_width, 0
    )
    silu_rows = jax.nn.silu(cond_rows).astype(jnp.bfloat16)
    mod_low = grad_modulation[:6].astype(jnp.bfloat16)
    grad_ada = jnp.einsum("r,jc->rjc", silu_rows, mod_low, preferred_element_type=jnp.float32)
    grad_silu = jnp.einsum("jc,rjc->r", mod_low, ada_full, preferred_element_type=jnp.float32)
    sigmoid_rows = jax.nn.sigmoid(cond_rows)
    grad_condition = grad_silu * sigmoid_rows * (1.0 + cond_rows * (1.0 - sigmoid_rows))
    own_cols = lax.dynamic_slice_in_dim(grad_modulation, col_start, part_width, 1)
    increments = (
        grad_ada,
        own_cols[:6].reshape(6, part_heads, head_dim),
        grad_qkv,
        grad_query_bias,
        grad_value_bias,
        grad_head_scale,
        grad_proj,
        own_cols[6].reshape(part_heads, head_dim),
        grad_up,
        grad_up_bias.reshape(part_heads, -1),
        grad_down,
        own_cols[7].reshape(part_heads, head_dim),
    )
    return (increments, grad_inputs, grad_condition)


def on_device(
    tokens,
    condition,
    scale_index,
    ada_weight,
    ada_bias,
    qkv_weight,
    query_bias,
    value_bias,
    head_scale,
    proj_weight,
    proj_bias,
    up_weight,
    up_bias,
    down_weight,
    down_bias,
    out_grad,
):

    def fetch_weights():
        return (
            lax.all_gather(ada_weight, "dp", axis=2, tiled=True),
            lax.all_gather(ada_bias, "dp", axis=2, tiled=True),
            lax.all_gather(qkv_weight, "dp", axis=1, tiled=True),
            lax.all_gather(query_bias, "dp", axis=1, tiled=True),
            lax.all_gather(value_bias, "dp", axis=1, tiled=True),
            lax.all_gather(proj_weight, "dp", axis=1, tiled=True),
            lax.all_gather(proj_bias, "dp", axis=1, tiled=True),
            lax.all_gather(up_weight, "dp", axis=0, tiled=True),
            lax.all_gather(up_bias, "dp", axis=1, tiled=True),
            lax.all_gather(down_weight, "dp", axis=1, tiled=True),
            lax.all_gather(down_bias, "dp", axis=1, tiled=True),
        )

    def forward_scan(carried, step_in):
        token_rows, condition_row, scale_row = step_in
        weights_now = fetch_weights()
        output, kept = forward_step(weights_now, token_rows, condition_row, scale_row, head_scale)
        return (carried, (output, kept))

    unused_carry, (outputs, kept_all) = lax.scan(
        forward_scan, jnp.zeros((), jnp.int32), (tokens, condition, scale_index)
    )
    width = tokens.shape[2]
    part_width = qkv_weight.shape[2]
    part_heads = head_scale.shape[0]
    head_dim = part_width // part_heads
    part_ff = up_weight.shape[1]
    zero_grads = (
        jnp.zeros((part_width, 6, width), jnp.float32),
        jnp.zeros((6, part_heads, head_dim), jnp.float32),
        jnp.zeros((3, width, part_width), jnp.float32),
        jnp.zeros((part_heads, head_dim), jnp.float32),
        jnp.zeros((part_heads, head_dim), jnp.float32),
        jnp.zeros((part_heads,), jnp.float32),
        jnp.zeros((part_width, width), jnp.float32),
        jnp.zeros((part_heads, head_dim), jnp.float32),
        jnp.zeros((width, part_ff), jnp.float32),
        jnp.zeros((part_heads, part_ff // part_heads), jnp.float32),
        jnp.zeros((part_ff, width), jnp.float32),
        jnp.zeros((part_heads, head_dim), jnp.float32),
    )

    def backward_scan(totals, step_in):
        kept, token_grad, condition_row, scale_row = step_in
        weights_now = fetch_weights()
        increments, grad_inputs, grad_condition = backward_step(
            weights_now, kept, token_grad, condition_row, scale_row, head_scale
        )
        totals = tuple((running + increment for running, increment in zip(totals, increments)))
        return (totals, (grad_inputs, grad_condition))

    totals, (grad_tokens, grad_condition) = lax.scan(
        backward_scan, zero_grads, (kept_all, out_grad, condition, scale_index), reverse=True
    )
    scale_total = lax.psum(totals[5], "dp")
    reduced = (
        lax.psum_scatter(
            totals[0].astype(jnp.bfloat16), "dp", scatter_dimension=2, tiled=True
        ).astype(jnp.float32),
        lax.psum_scatter(
            totals[1].astype(jnp.bfloat16), "dp", scatter_dimension=2, tiled=True
        ).astype(jnp.float32),
        lax.psum_scatter(
            totals[2].astype(jnp.bfloat16), "dp", scatter_dimension=1, tiled=True
        ).astype(jnp.float32),
        lax.psum_scatter(
            totals[3].astype(jnp.bfloat16), "dp", scatter_dimension=1, tiled=True
        ).astype(jnp.float32),
        lax.psum_scatter(
            totals[4].astype(jnp.bfloat16), "dp", scatter_dimension=1, tiled=True
        ).astype(jnp.float32),
        lax.psum_scatter(
            totals[6].astype(jnp.bfloat16), "dp", scatter_dimension=1, tiled=True
        ).astype(jnp.float32),
        lax.psum_scatter(
            totals[7].astype(jnp.bfloat16), "dp", scatter_dimension=1, tiled=True
        ).astype(jnp.float32),
        lax.psum_scatter(
            totals[8].astype(jnp.bfloat16), "dp", scatter_dimension=0, tiled=True
        ).astype(jnp.float32),
        lax.psum_scatter(
            totals[9].astype(jnp.bfloat16), "dp", scatter_dimension=1, tiled=True
        ).astype(jnp.float32),
        lax.psum_scatter(
            totals[10].astype(jnp.bfloat16), "dp", scatter_dimension=1, tiled=True
        ).astype(jnp.float32),
        lax.psum_scatter(
            totals[11].astype(jnp.bfloat16), "dp", scatter_dimension=1, tiled=True
        ).astype(jnp.float32),
    )
    return (
        outputs,
        grad_tokens,
        grad_condition,
        reduced[0],
        reduced[1],
        reduced[2],
        reduced[3],
        reduced[4],
        scale_total,
        reduced[5],
        reduced[6],
        reduced[7],
        reduced[8],
        reduced[9],
        reduced[10],
    )


GRIDS = {(16, 2): (4, 2, 2)}
MESH_ID = pl.DeviceIdType.MESH
ANY = pl.ANY
F32 = jnp.float32
BF16 = jnp.bfloat16
SCALES = 10
MASK = -16384.0


def place():
    return (lax.axis_index("dp"), lax.axis_index("tensor"))


def coords(grid):
    chip, core = place()
    nz, ny, nx = grid
    return (chip // (ny * nx), (chip // nx) % ny, chip % nx, core)


def greet_all(count):
    chip, core = place()
    me = chip * 2 + core
    barrier = pltpu.get_barrier_semaphore()
    for k in range(1, count):
        peer = (me + k) % count
        pl.semaphore_signal(barrier, inc=1, device_id=(peer // 2, peer % 2), device_id_type=MESH_ID)
    pl.semaphore_wait(barrier, count - 1)


def remote(src, dst, send_sem, recv_sem, device):
    return pltpu.make_async_remote_copy(
        src_ref=src,
        dst_ref=dst,
        send_sem=send_sem,
        recv_sem=recv_sem,
        device_id=device,
        device_id_type=MESH_ID,
    )


def swap_kernel(count, to_all, src_ref, dst_ref, local_sem, send_sem, recv_sem):
    chip, core = place()
    me = chip * 2 + core
    greet_all(count)
    own = pltpu.make_async_copy(src_ref if to_all else src_ref.at[me], dst_ref.at[me], local_sem)
    own.start()
    copies = []
    for k in range(1, count):
        peer = (me + k) % count
        copy = remote(
            src_ref if to_all else src_ref.at[peer],
            dst_ref.at[me],
            send_sem.at[k - 1],
            recv_sem.at[k - 1],
            (peer // 2, peer % 2),
        )
        copy.start()
        copies.append(copy)
    own.wait()
    for copy in copies:
        copy.wait()


def swap(values, count, to_all, collective_id, name):
    block = values.shape if to_all else values.shape[1:]
    return pl.pallas_call(
        functools.partial(swap_kernel, count, to_all),
        out_shape=jax.ShapeDtypeStruct((count,) + block, values.dtype),
        in_specs=[pl.BlockSpec(memory_space=pltpu.VMEM)],
        out_specs=pl.BlockSpec(memory_space=pltpu.VMEM),
        scratch_shapes=[
            pltpu.SemaphoreType.DMA,
            pltpu.SemaphoreType.DMA((count - 1,)),
            pltpu.SemaphoreType.DMA((count - 1,)),
        ],
        compiler_params=pltpu.CompilerParams(collective_id=collective_id, has_side_effects=True),
        name=name,
    )(values)

def greet(peers):
    barrier = pltpu.get_barrier_semaphore()
    for peer in peers:
        pl.semaphore_signal(barrier, inc=1, device_id=peer, device_id_type=MESH_ID)
    pl.semaphore_wait(barrier, len(peers))


def forward_kernel(
    grid,
    sizes,
    chunk_counts,
    shard,
    tok,
    grad_in,
    mod,
    query_spare,
    key_spare,
    query_bias,
    value_bias,
    key_scale,
    up_bias,
    ones,
    full,
    x_out,
    grad_out,
    mixed_out,
    qaug_out,
    kv_out,
    inverse_out,
    att_out,
    branch_out,
    mlp_out,
    slope_out,
    dm_out,
    grad_down_out,
    mlp_own,
    mlp_other,
    x,
    dm,
    mixed,
    part,
    other,
    turned,
    qaug,
    kv,
    inverses,
    att,
    w,
    slope,
    act,
    grad_down,
    local_sem,
    z_send,
    z_recv,
    p_send,
    p_recv,
    t_send,
    t_recv,
    load_sem,
    save_sem,
):
    nz, ny, nx = grid
    half = nz // 2
    seqs, pad = sizes
    chunks = shard.shape[0]
    ff_chunks = chunk_counts
    z, y, x_at, core = coords(grid)
    width = x.shape[1]
    part_width = att.shape[1]
    pairs = part_width // 128
    blocks = seqs * 2
    length = tok.shape[0]

    def dev(z_to, y_to, x_to):
        return ((z_to * ny + y_to) * nx + x_to, core)

    x_peer = dev(z, y, 1 - x_at)
    y_peer = dev(z, 1 - y, x_at)
    sibling = (place()[0], 1 - core)
    greet([x_peer, y_peer, sibling] + [dev((z + k) % nz, y, x_at) for k in range(1, nz)])

    def own_copy(c):
        return pltpu.make_async_copy(shard.at[c], full.at[c, z, y, x_at], local_sem.at[c])

    def z_copies(c):
        return [
            remote(
                shard.at[c],
                full.at[c, z, y, x_at],
                z_send.at[c, k - 1],
                z_recv.at[c, k - 1],
                dev((z + k) % nz, y, x_at),
            )
            for k in range(1, nz)
        ]

    def first_copies(c):
        low = full.at[c, pl.ds(0, half), y, x_at]
        high = full.at[c, pl.ds(half, half), y, x_at]
        return [
            remote(low, low, p_send.at[c, 0], p_recv.at[c, 0], x_peer),
            remote(high, high, p_send.at[c, 1], p_recv.at[c, 1], y_peer),
        ]

    def second_copies(c):
        low = full.at[c, pl.ds(0, half), y]
        high = full.at[c, pl.ds(half, half), :, x_at]
        return [
            remote(low, low, p_send.at[c, 2], p_recv.at[c, 2], y_peer),
            remote(high, high, p_send.at[c, 3], p_recv.at[c, 3], x_peer),
        ]

    ahead = 2
    progress = [-ahead]

    def advance(upto):
        while progress[0] <= upto:
            t = progress[0]
            if 0 <= t + ahead < chunks:
                own_copy(t + ahead).start()
                for copy in z_copies(t + ahead):
                    copy.start()
            if 0 <= t < chunks:
                own_copy(t).wait()
                for copy in z_copies(t):
                    copy.wait_recv()
                for copy in first_copies(t):
                    copy.start()
            if 0 <= t - 1 < chunks:
                for copy in first_copies(t - 1):
                    copy.wait_recv()
                for copy in second_copies(t - 1):
                    copy.start()
            if 0 <= t - 2 < chunks:
                for copy in second_copies(t - 2):
                    copy.wait_recv()
            progress[0] += 1

    def load(c):
        return pltpu.make_async_copy(full.at[c], w.at[c % 4], load_sem.at[c])

    def weight(c):
        return w[c % 4].reshape(width, part_width)

    saves = []

    def save(src, dst):
        copy = pltpu.make_async_copy(src, dst, save_sem.at[len(saves)])
        copy.start()
        saves.append(copy)
        return copy

    def block_rows(a):
        return pl.ds(pl.multiple_of(a * pad, 16), pad)

    advance(-1)

    def own_rows(s, which):
        return block_rows(s * 2 + which)

    swaps = []
    for i, (src, dst) in enumerate(((tok, x), (grad_in, dm))):
        for s in range(seqs):
            values = src[:, s, :].astype(F32).astype(BF16)
            start = pl.multiple_of((s * 2 + core) * pad, 16)
            dst[pl.ds(start + length // 16 * 16, pad - length // 16 * 16), :] = jnp.zeros(
                (pad - length // 16 * 16, width), BF16
            )
            dst[pl.ds(start, length), :] = values
            piece = dst.at[own_rows(s, core), :]
            copy = remote(piece, piece, t_send.at[i * seqs + s], t_recv.at[i * seqs + s], sibling)
            copy.start()
            swaps.append(copy)
    for copy in swaps[:seqs]:
        copy.wait()
    save(x, x_out)

    def mix_attn(a, rows):
        s = a // 2
        normed, unused = normalize(x[rows, :].astype(F32))
        mixed[rows, :] = (normed * (1.0 + mod[s, 2:3, :]) + mod[s, 4:5, :]).astype(BF16)

    for_blocks(blocks, pad, mix_attn)
    mixed_saved = save(mixed, mixed_out)
    advance(0)
    for copy in swaps[seqs:]:
        copy.wait()
    grad_saved = save(dm, grad_out)
    advance(1)
    grad_saved.wait()

    def scale_grad(a, rows):
        dm[rows, :] = (dm[rows, :].astype(F32) * mod[a // 2, 1:2, :]).astype(BF16)

    for_blocks(blocks, pad, scale_grad)
    save(dm, dm_out)
    advance(2)
    load(0).start()
    transpose_into(turned, dm)
    advance(3)
    load(1).start()

    load(0).wait()

    def project_q(a, rows):
        first, unused = lane_code(pad)
        q_spare = query_spare[rows, :].astype(F32)
        values = dot(mixed[rows, :], weight(0)) + query_bias[...]
        inv = lax.rsqrt(dot((values * values).astype(BF16), ones[...]) + HEAD_EPS)
        inverses[rows, 0:part_width] = inv.astype(BF16)
        values = values * inv * key_scale[...]
        for p in range(pairs):
            piece = values[:, p * 128 : p * 128 + 128]
            qaug[2 * p, rows, :] = jnp.where(first, piece, q_spare).astype(BF16)
            qaug[2 * p + 1, rows, :] = jnp.where(first, q_spare, piece).astype(BF16)

    for_blocks(blocks, pad, project_q)
    advance(4)
    load(2).start()
    load(1).wait()

    def project_k(a, rows):
        values = dot(mixed[rows, :], weight(1))
        inv = lax.rsqrt(dot((values * values).astype(BF16), ones[...]) + HEAD_EPS)
        inverses[rows, part_width : 2 * part_width] = inv.astype(BF16)
        kv[rows, 0:part_width] = (values * inv).astype(BF16)

    for_blocks(blocks, pad, project_k)
    save(inverses, inverse_out)
    load(2).wait()

    def project_v(a, rows):
        kv[rows, part_width : 2 * part_width] = (
            dot(mixed[rows, :], weight(2)) + value_bias[...]
        ).astype(BF16)

    for_blocks(blocks, pad, project_v)
    save(kv, kv_out)
    advance(5)
    load(3).start()

    def attend(i, carry):
        p = i // blocks
        block = i % blocks
        rows = block_rows(block)
        all_rows = pl.ds(pl.multiple_of((block // 2) * 2 * pad, 16), 2 * pad)
        at = pl.multiple_of(p * 128, 128)
        first, code = lane_code(pad)
        k_sides = both_heads(kv[all_rows, pl.ds(at, 128)], key_spare[all_rows, :])
        v_sides = both_heads(kv[all_rows, pl.ds(at + part_width, 128)], 1.0)
        outs = []
        for side in range(2):
            h = 2 * p + side
            q = qaug[h, rows, :]
            prob = jnp.exp2(dot_nt(q, k_sides[side])).astype(BF16)
            o = dot(prob, v_sides[side])
            outs.append(o / pltpu.roll(o, 64, 1))
            norm = -jnp.log2(o)
            high = norm.astype(BF16)
            rest = norm - high.astype(F32)
            middle = rest.astype(BF16)
            low = (rest - middle.astype(F32)).astype(BF16)
            spare = jnp.logical_not(first) if side == 0 else first
            q = q.astype(F32)
            for where, piece in enumerate((high, middle, low)):
                q = jnp.where(spare & (code == SCALES + where), piece.astype(F32), q)
            qaug[h, rows, :] = q.astype(BF16)
        att[rows, pl.ds(at, 128)] = jnp.where(first, outs[0], outs[1]).astype(BF16)
        return carry

    count = pairs * blocks
    for quarter in range(2):
        lax.fori_loop(quarter * count // 2, (quarter + 1) * count // 2, attend, 0)
        advance(6 + quarter)
        load(4 + quarter).start()
    save(qaug, qaug_out)
    save(att, att_out)
    load(3).wait()
    part_copies = []
    for a in range(blocks):
        rows = block_rows(a)
        part[rows, :] = dot_nt(att[rows, :], weight(3)).astype(BF16)
        copy = remote(
            part.at[rows, :], other.at[rows, :], t_send.at[2 * seqs + a], t_recv.at[2 * seqs + a], sibling
        )
        copy.start()
        part_copies.append(copy)
    mixed_saved.wait()
    mlp = mixed
    for a in range(blocks):
        rows = block_rows(a)
        s = a // 2
        part_copies[a].wait()
        b = part[rows, :].astype(F32) + other[rows, :].astype(F32) + mod[s, 6:7, :]
        other[rows, :] = b.astype(BF16)
        normed, unused = normalize(x[rows, :].astype(F32) + mod[s, 0:1, :] * b)
        mlp[rows, :] = (normed * (1.0 + mod[s, 3:4, :]) + mod[s, 5:6, :]).astype(BF16)
    save(other, branch_out)
    save(mlp, mlp_out)
    for c in range(ff_chunks):
        advance(6 + c)
        if c >= 2:
            load(4 + c).start()
        load(4 + c).wait()

        def raise_rows(a, rows):
            h = dot(mlp[rows, :], weight(4 + c)) + up_bias[c]
            square = h * h
            t = jnp.tanh(h * (GELU_COEF + GELU_COEF * GELU_CUBE * square))
            act[c, rows, :] = (0.5 * h * (1.0 + t)).astype(BF16)
            slope[c, rows, :] = (
                0.5 * (1.0 + t)
                + h * (1.0 - t * t) * (0.5 * GELU_COEF + 1.5 * GELU_COEF * GELU_CUBE * square)
            ).astype(BF16)

        for_blocks(blocks, pad, raise_rows)
        save(slope.at[c], slope_out.at[c])
    down_saved = []
    for c in range(ff_chunks):
        advance(10 + c)
        load(8 + c).start()
        if c >= 2:
            down_saved[c - 2].wait()
        weight_grad(grad_down.at[c % 2], turned, act.at[c])
        down_saved.append(save(grad_down.at[c % 2], grad_down_out.at[c]))
    for c in range(ff_chunks):
        load(8 + c).wait()
    end_copies = []
    for step in range(blocks):
        s = step % seqs
        which = 1 - core if step < seqs else core
        rows = own_rows(s, which)
        total = dot_nt(act[0, rows, :], weight(8))
        for c in range(1, ff_chunks):
            total = total + dot_nt(act[c, rows, :], weight(8 + c))
        part[rows, :] = total.astype(BF16)
        if step < seqs:
            copy = remote(
                part.at[rows, :],
                mlp_other.at[s],
                t_send.at[2 * seqs + blocks + s],
                t_recv.at[2 * seqs + blocks + s],
                sibling,
            )
            copy.start()
            end_copies.append(copy)
        else:
            save(part.at[rows, :], mlp_own.at[s])
    for copy in end_copies:
        copy.wait()
    done = [mixed_saved, grad_saved] + down_saved[:-2]
    for copy in saves:
        if all(copy is not other_copy for other_copy in done):
            copy.wait()
    for c in range(chunks):
        for copy in z_copies(c) + first_copies(c) + second_copies(c):
            copy.wait_send()


def forward_pass(grid, sizes, shard, tok, grad_in, mod, query_spare, key_spare, query_bias, value_bias, key_scale, up_bias, ones, collective_id):
    nz, ny, nx = grid
    seqs, pad = sizes
    chunks, own_rows, part = shard.shape
    ff_chunks = up_bias.shape[0]
    width = tok.shape[2]
    total = seqs * 2 * pad
    heads = part // 64
    wide = ((total, width), BF16)
    narrow = ((total, part), BF16)
    chunk = (nz, ny, nx, own_rows, part)
    outs = [
        ((chunks,) + chunk, BF16),
        wide,
        wide,
        wide,
        ((heads, total, 128), BF16),
        wide,
        wide,
        narrow,
        wide,
        wide,
        ((ff_chunks, total, part), BF16),
        wide,
        ((ff_chunks,) + chunk, BF16),
        ((seqs, pad, width), BF16),
        ((seqs, pad, width), BF16),
    ]
    scratch = [
        wide,
        wide,
        wide,
        wide,
        wide,
        ((width, total), BF16),
        ((heads, total, 128), BF16),
        wide,
        wide,
        narrow,
        ((4,) + chunk, BF16),
        ((ff_chunks, total, part), BF16),
        ((ff_chunks, total, part), BF16),
        ((2,) + chunk, BF16),
    ]
    swaps = 3 * seqs + seqs * 2
    vmem = pl.BlockSpec(memory_space=pltpu.VMEM)
    hbm = pl.BlockSpec(memory_space=ANY)
    return pl.pallas_call(
        functools.partial(forward_kernel, grid, sizes, ff_chunks),
        out_shape=[jax.ShapeDtypeStruct(shape, dtype) for shape, dtype in outs],
        in_specs=[hbm] + [vmem] * 10,
        out_specs=[hbm] * len(outs),
        scratch_shapes=[pltpu.VMEM(shape, dtype) for shape, dtype in scratch]
        + [
            pltpu.SemaphoreType.DMA((chunks,)),
            pltpu.SemaphoreType.DMA((chunks, nz - 1)),
            pltpu.SemaphoreType.DMA((chunks, nz - 1)),
            pltpu.SemaphoreType.DMA((chunks, 4)),
            pltpu.SemaphoreType.DMA((chunks, 4)),
            pltpu.SemaphoreType.DMA((swaps,)),
            pltpu.SemaphoreType.DMA((swaps,)),
            pltpu.SemaphoreType.DMA((chunks,)),
            pltpu.SemaphoreType.DMA((24,)),
        ],
        compiler_params=pltpu.CompilerParams(
            collective_id=collective_id, has_side_effects=True, vmem_limit_bytes=60 * 2**20
        ),
        name="forward_pass",
    )(shard, tok, grad_in, mod, query_spare, key_spare, query_bias, value_bias, key_scale, up_bias, ones)


def dot(a, b):
    return jnp.dot(a, b, preferred_element_type=F32)


def dot_nt(a, b):
    return lax.dot_general(a, b, (((1,), (1,)), ((), ())), preferred_element_type=F32)


def dot_tn(a, b):
    return lax.dot_general(a, b, (((0,), (0,)), ((), ())), preferred_element_type=F32)


def lane_code(rows):
    lane = lax.broadcasted_iota(jnp.int32, (rows, 128), 1)
    return lane < 64, lane & 63


def both_heads(pair, spare):
    first, unused = lane_code(pair.shape[0])
    pair = pair.astype(F32)
    if not isinstance(spare, float):
        spare = spare.astype(F32)
    return (
        jnp.where(first, pair, spare).astype(BF16),
        jnp.where(first, spare, pair).astype(BF16),
    )


def column_sum(values):
    return jnp.sum(values, axis=0, keepdims=True)


def transpose_into(dst, src):
    def step(i, carry):
        at = pl.multiple_of(i * 128, 128)
        dst[:, pl.ds(at, 128)] = src[pl.ds(at, 128), :].T
        return carry

    lax.fori_loop(0, src.shape[0] // 128, step, 0)


def weight_grad(dst, turned, right):
    rows = turned.shape[0] // dst.shape[0]

    def step(i, carry):
        at = pl.ds(pl.multiple_of(i * rows, rows), rows)
        dst[i] = dot(turned[at, :], right[...]).astype(BF16).reshape(dst.shape[1:])
        return carry

    lax.fori_loop(0, dst.shape[0], step, 0)


def for_blocks(count, rows, body):
    def step(a, carry):
        body(a, pl.ds(pl.multiple_of(a * rows, 16), rows))
        return carry

    lax.fori_loop(0, count, step, 0)

def backward_kernel(
    grid,
    sizes,
    full,
    x_in,
    grad_in,
    mixed_in,
    qaug_in,
    kv_in,
    inverse_in,
    att_in,
    branch_in,
    mlp_in,
    slope_in,
    dm_in,
    grad_down_in,
    mod,
    key_spare,
    key_scale,
    ones,
    out,
    mid_own,
    ga_own,
    ga_other,
    stats,
    up_sum,
    qkv_sum,
    b0,
    b1,
    b2,
    b3,
    b4,
    turned,
    pool,
    qaug,
    w,
    work,
    got_low,
    got_high,
    next_low,
    next_high,
    got_z,
    p_send,
    p_recv,
    z_send,
    z_recv,
    t_send,
    t_recv,
    load_sem,
):
    nz, ny, nx = grid
    half = nz // 2
    seqs, pad = sizes
    chunks = out.shape[0]
    slots = work.shape[0]
    ff_chunks = slope_in.shape[0]
    z, y, x_at, core = coords(grid)
    width = b0.shape[1]
    part_width = pool.shape[2]
    pairs = part_width // 128
    blocks = seqs * 2
    ln2 = 0.6931471805599453

    def dev(z_to, y_to, x_to):
        return ((z_to * ny + y_to) * nx + x_to, core)

    x_peer = dev(z, y, 1 - x_at)
    y_peer = dev(z, 1 - y, x_at)
    sibling = (place()[0], 1 - core)
    greet([x_peer, y_peer, sibling] + [dev((z + k) % nz, y, x_at) for k in range(1, nz)])

    def block_rows(a):
        return pl.ds(pl.multiple_of(a * pad, 16), pad)

    loads = []

    def load(src, dst):
        copy = pltpu.make_async_copy(src, dst, load_sem.at[len(loads)])
        copy.start()
        loads.append(copy)
        return copy

    def first_copies(c):
        s = c % slots
        return [
            remote(
                work.at[s, pl.ds(0, half), 1 - y], got_low.at[c], p_send.at[c, 0], p_recv.at[c, 0], y_peer
            ),
            remote(
                work.at[s, pl.ds(half, half), :, 1 - x_at],
                got_high.at[c],
                p_send.at[c, 1],
                p_recv.at[c, 1],
                x_peer,
            ),
        ]

    def second_copies(c):
        s = c % slots
        return [
            remote(
                work.at[s, pl.ds(0, half), y, 1 - x_at],
                next_low.at[c],
                p_send.at[c, 2],
                p_recv.at[c, 2],
                x_peer,
            ),
            remote(
                work.at[s, pl.ds(half, half), 1 - y, x_at],
                next_high.at[c],
                p_send.at[c, 3],
                p_recv.at[c, 3],
                y_peer,
            ),
        ]

    def z_copies(c):
        s = c % slots
        return [
            remote(
                work.at[s, (z + k) % nz, y, x_at],
                got_z.at[c, k - 1],
                z_send.at[c, k - 1],
                z_recv.at[c, k - 1],
                dev((z + k) % nz, y, x_at),
            )
            for k in range(1, nz)
        ]

    def add(a, b):
        return (a.astype(F32) + b.astype(F32)).astype(BF16)

    def begin(c):
        for copy in first_copies(c):
            copy.start()

    def second(c):
        s = c % slots
        for copy in first_copies(c):
            copy.wait_recv()
        work[s, 0:half, y] = add(work[s, 0:half, y], got_low[c])
        work[s, half:nz, :, x_at] = add(work[s, half:nz, :, x_at], got_high[c])
        for copy in second_copies(c):
            copy.start()

    def third(c):
        s = c % slots
        for copy in second_copies(c):
            copy.wait_recv()
        work[s, 0:half, y, x_at] = add(work[s, 0:half, y, x_at], next_low[c])
        work[s, half:nz, y, x_at] = add(work[s, half:nz, y, x_at], next_high[c])
        for copy in z_copies(c):
            copy.start()

    def last(c):
        s = c % slots
        for copy in z_copies(c):
            copy.wait_recv()
        total = work[s, z, y, x_at].astype(F32)
        for k in range(nz - 1):
            total = total + got_z[c, k].astype(F32)
        out[c] = total

    def sent(c):
        for copy in first_copies(c) + second_copies(c) + z_copies(c):
            copy.wait_send()

    def put(c, right):
        if c >= slots:
            sent(c - slots)
        weight_grad(work.at[c % slots], turned, right)

    def step(t, start=True):
        if start and t < chunks:
            begin(t)
        if 0 <= t - 2 < chunks:
            second(t - 2)
        if 0 <= t - 3 < chunks:
            third(t - 3)
        if 0 <= t - 4 < chunks:
            last(t - 4)

    def weight(slot):
        return w[slot].reshape(width, part_width)

    down_grads = [load(grad_down_in.at[c], work.at[c]) for c in range(ff_chunks)]
    mlp_load = load(mlp_in, b1)
    dm_load = load(dm_in, b0)
    down_loads = [
        (load(full.at[chunks - ff_chunks + c], w.at[c]), load(slope_in.at[c], pool.at[c]))
        for c in range(ff_chunks)
    ]
    branch_load = load(branch_in, b4)
    qaug_load = load(qaug_in, qaug)
    for c in range(2):
        down_grads[c].wait()
        step(c)
    for c in range(2, ff_chunks):
        down_grads[c].wait()
    mlp_load.wait()
    transpose_into(turned, b1)
    grad_load = load(grad_in, b1)
    dm_load.wait()
    up_sum[...] = jnp.zeros_like(up_sum)
    up_loads = []
    for c in range(ff_chunks):
        for copy in down_loads[c]:
            copy.wait()

        def back(a, rows):
            gh = dot(b0[rows, :], weight(c)) * pool[c, rows, :].astype(F32)
            up_sum[c] += column_sum(gh)
            pool[c, rows, :] = gh.astype(BF16)

        for_blocks(blocks, pad, back)
        up_loads.append(load(full.at[4 + c], w.at[c]))
        put(ff_chunks + c, pool.at[c])
        if c != 1:
            step(2 + (c + 1) // 2)
    x_load = load(x_in, b0)
    for copy in up_loads:
        copy.wait()
    swaps = []
    for a in range(blocks):
        rows = block_rows(a)
        total = dot_nt(pool[0, rows, :], weight(0))
        for c in range(1, ff_chunks):
            total = total + dot_nt(pool[c, rows, :], weight(c))
        b2[rows, :] = total.astype(BF16)
        copy = remote(b2.at[rows, :], b3.at[rows, :], t_send.at[a], t_recv.at[a], sibling)
        copy.start()
        swaps.append(copy)
    proj_load = load(full.at[3], w.at[3])
    qkv_loads = [load(full.at[j], w.at[j]) for j in range(3)]
    step(5)
    for copy in (x_load, grad_load, branch_load, proj_load):
        copy.wait()
    stats[...] = jnp.zeros_like(stats)
    grad_att = pool.at[3]
    for a in range(blocks):
        rows = block_rows(a)
        s = a // 2
        swaps[a].wait()
        b = b4[rows, :].astype(F32)
        gm = b2[rows, :].astype(F32) + b3[rows, :].astype(F32)
        normed, inverse = normalize(b0[rows, :].astype(F32) + mod[s, 0:1, :] * b)
        stats[s, 1:2, :] += 0.5 * column_sum(gm * normed)
        stats[s, 2:3, :] += 0.5 * column_sum(gm)
        mid = b1[rows, :].astype(F32) + norm_back(gm * (1.0 + mod[s, 3:4, :]), normed, inverse)
        b1[rows, :] = mid.astype(BF16)
        stats[s, 0:1, :] += 0.5 * column_sum(mid * b)
        branch_grad = mid * mod[s, 0:1, :]
        stats[s, 3:4, :] += 0.5 * column_sum(branch_grad)
        low = branch_grad.astype(BF16)
        b4[rows, :] = low
        grad_att[rows, :] = dot(low, weight(3)).astype(BF16)
        if a == 1:
            step(6)
    mid_saves = [load(b1.at[block_rows(s * 2 + core), :], mid_own.at[s]) for s in range(seqs)]
    att = b2.at[:, pl.ds(0, part_width)]
    att_load = load(att_in, att)
    kv_load = load(kv_in, b3)
    transpose_into(turned, b4)
    step(7)
    mixed_load = load(mixed_in, b4)
    att_load.wait()
    put(8, att)
    inverse_load = load(inverse_in, b2)
    kv_load.wait()
    qaug_load.wait()
    qkv_sum[...] = jnp.zeros_like(qkv_sum)

    def attend(i, carry):
        p = i // seqs
        s = i % seqs
        start = pl.multiple_of(s * 2 * pad, 16)
        all_rows = pl.ds(start, 2 * pad)
        at = pl.multiple_of(p * 128, 128)
        lanes = pl.ds(at, 128)
        first, unused = lane_code(pad)
        first_all, unused = lane_code(2 * pad)
        k_sides = both_heads(b3[all_rows, lanes], key_spare[all_rows, :])
        v_sides = both_heads(b3[all_rows, pl.ds(at + part_width, 128)], 0.0)
        g_sides = both_heads(pool[3, all_rows, lanes], 0.0)
        grads_k, grads_v, grads_q = [], [], [[], []]
        for side in range(2):
            h = 2 * p + side
            k = k_sides[side]
            v = v_sides[side]
            sum_k = sum_v = None
            for t in range(2):
                rows = pl.ds(pl.multiple_of(start + t * pad, 16), pad)
                q = qaug[h, rows, :]
                g = g_sides[side][t * pad : t * pad + pad]
                prob = jnp.exp2(dot_nt(k, q))
                grad_prob = dot_nt(v, g)
                ds = (prob * (grad_prob - column_sum(prob * grad_prob))).astype(BF16)
                gv = dot(prob.astype(BF16), g)
                gk = dot(ds, q)
                sum_v = gv if t == 0 else sum_v + gv
                sum_k = gk if t == 0 else sum_k + gk
                grads_q[t].append(dot_tn(ds, k))
            grads_k.append(sum_k)
            grads_v.append(sum_v)
        for t in range(2):
            rows = pl.ds(pl.multiple_of(start + t * pad, 16), pad)
            gq = jnp.where(first, grads_q[t][0], grads_q[t][1])
            q = jnp.where(first, qaug[2 * p, rows, :].astype(F32), qaug[2 * p + 1, rows, :].astype(F32))
            qkv_sum[2:3, lanes] += ln2 * column_sum(gq * q)
            pool[0, rows, lanes] = gq.astype(BF16)
        pool[1, all_rows, lanes] = (ln2 * jnp.where(first_all, grads_k[0], grads_k[1])).astype(BF16)
        gv = jnp.where(first_all, grads_v[0], grads_v[1])
        qkv_sum[1:2, lanes] += column_sum(gv)
        pool[2, all_rows, lanes] = gv.astype(BF16)
        return carry

    count = pairs * seqs
    for quarter in range(4):
        lax.fori_loop(quarter * count // 4, (quarter + 1) * count // 4, attend, 0)
        if quarter == 0:
            step(8)
        elif quarter < 3:
            step(8 + quarter, start=False)
    third(8)
    last(7)
    mixed_load.wait()
    transpose_into(turned, b4)
    put(9, pool.at[2])
    begin(9)
    inverse_load.wait()

    def finish_q(a, rows):
        first, unused = lane_code(pad)
        scale = key_scale[...]
        unit = jnp.concatenate(
            [
                jnp.where(first, qaug[2 * p, rows, :].astype(F32), qaug[2 * p + 1, rows, :].astype(F32))
                for p in range(pairs)
            ],
            axis=1,
        )
        unit = unit / scale
        f = pool[0, rows, :].astype(F32) * (scale * ln2)
        gq = b2[rows, 0:part_width].astype(F32) * (f - unit * dot((f * unit).astype(BF16), ones[...]))
        qkv_sum[0:1, :] += column_sum(gq)
        pool[0, rows, :] = gq.astype(BF16)

    def finish_k(a, rows):
        unit = b3[rows, 0:part_width].astype(F32)
        f = pool[1, rows, :].astype(F32)
        gk = b2[rows, part_width : 2 * part_width].astype(F32) * (
            f - unit * dot((f * unit).astype(BF16), ones[...])
        )
        pool[1, rows, :] = gk.astype(BF16)

    for_blocks(blocks, pad, finish_q)
    put(10, pool.at[0])
    begin(10)
    last(8)
    for_blocks(blocks, pad, finish_k)
    put(11, pool.at[1])
    begin(11)
    second(9)
    for copy in qkv_loads:
        copy.wait()
    end_copies = []
    end_saves = []
    for i in range(blocks):
        s = i % seqs
        which = 1 - core if i < seqs else core
        rows = block_rows(s * 2 + which)
        total = dot_nt(pool[0, rows, :], weight(0))
        for j in range(1, 3):
            total = total + dot_nt(pool[j, rows, :], weight(j))
        b0[rows, :] = total.astype(BF16)
        if i < seqs:
            copy = remote(b0.at[rows, :], ga_other.at[s], t_send.at[blocks + s], t_recv.at[blocks + s], sibling)
            copy.start()
            end_copies.append(copy)
        else:
            end_saves.append(load(b0.at[rows, :], ga_own.at[s]))
        if i == 1:
            second(10)
            third(9)
    second(11)
    third(10)
    last(9)
    third(11)
    last(10)
    last(11)
    for copy in end_copies + end_saves + mid_saves:
        copy.wait()
    for c in range(chunks - slots, chunks):
        sent(c)


def backward_pass(grid, sizes, operands, mod, key_spare, key_scale, ones, collective_id):
    nz, ny, nx = grid
    half = nz // 2
    seqs, pad = sizes
    full, slope = operands[0], operands[10]
    chunks = full.shape[0]
    own_rows, part = full.shape[4:]
    ff_chunks = slope.shape[0]
    total = seqs * 2 * pad
    width = nz * ny * nx * own_rows
    heads = part // 64
    wide = ((total, width), BF16)
    chunk = (nz, ny, nx, own_rows, part)
    block = (own_rows, part)
    slots = 8
    outs = [
        ((chunks,) + block, F32),
        ((seqs, pad, width), BF16),
        ((seqs, pad, width), BF16),
        ((seqs, pad, width), BF16),
        ((seqs, 4, width), F32),
        ((ff_chunks, 1, part), F32),
        ((8, part), F32),
    ]
    scratch = [wide] * 5 + [
        ((width, total), BF16),
        ((ff_chunks, total, part), BF16),
        ((heads, total, 128), BF16),
        ((4,) + chunk, BF16),
        ((slots,) + chunk, BF16),
        ((chunks, half, nx) + block, BF16),
        ((chunks, half, ny) + block, BF16),
        ((chunks, half) + block, BF16),
        ((chunks, half) + block, BF16),
        ((chunks, nz - 1) + block, BF16),
    ]
    vmem = pl.BlockSpec(memory_space=pltpu.VMEM)
    hbm = pl.BlockSpec(memory_space=ANY)
    swaps = seqs * 2 + seqs
    return pl.pallas_call(
        functools.partial(backward_kernel, grid, sizes),
        out_shape=[jax.ShapeDtypeStruct(shape, dtype) for shape, dtype in outs],
        in_specs=[hbm] * 13 + [vmem] * 4,
        out_specs=[vmem] + [hbm] * 3 + [vmem] * 3,
        scratch_shapes=[pltpu.VMEM(shape, dtype) for shape, dtype in scratch]
        + [
            pltpu.SemaphoreType.DMA((chunks, 4)),
            pltpu.SemaphoreType.DMA((chunks, 4)),
            pltpu.SemaphoreType.DMA((chunks, nz - 1)),
            pltpu.SemaphoreType.DMA((chunks, nz - 1)),
            pltpu.SemaphoreType.DMA((swaps,)),
            pltpu.SemaphoreType.DMA((swaps,)),
            pltpu.SemaphoreType.DMA((40,)),
        ],
        compiler_params=pltpu.CompilerParams(
            collective_id=collective_id, has_side_effects=True, vmem_limit_bytes=60 * 2**20
        ),
        name="backward_pass",
    )(*operands, mod, key_spare, key_scale, ones)


def finish_rows(sizes, x, grad, branch, mlp_part, mlp_other, grad_mid, grad_part, grad_other, mod, output, grad_tokens, stats):
    seqs, pad = sizes
    core = lax.axis_index("tensor")
    length = output.shape[0]
    for s in range(seqs):
        rows = pl.ds(pl.multiple_of((s * 2 + core) * pad, 16), pad)
        b = mlp_part[s].astype(F32) + mlp_other[s].astype(F32) + mod[s, 7:8, :]
        g = grad[rows, :].astype(F32)
        xs = x[rows, :].astype(F32)
        middle = xs + mod[s, 0:1, :] * branch[rows, :].astype(F32)
        out = middle + mod[s, 1:2, :] * b
        output[:, s, :] = out[0:length]
        stats[s, 0:1, :] = column_sum(g * b)
        stats[s, 1:2, :] = column_sum(g * mod[s, 1:2, :])
        normed, inverse = normalize(xs)
        gm = grad_part[s].astype(F32) + grad_other[s].astype(F32)
        stats[s, 2:3, :] = column_sum(gm * normed)
        stats[s, 3:4, :] = column_sum(gm)
        gt = grad_mid[s].astype(F32) + norm_back(gm * (1.0 + mod[s, 2:3, :]), normed, inverse)
        grad_tokens[:, s, :] = gt[0:length]
        stats[s, 4:8, :] = jnp.zeros_like(stats[s, 4:8, :])


def run(body, sizes, operands, outs, scratch=(), name=None):
    def kernel(*refs):
        body(sizes, *refs)

    return pl.pallas_call(
        kernel,
        out_shape=[jax.ShapeDtypeStruct(shape, dtype) for shape, dtype in outs],
        in_specs=[pl.BlockSpec(memory_space=pltpu.VMEM)] * len(operands),
        out_specs=[pl.BlockSpec(memory_space=pltpu.VMEM)] * len(outs),
        scratch_shapes=[pltpu.VMEM(shape, dtype) for shape, dtype in scratch],
        compiler_params=pltpu.CompilerParams(vmem_limit_bytes=60 * 2**20),
        name=name,
    )(*operands)


def pad_rows(values, rows):
    count, length = values.shape
    return jnp.pad(values, ((0, 0), (0, rows * 128 - length))).reshape(count, rows, 128)


def fast_device(
    grid,
    tokens,
    condition,
    scale_index,
    ada_weight,
    ada_bias,
    qkv_weight,
    query_bias,
    value_bias,
    head_scale,
    proj_weight,
    proj_bias,
    up_weight,
    up_bias,
    down_weight,
    down_bias,
    out_grad,
):
    nz, ny, nx = grid
    dp = nz * ny * nx
    count = dp * 2
    seqs, own_len, width = tokens.shape
    seq_len = own_len * 2
    part = qkv_weight.shape[2]
    heads = head_scale.shape[0]
    head_dim = part // heads
    own_rows = qkv_weight.shape[1]
    ff_chunks = up_weight.shape[1] // part
    chip, core = place()

    shard = jnp.concatenate(
        [
            qkv_weight,
            proj_weight.T[None],
            up_weight.reshape(own_rows, ff_chunks, part).transpose(1, 0, 2),
            down_weight.T.reshape(own_rows, ff_chunks, part).transpose(1, 0, 2),
        ],
        axis=0,
    )
    pad = -(-own_len // 16) * 16
    total = seqs * 2 * pad
    sizes = (seqs, pad)
    pieces = [condition, ada_bias, query_bias, value_bias, proj_bias, up_bias, down_bias]
    small = jnp.concatenate([piece.reshape(1, -1) for piece in pieces], axis=1)
    small_rows = -(-small.shape[1] // (16 * 128)) * 16
    every = swap(pad_rows(small, small_rows)[0], count, True, 1, "gather_small")
    every = every.reshape(dp, 2, small_rows * 128)
    parts, at = [], 0
    for piece in pieces:
        parts.append(every[:, :, at : at + piece.size].reshape((dp, 2) + piece.shape).astype(F32))
        at += piece.size
    cond_all = parts[0][:, 0].reshape(dp * seqs, width)
    own_of = lambda values: lax.dynamic_index_in_dim(values, core, 1, keepdims=False)
    spread = lambda values: values.transpose(1, 0, 2).reshape(-1)
    both = lambda values: values.transpose(1, 2, 0, 3).reshape(-1)
    ada_bias_full = parts[1].transpose(2, 1, 3, 0, 4).reshape(6, width)
    query_bias_own = spread(own_of(parts[2]))
    value_bias_own = spread(own_of(parts[3]))
    proj_bias_full = both(parts[4])
    up_bias_own = spread(own_of(parts[5]))
    down_bias_full = both(parts[6])

    cond_half = lax.dynamic_slice_in_dim(cond_all, core * part, part, 1)
    silu_half = jax.nn.silu(cond_half).astype(BF16)
    mod_part = jnp.einsum("sr,rjc->sjc", silu_half, ada_weight, preferred_element_type=F32)
    cols = mod_part.shape[2]
    mod_send = jnp.repeat(pad_rows(mod_part.reshape(dp, seqs * 6 * cols), 8), 2, axis=0)
    mod_got = swap(mod_send, count, False, 2, "swap_modulation")
    mod_got = mod_got.reshape(dp, 2, -1)[:, :, : seqs * 6 * cols].sum(axis=1)
    modulation = mod_got.reshape(dp, seqs, 6, cols).transpose(1, 2, 0, 3).reshape(seqs, 6, width)
    modulation = modulation + ada_bias_full
    ends = jnp.stack([proj_bias_full, down_bias_full])
    mod = jnp.concatenate([modulation, jnp.broadcast_to(ends, (seqs,) + ends.shape)], axis=1)

    level = jnp.pad(
        scale_index.reshape(seqs, 2, own_len), ((0, 0), (0, 0), (0, pad - own_len)), constant_values=100
    ).reshape(total, 1)
    code = jnp.arange(128)[None] % 64
    query_spare = jnp.where(code == level, 1.0, 0.0).astype(BF16)
    key_spare = jnp.where(
        code < SCALES, jnp.where(level > code, MASK, 0.0), jnp.where(code < SCALES + 3, 1.0, 0.0)
    ).astype(BF16)
    key_scale = jnp.repeat(jnp.exp(head_scale) * 1.4426950408889634, head_dim).reshape(1, part)
    head_at = jnp.arange(part) // head_dim
    ones = (head_at[:, None] == head_at[None, :]).astype(BF16)
    (
        full,
        x,
        grad,
        mixed,
        qaug,
        kv,
        inverses,
        att,
        branch,
        mlp,
        slope,
        dm,
        grad_down,
        mlp_part,
        mlp_other,
    ) = forward_pass(
        grid,
        sizes,
        shard,
        tokens.transpose(1, 0, 2),
        out_grad.transpose(1, 0, 2),
        mod,
        query_spare,
        key_spare,
        query_bias_own[None],
        value_bias_own[None],
        key_scale,
        up_bias_own.reshape(ff_chunks, 1, part),
        ones,
        0,
    )
    reduced, grad_mid, ga_part, ga_other, mid_stats, up_sum, qkv_sum = backward_pass(
        grid,
        sizes,
        (full, x, grad, mixed, qaug, kv, inverses, att, branch, mlp, slope, dm, grad_down),
        mod,
        key_spare,
        key_scale,
        ones,
        5,
    )
    output, grad_inputs, end_stats = run(
        finish_rows,
        sizes,
        (x, grad, branch, mlp_part, mlp_other, grad_mid, ga_part, ga_other, mod),
        [((own_len, seqs, width), F32), ((own_len, seqs, width), F32), ((seqs, 8, width), F32)],
        name="finish_rows",
    )
    grad_head_scale = jnp.sum(qkv_sum[2].reshape(heads, head_dim), axis=1)

    grad_mod = jnp.stack(
        [
            mid_stats[:, 0],
            end_stats[:, 0],
            end_stats[:, 2],
            mid_stats[:, 1],
            end_stats[:, 3],
            mid_stats[:, 2],
        ],
        axis=1,
    )
    grad_proj_bias = jnp.sum(mid_stats[:, 3], axis=0)
    grad_down_bias = jnp.sum(end_stats[:, 1], axis=0)
    twice = lambda values: jnp.repeat(values[:, None], 2, axis=1)
    to_owner = lambda values: values.reshape(heads, dp, -1).transpose(1, 0, 2).reshape(dp, -1)
    to_both = lambda values: (
        values.reshape(2, heads, dp, -1).transpose(2, 0, 1, 3).reshape(dp, 2, -1)
    )
    send = jnp.concatenate(
        [
            twice(grad_mod.reshape(seqs, 6, dp, cols).transpose(2, 0, 1, 3).reshape(dp, -1)),
            twice(to_owner(qkv_sum[0])),
            twice(to_owner(qkv_sum[1])),
            twice(to_owner(up_sum)),
            jnp.broadcast_to(grad_head_scale, (dp, 2, heads)),
            to_both(grad_proj_bias),
            to_both(grad_down_bias),
        ],
        axis=2,
    )
    rows = -(-send.shape[2] // (8 * 128)) * 8
    got = swap(pad_rows(send.reshape(count, -1), rows), count, False, 3, "swap_grads")
    got = got.reshape(dp, 2, -1)
    n_mod = seqs * 6 * cols
    mod_low = jnp.sum(got[:, :, :n_mod], axis=1).reshape(dp * seqs, 6, cols)
    grad_ada_bias_cols = jnp.sum(mod_low, axis=0)
    mod_low = mod_low.astype(BF16)
    own_sums = jnp.sum(own_of(got), axis=0)
    all_sums = jnp.sum(got, axis=(0, 1))
    owned, at = [], n_mod
    for piece, sums in (
        (query_bias, own_sums),
        (value_bias, own_sums),
        (up_bias, own_sums),
        (head_scale, own_sums),
        (proj_bias, all_sums),
        (down_bias, all_sums),
    ):
        owned.append(sums[at : at + piece.size].reshape(piece.shape))
        at += piece.size
    grad_ada = jnp.einsum("sr,sjc->rjc", silu_half, mod_low, preferred_element_type=F32)
    cond_part = jnp.einsum("sjc,rjc->sr", mod_low, ada_weight, preferred_element_type=F32)
    return_send = jnp.repeat(cond_part.reshape(dp, seqs * part // 128, 128), 2, axis=0)
    ada_bias_send = jnp.broadcast_to(
        jnp.pad(grad_ada_bias_cols.reshape(1, -1), ((0, 0), (0, 1024 - 6 * cols))).reshape(1, 8, 128),
        (count, 8, 128),
    )
    last = swap(
        jnp.concatenate([return_send, ada_bias_send], axis=1), count, False, 4, "swap_condition"
    )
    last = own_of(last.reshape(dp, 2, -1))
    grad_silu = jnp.sum(last[:, : seqs * part], axis=0).reshape(seqs, part)
    cond_own = lax.dynamic_slice_in_dim(condition.astype(F32), core * part, part, 1)
    sigmoid = jax.nn.sigmoid(cond_own)
    grad_condition = grad_silu * sigmoid * (1.0 + cond_own * (1.0 - sigmoid))
    ada_cols = last[:, seqs * part : seqs * part + 6 * cols].reshape(dp, 6, cols)
    ada_rows = lax.dynamic_slice_in_dim(ada_cols, core * heads, heads, 0).transpose(1, 0, 2)
    grad_ada_bias = lax.dynamic_slice_in_dim(ada_rows, chip * ada_bias.shape[2], ada_bias.shape[2], 2)

    chunks = reduced.shape[0]
    wide = lambda values: values.transpose(1, 0, 2).reshape(own_rows, -1)
    return (
        output.transpose(1, 0, 2),
        grad_inputs.transpose(1, 0, 2),
        grad_condition,
        grad_ada,
        grad_ada_bias,
        jnp.stack([reduced[chunks - 2], reduced[chunks - 1], reduced[chunks - 3]]),
        owned[0],
        owned[1],
        owned[3],
        reduced[2 * ff_chunks].T,
        owned[4],
        wide(reduced[ff_chunks : 2 * ff_chunks]),
        owned[2],
        wide(reduced[:ff_chunks]).T,
        owned[5],
    )


def solution(mesh):
    in_specs = (
        P("dp", "tensor", None),
        P("dp", None),
        P("dp", None),
        P("tensor", None, "dp"),
        P(None, "tensor", "dp"),
        P(None, "dp", "tensor"),
        P("tensor", "dp"),
        P("tensor", "dp"),
        P("tensor"),
        P("tensor", "dp"),
        P("tensor", "dp"),
        P("dp", "tensor"),
        P("tensor", "dp"),
        P("tensor", "dp"),
        P("tensor", "dp"),
        P("dp", "tensor", None),
    )
    out_specs = (
        P("dp", "tensor", None),
        P("dp", "tensor", None),
        P("dp", "tensor"),
        P("tensor", None, "dp"),
        P(None, "tensor", "dp"),
        P(None, "dp", "tensor"),
        P("tensor", "dp"),
        P("tensor", "dp"),
        P("tensor"),
        P("tensor", "dp"),
        P("tensor", "dp"),
        P("dp", "tensor"),
        P("tensor", "dp"),
        P("tensor", "dp"),
        P("tensor", "dp"),
    )
    grid = GRIDS.get((mesh.shape["dp"], mesh.shape["tensor"]))
    body = on_device if grid is None else functools.partial(fast_device, grid)
    return jax.shard_map(
        body, mesh=mesh, in_specs=in_specs, out_specs=out_specs, check_vma=False
    )
```

```python
import functools

import jax
import jax.numpy as jnp
from jax import lax
from jax.experimental import pallas as pl
from jax.experimental.pallas import tpu as pltpu
from jax.sharding import PartitionSpec as P

NORM_EPS = 1e-06
HEAD_EPS = 1e-06
GELU_COEF = 0.7978845608028654
GELU_CUBE = 0.044715


def normalize(values):
    centred = values - jnp.mean(values, axis=-1, keepdims=True)
    inverse = lax.rsqrt(jnp.mean(centred * centred, axis=-1, keepdims=True) + NORM_EPS)
    return (centred * inverse, inverse)


def norm_back(grad_normed, normed, inverse):
    return inverse * (
        grad_normed
        - jnp.mean(grad_normed, axis=-1, keepdims=True)
        - normed * jnp.mean(grad_normed * normed, axis=-1, keepdims=True)
    )


def gelu_slope(hidden):
    inner = jnp.tanh(GELU_COEF * (hidden + GELU_CUBE * hidden * hidden * hidden))
    return 0.5 * (1.0 + inner) + 0.5 * hidden * (1.0 - inner * inner) * GELU_COEF * (
        1.0 + 3.0 * GELU_CUBE * hidden * hidden
    )


def masked_scores(query_unit, key_unit, scale_factor, scale_row):
    query_low = (query_unit * scale_factor).astype(jnp.bfloat16)
    key_low = key_unit.astype(jnp.bfloat16)
    scores = jnp.einsum("qhe,khe->hqk", query_low, key_low, preferred_element_type=jnp.float32)
    allowed = scale_row[None, :] <= scale_row[:, None]
    return (jnp.where(allowed[None, :, :], scores, -1e30), query_low, key_low)


def attention_core(mixed_all, qkv_full, query_bias_part, value_bias_part, head_scale, scale_row):
    part_width = qkv_full.shape[2]
    part_heads = head_scale.shape[0]
    head_dim = part_width // part_heads
    seq_len = scale_row.shape[0]
    projected = jnp.einsum("ld,jdc->jlc", mixed_all, qkv_full, preferred_element_type=jnp.float32)
    queries = (projected[0] + query_bias_part.reshape(part_width).astype(jnp.float32)).reshape(
        seq_len, part_heads, head_dim
    )
    keys_raw = projected[1].reshape(seq_len, part_heads, head_dim)
    values_low = (projected[2] + value_bias_part.reshape(part_width).astype(jnp.float32)).astype(
        jnp.bfloat16
    )
    values_low = values_low.reshape(seq_len, part_heads, head_dim)
    query_inverse = lax.rsqrt(jnp.sum(queries * queries, axis=-1, keepdims=True) + HEAD_EPS)
    key_inverse = lax.rsqrt(jnp.sum(keys_raw * keys_raw, axis=-1, keepdims=True) + HEAD_EPS)
    query_unit = queries * query_inverse
    key_unit = keys_raw * key_inverse
    scale_factor = jnp.exp(head_scale)[:, None]
    scores, query_low, key_low = masked_scores(query_unit, key_unit, scale_factor, scale_row)
    row_max = jnp.max(scores, axis=-1, keepdims=True)
    weights_exp = jnp.exp(scores - row_max)
    row_total = jnp.sum(weights_exp, axis=-1, keepdims=True)
    attn_prob = weights_exp / row_total
    log_norm = row_max + jnp.log(row_total)
    attended = jnp.einsum(
        "hqk,khe->qhe",
        attn_prob.astype(jnp.bfloat16),
        values_low,
        preferred_element_type=jnp.float32,
    )
    attended = attended.reshape(seq_len, part_width).astype(jnp.bfloat16)
    return (attended, (query_unit, key_unit, query_inverse, key_inverse, values_low, log_norm))


def forward_step(weights, token_rows, condition_row, scale_row, head_scale):
    (
        ada_full,
        ada_bias_part,
        qkv_full,
        query_bias_part,
        value_bias_part,
        proj_full,
        proj_bias_part,
        up_full,
        up_bias_part,
        down_full,
        down_bias_part,
    ) = weights
    width = token_rows.shape[1]
    part_width = qkv_full.shape[2]
    col_start = lax.axis_index("tensor") * part_width
    cond_rows = lax.dynamic_slice_in_dim(
        condition_row.astype(jnp.float32), col_start, part_width, 0
    )
    silu_rows = jax.nn.silu(cond_rows).astype(jnp.bfloat16)
    mod_terms = jnp.einsum("r,rjc->jc", silu_rows, ada_full, preferred_element_type=jnp.float32)
    own_cols = jnp.concatenate(
        [
            ada_bias_part.reshape(6, part_width),
            proj_bias_part.reshape(1, part_width),
            down_bias_part.reshape(1, part_width),
        ],
        axis=0,
    ).astype(jnp.float32)
    placed = lax.dynamic_update_slice(jnp.zeros((8, width), jnp.float32), own_cols, (0, col_start))
    local_mod = placed + jnp.concatenate([mod_terms, jnp.zeros((2, width), jnp.float32)], axis=0)
    modulation = lax.psum(local_mod, "tensor")
    inputs = token_rows.astype(jnp.float32)
    normed_attn, inverse_attn = normalize(inputs)
    mixed_attn = (normed_attn * (1.0 + modulation[2]) + modulation[4]).astype(jnp.bfloat16)
    mixed_all = lax.all_gather(mixed_attn, "tensor", axis=0, tiled=True)
    attended, attn_kept = attention_core(
        mixed_all, qkv_full, query_bias_part, value_bias_part, head_scale, scale_row
    )
    branch_attn = (
        lax.psum_scatter(
            jnp.dot(attended, proj_full, preferred_element_type=jnp.float32).astype(jnp.bfloat16),
            "tensor",
            scatter_dimension=0,
            tiled=True,
        ).astype(jnp.float32)
        + modulation[6]
    )
    middle = inputs + modulation[0] * branch_attn
    normed_mlp, inverse_mlp = normalize(middle)
    mixed_mlp = (normed_mlp * (1.0 + modulation[3]) + modulation[5]).astype(jnp.bfloat16)
    mlp_all = lax.all_gather(mixed_mlp, "tensor", axis=0, tiled=True)
    hidden = jnp.dot(mlp_all, up_full, preferred_element_type=jnp.float32) + up_bias_part.reshape(
        -1
    ).astype(jnp.float32)
    activated = jax.nn.gelu(hidden, approximate=True).astype(jnp.bfloat16)
    branch_mlp = (
        lax.psum_scatter(
            jnp.dot(activated, down_full, preferred_element_type=jnp.float32).astype(jnp.bfloat16),
            "tensor",
            scatter_dimension=0,
            tiled=True,
        ).astype(jnp.float32)
        + modulation[7]
    )
    output = middle + modulation[1] * branch_mlp
    query_unit, key_unit, query_inverse, key_inverse, values_low, log_norm = attn_kept
    kept = (
        modulation,
        normed_attn,
        inverse_attn,
        mixed_all,
        query_unit,
        key_unit,
        query_inverse,
        key_inverse,
        values_low,
        log_norm,
        attended,
        branch_attn,
        normed_mlp,
        inverse_mlp,
        mlp_all,
        hidden,
        activated,
        branch_mlp,
    )
    return (output, kept)


def backward_step(weights, kept, token_grad, condition_row, scale_row, head_scale):
    (
        ada_full,
        ada_bias_part,
        qkv_full,
        query_bias_part,
        value_bias_part,
        proj_full,
        proj_bias_part,
        up_full,
        up_bias_part,
        down_full,
        down_bias_part,
    ) = weights
    (
        modulation,
        normed_attn,
        inverse_attn,
        mixed_all,
        query_unit,
        key_unit,
        query_inverse,
        key_inverse,
        values_low,
        log_norm,
        attended,
        branch_attn,
        normed_mlp,
        inverse_mlp,
        mlp_all,
        hidden,
        activated,
        branch_mlp,
    ) = kept
    part_width = qkv_full.shape[2]
    part_heads = head_scale.shape[0]
    head_dim = part_width // part_heads
    seq_len = scale_row.shape[0]
    scale_factor = jnp.exp(head_scale)[:, None]
    grad_rows = token_grad.astype(jnp.float32)
    grad_branch_mlp = grad_rows * modulation[1]
    grad_gamma_mlp = jnp.sum(grad_rows * branch_mlp, axis=0)
    grad_down_bias = jnp.sum(grad_branch_mlp, axis=0)
    grad_mlp_all = lax.all_gather(
        grad_branch_mlp.astype(jnp.bfloat16), "tensor", axis=0, tiled=True
    )
    grad_down = jnp.einsum("lf,ld->fd", activated, grad_mlp_all, preferred_element_type=jnp.float32)
    grad_act = jnp.einsum("ld,fd->lf", grad_mlp_all, down_full, preferred_element_type=jnp.float32)
    grad_hidden = grad_act * gelu_slope(hidden)
    grad_up_bias = jnp.sum(grad_hidden, axis=0)
    hidden_low = grad_hidden.astype(jnp.bfloat16)
    grad_up = jnp.einsum("ld,lf->df", mlp_all, hidden_low, preferred_element_type=jnp.float32)
    grad_mixed_mlp = lax.psum_scatter(
        jnp.einsum("lf,df->ld", hidden_low, up_full, preferred_element_type=jnp.float32).astype(
            jnp.bfloat16
        ),
        "tensor",
        scatter_dimension=0,
        tiled=True,
    ).astype(jnp.float32)
    grad_scale_mlp = jnp.sum(grad_mixed_mlp * normed_mlp, axis=0)
    grad_shift_mlp = jnp.sum(grad_mixed_mlp, axis=0)
    grad_middle = grad_rows + norm_back(
        grad_mixed_mlp * (1.0 + modulation[3]), normed_mlp, inverse_mlp
    )
    grad_branch_attn = grad_middle * modulation[0]
    grad_gamma_attn = jnp.sum(grad_middle * branch_attn, axis=0)
    grad_proj_bias = jnp.sum(grad_branch_attn, axis=0)
    grad_attn_all = lax.all_gather(
        grad_branch_attn.astype(jnp.bfloat16), "tensor", axis=0, tiled=True
    )
    grad_proj = jnp.einsum("lc,ld->cd", attended, grad_attn_all, preferred_element_type=jnp.float32)
    grad_attended = jnp.einsum(
        "ld,cd->lc", grad_attn_all, proj_full, preferred_element_type=jnp.float32
    )
    grad_attended = grad_attended.astype(jnp.bfloat16).reshape(seq_len, part_heads, head_dim)
    scores, query_low, key_low = masked_scores(query_unit, key_unit, scale_factor, scale_row)
    attn_prob = jnp.exp(scores - log_norm)
    grad_prob = jnp.einsum(
        "qhe,khe->hqk", grad_attended, values_low, preferred_element_type=jnp.float32
    )
    row_dot = jnp.sum(attn_prob * grad_prob, axis=-1, keepdims=True)
    grad_scores = (attn_prob * (grad_prob - row_dot)).astype(jnp.bfloat16)
    grad_values = jnp.einsum(
        "hqk,qhe->khe",
        attn_prob.astype(jnp.bfloat16),
        grad_attended,
        preferred_element_type=jnp.float32,
    )
    grad_query_scaled = jnp.einsum(
        "hqk,khe->qhe", grad_scores, key_low, preferred_element_type=jnp.float32
    )
    grad_key_unit = jnp.einsum(
        "hqk,qhe->khe", grad_scores, query_low, preferred_element_type=jnp.float32
    )
    grad_head_scale = jnp.sum(grad_query_scaled * query_unit, axis=(0, 2)) * jnp.exp(head_scale)
    grad_query_unit = grad_query_scaled * scale_factor
    grad_queries = query_inverse * (
        grad_query_unit - query_unit * jnp.sum(grad_query_unit * query_unit, axis=-1, keepdims=True)
    )
    grad_keys = key_inverse * (
        grad_key_unit - key_unit * jnp.sum(grad_key_unit * key_unit, axis=-1, keepdims=True)
    )
    grad_query_bias = jnp.sum(grad_queries, axis=0)
    grad_value_bias = jnp.sum(grad_values, axis=0)
    grad_projected = (
        jnp.stack([grad_queries, grad_keys, grad_values])
        .reshape(3, seq_len, part_width)
        .astype(jnp.bfloat16)
    )
    grad_qkv = jnp.einsum(
        "ld,jlc->jdc", mixed_all, grad_projected, preferred_element_type=jnp.float32
    )
    grad_mixed_attn = lax.psum_scatter(
        jnp.einsum(
            "jlc,jdc->ld", grad_projected, qkv_full, preferred_element_type=jnp.float32
        ).astype(jnp.bfloat16),
        "tensor",
        scatter_dimension=0,
        tiled=True,
    ).astype(jnp.float32)
    grad_scale_attn = jnp.sum(grad_mixed_attn * normed_attn, axis=0)
    grad_shift_attn = jnp.sum(grad_mixed_attn, axis=0)
    grad_inputs = grad_middle + norm_back(
        grad_mixed_attn * (1.0 + modulation[2]), normed_attn, inverse_attn
    )
    mod_rows = jnp.stack(
        [
            grad_gamma_attn,
            grad_gamma_mlp,
            grad_scale_attn,
            grad_scale_mlp,
            grad_shift_attn,
            grad_shift_mlp,
            grad_proj_bias,
            grad_down_bias,
        ]
    )
    grad_modulation = lax.psum(mod_rows.astype(jnp.bfloat16), "tensor").astype(jnp.float32)
    col_start = lax.axis_index("tensor") * part_width
    cond_rows = lax.dynamic_slice_in_dim(
        condition_row.astype(jnp.float32), col_start, part_width, 0
    )
    silu_rows = jax.nn.silu(cond_rows).astype(jnp.bfloat16)
    mod_low = grad_modulation[:6].astype(jnp.bfloat16)
    grad_ada = jnp.einsum("r,jc->rjc", silu_rows, mod_low, preferred_element_type=jnp.float32)
    grad_silu = jnp.einsum("jc,rjc->r", mod_low, ada_full, preferred_element_type=jnp.float32)
    sigmoid_rows = jax.nn.sigmoid(cond_rows)
    grad_condition = grad_silu * sigmoid_rows * (1.0 + cond_rows * (1.0 - sigmoid_rows))
    own_cols = lax.dynamic_slice_in_dim(grad_modulation, col_start, part_width, 1)
    increments = (
        grad_ada,
        own_cols[:6].reshape(6, part_heads, head_dim),
        grad_qkv,
        grad_query_bias,
        grad_value_bias,
        grad_head_scale,
        grad_proj,
        own_cols[6].reshape(part_heads, head_dim),
        grad_up,
        grad_up_bias.reshape(part_heads, -1),
        grad_down,
        own_cols[7].reshape(part_heads, head_dim),
    )
    return (increments, grad_inputs, grad_condition)


def on_device(
    tokens,
    condition,
    scale_index,
    ada_weight,
    ada_bias,
    qkv_weight,
    query_bias,
    value_bias,
    head_scale,
    proj_weight,
    proj_bias,
    up_weight,
    up_bias,
    down_weight,
    down_bias,
    out_grad,
):

    def fetch_weights():
        return (
            lax.all_gather(ada_weight, "dp", axis=2, tiled=True),
            lax.all_gather(ada_bias, "dp", axis=2, tiled=True),
            lax.all_gather(qkv_weight, "dp", axis=1, tiled=True),
            lax.all_gather(query_bias, "dp", axis=1, tiled=True),
            lax.all_gather(value_bias, "dp", axis=1, tiled=True),
            lax.all_gather(proj_weight, "dp", axis=1, tiled=True),
            lax.all_gather(proj_bias, "dp", axis=1, tiled=True),
            lax.all_gather(up_weight, "dp", axis=0, tiled=True),
            lax.all_gather(up_bias, "dp", axis=1, tiled=True),
            lax.all_gather(down_weight, "dp", axis=1, tiled=True),
            lax.all_gather(down_bias, "dp", axis=1, tiled=True),
        )

    def forward_scan(carried, step_in):
        token_rows, condition_row, scale_row = step_in
        weights_now = fetch_weights()
        output, kept = forward_step(weights_now, token_rows, condition_row, scale_row, head_scale)
        return (carried, (output, kept))

    unused_carry, (outputs, kept_all) = lax.scan(
        forward_scan, jnp.zeros((), jnp.int32), (tokens, condition, scale_index)
    )
    width = tokens.shape[2]
    part_width = qkv_weight.shape[2]
    part_heads = head_scale.shape[0]
    head_dim = part_width // part_heads
    part_ff = up_weight.shape[1]
    zero_grads = (
        jnp.zeros((part_width, 6, width), jnp.float32),
        jnp.zeros((6, part_heads, head_dim), jnp.float32),
        jnp.zeros((3, width, part_width), jnp.float32),
        jnp.zeros((part_heads, head_dim), jnp.float32),
        jnp.zeros((part_heads, head_dim), jnp.float32),
        jnp.zeros((part_heads,), jnp.float32),
        jnp.zeros((part_width, width), jnp.float32),
        jnp.zeros((part_heads, head_dim), jnp.float32),
        jnp.zeros((width, part_ff), jnp.float32),
        jnp.zeros((part_heads, part_ff // part_heads), jnp.float32),
        jnp.zeros((part_ff, width), jnp.float32),
        jnp.zeros((part_heads, head_dim), jnp.float32),
    )

    def backward_scan(totals, step_in):
        kept, token_grad, condition_row, scale_row = step_in
        weights_now = fetch_weights()
        increments, grad_inputs, grad_condition = backward_step(
            weights_now, kept, token_grad, condition_row, scale_row, head_scale
        )
        totals = tuple((running + increment for running, increment in zip(totals, increments)))
        return (totals, (grad_inputs, grad_condition))

    totals, (grad_tokens, grad_condition) = lax.scan(
        backward_scan, zero_grads, (kept_all, out_grad, condition, scale_index), reverse=True
    )
    scale_total = lax.psum(totals[5], "dp")
    reduced = (
        lax.psum_scatter(
            totals[0].astype(jnp.bfloat16), "dp", scatter_dimension=2, tiled=True
        ).astype(jnp.float32),
        lax.psum_scatter(
            totals[1].astype(jnp.bfloat16), "dp", scatter_dimension=2, tiled=True
        ).astype(jnp.float32),
        lax.psum_scatter(
            totals[2].astype(jnp.bfloat16), "dp", scatter_dimension=1, tiled=True
        ).astype(jnp.float32),
        lax.psum_scatter(
            totals[3].astype(jnp.bfloat16), "dp", scatter_dimension=1, tiled=True
        ).astype(jnp.float32),
        lax.psum_scatter(
            totals[4].astype(jnp.bfloat16), "dp", scatter_dimension=1, tiled=True
        ).astype(jnp.float32),
        lax.psum_scatter(
            totals[6].astype(jnp.bfloat16), "dp", scatter_dimension=1, tiled=True
        ).astype(jnp.float32),
        lax.psum_scatter(
            totals[7].astype(jnp.bfloat16), "dp", scatter_dimension=1, tiled=True
        ).astype(jnp.float32),
        lax.psum_scatter(
            totals[8].astype(jnp.bfloat16), "dp", scatter_dimension=0, tiled=True
        ).astype(jnp.float32),
        lax.psum_scatter(
            totals[9].astype(jnp.bfloat16), "dp", scatter_dimension=1, tiled=True
        ).astype(jnp.float32),
        lax.psum_scatter(
            totals[10].astype(jnp.bfloat16), "dp", scatter_dimension=1, tiled=True
        ).astype(jnp.float32),
        lax.psum_scatter(
            totals[11].astype(jnp.bfloat16), "dp", scatter_dimension=1, tiled=True
        ).astype(jnp.float32),
    )
    return (
        outputs,
        grad_tokens,
        grad_condition,
        reduced[0],
        reduced[1],
        reduced[2],
        reduced[3],
        reduced[4],
        scale_total,
        reduced[5],
        reduced[6],
        reduced[7],
        reduced[8],
        reduced[9],
        reduced[10],
    )


GRIDS = {(16, 2): (4, 2, 2)}
MESH_ID = pl.DeviceIdType.MESH
ANY = pl.ANY
F32 = jnp.float32
BF16 = jnp.bfloat16
SCALES = 10
MASK = -16384.0


def place():
    return (lax.axis_index("dp"), lax.axis_index("tensor"))


def coords(grid):
    chip, core = place()
    nz, ny, nx = grid
    return (chip // (ny * nx), (chip // nx) % ny, chip % nx, core)


def greet_all(count):
    chip, core = place()
    me = chip * 2 + core
    barrier = pltpu.get_barrier_semaphore()
    for k in range(1, count):
        peer = (me + k) % count
        pl.semaphore_signal(barrier, inc=1, device_id=(peer // 2, peer % 2), device_id_type=MESH_ID)
    pl.semaphore_wait(barrier, count - 1)


def remote(src, dst, send_sem, recv_sem, device):
    return pltpu.make_async_remote_copy(
        src_ref=src,
        dst_ref=dst,
        send_sem=send_sem,
        recv_sem=recv_sem,
        device_id=device,
        device_id_type=MESH_ID,
    )


def greet(peers):
    barrier = pltpu.get_barrier_semaphore()
    for peer in peers:
        pl.semaphore_signal(barrier, inc=1, device_id=peer, device_id_type=MESH_ID)
    pl.semaphore_wait(barrier, len(peers))


def forward_kernel(
    grid,
    sizes,
    chunk_counts,
    shard,
    tok,
    grad_in,
    small,
    ada,
    query_spare,
    key_spare,
    key_scale,
    ones,
    full,
    x_out,
    grad_out,
    mixed_out,
    qaug_out,
    kv_out,
    inverse_out,
    att_out,
    branch_out,
    mlp_out,
    slope_out,
    dm_out,
    grad_down_out,
    mlp_own,
    mlp_other,
    mod,
    silu_out,
    x,
    dm,
    mixed,
    other,
    turned,
    qaug,
    kv,
    inverses,
    att,
    w,
    slope,
    act,
    grad_down,
    every,
    mod_send,
    mod_got,
    head_bias,
    up_bias,
    local_sem,
    p_send,
    p_recv,
    t_send,
    t_recv,
    load_sem,
    save_sem,
    a_send,
    a_recv,
):
    nz, ny, nx = grid
    half = nz // 2
    seqs, pad = sizes
    chunks = shard.shape[0]
    ff_chunks = chunk_counts
    dp = nz * ny * nx
    devices = dp * 2
    mod_rows = ada.shape[0] // 128
    z, y, x_at, core = coords(grid)
    width = x.shape[1]
    part_width = att.shape[1]
    pairs = part_width // 128
    blocks = seqs * 2
    length = tok.shape[0]

    def dev(z_to, y_to, x_to):
        return ((z_to * ny + y_to) * nx + x_to, core)

    x_peer = dev(z, y, 1 - x_at)
    y_peer = dev(z, 1 - y, x_at)
    sibling = (place()[0], 1 - core)
    greet_all(devices)

    me = place()[0] * 2 + core
    every[place()[0], core] = small[core]
    mod_send[...] = jnp.zeros_like(mod_send)

    def to_all(round_at, source, target):
        copies = []
        for k in range(1, devices):
            peer = (me + k) % devices
            copy = remote(
                source(peer // 2, peer % 2),
                target.at[place()[0], core],
                a_send.at[round_at, k - 1],
                a_recv.at[round_at, k - 1],
                (peer // 2, peer % 2),
            )
            copy.start()
            copies.append(copy)
        return copies

    small_copies = to_all(0, lambda to, core_to: small.at[core_to], every)

    def own_copy(c):
        return pltpu.make_async_copy(shard.at[c], full.at[c, z, y, x_at], local_sem.at[c])

    low_rows, high_rows = (pl.ds(i * shard.shape[1] // 2, shard.shape[1] // 2) for i in range(2))

    def spread_out(c):
        return c % 3 == 1

    def stage(c, number):
        z_peers = [dev((z + k) % nz, y, x_at) for k in range(1, nz)]
        if not spread_out(c):
            if number == 0:
                moves = [(shard.at[c], full.at[c, z, y, x_at], peer) for peer in z_peers]
            elif number == 1:
                low = full.at[c, pl.ds(0, half), y, x_at]
                high = full.at[c, pl.ds(half, half), y, x_at]
                moves = [(low, low, x_peer), (high, high, y_peer)]
            else:
                low = full.at[c, pl.ds(0, half), y]
                high = full.at[c, pl.ds(half, half), :, x_at]
                moves = [(low, low, y_peer), (high, high, x_peer)]
        elif number == 0:
            moves = [
                (shard.at[c, low_rows], full.at[c, z, y, x_at, low_rows], x_peer),
                (shard.at[c, high_rows], full.at[c, z, y, x_at, high_rows], y_peer),
            ]
        elif number == 1:
            low = full.at[c, z, y, :, low_rows]
            high = full.at[c, z, :, x_at, high_rows]
            moves = [(piece, piece, peer) for peer in z_peers for piece in (low, high)]
        else:
            low = full.at[c, :, y, :, low_rows]
            high = full.at[c, :, :, x_at, high_rows]
            moves = [(low, low, y_peer), (high, high, x_peer)]
        first = (0, 3, 9)[number]
        return [
            remote(src, dst, p_send.at[c, first + i], p_recv.at[c, first + i], peer)
            for i, (src, dst, peer) in enumerate(moves)
        ]

    ahead = 2
    progress = [-ahead]

    def begin_stage(c, number):
        if number == 1:
            own_copy(c).wait()
        for copy in stage(c, number - 1) if number else ():
            copy.wait_recv()
        for copy in stage(c, number):
            copy.start()

    def advance(upto):
        while progress[0] <= upto:
            t = progress[0]
            if 0 <= t + ahead < chunks:
                own_copy(t + ahead).start()
                begin_stage(t + ahead, 0)
            if 0 <= t + 1 < chunks and spread_out(t + 1):
                begin_stage(t + 1, 1)
            if 0 <= t < chunks and not spread_out(t):
                begin_stage(t, 1)
            if 0 <= t - 1 < chunks:
                begin_stage(t - 1, 2)
            progress[0] += 1

    def load(c):
        return pltpu.make_async_copy(full.at[c], w.at[c % 4], load_sem.at[c])

    def begin_load(c):
        for copy in stage(c, 2):
            copy.wait_recv()
        load(c).start()

    def weight(c):
        return w[c % 4].reshape(width, part_width)

    saves = []

    def save(src, dst):
        copy = pltpu.make_async_copy(src, dst, save_sem.at[len(saves)])
        copy.start()
        saves.append(copy)
        return copy

    def block_rows(a):
        return pl.ds(pl.multiple_of(a * pad, 16), pad)

    advance(-2)

    def own_rows(s, which):
        return block_rows(s * 2 + which)

    def conditions():
        for copy in small_copies:
            copy.wait()
        groups = ada.shape[1] // 128
        cond = every[:, 0].astype(F32)
        for s in range(seqs):
            total = None
            for g in range(groups):
                c = cond[:, s * groups + g, :]
                silu = (c / (1.0 + jnp.exp(-c))).astype(BF16)
                silu_out[s, :, g * 128 : g * 128 + 128] = silu
                term = dot_nt(silu, ada[:, g * 128 : g * 128 + 128])
                total = term if g == 0 else total + term
            for i in range(mod_rows):
                mod_send[:, i * seqs + s, :] = total[:, i * 128 : i * 128 + 128]
        return to_all(1, lambda to, core_to: mod_send.at[to], mod_got)

    def iota(shape, dim):
        return lax.broadcasted_iota(jnp.int32, shape, dim)

    def spread(rows, cols, at, unit, span):
        share = span // dp
        row, col = iota((128, cols), 0) - at, iota((128, cols), 1)
        here = (row >= 0) & (row < unit) & (col // span == row // share) & (col % share == row % share)
        placed = dot(rows, jnp.where(here, 1.0, 0.0).astype(BF16)).reshape(dp, -1, cols)
        mine = (iota((dp, 1, cols), 2) % span) // share == iota((dp, 1, cols), 0)
        return jnp.sum(jnp.where(mine, placed, 0.0), axis=0)

    def modulation():
        for copy in mod_copies:
            copy.wait()
        mod_got[place()[0], core] = mod_send[place()[0]]
        first_row = 8
        count = every.shape[2]
        for t in range(2):
            rows = every[:, t].reshape(dp * count, 128)
            at = t * part_width
            quarters = [spread(rows, part_width, q * 32, 32, 64) for q in range(4)]
            for j in range(8):
                vector = j if j < 6 else j + 2
                piece = quarters[vector % 4][first_row + vector // 4 : first_row + vector // 4 + 1]
                for s in range(seqs):
                    mod[s, j : j + 1, at : at + part_width] = piece
        rows = every[:, pl.ds(core, 1)].reshape(dp * count, 128)
        for j in (6, 7):
            piece = spread(rows, part_width, j % 4 * 32, 32, 64)
            head_bias[j : j + 1, :] = piece[first_row + j // 4 : first_row + j // 4 + 1]
        rows = spread(rows, part_width * ff_chunks, 0, 128, 256)
        for c in range(ff_chunks):
            up_bias[c] = rows[first_row + 3 : first_row + 4, c * part_width : (c + 1) * part_width]
        sums = [mod_got[d, 0] + mod_got[d, 1] for d in range(dp)]
        for j in range(6):
            at = j // 2 * seqs
            lanes = j % 2 * 64
            row = jnp.concatenate([total[at : at + seqs, lanes : lanes + 64] for total in sums], axis=1)
            for s in range(seqs):
                mod[s, j : j + 1, :] += row[s : s + 1]

    swaps = []
    for i, (src, dst) in enumerate(((tok, x), (grad_in, dm))):
        for s in range(seqs):
            values = src[:, s, :].astype(F32).astype(BF16)
            start = pl.multiple_of((s * 2 + core) * pad, 16)
            dst[pl.ds(start + length // 16 * 16, pad - length // 16 * 16), :] = jnp.zeros(
                (pad - length // 16 * 16, width), BF16
            )
            dst[pl.ds(start, length), :] = values
            piece = dst.at[own_rows(s, core), :]
            copy = remote(piece, piece, t_send.at[i * seqs + s], t_recv.at[i * seqs + s], sibling)
            copy.start()
            swaps.append(copy)
    advance(-1)
    mod_copies = conditions()
    for copy in swaps[:seqs]:
        copy.wait()
    x_saved = save(x, x_out)
    advance(0)
    for copy in swaps[seqs:]:
        copy.wait()
    grad_saved = save(dm, grad_out)
    advance(1)
    modulation()

    def mix_attn(a, rows):
        s = a // 2
        normed, unused = normalize(x[rows, :].astype(F32))
        mixed[rows, :] = (normed * (1.0 + mod[s, 2:3, :]) + mod[s, 4:5, :]).astype(BF16)

    for_blocks(blocks, pad, mix_attn)
    mixed_saved = save(mixed, mixed_out)
    grad_saved.wait()

    def scale_grad(a, rows):
        dm[rows, :] = (dm[rows, :].astype(F32) * mod[a // 2, 1:2, :]).astype(BF16)

    for_blocks(blocks, pad, scale_grad)
    save(dm, dm_out)
    transpose_into(turned, dm)
    advance(2)
    begin_load(0)
    load(0).wait()

    def project_q(a, rows):
        first, unused = lane_code(pad)
        q_spare = query_spare[rows, :].astype(F32)
        values = dot(mixed[rows, :], weight(0)) + head_bias[6:7, :]
        inv = lax.rsqrt(dot((values * values).astype(BF16), ones[...]) + HEAD_EPS)
        inverses[rows, 0:part_width] = inv.astype(BF16)
        values = values * inv * key_scale[...]
        for p in range(pairs):
            piece = values[:, p * 128 : p * 128 + 128]
            qaug[2 * p, rows, :] = jnp.where(first, piece, q_spare).astype(BF16)
            qaug[2 * p + 1, rows, :] = jnp.where(first, q_spare, piece).astype(BF16)

    for_blocks(blocks, pad, project_q)
    advance(3)
    begin_load(1)
    load(1).wait()

    def project_k(a, rows):
        values = dot(mixed[rows, :], weight(1))
        inv = lax.rsqrt(dot((values * values).astype(BF16), ones[...]) + HEAD_EPS)
        inverses[rows, part_width : 2 * part_width] = inv.astype(BF16)
        kv[rows, 0:part_width] = (values * inv).astype(BF16)

    for_blocks(blocks, pad, project_k)
    inverse_saved = save(inverses, inverse_out)
    advance(4)
    begin_load(2)
    load(2).wait()

    def project_v(a, rows):
        kv[rows, part_width : 2 * part_width] = (
            dot(mixed[rows, :], weight(2)) + head_bias[7:8, :]
        ).astype(BF16)

    for_blocks(blocks, pad, project_v)
    save(kv, kv_out)

    def attend(i, carry):
        p = i // blocks
        block = i % blocks
        rows = block_rows(block)
        all_rows = pl.ds(pl.multiple_of((block // 2) * 2 * pad, 16), 2 * pad)
        at = pl.multiple_of(p * 128, 128)
        first, code = lane_code(pad)
        k_sides = both_heads(kv[all_rows, pl.ds(at, 128)], key_spare[all_rows, :])
        v_sides = both_heads(kv[all_rows, pl.ds(at + part_width, 128)], 1.0)
        outs = []
        for side in range(2):
            h = 2 * p + side
            q = qaug[h, rows, :]
            prob = jnp.exp2(dot_nt(q, k_sides[side])).astype(BF16)
            o = dot(prob, v_sides[side])
            outs.append(o / pltpu.roll(o, 64, 1))
            norm = -jnp.log2(o)
            high = norm.astype(BF16)
            rest = norm - high.astype(F32)
            middle = rest.astype(BF16)
            low = (rest - middle.astype(F32)).astype(BF16)
            spare = jnp.logical_not(first) if side == 0 else first
            q = q.astype(F32)
            for where, piece in enumerate((high, middle, low)):
                q = jnp.where(spare & (code == SCALES + where), piece.astype(F32), q)
            qaug[h, rows, :] = q.astype(BF16)
        att[rows, pl.ds(at, 128)] = jnp.where(first, outs[0], outs[1]).astype(BF16)
        return carry

    count = pairs * blocks
    for quarter in range(4):
        lax.fori_loop(quarter * count // 4, (quarter + 1) * count // 4, attend, 0)
        if quarter == 0:
            advance(5)
        if quarter == 2:
            advance(6)
    begin_load(3)
    save(qaug, qaug_out)
    save(att, att_out)
    load(3).wait()
    inverse_saved.wait()
    part = inverses
    part_copies = []
    for a in range(blocks):
        rows = block_rows(a)
        part[rows, :] = dot_nt(att[rows, :], weight(3)).astype(BF16)
        copy = remote(
            part.at[rows, :], other.at[rows, :], t_send.at[2 * seqs + a], t_recv.at[2 * seqs + a], sibling
        )
        copy.start()
        part_copies.append(copy)
    mixed_saved.wait()
    mlp = mixed
    begin_load(4)
    for a in range(blocks):
        rows = block_rows(a)
        s = a // 2
        part_copies[a].wait()
        b = part[rows, :].astype(F32) + other[rows, :].astype(F32) + mod[s, 6:7, :]
        other[rows, :] = b.astype(BF16)
        normed, unused = normalize(x[rows, :].astype(F32) + mod[s, 0:1, :] * b)
        mlp[rows, :] = (normed * (1.0 + mod[s, 3:4, :]) + mod[s, 5:6, :]).astype(BF16)
    branch_saved = save(other, branch_out)
    save(mlp, mlp_out)
    down_saved = []

    def raise_chunk(c):
        load(4 + c).wait()

        def raise_rows(a, rows):
            h = dot(mlp[rows, :], weight(4 + c)) + up_bias[c]
            square = h * h
            t = jnp.tanh(h * (GELU_COEF + GELU_COEF * GELU_CUBE * square))
            act[c, rows, :] = (0.5 * h * (1.0 + t)).astype(BF16)
            slope[c, rows, :] = (
                0.5 * (1.0 + t)
                + h * (1.0 - t * t) * (0.5 * GELU_COEF + 1.5 * GELU_COEF * GELU_CUBE * square)
            ).astype(BF16)

        for_blocks(blocks, pad, raise_rows)
        save(slope.at[c], slope_out.at[c])

    def down_chunk(c):
        if c >= 2:
            down_saved[c - 2].wait()
        weight_grad(grad_down.at[c % 2], turned, act.at[c])
        down_saved.append(save(grad_down.at[c % 2], grad_down_out.at[c]))

    advance(7)
    begin_load(5)
    raise_chunk(0)
    raise_chunk(1)
    advance(8)
    begin_load(6)
    down_chunk(0)
    raise_chunk(2)
    down_chunk(1)
    advance(9)
    begin_load(7)
    raise_chunk(3)
    advance(10)
    begin_load(8)
    down_chunk(2)
    down_chunk(3)
    advance(11)
    begin_load(9)
    advance(12)
    begin_load(10)
    for copy in (x_saved, branch_saved, load(8), load(9), load(10)):
        copy.wait()

    def lower_most(a, rows):
        total = dot_nt(act[0, rows, :], weight(8))
        for c in range(1, ff_chunks - 1):
            total = total + dot_nt(act[c, rows, :], weight(8 + c))
        high = total.astype(BF16)
        x[rows, :] = high
        other[rows, :] = (total - high.astype(F32)).astype(BF16)

    for_blocks(blocks, pad, lower_most)
    begin_load(11)
    load(11).wait()
    end_copies = []
    for step in range(blocks):
        s = step % seqs
        which = 1 - core if step < seqs else core
        rows = own_rows(s, which)
        total = dot_nt(act[ff_chunks - 1, rows, :], weight(7 + ff_chunks))
        total = total + x[rows, :].astype(F32) + other[rows, :].astype(F32)
        part[rows, :] = total.astype(BF16)
        if step < seqs:
            copy = remote(
                part.at[rows, :],
                mlp_other.at[s],
                t_send.at[2 * seqs + blocks + s],
                t_recv.at[2 * seqs + blocks + s],
                sibling,
            )
            copy.start()
            end_copies.append(copy)
        else:
            save(part.at[rows, :], mlp_own.at[s])
    for copy in end_copies:
        copy.wait()
    done = [mixed_saved, grad_saved, inverse_saved, x_saved, branch_saved] + down_saved[:-2]
    for copy in saves:
        if all(copy is not other_copy for other_copy in done):
            copy.wait()
    for c in range(chunks):
        for number in range(3):
            for copy in stage(c, number):
                copy.wait_send()


def forward_pass(grid, sizes, shard, tok, grad_in, small, ada, query_spare, key_spare, key_scale, ones, collective_id):
    nz, ny, nx = grid
    seqs, pad = sizes
    chunks, own_rows, part = shard.shape
    ff_chunks = (chunks - 4) // 2
    dp = nz * ny * nx
    width = tok.shape[2]
    total = seqs * 2 * pad
    heads = part // 64
    wide = ((total, width), BF16)
    narrow = ((total, part), BF16)
    chunk = (nz, ny, nx, own_rows, part)
    outs = [
        ((chunks,) + chunk, BF16),
        wide,
        wide,
        wide,
        ((heads, total, 128), BF16),
        wide,
        wide,
        narrow,
        wide,
        wide,
        ((ff_chunks, total, part), BF16),
        wide,
        ((ff_chunks,) + chunk, BF16),
        ((seqs, pad, width), BF16),
        ((seqs, pad, width), BF16),
        ((seqs, 8, width), F32),
        ((seqs, dp, part), BF16),
    ]
    scratch = [
        wide,
        wide,
        wide,
        wide,
        ((width, total), BF16),
        ((heads, total, 128), BF16),
        wide,
        wide,
        narrow,
        ((4,) + chunk, BF16),
        ((ff_chunks, total, part), BF16),
        ((ff_chunks, total, part), BF16),
        ((2,) + chunk, BF16),
        ((dp, 2) + small.shape[1:], BF16),
        ((dp, 8, 128), F32),
        ((dp, 2, 8, 128), F32),
        ((8, part), F32),
        ((ff_chunks, 1, part), F32),
    ]
    swaps = 3 * seqs + seqs * 2
    vmem = pl.BlockSpec(memory_space=pltpu.VMEM)
    hbm = pl.BlockSpec(memory_space=ANY)
    return pl.pallas_call(
        functools.partial(forward_kernel, grid, sizes, ff_chunks),
        out_shape=[jax.ShapeDtypeStruct(shape, dtype) for shape, dtype in outs],
        in_specs=[hbm] + [vmem] * 8,
        out_specs=[hbm] * (len(outs) - 2) + [vmem] * 2,
        scratch_shapes=[pltpu.VMEM(shape, dtype) for shape, dtype in scratch]
        + [
            pltpu.SemaphoreType.DMA((chunks,)),
            pltpu.SemaphoreType.DMA((chunks, 14)),
            pltpu.SemaphoreType.DMA((chunks, 14)),
            pltpu.SemaphoreType.DMA((swaps,)),
            pltpu.SemaphoreType.DMA((swaps,)),
            pltpu.SemaphoreType.DMA((chunks,)),
            pltpu.SemaphoreType.DMA((24,)),
            pltpu.SemaphoreType.DMA((2, 2 * dp - 1)),
            pltpu.SemaphoreType.DMA((2, 2 * dp - 1)),
        ],
        compiler_params=pltpu.CompilerParams(
            collective_id=collective_id, has_side_effects=True, vmem_limit_bytes=60 * 2**20
        ),
        name="forward_pass",
    )(shard, tok, grad_in, small, ada, query_spare, key_spare, key_scale, ones)


def dot(a, b):
    return jnp.dot(a, b, preferred_element_type=F32)


def dot_nt(a, b):
    return lax.dot_general(a, b, (((1,), (1,)), ((), ())), preferred_element_type=F32)


def dot_tn(a, b):
    return lax.dot_general(a, b, (((0,), (0,)), ((), ())), preferred_element_type=F32)


def lane_code(rows):
    lane = lax.broadcasted_iota(jnp.int32, (rows, 128), 1)
    return lane < 64, lane & 63


def both_heads(pair, spare):
    first, unused = lane_code(pair.shape[0])
    pair = pair.astype(F32)
    if not isinstance(spare, float):
        spare = spare.astype(F32)
    return (
        jnp.where(first, pair, spare).astype(BF16),
        jnp.where(first, spare, pair).astype(BF16),
    )


def column_sum(values):
    return jnp.sum(values, axis=0, keepdims=True)


def transpose_into(dst, src):
    def step(i, carry):
        at = pl.multiple_of(i * 128, 128)
        dst[:, pl.ds(at, 128)] = src[pl.ds(at, 128), :].T
        return carry

    lax.fori_loop(0, src.shape[0] // 128, step, 0)


def weight_grad(dst, turned, right):
    rows = turned.shape[0] // dst.shape[0]

    def step(i, carry):
        at = pl.ds(pl.multiple_of(i * rows, rows), rows)
        dst[i] = dot(turned[at, :], right[...]).astype(BF16).reshape(dst.shape[1:])
        return carry

    lax.fori_loop(0, dst.shape[0], step, 0)


def for_blocks(count, rows, body):
    def step(a, carry):
        body(a, pl.ds(pl.multiple_of(a * rows, 16), rows))
        return carry

    lax.fori_loop(0, count, step, 0)

def backward_kernel(
    grid,
    sizes,
    full,
    x_in,
    grad_in,
    mixed_in,
    qaug_in,
    kv_in,
    inverse_in,
    att_in,
    branch_in,
    mlp_in,
    slope_in,
    dm_in,
    grad_down_in,
    mod,
    key_spare,
    key_scale,
    ones,
    out,
    mid_own,
    ga_own,
    ga_other,
    stats,
    up_sum,
    qkv_sum,
    b0,
    b1,
    b2,
    b3,
    b4,
    turned,
    pool,
    qaug,
    w,
    work,
    got_low,
    got_high,
    next_low,
    next_high,
    got_z,
    p_send,
    p_recv,
    z_send,
    z_recv,
    t_send,
    t_recv,
    load_sem,
):
    nz, ny, nx = grid
    half = nz // 2
    seqs, pad = sizes
    chunks = out.shape[0]
    slots = work.shape[0]
    ff_chunks = slope_in.shape[0]
    z, y, x_at, core = coords(grid)
    width = b0.shape[1]
    part_width = pool.shape[2]
    pairs = part_width // 128
    blocks = seqs * 2
    ln2 = 0.6931471805599453

    def dev(z_to, y_to, x_to):
        return ((z_to * ny + y_to) * nx + x_to, core)

    x_peer = dev(z, y, 1 - x_at)
    y_peer = dev(z, 1 - y, x_at)
    sibling = (place()[0], 1 - core)
    greet([x_peer, y_peer, sibling] + [dev((z + k) % nz, y, x_at) for k in range(1, nz)])

    def block_rows(a):
        return pl.ds(pl.multiple_of(a * pad, 16), pad)

    loads = []

    def load(src, dst):
        copy = pltpu.make_async_copy(src, dst, load_sem.at[len(loads)])
        copy.start()
        loads.append(copy)
        return copy

    def first_copies(c):
        s = c % slots
        return [
            remote(
                work.at[s, pl.ds(0, half), 1 - y], got_low.at[c], p_send.at[c, 0], p_recv.at[c, 0], y_peer
            ),
            remote(
                work.at[s, pl.ds(half, half), :, 1 - x_at],
                got_high.at[c],
                p_send.at[c, 1],
                p_recv.at[c, 1],
                x_peer,
            ),
        ]

    def second_copies(c):
        s = c % slots
        return [
            remote(
                work.at[s, pl.ds(0, half), y, 1 - x_at],
                next_low.at[c],
                p_send.at[c, 2],
                p_recv.at[c, 2],
                x_peer,
            ),
            remote(
                work.at[s, pl.ds(half, half), 1 - y, x_at],
                next_high.at[c],
                p_send.at[c, 3],
                p_recv.at[c, 3],
                y_peer,
            ),
        ]

    def z_copies(c):
        s = c % slots
        return [
            remote(
                work.at[s, (z + k) % nz, y, x_at],
                got_z.at[c, k - 1],
                z_send.at[c, k - 1],
                z_recv.at[c, k - 1],
                dev((z + k) % nz, y, x_at),
            )
            for k in range(1, nz)
        ]

    def add(a, b):
        return (a.astype(F32) + b.astype(F32)).astype(BF16)

    def begin(c):
        for copy in first_copies(c):
            copy.start()

    def second(c):
        s = c % slots
        for copy in first_copies(c):
            copy.wait_recv()
        work[s, 0:half, y] = add(work[s, 0:half, y], got_low[c])
        work[s, half:nz, :, x_at] = add(work[s, half:nz, :, x_at], got_high[c])
        for copy in second_copies(c):
            copy.start()

    def third(c):
        s = c % slots
        for copy in second_copies(c):
            copy.wait_recv()
        work[s, 0:half, y, x_at] = add(work[s, 0:half, y, x_at], next_low[c])
        work[s, half:nz, y, x_at] = add(work[s, half:nz, y, x_at], next_high[c])
        for copy in z_copies(c):
            copy.start()

    def last(c):
        s = c % slots
        for copy in z_copies(c):
            copy.wait_recv()
        total = work[s, z, y, x_at].astype(F32)
        for k in range(nz - 1):
            total = total + got_z[c, k].astype(F32)
        out[c] = total

    def sent(c):
        for copy in first_copies(c) + second_copies(c) + z_copies(c):
            copy.wait_send()

    def put(c, right):
        if c >= slots:
            sent(c - slots)
        weight_grad(work.at[c % slots], turned, right)

    def step(t, start=True):
        if start and t < chunks:
            begin(t)
        if 0 <= t - 2 < chunks:
            second(t - 2)
        if 0 <= t - 3 < chunks:
            third(t - 3)
        if 0 <= t - 4 < chunks:
            last(t - 4)

    def weight(slot):
        return w[slot].reshape(width, part_width)

    down_grads = [load(grad_down_in.at[c], work.at[c]) for c in range(ff_chunks)]
    mlp_load = load(mlp_in, b1)
    dm_load = load(dm_in, b0)
    down_loads = [
        (load(full.at[chunks - ff_chunks + c], w.at[c]), load(slope_in.at[c], pool.at[c]))
        for c in range(ff_chunks)
    ]
    branch_load = load(branch_in, b4)
    qaug_load = load(qaug_in, qaug)
    for c in range(2):
        down_grads[c].wait()
        step(c)
    for c in range(2, ff_chunks):
        down_grads[c].wait()
    mlp_load.wait()
    transpose_into(turned, b1)
    grad_load = load(grad_in, b1)
    dm_load.wait()
    up_sum[...] = jnp.zeros_like(up_sum)
    up_loads = []
    for c in range(ff_chunks):
        for copy in down_loads[c]:
            copy.wait()

        def back(a, rows):
            gh = dot(b0[rows, :], weight(c)) * pool[c, rows, :].astype(F32)
            up_sum[c] += column_sum(gh)
            pool[c, rows, :] = gh.astype(BF16)

        for_blocks(blocks, pad, back)
        up_loads.append(load(full.at[4 + c], w.at[c]))
        put(ff_chunks + c, pool.at[c])
        if c != 1:
            step(2 + (c + 1) // 2)
    x_load = load(x_in, b0)
    for copy in up_loads:
        copy.wait()
    swaps = []
    for a in range(blocks):
        rows = block_rows(a)
        total = dot_nt(pool[0, rows, :], weight(0))
        for c in range(1, ff_chunks):
            total = total + dot_nt(pool[c, rows, :], weight(c))
        b2[rows, :] = total.astype(BF16)
        copy = remote(b2.at[rows, :], b3.at[rows, :], t_send.at[a], t_recv.at[a], sibling)
        copy.start()
        swaps.append(copy)
    proj_load = load(full.at[3], w.at[3])
    qkv_loads = [load(full.at[j], w.at[j]) for j in range(3)]
    step(5)
    for copy in (x_load, grad_load, branch_load, proj_load):
        copy.wait()
    stats[...] = jnp.zeros_like(stats)
    grad_att = pool.at[3]
    for a in range(blocks):
        rows = block_rows(a)
        s = a // 2
        swaps[a].wait()
        b = b4[rows, :].astype(F32)
        gm = b2[rows, :].astype(F32) + b3[rows, :].astype(F32)
        normed, inverse = normalize(b0[rows, :].astype(F32) + mod[s, 0:1, :] * b)
        stats[s, 1:2, :] += 0.5 * column_sum(gm * normed)
        stats[s, 2:3, :] += 0.5 * column_sum(gm)
        mid = b1[rows, :].astype(F32) + norm_back(gm * (1.0 + mod[s, 3:4, :]), normed, inverse)
        b1[rows, :] = mid.astype(BF16)
        stats[s, 0:1, :] += 0.5 * column_sum(mid * b)
        branch_grad = mid * mod[s, 0:1, :]
        stats[s, 3:4, :] += 0.5 * column_sum(branch_grad)
        low = branch_grad.astype(BF16)
        b4[rows, :] = low
        grad_att[rows, :] = dot(low, weight(3)).astype(BF16)
        if a == 1:
            step(6)
    mid_saves = [load(b1.at[block_rows(s * 2 + core), :], mid_own.at[s]) for s in range(seqs)]
    att = b2.at[:, pl.ds(0, part_width)]
    att_load = load(att_in, att)
    kv_load = load(kv_in, b3)
    transpose_into(turned, b4)
    step(7)
    mixed_load = load(mixed_in, b4)
    att_load.wait()
    put(8, att)
    inverse_load = load(inverse_in, b2)
    kv_load.wait()
    qaug_load.wait()
    qkv_sum[...] = jnp.zeros_like(qkv_sum)

    def attend(i, carry):
        p = i // seqs
        s = i % seqs
        start = pl.multiple_of(s * 2 * pad, 16)
        all_rows = pl.ds(start, 2 * pad)
        at = pl.multiple_of(p * 128, 128)
        lanes = pl.ds(at, 128)
        first, unused = lane_code(pad)
        first_all, unused = lane_code(2 * pad)
        k_sides = both_heads(b3[all_rows, lanes], key_spare[all_rows, :])
        v_sides = both_heads(b3[all_rows, pl.ds(at + part_width, 128)], 0.0)
        g_sides = both_heads(pool[3, all_rows, lanes], 0.0)
        grads_k, grads_v, grads_q = [], [], [[], []]
        for side in range(2):
            h = 2 * p + side
            k = k_sides[side]
            v = v_sides[side]
            sum_k = sum_v = None
            for t in range(2):
                rows = pl.ds(pl.multiple_of(start + t * pad, 16), pad)
                q = qaug[h, rows, :]
                g = g_sides[side][t * pad : t * pad + pad]
                prob = jnp.exp2(dot_nt(k, q))
                grad_prob = dot_nt(v, g)
                ds = (prob * (grad_prob - column_sum(prob * grad_prob))).astype(BF16)
                gv = dot(prob.astype(BF16), g)
                gk = dot(ds, q)
                sum_v = gv if t == 0 else sum_v + gv
                sum_k = gk if t == 0 else sum_k + gk
                grads_q[t].append(dot_tn(ds, k))
            grads_k.append(sum_k)
            grads_v.append(sum_v)
        for t in range(2):
            rows = pl.ds(pl.multiple_of(start + t * pad, 16), pad)
            gq = jnp.where(first, grads_q[t][0], grads_q[t][1])
            q = jnp.where(first, qaug[2 * p, rows, :].astype(F32), qaug[2 * p + 1, rows, :].astype(F32))
            qkv_sum[2:3, lanes] += ln2 * column_sum(gq * q)
            pool[0, rows, lanes] = gq.astype(BF16)
        pool[1, all_rows, lanes] = (ln2 * jnp.where(first_all, grads_k[0], grads_k[1])).astype(BF16)
        gv = jnp.where(first_all, grads_v[0], grads_v[1])
        qkv_sum[1:2, lanes] += column_sum(gv)
        pool[2, all_rows, lanes] = gv.astype(BF16)
        return carry

    count = pairs * seqs
    for quarter in range(4):
        lax.fori_loop(quarter * count // 4, (quarter + 1) * count // 4, attend, 0)
        if quarter == 0:
            step(8)
        elif quarter < 3:
            step(8 + quarter, start=False)
    third(8)
    last(7)
    mixed_load.wait()
    transpose_into(turned, b4)
    put(9, pool.at[2])
    begin(9)
    inverse_load.wait()

    def finish_q(a, rows):
        first, unused = lane_code(pad)
        scale = key_scale[...]
        unit = jnp.concatenate(
            [
                jnp.where(first, qaug[2 * p, rows, :].astype(F32), qaug[2 * p + 1, rows, :].astype(F32))
                for p in range(pairs)
            ],
            axis=1,
        )
        unit = unit / scale
        f = pool[0, rows, :].astype(F32) * (scale * ln2)
        gq = b2[rows, 0:part_width].astype(F32) * (f - unit * dot((f * unit).astype(BF16), ones[...]))
        qkv_sum[0:1, :] += column_sum(gq)
        pool[0, rows, :] = gq.astype(BF16)

    def finish_k(a, rows):
        unit = b3[rows, 0:part_width].astype(F32)
        f = pool[1, rows, :].astype(F32)
        gk = b2[rows, part_width : 2 * part_width].astype(F32) * (
            f - unit * dot((f * unit).astype(BF16), ones[...])
        )
        pool[1, rows, :] = gk.astype(BF16)

    for_blocks(blocks, pad, finish_q)
    put(10, pool.at[0])
    begin(10)
    last(8)
    for_blocks(blocks, pad, finish_k)
    put(11, pool.at[1])
    begin(11)
    second(9)
    for copy in qkv_loads:
        copy.wait()
    end_copies = []
    end_saves = []
    for i in range(blocks):
        s = i % seqs
        which = 1 - core if i < seqs else core
        rows = block_rows(s * 2 + which)
        total = dot_nt(pool[0, rows, :], weight(0))
        for j in range(1, 3):
            total = total + dot_nt(pool[j, rows, :], weight(j))
        b0[rows, :] = total.astype(BF16)
        if i < seqs:
            copy = remote(b0.at[rows, :], ga_other.at[s], t_send.at[blocks + s], t_recv.at[blocks + s], sibling)
            copy.start()
            end_copies.append(copy)
        else:
            end_saves.append(load(b0.at[rows, :], ga_own.at[s]))
        if i == 1:
            second(10)
            third(9)
    second(11)
    third(10)
    last(9)
    third(11)
    last(10)
    last(11)
    for copy in end_copies + end_saves + mid_saves:
        copy.wait()
    for c in range(chunks - slots, chunks):
        sent(c)


def backward_pass(grid, sizes, operands, mod, key_spare, key_scale, ones, collective_id):
    nz, ny, nx = grid
    half = nz // 2
    seqs, pad = sizes
    full, slope = operands[0], operands[10]
    chunks = full.shape[0]
    own_rows, part = full.shape[4:]
    ff_chunks = slope.shape[0]
    total = seqs * 2 * pad
    width = nz * ny * nx * own_rows
    heads = part // 64
    wide = ((total, width), BF16)
    chunk = (nz, ny, nx, own_rows, part)
    block = (own_rows, part)
    slots = 8
    outs = [
        ((chunks,) + block, F32),
        ((seqs, pad, width), BF16),
        ((seqs, pad, width), BF16),
        ((seqs, pad, width), BF16),
        ((seqs, 4, width), F32),
        ((ff_chunks, 1, part), F32),
        ((8, part), F32),
    ]
    scratch = [wide] * 5 + [
        ((width, total), BF16),
        ((ff_chunks, total, part), BF16),
        ((heads, total, 128), BF16),
        ((4,) + chunk, BF16),
        ((slots,) + chunk, BF16),
        ((chunks, half, nx) + block, BF16),
        ((chunks, half, ny) + block, BF16),
        ((chunks, half) + block, BF16),
        ((chunks, half) + block, BF16),
        ((chunks, nz - 1) + block, BF16),
    ]
    vmem = pl.BlockSpec(memory_space=pltpu.VMEM)
    hbm = pl.BlockSpec(memory_space=ANY)
    swaps = seqs * 2 + seqs
    return pl.pallas_call(
        functools.partial(backward_kernel, grid, sizes),
        out_shape=[jax.ShapeDtypeStruct(shape, dtype) for shape, dtype in outs],
        in_specs=[hbm] * 13 + [vmem] * 4,
        out_specs=[vmem] + [hbm] * 3 + [vmem] * 3,
        scratch_shapes=[pltpu.VMEM(shape, dtype) for shape, dtype in scratch]
        + [
            pltpu.SemaphoreType.DMA((chunks, 4)),
            pltpu.SemaphoreType.DMA((chunks, 4)),
            pltpu.SemaphoreType.DMA((chunks, nz - 1)),
            pltpu.SemaphoreType.DMA((chunks, nz - 1)),
            pltpu.SemaphoreType.DMA((swaps,)),
            pltpu.SemaphoreType.DMA((swaps,)),
            pltpu.SemaphoreType.DMA((40,)),
        ],
        compiler_params=pltpu.CompilerParams(
            collective_id=collective_id, has_side_effects=True, vmem_limit_bytes=60 * 2**20
        ),
        name="backward_pass",
    )(*operands, mod, key_spare, key_scale, ones)


def finish_kernel(
    grid,
    sizes,
    x_in,
    grad_in,
    branch_in,
    mlp_own,
    mlp_other,
    mid_own,
    ga_own,
    ga_other,
    mod,
    mid_stats,
    up_sum,
    qkv_sum,
    ada,
    output,
    grad_tokens,
    got,
    mod_low,
    back_got,
    rows_in,
    stats,
    message,
    back_message,
    load_sem,
    a_send,
    a_recv,
    c_send,
    c_recv,
):
    nz, ny, nx = grid
    dp = nz * ny * nx
    devices = dp * 2
    seqs, pad = sizes
    chip, core = place()
    me = chip * 2 + core
    length = output.shape[0]
    part_width = qkv_sum.shape[1]
    barrier = pltpu.get_barrier_semaphore()
    for k in range(1, devices):
        peer = (me + k) % devices
        pl.semaphore_signal(barrier, inc=1, device_id=(peer // 2, peer % 2), device_id_type=MESH_ID)

    loads = []
    for s in range(seqs):
        own = pl.ds(pl.multiple_of((s * 2 + core) * pad, 16), pad)
        pieces = [ref.at[own, :] for ref in (x_in, grad_in, branch_in)]
        pieces += [ref.at[s] for ref in (mlp_own, mlp_other, mid_own, ga_own, ga_other)]
        for i, piece in enumerate(pieces):
            copy = pltpu.make_async_copy(piece, rows_in.at[s, i], load_sem.at[s, i])
            copy.start()
            loads.append(copy)
    message[...] = jnp.zeros_like(message)
    back_message[...] = jnp.zeros_like(back_message)
    for s in range(seqs):
        for copy in loads[s * 8 : s * 8 + 8]:
            copy.wait()
        xs, g, unused, own_b, other_b, mid, own_g, other_g = (rows_in[s, i].astype(F32) for i in range(8))
        b = own_b + other_b + mod[s, 7:8, :]
        normed, inverse = normalize(xs)
        gm = own_g + other_g
        gt = mid + norm_back(gm * (1.0 + mod[s, 2:3, :]), normed, inverse)
        grad_tokens[:, s, :] = gt[0:length]
        stats[s, 0:1, :] = mid_stats[s, 0:1, :]
        stats[s, 1:2, :] = column_sum(g * b)
        stats[s, 2:3, :] = column_sum(gm * normed)
        stats[s, 3:4, :] = mid_stats[s, 1:2, :]
        stats[s, 4:5, :] = column_sum(gm)
        stats[s, 5:6, :] = mid_stats[s, 2:3, :]
        stats[s, 6:7, :] = mid_stats[s, 3:4, :]
        stats[s, 7:8, :] = column_sum(g) * mod[s, 1:2, :]

    def iota(shape, dim):
        return lax.broadcasted_iota(jnp.int32, shape, dim)

    def shares(values, span):
        count, lanes = values.shape
        share = span // dp
        mine = (iota((dp, 1, lanes), 2) % span) // share == iota((dp, 1, lanes), 0)
        lane = iota((lanes, 128), 0)
        table = jnp.where(lane // span * share + lane % share == iota((lanes, 128), 1) - 64, 1.0, 0.0)
        split = jnp.where(mine, values, 0.0).reshape(dp * count, lanes).astype(BF16)
        return dot(split, table.astype(BF16)).reshape(dp, count, 128)

    ends = [stats[0, r : r + 1, :] + stats[1, r : r + 1, :] for r in (6, 7)]
    lane = iota((part_width, 128), 0)
    heads_table = jnp.where(lane // 64 == iota((part_width, 128), 1) - 64, 1.0, 0.0).astype(BF16)
    terms = qkv_sum[2:3, :]
    terms_high = terms.astype(BF16)
    terms_low = (terms - terms_high.astype(F32)).astype(BF16)
    both = jnp.concatenate([terms_high.astype(F32), terms_low.astype(F32)], axis=0)
    both = jnp.concatenate([both, jnp.zeros((6, part_width), F32)], axis=0).astype(BF16)
    head_terms = dot(both, heads_table)
    head_sums = head_terms[0:1] + head_terms[1:2]
    head_high = head_sums.astype(BF16).astype(F32)
    vectors = [qkv_sum[0:1, :], qkv_sum[1:2, :]]
    vectors += [end[:, t * part_width : (t + 1) * part_width] for end in ends for t in range(2)]
    vectors += [jnp.zeros((2, part_width), F32)]
    small = shares(jnp.concatenate(vectors, axis=0), 64)
    ups = jnp.concatenate([up_sum[c] for c in range(up_sum.shape[0])] + [jnp.zeros((4, part_width), F32)], axis=0)
    ups = shares(ups, 256)
    six = jnp.concatenate([stats[s, 0:6, :] for s in range(seqs)] + [jnp.zeros((4, stats.shape[2]), F32)], axis=0)
    for d in range(dp):
        at = d // 2 * 128
        cols = six[:, at : at + 128]
        cols = cols if d % 2 == 0 else pltpu.roll(cols, 64, 1)
        right = jnp.concatenate([small[d, 0:6], head_high, head_sums - head_high, ups[d, 0:8]], axis=0)
        message[d] = jnp.where(iota((16, 128), 1) < 64, cols, right).astype(BF16)
    pl.semaphore_wait(barrier, devices - 1)
    copies = []
    for k in range(1, devices):
        peer = (me + k) % devices
        copy = remote(
            message.at[peer // 2], got.at[chip, core], a_send.at[k - 1], a_recv.at[k - 1], (peer // 2, peer % 2)
        )
        copy.start()
        copies.append(copy)
    got[chip, core] = message[chip]
    for s in range(seqs):
        xs, g, branch, own_b, other_b = (rows_in[s, i].astype(F32) for i in range(5))
        b = own_b + other_b + mod[s, 7:8, :]
        output[:, s, :] = (xs + mod[s, 0:1, :] * branch + mod[s, 1:2, :] * b)[0:length]
    for copy in copies:
        copy.wait()
    sums = got[:, 0].astype(F32) + got[:, 1].astype(F32)
    for s in range(seqs):
        low = jnp.concatenate([sums[:, s * 6 + j, 0:64] for j in range(6)], axis=1).astype(BF16)
        mod_low[s] = low
        back = dot(low, ada[...])
        for g in range(part_width // 128):
            back_message[:, s * 4 + g, :] = back[:, g * 128 : g * 128 + 128]
    bias = jnp.sum(sums, axis=0)
    bias = bias[0:6] + bias[6:12]
    back_message[:, 8:14, :] = jnp.broadcast_to(bias, (dp,) + bias.shape)
    copies = []
    for k in range(1, dp):
        to = (chip + k) % dp
        copy = remote(back_message.at[to], back_got.at[chip], c_send.at[k - 1], c_recv.at[k - 1], (to, core))
        copy.start()
        copies.append(copy)
    back_got[chip] = back_message[chip]
    for copy in copies:
        copy.wait()


def finish(grid, sizes, length, operands, collective_id):
    nz, ny, nx = grid
    dp = nz * ny * nx
    seqs, pad = sizes
    width = operands[0].shape[1]
    ada = operands[-1]
    outs = [
        ((length, seqs, width), F32),
        ((length, seqs, width), F32),
        ((dp, 2, 16, 128), BF16),
        ((seqs, dp, ada.shape[0]), BF16),
        ((dp, 16, 128), F32),
    ]
    scratch = [
        ((seqs, 8, pad, width), BF16),
        ((seqs, 8, width), F32),
        ((dp, 16, 128), BF16),
        ((dp, 16, 128), F32),
    ]
    vmem = pl.BlockSpec(memory_space=pltpu.VMEM)
    hbm = pl.BlockSpec(memory_space=ANY)
    return pl.pallas_call(
        functools.partial(finish_kernel, grid, sizes),
        out_shape=[jax.ShapeDtypeStruct(shape, dtype) for shape, dtype in outs],
        in_specs=[hbm] * 8 + [vmem] * 5,
        out_specs=[vmem] * len(outs),
        scratch_shapes=[pltpu.VMEM(shape, dtype) for shape, dtype in scratch]
        + [
            pltpu.SemaphoreType.DMA((seqs, 8)),
            pltpu.SemaphoreType.DMA((2 * dp - 1,)),
            pltpu.SemaphoreType.DMA((2 * dp - 1,)),
            pltpu.SemaphoreType.DMA((dp - 1,)),
            pltpu.SemaphoreType.DMA((dp - 1,)),
        ],
        compiler_params=pltpu.CompilerParams(
            collective_id=collective_id, has_side_effects=True, vmem_limit_bytes=60 * 2**20
        ),
        name="finish",
    )(*operands)


def fast_device(
    grid,
    tokens,
    condition,
    scale_index,
    ada_weight,
    ada_bias,
    qkv_weight,
    query_bias,
    value_bias,
    head_scale,
    proj_weight,
    proj_bias,
    up_weight,
    up_bias,
    down_weight,
    down_bias,
    out_grad,
):
    nz, ny, nx = grid
    dp = nz * ny * nx
    count = dp * 2
    seqs, own_len, width = tokens.shape
    seq_len = own_len * 2
    part = qkv_weight.shape[2]
    heads = head_scale.shape[0]
    head_dim = part // heads
    own_rows = qkv_weight.shape[1]
    ff_chunks = up_weight.shape[1] // part
    chip, core = place()

    shard = jnp.concatenate(
        [
            qkv_weight,
            proj_weight.T[None],
            up_weight.reshape(own_rows, ff_chunks, part).transpose(1, 0, 2),
            down_weight.T.reshape(own_rows, ff_chunks, part).transpose(1, 0, 2),
        ],
        axis=0,
    )
    pad = -(-own_len // 16) * 16
    total = seqs * 2 * pad
    sizes = (seqs, pad)
    halves = condition.reshape(seqs, 2, -1, 128).transpose(1, 0, 2, 3).reshape(2, -1, 128)
    shares = [values.reshape(-1) for values in (ada_bias, query_bias, value_bias, proj_bias, down_bias)]
    shares = jnp.concatenate(shares)
    shares = jnp.pad(shares, (0, -shares.size % 128)).reshape(-1, 128)
    shares = jnp.concatenate([shares, up_bias.reshape(-1, 128)], axis=0)
    small = jnp.concatenate([halves, jnp.broadcast_to(shares, (2,) + shares.shape)], axis=1)
    small = jnp.pad(small, ((0, 0), (0, -small.shape[1] % 16), (0, 0)))
    cols = ada_weight.shape[2]
    ada = ada_weight.transpose(1, 2, 0).reshape(-1, part)
    own_of = lambda values: lax.dynamic_index_in_dim(values, core, 1, keepdims=False)

    level = jnp.pad(
        scale_index.reshape(seqs, 2, own_len), ((0, 0), (0, 0), (0, pad - own_len)), constant_values=100
    ).reshape(total, 1)
    code = jnp.arange(128)[None] % 64
    query_spare = jnp.where(code == level, 1.0, 0.0).astype(BF16)
    key_spare = jnp.where(
        code < SCALES, jnp.where(level > code, MASK, 0.0), jnp.where(code < SCALES + 3, 1.0, 0.0)
    ).astype(BF16)
    key_scale = jnp.repeat(jnp.exp(head_scale) * 1.4426950408889634, head_dim).reshape(1, part)
    head_at = jnp.arange(part) // head_dim
    ones = (head_at[:, None] == head_at[None, :]).astype(BF16)
    (
        full,
        x,
        grad,
        mixed,
        qaug,
        kv,
        inverses,
        att,
        branch,
        mlp,
        slope,
        dm,
        grad_down,
        mlp_part,
        mlp_other,
        mod,
        silu_half,
    ) = forward_pass(
        grid,
        sizes,
        shard,
        tokens.transpose(1, 0, 2),
        out_grad.transpose(1, 0, 2),
        small,
        ada,
        query_spare,
        key_spare,
        key_scale,
        ones,
        0,
    )
    reduced, grad_mid, ga_part, ga_other, mid_stats, up_sum, qkv_sum = backward_pass(
        grid,
        sizes,
        (full, x, grad, mixed, qaug, kv, inverses, att, branch, mlp, slope, dm, grad_down),
        mod,
        key_spare,
        key_scale,
        ones,
        5,
    )
    output, grad_inputs, got, mod_low, back_got = finish(
        grid,
        sizes,
        own_len,
        (x, grad, branch, mlp_part, mlp_other, grad_mid, ga_part, ga_other, mod, mid_stats, up_sum, qkv_sum, ada),
        1,
    )
    grad_ada = jnp.einsum(
        "sdr,sdc->rc", silu_half, mod_low, preferred_element_type=F32
    ).reshape(part, 6, cols)
    same_core = jnp.sum(own_of(got)[:, :, 64:96].astype(F32), axis=0)
    every_core = jnp.sum(got[:, :, :, 64:96].astype(F32), axis=(0, 1))
    owned_ends = [
        lax.dynamic_index_in_dim(every_core, at + core, 0, keepdims=False).reshape(proj_bias.shape) for at in (2, 4)
    ]
    back_sum = jnp.sum(back_got[:, 0:8, :], axis=0)
    grad_silu = back_sum.reshape(seqs, part)
    cond_own = lax.dynamic_slice_in_dim(condition.astype(F32), core * part, part, 1)
    sigmoid = jax.nn.sigmoid(cond_own)
    grad_condition = grad_silu * sigmoid * (1.0 + cond_own * (1.0 - sigmoid))
    ada_rows = lax.dynamic_slice(
        back_got,
        (core * heads, 8, chip * ada_bias.shape[2]),
        (heads, 6, ada_bias.shape[2]),
    )
    grad_ada_bias = ada_rows.transpose(1, 0, 2)

    chunks = reduced.shape[0]
    wide = lambda values: values.transpose(1, 0, 2).reshape(own_rows, -1)
    return (
        output.transpose(1, 0, 2),
        grad_inputs.transpose(1, 0, 2),
        grad_condition,
        grad_ada,
        grad_ada_bias,
        jnp.stack([reduced[chunks - 2], reduced[chunks - 1], reduced[chunks - 3]]),
        same_core[0].reshape(query_bias.shape),
        same_core[1].reshape(value_bias.shape),
        same_core[6, :heads] + same_core[7, :heads],
        reduced[2 * ff_chunks].T,
        owned_ends[0],
        wide(reduced[ff_chunks : 2 * ff_chunks]),
        same_core[8:12].reshape(up_bias.shape),
        wide(reduced[:ff_chunks]).T,
        owned_ends[1],
    )


def solution(mesh):
    in_specs = (
        P("dp", "tensor", None),
        P("dp", None),
        P("dp", None),
        P("tensor", None, "dp"),
        P(None, "tensor", "dp"),
        P(None, "dp", "tensor"),
        P("tensor", "dp"),
        P("tensor", "dp"),
        P("tensor"),
        P("tensor", "dp"),
        P("tensor", "dp"),
        P("dp", "tensor"),
        P("tensor", "dp"),
        P("tensor", "dp"),
        P("tensor", "dp"),
        P("dp", "tensor", None),
    )
    out_specs = (
        P("dp", "tensor", None),
        P("dp", "tensor", None),
        P("dp", "tensor"),
        P("tensor", None, "dp"),
        P(None, "tensor", "dp"),
        P(None, "dp", "tensor"),
        P("tensor", "dp"),
        P("tensor", "dp"),
        P("tensor"),
        P("tensor", "dp"),
        P("tensor", "dp"),
        P("dp", "tensor"),
        P("tensor", "dp"),
        P("tensor", "dp"),
        P("tensor", "dp"),
    )
    grid = GRIDS.get((mesh.shape["dp"], mesh.shape["tensor"]))
    body = on_device if grid is None else functools.partial(fast_device, grid)
    return jax.shard_map(
        body, mesh=mesh, in_specs=in_specs, out_specs=out_specs, check_vma=False
    )
```

```python
import functools

import jax
import jax.numpy as jnp
from jax import lax
from jax.experimental import pallas as pl
from jax.experimental.pallas import tpu as pltpu
from jax.sharding import PartitionSpec as P

NORM_EPS = 1e-06
HEAD_EPS = 1e-06
GELU_COEF = 0.7978845608028654
GELU_CUBE = 0.044715


def normalize(values):
    centred = values - jnp.mean(values, axis=-1, keepdims=True)
    inverse = lax.rsqrt(jnp.mean(centred * centred, axis=-1, keepdims=True) + NORM_EPS)
    return (centred * inverse, inverse)


def norm_back(grad_normed, normed, inverse):
    return inverse * (
        grad_normed
        - jnp.mean(grad_normed, axis=-1, keepdims=True)
        - normed * jnp.mean(grad_normed * normed, axis=-1, keepdims=True)
    )


def gelu_slope(hidden):
    inner = jnp.tanh(GELU_COEF * (hidden + GELU_CUBE * hidden * hidden * hidden))
    return 0.5 * (1.0 + inner) + 0.5 * hidden * (1.0 - inner * inner) * GELU_COEF * (
        1.0 + 3.0 * GELU_CUBE * hidden * hidden
    )


def masked_scores(query_unit, key_unit, scale_factor, scale_row):
    query_low = (query_unit * scale_factor).astype(jnp.bfloat16)
    key_low = key_unit.astype(jnp.bfloat16)
    scores = jnp.einsum("qhe,khe->hqk", query_low, key_low, preferred_element_type=jnp.float32)
    allowed = scale_row[None, :] <= scale_row[:, None]
    return (jnp.where(allowed[None, :, :], scores, -1e30), query_low, key_low)


def attention_core(mixed_all, qkv_full, query_bias_part, value_bias_part, head_scale, scale_row):
    part_width = qkv_full.shape[2]
    part_heads = head_scale.shape[0]
    head_dim = part_width // part_heads
    seq_len = scale_row.shape[0]
    projected = jnp.einsum("ld,jdc->jlc", mixed_all, qkv_full, preferred_element_type=jnp.float32)
    queries = (projected[0] + query_bias_part.reshape(part_width).astype(jnp.float32)).reshape(
        seq_len, part_heads, head_dim
    )
    keys_raw = projected[1].reshape(seq_len, part_heads, head_dim)
    values_low = (projected[2] + value_bias_part.reshape(part_width).astype(jnp.float32)).astype(
        jnp.bfloat16
    )
    values_low = values_low.reshape(seq_len, part_heads, head_dim)
    query_inverse = lax.rsqrt(jnp.sum(queries * queries, axis=-1, keepdims=True) + HEAD_EPS)
    key_inverse = lax.rsqrt(jnp.sum(keys_raw * keys_raw, axis=-1, keepdims=True) + HEAD_EPS)
    query_unit = queries * query_inverse
    key_unit = keys_raw * key_inverse
    scale_factor = jnp.exp(head_scale)[:, None]
    scores, query_low, key_low = masked_scores(query_unit, key_unit, scale_factor, scale_row)
    row_max = jnp.max(scores, axis=-1, keepdims=True)
    weights_exp = jnp.exp(scores - row_max)
    row_total = jnp.sum(weights_exp, axis=-1, keepdims=True)
    attn_prob = weights_exp / row_total
    log_norm = row_max + jnp.log(row_total)
    attended = jnp.einsum(
        "hqk,khe->qhe",
        attn_prob.astype(jnp.bfloat16),
        values_low,
        preferred_element_type=jnp.float32,
    )
    attended = attended.reshape(seq_len, part_width).astype(jnp.bfloat16)
    return (attended, (query_unit, key_unit, query_inverse, key_inverse, values_low, log_norm))


def forward_step(weights, token_rows, condition_row, scale_row, head_scale):
    (
        ada_full,
        ada_bias_part,
        qkv_full,
        query_bias_part,
        value_bias_part,
        proj_full,
        proj_bias_part,
        up_full,
        up_bias_part,
        down_full,
        down_bias_part,
    ) = weights
    width = token_rows.shape[1]
    part_width = qkv_full.shape[2]
    col_start = lax.axis_index("tensor") * part_width
    cond_rows = lax.dynamic_slice_in_dim(
        condition_row.astype(jnp.float32), col_start, part_width, 0
    )
    silu_rows = jax.nn.silu(cond_rows).astype(jnp.bfloat16)
    mod_terms = jnp.einsum("r,rjc->jc", silu_rows, ada_full, preferred_element_type=jnp.float32)
    own_cols = jnp.concatenate(
        [
            ada_bias_part.reshape(6, part_width),
            proj_bias_part.reshape(1, part_width),
            down_bias_part.reshape(1, part_width),
        ],
        axis=0,
    ).astype(jnp.float32)
    placed = lax.dynamic_update_slice(jnp.zeros((8, width), jnp.float32), own_cols, (0, col_start))
    local_mod = placed + jnp.concatenate([mod_terms, jnp.zeros((2, width), jnp.float32)], axis=0)
    modulation = lax.psum(local_mod, "tensor")
    inputs = token_rows.astype(jnp.float32)
    normed_attn, inverse_attn = normalize(inputs)
    mixed_attn = (normed_attn * (1.0 + modulation[2]) + modulation[4]).astype(jnp.bfloat16)
    mixed_all = lax.all_gather(mixed_attn, "tensor", axis=0, tiled=True)
    attended, attn_kept = attention_core(
        mixed_all, qkv_full, query_bias_part, value_bias_part, head_scale, scale_row
    )
    branch_attn = (
        lax.psum_scatter(
            jnp.dot(attended, proj_full, preferred_element_type=jnp.float32).astype(jnp.bfloat16),
            "tensor",
            scatter_dimension=0,
            tiled=True,
        ).astype(jnp.float32)
        + modulation[6]
    )
    middle = inputs + modulation[0] * branch_attn
    normed_mlp, inverse_mlp = normalize(middle)
    mixed_mlp = (normed_mlp * (1.0 + modulation[3]) + modulation[5]).astype(jnp.bfloat16)
    mlp_all = lax.all_gather(mixed_mlp, "tensor", axis=0, tiled=True)
    hidden = jnp.dot(mlp_all, up_full, preferred_element_type=jnp.float32) + up_bias_part.reshape(
        -1
    ).astype(jnp.float32)
    activated = jax.nn.gelu(hidden, approximate=True).astype(jnp.bfloat16)
    branch_mlp = (
        lax.psum_scatter(
            jnp.dot(activated, down_full, preferred_element_type=jnp.float32).astype(jnp.bfloat16),
            "tensor",
            scatter_dimension=0,
            tiled=True,
        ).astype(jnp.float32)
        + modulation[7]
    )
    output = middle + modulation[1] * branch_mlp
    query_unit, key_unit, query_inverse, key_inverse, values_low, log_norm = attn_kept
    kept = (
        modulation,
        normed_attn,
        inverse_attn,
        mixed_all,
        query_unit,
        key_unit,
        query_inverse,
        key_inverse,
        values_low,
        log_norm,
        attended,
        branch_attn,
        normed_mlp,
        inverse_mlp,
        mlp_all,
        hidden,
        activated,
        branch_mlp,
    )
    return (output, kept)


def backward_step(weights, kept, token_grad, condition_row, scale_row, head_scale):
    (
        ada_full,
        ada_bias_part,
        qkv_full,
        query_bias_part,
        value_bias_part,
        proj_full,
        proj_bias_part,
        up_full,
        up_bias_part,
        down_full,
        down_bias_part,
    ) = weights
    (
        modulation,
        normed_attn,
        inverse_attn,
        mixed_all,
        query_unit,
        key_unit,
        query_inverse,
        key_inverse,
        values_low,
        log_norm,
        attended,
        branch_attn,
        normed_mlp,
        inverse_mlp,
        mlp_all,
        hidden,
        activated,
        branch_mlp,
    ) = kept
    part_width = qkv_full.shape[2]
    part_heads = head_scale.shape[0]
    head_dim = part_width // part_heads
    seq_len = scale_row.shape[0]
    scale_factor = jnp.exp(head_scale)[:, None]
    grad_rows = token_grad.astype(jnp.float32)
    grad_branch_mlp = grad_rows * modulation[1]
    grad_gamma_mlp = jnp.sum(grad_rows * branch_mlp, axis=0)
    grad_down_bias = jnp.sum(grad_branch_mlp, axis=0)
    grad_mlp_all = lax.all_gather(
        grad_branch_mlp.astype(jnp.bfloat16), "tensor", axis=0, tiled=True
    )
    grad_down = jnp.einsum("lf,ld->fd", activated, grad_mlp_all, preferred_element_type=jnp.float32)
    grad_act = jnp.einsum("ld,fd->lf", grad_mlp_all, down_full, preferred_element_type=jnp.float32)
    grad_hidden = grad_act * gelu_slope(hidden)
    grad_up_bias = jnp.sum(grad_hidden, axis=0)
    hidden_low = grad_hidden.astype(jnp.bfloat16)
    grad_up = jnp.einsum("ld,lf->df", mlp_all, hidden_low, preferred_element_type=jnp.float32)
    grad_mixed_mlp = lax.psum_scatter(
        jnp.einsum("lf,df->ld", hidden_low, up_full, preferred_element_type=jnp.float32).astype(
            jnp.bfloat16
        ),
        "tensor",
        scatter_dimension=0,
        tiled=True,
    ).astype(jnp.float32)
    grad_scale_mlp = jnp.sum(grad_mixed_mlp * normed_mlp, axis=0)
    grad_shift_mlp = jnp.sum(grad_mixed_mlp, axis=0)
    grad_middle = grad_rows + norm_back(
        grad_mixed_mlp * (1.0 + modulation[3]), normed_mlp, inverse_mlp
    )
    grad_branch_attn = grad_middle * modulation[0]
    grad_gamma_attn = jnp.sum(grad_middle * branch_attn, axis=0)
    grad_proj_bias = jnp.sum(grad_branch_attn, axis=0)
    grad_attn_all = lax.all_gather(
        grad_branch_attn.astype(jnp.bfloat16), "tensor", axis=0, tiled=True
    )
    grad_proj = jnp.einsum("lc,ld->cd", attended, grad_attn_all, preferred_element_type=jnp.float32)
    grad_attended = jnp.einsum(
        "ld,cd->lc", grad_attn_all, proj_full, preferred_element_type=jnp.float32
    )
    grad_attended = grad_attended.astype(jnp.bfloat16).reshape(seq_len, part_heads, head_dim)
    scores, query_low, key_low = masked_scores(query_unit, key_unit, scale_factor, scale_row)
    attn_prob = jnp.exp(scores - log_norm)
    grad_prob = jnp.einsum(
        "qhe,khe->hqk", grad_attended, values_low, preferred_element_type=jnp.float32
    )
    row_dot = jnp.sum(attn_prob * grad_prob, axis=-1, keepdims=True)
    grad_scores = (attn_prob * (grad_prob - row_dot)).astype(jnp.bfloat16)
    grad_values = jnp.einsum(
        "hqk,qhe->khe",
        attn_prob.astype(jnp.bfloat16),
        grad_attended,
        preferred_element_type=jnp.float32,
    )
    grad_query_scaled = jnp.einsum(
        "hqk,khe->qhe", grad_scores, key_low, preferred_element_type=jnp.float32
    )
    grad_key_unit = jnp.einsum(
        "hqk,qhe->khe", grad_scores, query_low, preferred_element_type=jnp.float32
    )
    grad_head_scale = jnp.sum(grad_query_scaled * query_unit, axis=(0, 2)) * jnp.exp(head_scale)
    grad_query_unit = grad_query_scaled * scale_factor
    grad_queries = query_inverse * (
        grad_query_unit - query_unit * jnp.sum(grad_query_unit * query_unit, axis=-1, keepdims=True)
    )
    grad_keys = key_inverse * (
        grad_key_unit - key_unit * jnp.sum(grad_key_unit * key_unit, axis=-1, keepdims=True)
    )
    grad_query_bias = jnp.sum(grad_queries, axis=0)
    grad_value_bias = jnp.sum(grad_values, axis=0)
    grad_projected = (
        jnp.stack([grad_queries, grad_keys, grad_values])
        .reshape(3, seq_len, part_width)
        .astype(jnp.bfloat16)
    )
    grad_qkv = jnp.einsum(
        "ld,jlc->jdc", mixed_all, grad_projected, preferred_element_type=jnp.float32
    )
    grad_mixed_attn = lax.psum_scatter(
        jnp.einsum(
            "jlc,jdc->ld", grad_projected, qkv_full, preferred_element_type=jnp.float32
        ).astype(jnp.bfloat16),
        "tensor",
        scatter_dimension=0,
        tiled=True,
    ).astype(jnp.float32)
    grad_scale_attn = jnp.sum(grad_mixed_attn * normed_attn, axis=0)
    grad_shift_attn = jnp.sum(grad_mixed_attn, axis=0)
    grad_inputs = grad_middle + norm_back(
        grad_mixed_attn * (1.0 + modulation[2]), normed_attn, inverse_attn
    )
    mod_rows = jnp.stack(
        [
            grad_gamma_attn,
            grad_gamma_mlp,
            grad_scale_attn,
            grad_scale_mlp,
            grad_shift_attn,
            grad_shift_mlp,
            grad_proj_bias,
            grad_down_bias,
        ]
    )
    grad_modulation = lax.psum(mod_rows.astype(jnp.bfloat16), "tensor").astype(jnp.float32)
    col_start = lax.axis_index("tensor") * part_width
    cond_rows = lax.dynamic_slice_in_dim(
        condition_row.astype(jnp.float32), col_start, part_width, 0
    )
    silu_rows = jax.nn.silu(cond_rows).astype(jnp.bfloat16)
    mod_low = grad_modulation[:6].astype(jnp.bfloat16)
    grad_ada = jnp.einsum("r,jc->rjc", silu_rows, mod_low, preferred_element_type=jnp.float32)
    grad_silu = jnp.einsum("jc,rjc->r", mod_low, ada_full, preferred_element_type=jnp.float32)
    sigmoid_rows = jax.nn.sigmoid(cond_rows)
    grad_condition = grad_silu * sigmoid_rows * (1.0 + cond_rows * (1.0 - sigmoid_rows))
    own_cols = lax.dynamic_slice_in_dim(grad_modulation, col_start, part_width, 1)
    increments = (
        grad_ada,
        own_cols[:6].reshape(6, part_heads, head_dim),
        grad_qkv,
        grad_query_bias,
        grad_value_bias,
        grad_head_scale,
        grad_proj,
        own_cols[6].reshape(part_heads, head_dim),
        grad_up,
        grad_up_bias.reshape(part_heads, -1),
        grad_down,
        own_cols[7].reshape(part_heads, head_dim),
    )
    return (increments, grad_inputs, grad_condition)


def on_device(
    tokens,
    condition,
    scale_index,
    ada_weight,
    ada_bias,
    qkv_weight,
    query_bias,
    value_bias,
    head_scale,
    proj_weight,
    proj_bias,
    up_weight,
    up_bias,
    down_weight,
    down_bias,
    out_grad,
):

    def fetch_weights():
        return (
            lax.all_gather(ada_weight, "dp", axis=2, tiled=True),
            lax.all_gather(ada_bias, "dp", axis=2, tiled=True),
            lax.all_gather(qkv_weight, "dp", axis=1, tiled=True),
            lax.all_gather(query_bias, "dp", axis=1, tiled=True),
            lax.all_gather(value_bias, "dp", axis=1, tiled=True),
            lax.all_gather(proj_weight, "dp", axis=1, tiled=True),
            lax.all_gather(proj_bias, "dp", axis=1, tiled=True),
            lax.all_gather(up_weight, "dp", axis=0, tiled=True),
            lax.all_gather(up_bias, "dp", axis=1, tiled=True),
            lax.all_gather(down_weight, "dp", axis=1, tiled=True),
            lax.all_gather(down_bias, "dp", axis=1, tiled=True),
        )

    def forward_scan(carried, step_in):
        token_rows, condition_row, scale_row = step_in
        weights_now = fetch_weights()
        output, kept = forward_step(weights_now, token_rows, condition_row, scale_row, head_scale)
        return (carried, (output, kept))

    unused_carry, (outputs, kept_all) = lax.scan(
        forward_scan, jnp.zeros((), jnp.int32), (tokens, condition, scale_index)
    )
    width = tokens.shape[2]
    part_width = qkv_weight.shape[2]
    part_heads = head_scale.shape[0]
    head_dim = part_width // part_heads
    part_ff = up_weight.shape[1]
    zero_grads = (
        jnp.zeros((part_width, 6, width), jnp.float32),
        jnp.zeros((6, part_heads, head_dim), jnp.float32),
        jnp.zeros((3, width, part_width), jnp.float32),
        jnp.zeros((part_heads, head_dim), jnp.float32),
        jnp.zeros((part_heads, head_dim), jnp.float32),
        jnp.zeros((part_heads,), jnp.float32),
        jnp.zeros((part_width, width), jnp.float32),
        jnp.zeros((part_heads, head_dim), jnp.float32),
        jnp.zeros((width, part_ff), jnp.float32),
        jnp.zeros((part_heads, part_ff // part_heads), jnp.float32),
        jnp.zeros((part_ff, width), jnp.float32),
        jnp.zeros((part_heads, head_dim), jnp.float32),
    )

    def backward_scan(totals, step_in):
        kept, token_grad, condition_row, scale_row = step_in
        weights_now = fetch_weights()
        increments, grad_inputs, grad_condition = backward_step(
            weights_now, kept, token_grad, condition_row, scale_row, head_scale
        )
        totals = tuple((running + increment for running, increment in zip(totals, increments)))
        return (totals, (grad_inputs, grad_condition))

    totals, (grad_tokens, grad_condition) = lax.scan(
        backward_scan, zero_grads, (kept_all, out_grad, condition, scale_index), reverse=True
    )
    scale_total = lax.psum(totals[5], "dp")
    reduced = (
        lax.psum_scatter(
            totals[0].astype(jnp.bfloat16), "dp", scatter_dimension=2, tiled=True
        ).astype(jnp.float32),
        lax.psum_scatter(
            totals[1].astype(jnp.bfloat16), "dp", scatter_dimension=2, tiled=True
        ).astype(jnp.float32),
        lax.psum_scatter(
            totals[2].astype(jnp.bfloat16), "dp", scatter_dimension=1, tiled=True
        ).astype(jnp.float32),
        lax.psum_scatter(
            totals[3].astype(jnp.bfloat16), "dp", scatter_dimension=1, tiled=True
        ).astype(jnp.float32),
        lax.psum_scatter(
            totals[4].astype(jnp.bfloat16), "dp", scatter_dimension=1, tiled=True
        ).astype(jnp.float32),
        lax.psum_scatter(
            totals[6].astype(jnp.bfloat16), "dp", scatter_dimension=1, tiled=True
        ).astype(jnp.float32),
        lax.psum_scatter(
            totals[7].astype(jnp.bfloat16), "dp", scatter_dimension=1, tiled=True
        ).astype(jnp.float32),
        lax.psum_scatter(
            totals[8].astype(jnp.bfloat16), "dp", scatter_dimension=0, tiled=True
        ).astype(jnp.float32),
        lax.psum_scatter(
            totals[9].astype(jnp.bfloat16), "dp", scatter_dimension=1, tiled=True
        ).astype(jnp.float32),
        lax.psum_scatter(
            totals[10].astype(jnp.bfloat16), "dp", scatter_dimension=1, tiled=True
        ).astype(jnp.float32),
        lax.psum_scatter(
            totals[11].astype(jnp.bfloat16), "dp", scatter_dimension=1, tiled=True
        ).astype(jnp.float32),
    )
    return (
        outputs,
        grad_tokens,
        grad_condition,
        reduced[0],
        reduced[1],
        reduced[2],
        reduced[3],
        reduced[4],
        scale_total,
        reduced[5],
        reduced[6],
        reduced[7],
        reduced[8],
        reduced[9],
        reduced[10],
    )


GRIDS = {(16, 2): (4, 2, 2)}
MESH_ID = pl.DeviceIdType.MESH
ANY = pl.ANY
F32 = jnp.float32
BF16 = jnp.bfloat16
SCALES = 10
MASK = -16384.0


def place():
    return (lax.axis_index("dp"), lax.axis_index("tensor"))


def coords(grid):
    chip, core = place()
    nz, ny, nx = grid
    return (chip // (ny * nx), (chip // nx) % ny, chip % nx, core)


def greet_all(count):
    chip, core = place()
    me = chip * 2 + core
    barrier = pltpu.get_barrier_semaphore()
    for k in range(1, count):
        peer = (me + k) % count
        pl.semaphore_signal(barrier, inc=1, device_id=(peer // 2, peer % 2), device_id_type=MESH_ID)
    pl.semaphore_wait(barrier, count - 1)


def remote(src, dst, send_sem, recv_sem, device):
    return pltpu.make_async_remote_copy(
        src_ref=src,
        dst_ref=dst,
        send_sem=send_sem,
        recv_sem=recv_sem,
        device_id=device,
        device_id_type=MESH_ID,
    )


def greet(peers):
    barrier = pltpu.get_barrier_semaphore()
    for peer in peers:
        pl.semaphore_signal(barrier, inc=1, device_id=peer, device_id_type=MESH_ID)
    pl.semaphore_wait(barrier, len(peers))


def forward_kernel(
    grid,
    sizes,
    chunk_counts,
    shard,
    tok,
    grad_in,
    small,
    ada,
    query_spare,
    key_spare,
    key_scale,
    ones,
    full,
    x_out,
    grad_out,
    mixed_out,
    qaug_out,
    kv_out,
    inverse_out,
    att_out,
    branch_out,
    mlp_out,
    slope_out,
    dm_out,
    grad_down_out,
    mlp_own,
    mlp_other,
    mod,
    silu_out,
    x,
    dm,
    mixed,
    other,
    turned,
    qaug,
    kv,
    inverses,
    att,
    w,
    slope,
    act,
    grad_down,
    every,
    mod_send,
    mod_got,
    head_bias,
    up_bias,
    local_sem,
    p_send,
    p_recv,
    t_send,
    t_recv,
    load_sem,
    save_sem,
    a_send,
    a_recv,
):
    nz, ny, nx = grid
    half = nz // 2
    seqs, pad = sizes
    chunks = shard.shape[0]
    ff_chunks = chunk_counts
    dp = nz * ny * nx
    devices = dp * 2
    mod_rows = ada.shape[0] // 128
    z, y, x_at, core = coords(grid)
    width = x.shape[1]
    part_width = att.shape[1]
    pairs = part_width // 128
    blocks = seqs * 2
    length = tok.shape[0]

    def dev(z_to, y_to, x_to):
        return ((z_to * ny + y_to) * nx + x_to, core)

    x_peer = dev(z, y, 1 - x_at)
    y_peer = dev(z, 1 - y, x_at)
    sibling = (place()[0], 1 - core)
    greet_all(devices)

    me = place()[0] * 2 + core
    every[place()[0], core] = small[core]
    mod_send[...] = jnp.zeros_like(mod_send)

    def to_all(round_at, source, target):
        copies = []
        for k in range(1, devices):
            peer = (me + k) % devices
            copy = remote(
                source(peer // 2, peer % 2),
                target.at[place()[0], core],
                a_send.at[round_at, k - 1],
                a_recv.at[round_at, k - 1],
                (peer // 2, peer % 2),
            )
            copy.start()
            copies.append(copy)
        return copies

    small_copies = to_all(0, lambda to, core_to: small.at[core_to], every)

    def own_copy(c):
        return pltpu.make_async_copy(shard.at[c], full.at[c, z, y, x_at], local_sem.at[c])

    low_rows, high_rows = (pl.ds(i * shard.shape[1] // 2, shard.shape[1] // 2) for i in range(2))

    def spread_out(c):
        return c % 3 == 1

    def stage(c, number):
        z_peers = [dev((z + k) % nz, y, x_at) for k in range(1, nz)]
        if not spread_out(c):
            if number == 0:
                moves = [(shard.at[c], full.at[c, z, y, x_at], peer) for peer in z_peers]
            elif number == 1:
                low = full.at[c, pl.ds(0, half), y, x_at]
                high = full.at[c, pl.ds(half, half), y, x_at]
                moves = [(low, low, x_peer), (high, high, y_peer)]
            else:
                low = full.at[c, pl.ds(0, half), y]
                high = full.at[c, pl.ds(half, half), :, x_at]
                moves = [(low, low, y_peer), (high, high, x_peer)]
        elif number == 0:
            moves = [
                (shard.at[c, low_rows], full.at[c, z, y, x_at, low_rows], x_peer),
                (shard.at[c, high_rows], full.at[c, z, y, x_at, high_rows], y_peer),
            ]
        elif number == 1:
            low = full.at[c, z, y, :, low_rows]
            high = full.at[c, z, :, x_at, high_rows]
            moves = [(piece, piece, peer) for peer in z_peers for piece in (low, high)]
        else:
            low = full.at[c, :, y, :, low_rows]
            high = full.at[c, :, :, x_at, high_rows]
            moves = [(low, low, y_peer), (high, high, x_peer)]
        first = (0, 3, 9)[number]
        return [
            remote(src, dst, p_send.at[c, first + i], p_recv.at[c, first + i], peer)
            for i, (src, dst, peer) in enumerate(moves)
        ]

    ahead = 2
    progress = [-ahead]

    def begin_stage(c, number):
        if number == 1:
            own_copy(c).wait()
        for copy in stage(c, number - 1) if number else ():
            copy.wait_recv()
        for copy in stage(c, number):
            copy.start()

    def advance(upto):
        while progress[0] <= upto:
            t = progress[0]
            if 0 <= t + ahead < chunks:
                own_copy(t + ahead).start()
                begin_stage(t + ahead, 0)
            if 0 <= t + 1 < chunks and spread_out(t + 1):
                begin_stage(t + 1, 1)
            if 0 <= t < chunks and not spread_out(t):
                begin_stage(t, 1)
            if 0 <= t - 1 < chunks:
                begin_stage(t - 1, 2)
            progress[0] += 1

    def load(c):
        return pltpu.make_async_copy(full.at[c], w.at[c % 4], load_sem.at[c])

    def begin_load(c):
        for copy in stage(c, 2):
            copy.wait_recv()
        load(c).start()

    def weight(c):
        return w[c % 4].reshape(width, part_width)

    saves = []

    def save(src, dst):
        copy = pltpu.make_async_copy(src, dst, save_sem.at[len(saves)])
        copy.start()
        saves.append(copy)
        return copy

    def block_rows(a):
        return pl.ds(pl.multiple_of(a * pad, 16), pad)

    advance(-2)

    def own_rows(s, which):
        return block_rows(s * 2 + which)

    def conditions():
        for copy in small_copies:
            copy.wait()
        groups = ada.shape[1] // 128
        cond = every[:, 0].astype(F32)
        for s in range(seqs):
            total = None
            for g in range(groups):
                c = cond[:, s * groups + g, :]
                silu = (c / (1.0 + jnp.exp(-c))).astype(BF16)
                silu_out[s, :, g * 128 : g * 128 + 128] = silu
                term = dot_nt(silu, ada[:, g * 128 : g * 128 + 128])
                total = term if g == 0 else total + term
            for i in range(mod_rows):
                mod_send[:, i * seqs + s, :] = total[:, i * 128 : i * 128 + 128]
        return to_all(1, lambda to, core_to: mod_send.at[to], mod_got)

    def iota(shape, dim):
        return lax.broadcasted_iota(jnp.int32, shape, dim)

    def spread(rows, cols, at, unit, span):
        share = span // dp
        row, col = iota((128, cols), 0) - at, iota((128, cols), 1)
        here = (row >= 0) & (row < unit) & (col // span == row // share) & (col % share == row % share)
        placed = dot(rows, jnp.where(here, 1.0, 0.0).astype(BF16)).reshape(dp, -1, cols)
        mine = (iota((dp, 1, cols), 2) % span) // share == iota((dp, 1, cols), 0)
        return jnp.sum(jnp.where(mine, placed, 0.0), axis=0)

    def modulation():
        for copy in mod_copies:
            copy.wait()
        mod_got[place()[0], core] = mod_send[place()[0]]
        first_row = 8
        count = every.shape[2]
        for t in range(2):
            rows = every[:, t].reshape(dp * count, 128)
            at = t * part_width
            quarters = [spread(rows, part_width, q * 32, 32, 64) for q in range(4)]
            for j in range(8):
                vector = j if j < 6 else j + 2
                piece = quarters[vector % 4][first_row + vector // 4 : first_row + vector // 4 + 1]
                for s in range(seqs):
                    mod[s, j : j + 1, at : at + part_width] = piece
        rows = every[:, pl.ds(core, 1)].reshape(dp * count, 128)
        for j in (6, 7):
            piece = spread(rows, part_width, j % 4 * 32, 32, 64)
            head_bias[j : j + 1, :] = piece[first_row + j // 4 : first_row + j // 4 + 1]
        rows = spread(rows, part_width * ff_chunks, 0, 128, 256)
        for c in range(ff_chunks):
            up_bias[c] = rows[first_row + 3 : first_row + 4, c * part_width : (c + 1) * part_width]
        sums = [mod_got[d, 0] + mod_got[d, 1] for d in range(dp)]
        for j in range(6):
            at = j // 2 * seqs
            lanes = j % 2 * 64
            row = jnp.concatenate([total[at : at + seqs, lanes : lanes + 64] for total in sums], axis=1)
            for s in range(seqs):
                mod[s, j : j + 1, :] += row[s : s + 1]

    swaps = []
    for i, (src, dst) in enumerate(((tok, x), (grad_in, dm))):
        for s in range(seqs):
            values = src[:, s, :].astype(F32).astype(BF16)
            start = pl.multiple_of((s * 2 + core) * pad, 16)
            dst[pl.ds(start + length // 16 * 16, pad - length // 16 * 16), :] = jnp.zeros(
                (pad - length // 16 * 16, width), BF16
            )
            dst[pl.ds(start, length), :] = values
            piece = dst.at[own_rows(s, core), :]
            copy = remote(piece, piece, t_send.at[i * seqs + s], t_recv.at[i * seqs + s], sibling)
            copy.start()
            swaps.append(copy)
    advance(-1)
    mod_copies = conditions()
    for copy in swaps[:seqs]:
        copy.wait()
    x_saved = save(x, x_out)
    advance(0)
    for copy in swaps[seqs:]:
        copy.wait()
    grad_saved = save(dm, grad_out)
    advance(1)
    modulation()

    def mix_attn(a, rows):
        s = a // 2
        normed, unused = normalize(x[rows, :].astype(F32))
        mixed[rows, :] = (normed * (1.0 + mod[s, 2:3, :]) + mod[s, 4:5, :]).astype(BF16)

    for_blocks(blocks, pad, mix_attn)
    mixed_saved = save(mixed, mixed_out)
    grad_saved.wait()

    def scale_grad(a, rows):
        dm[rows, :] = (dm[rows, :].astype(F32) * mod[a // 2, 1:2, :]).astype(BF16)

    for_blocks(blocks, pad, scale_grad)
    save(dm, dm_out)
    transpose_into(turned, dm)
    advance(2)
    begin_load(0)
    load(0).wait()

    def project_q(a, rows):
        first, unused = lane_code(pad)
        q_spare = query_spare[rows, :].astype(F32)
        values = dot(mixed[rows, :], weight(0)) + head_bias[6:7, :]
        inv = lax.rsqrt(dot((values * values).astype(BF16), ones[...]) + HEAD_EPS)
        inverses[rows, 0:part_width] = inv.astype(BF16)
        values = values * inv * key_scale[...]
        for p in range(pairs):
            piece = values[:, p * 128 : p * 128 + 128]
            qaug[2 * p, rows, :] = jnp.where(first, piece, q_spare).astype(BF16)
            qaug[2 * p + 1, rows, :] = jnp.where(first, q_spare, piece).astype(BF16)

    for_blocks(blocks, pad, project_q)
    advance(3)
    begin_load(1)
    load(1).wait()

    def project_k(a, rows):
        values = dot(mixed[rows, :], weight(1))
        inv = lax.rsqrt(dot((values * values).astype(BF16), ones[...]) + HEAD_EPS)
        inverses[rows, part_width : 2 * part_width] = inv.astype(BF16)
        kv[rows, 0:part_width] = (values * inv).astype(BF16)

    for_blocks(blocks, pad, project_k)
    inverse_saved = save(inverses, inverse_out)
    advance(4)
    begin_load(2)
    load(2).wait()

    def project_v(a, rows):
        kv[rows, part_width : 2 * part_width] = (
            dot(mixed[rows, :], weight(2)) + head_bias[7:8, :]
        ).astype(BF16)

    for_blocks(blocks, pad, project_v)
    save(kv, kv_out)

    def attend(i, carry):
        p = i // blocks
        block = i % blocks
        rows = block_rows(block)
        all_rows = pl.ds(pl.multiple_of((block // 2) * 2 * pad, 16), 2 * pad)
        at = pl.multiple_of(p * 128, 128)
        first, code = lane_code(pad)
        k_sides = both_heads(kv[all_rows, pl.ds(at, 128)], key_spare[all_rows, :])
        v_sides = both_heads(kv[all_rows, pl.ds(at + part_width, 128)], 1.0)
        outs = []
        for side in range(2):
            h = 2 * p + side
            q = qaug[h, rows, :]
            prob = jnp.exp2(dot_nt(q, k_sides[side])).astype(BF16)
            o = dot(prob, v_sides[side])
            outs.append(o / pltpu.roll(o, 64, 1))
            norm = -jnp.log2(o)
            high = norm.astype(BF16)
            rest = norm - high.astype(F32)
            middle = rest.astype(BF16)
            low = (rest - middle.astype(F32)).astype(BF16)
            spare = jnp.logical_not(first) if side == 0 else first
            q = q.astype(F32)
            for where, piece in enumerate((high, middle, low)):
                q = jnp.where(spare & (code == SCALES + where), piece.astype(F32), q)
            qaug[h, rows, :] = q.astype(BF16)
        att[rows, pl.ds(at, 128)] = jnp.where(first, outs[0], outs[1]).astype(BF16)
        return carry

    count = pairs * blocks
    for quarter in range(4):
        lax.fori_loop(quarter * count // 4, (quarter + 1) * count // 4, attend, 0)
        if quarter == 0:
            advance(5)
        if quarter == 2:
            advance(6)
    begin_load(3)
    save(qaug, qaug_out)
    save(att, att_out)
    load(3).wait()
    inverse_saved.wait()
    part = inverses
    part_copies = []
    for a in range(blocks):
        rows = block_rows(a)
        part[rows, :] = dot_nt(att[rows, :], weight(3)).astype(BF16)
        copy = remote(
            part.at[rows, :], other.at[rows, :], t_send.at[2 * seqs + a], t_recv.at[2 * seqs + a], sibling
        )
        copy.start()
        part_copies.append(copy)
    mixed_saved.wait()
    mlp = mixed
    begin_load(4)
    for a in range(blocks):
        rows = block_rows(a)
        s = a // 2
        part_copies[a].wait()
        b = part[rows, :].astype(F32) + other[rows, :].astype(F32) + mod[s, 6:7, :]
        other[rows, :] = b.astype(BF16)
        normed, unused = normalize(x[rows, :].astype(F32) + mod[s, 0:1, :] * b)
        mlp[rows, :] = (normed * (1.0 + mod[s, 3:4, :]) + mod[s, 5:6, :]).astype(BF16)
    branch_saved = save(other, branch_out)
    save(mlp, mlp_out)
    down_saved = []

    def raise_chunk(c):
        load(4 + c).wait()

        def raise_rows(a, rows):
            h = dot(mlp[rows, :], weight(4 + c)) + up_bias[c]
            square = h * h
            t = jnp.tanh(h * (GELU_COEF + GELU_COEF * GELU_CUBE * square))
            act[c, rows, :] = (0.5 * h * (1.0 + t)).astype(BF16)
            slope[c, rows, :] = (
                0.5 * (1.0 + t)
                + h * (1.0 - t * t) * (0.5 * GELU_COEF + 1.5 * GELU_COEF * GELU_CUBE * square)
            ).astype(BF16)

        for_blocks(blocks, pad, raise_rows)
        save(slope.at[c], slope_out.at[c])

    def down_chunk(c):
        if c >= 2:
            down_saved[c - 2].wait()
        weight_grad(grad_down.at[c % 2], turned, act.at[c])
        down_saved.append(save(grad_down.at[c % 2], grad_down_out.at[c]))

    advance(7)
    begin_load(5)
    raise_chunk(0)
    raise_chunk(1)
    advance(8)
    begin_load(6)
    down_chunk(0)
    raise_chunk(2)
    down_chunk(1)
    advance(9)
    begin_load(7)
    raise_chunk(3)
    advance(10)
    begin_load(8)
    down_chunk(2)
    down_chunk(3)
    advance(11)
    begin_load(9)
    advance(12)
    begin_load(10)
    for copy in (x_saved, branch_saved, load(8), load(9), load(10)):
        copy.wait()

    def lower_most(a, rows):
        total = dot_nt(act[0, rows, :], weight(8))
        for c in range(1, ff_chunks - 1):
            total = total + dot_nt(act[c, rows, :], weight(8 + c))
        high = total.astype(BF16)
        x[rows, :] = high
        other[rows, :] = (total - high.astype(F32)).astype(BF16)

    for_blocks(blocks, pad, lower_most)
    begin_load(11)
    load(11).wait()
    end_copies = []
    for step in range(blocks):
        s = step % seqs
        which = 1 - core if step < seqs else core
        rows = own_rows(s, which)
        total = dot_nt(act[ff_chunks - 1, rows, :], weight(7 + ff_chunks))
        total = total + x[rows, :].astype(F32) + other[rows, :].astype(F32)
        part[rows, :] = total.astype(BF16)
        if step < seqs:
            copy = remote(
                part.at[rows, :],
                mlp_other.at[s],
                t_send.at[2 * seqs + blocks + s],
                t_recv.at[2 * seqs + blocks + s],
                sibling,
            )
            copy.start()
            end_copies.append(copy)
        else:
            save(part.at[rows, :], mlp_own.at[s])
    for copy in end_copies:
        copy.wait()
    done = [mixed_saved, grad_saved, inverse_saved, x_saved, branch_saved] + down_saved[:-2]
    for copy in saves:
        if all(copy is not other_copy for other_copy in done):
            copy.wait()
    for c in range(chunks):
        for number in range(3):
            for copy in stage(c, number):
                copy.wait_send()


def forward_pass(grid, sizes, shard, tok, grad_in, small, ada, query_spare, key_spare, key_scale, ones, collective_id):
    nz, ny, nx = grid
    seqs, pad = sizes
    chunks, own_rows, part = shard.shape
    ff_chunks = (chunks - 4) // 2
    dp = nz * ny * nx
    width = tok.shape[2]
    total = seqs * 2 * pad
    heads = part // 64
    wide = ((total, width), BF16)
    narrow = ((total, part), BF16)
    chunk = (nz, ny, nx, own_rows, part)
    outs = [
        ((chunks,) + chunk, BF16),
        wide,
        wide,
        wide,
        ((heads, total, 128), BF16),
        wide,
        wide,
        narrow,
        wide,
        wide,
        ((ff_chunks, total, part), BF16),
        wide,
        ((ff_chunks,) + chunk, BF16),
        ((seqs, pad, width), BF16),
        ((seqs, pad, width), BF16),
        ((seqs, 8, width), F32),
        ((seqs, dp, part), BF16),
    ]
    scratch = [
        wide,
        wide,
        wide,
        wide,
        ((width, total), BF16),
        ((heads, total, 128), BF16),
        wide,
        wide,
        narrow,
        ((4,) + chunk, BF16),
        ((ff_chunks, total, part), BF16),
        ((ff_chunks, total, part), BF16),
        ((2,) + chunk, BF16),
        ((dp, 2) + small.shape[1:], BF16),
        ((dp, 8, 128), F32),
        ((dp, 2, 8, 128), F32),
        ((8, part), F32),
        ((ff_chunks, 1, part), F32),
    ]
    swaps = 3 * seqs + seqs * 2
    vmem = pl.BlockSpec(memory_space=pltpu.VMEM)
    hbm = pl.BlockSpec(memory_space=ANY)
    return pl.pallas_call(
        functools.partial(forward_kernel, grid, sizes, ff_chunks),
        out_shape=[jax.ShapeDtypeStruct(shape, dtype) for shape, dtype in outs],
        in_specs=[hbm] + [vmem] * 8,
        out_specs=[hbm] * (len(outs) - 2) + [vmem] * 2,
        scratch_shapes=[pltpu.VMEM(shape, dtype) for shape, dtype in scratch]
        + [
            pltpu.SemaphoreType.DMA((chunks,)),
            pltpu.SemaphoreType.DMA((chunks, 14)),
            pltpu.SemaphoreType.DMA((chunks, 14)),
            pltpu.SemaphoreType.DMA((swaps,)),
            pltpu.SemaphoreType.DMA((swaps,)),
            pltpu.SemaphoreType.DMA((chunks,)),
            pltpu.SemaphoreType.DMA((24,)),
            pltpu.SemaphoreType.DMA((2, 2 * dp - 1)),
            pltpu.SemaphoreType.DMA((2, 2 * dp - 1)),
        ],
        compiler_params=pltpu.CompilerParams(
            collective_id=collective_id, has_side_effects=True, vmem_limit_bytes=60 * 2**20
        ),
        name="forward_pass",
    )(shard, tok, grad_in, small, ada, query_spare, key_spare, key_scale, ones)


def dot(a, b):
    return jnp.dot(a, b, preferred_element_type=F32)


def dot_nt(a, b):
    return lax.dot_general(a, b, (((1,), (1,)), ((), ())), preferred_element_type=F32)


def dot_tn(a, b):
    return lax.dot_general(a, b, (((0,), (0,)), ((), ())), preferred_element_type=F32)


def lane_code(rows):
    lane = lax.broadcasted_iota(jnp.int32, (rows, 128), 1)
    return lane < 64, lane & 63


def both_heads(pair, spare):
    first, unused = lane_code(pair.shape[0])
    pair = pair.astype(F32)
    if not isinstance(spare, float):
        spare = spare.astype(F32)
    return (
        jnp.where(first, pair, spare).astype(BF16),
        jnp.where(first, spare, pair).astype(BF16),
    )


def column_sum(values):
    return jnp.sum(values, axis=0, keepdims=True)


def transpose_into(dst, src):
    def step(i, carry):
        at = pl.multiple_of(i * 128, 128)
        dst[:, pl.ds(at, 128)] = src[pl.ds(at, 128), :].T
        return carry

    lax.fori_loop(0, src.shape[0] // 128, step, 0)


def weight_grad(dst, turned, right):
    rows = turned.shape[0] // dst.shape[0]

    def step(i, carry):
        at = pl.ds(pl.multiple_of(i * rows, rows), rows)
        dst[i] = dot(turned[at, :], right[...]).astype(BF16).reshape(dst.shape[1:])
        return carry

    lax.fori_loop(0, dst.shape[0], step, 0)


def for_blocks(count, rows, body):
    def step(a, carry):
        body(a, pl.ds(pl.multiple_of(a * rows, 16), rows))
        return carry

    lax.fori_loop(0, count, step, 0)

def backward_kernel(
    grid,
    sizes,
    full,
    x_in,
    grad_in,
    mixed_in,
    qaug_in,
    kv_in,
    inverse_in,
    att_in,
    branch_in,
    mlp_in,
    slope_in,
    dm_in,
    grad_down_in,
    mod,
    key_spare,
    key_scale,
    ones,
    out,
    mid_own,
    ga_own,
    ga_other,
    stats,
    up_sum,
    qkv_sum,
    b0,
    b1,
    b2,
    b3,
    b4,
    turned,
    pool,
    qaug,
    w,
    work,
    got_low,
    got_high,
    next_low,
    next_high,
    got_z,
    p_send,
    p_recv,
    z_send,
    z_recv,
    t_send,
    t_recv,
    load_sem,
):
    nz, ny, nx = grid
    half = nz // 2
    seqs, pad = sizes
    chunks = out.shape[0]
    slots = work.shape[0]
    ff_chunks = slope_in.shape[0]
    z, y, x_at, core = coords(grid)
    width = b0.shape[1]
    part_width = pool.shape[2]
    pairs = part_width // 128
    blocks = seqs * 2
    ln2 = 0.6931471805599453

    def dev(z_to, y_to, x_to):
        return ((z_to * ny + y_to) * nx + x_to, core)

    x_peer = dev(z, y, 1 - x_at)
    y_peer = dev(z, 1 - y, x_at)
    sibling = (place()[0], 1 - core)
    greet([x_peer, y_peer, sibling] + [dev((z + k) % nz, y, x_at) for k in range(1, nz)])

    def block_rows(a):
        return pl.ds(pl.multiple_of(a * pad, 16), pad)

    loads = []

    def load(src, dst):
        copy = pltpu.make_async_copy(src, dst, load_sem.at[len(loads)])
        copy.start()
        loads.append(copy)
        return copy

    def first_copies(c):
        s = c % slots
        return [
            remote(
                work.at[s, pl.ds(0, half), 1 - y], got_low.at[c], p_send.at[c, 0], p_recv.at[c, 0], y_peer
            ),
            remote(
                work.at[s, pl.ds(half, half), :, 1 - x_at],
                got_high.at[c],
                p_send.at[c, 1],
                p_recv.at[c, 1],
                x_peer,
            ),
        ]

    def second_copies(c):
        s = c % slots
        return [
            remote(
                work.at[s, pl.ds(0, half), y, 1 - x_at],
                next_low.at[c],
                p_send.at[c, 2],
                p_recv.at[c, 2],
                x_peer,
            ),
            remote(
                work.at[s, pl.ds(half, half), 1 - y, x_at],
                next_high.at[c],
                p_send.at[c, 3],
                p_recv.at[c, 3],
                y_peer,
            ),
        ]

    def z_copies(c):
        s = c % slots
        return [
            remote(
                work.at[s, (z + k) % nz, y, x_at],
                got_z.at[c, k - 1],
                z_send.at[c, k - 1],
                z_recv.at[c, k - 1],
                dev((z + k) % nz, y, x_at),
            )
            for k in range(1, nz)
        ]

    def add(a, b):
        return (a.astype(F32) + b.astype(F32)).astype(BF16)

    def begin(c):
        for copy in first_copies(c):
            copy.start()

    def second(c):
        s = c % slots
        for copy in first_copies(c):
            copy.wait_recv()
        work[s, 0:half, y] = add(work[s, 0:half, y], got_low[c])
        work[s, half:nz, :, x_at] = add(work[s, half:nz, :, x_at], got_high[c])
        for copy in second_copies(c):
            copy.start()

    def third(c):
        s = c % slots
        for copy in second_copies(c):
            copy.wait_recv()
        work[s, 0:half, y, x_at] = add(work[s, 0:half, y, x_at], next_low[c])
        work[s, half:nz, y, x_at] = add(work[s, half:nz, y, x_at], next_high[c])
        for copy in z_copies(c):
            copy.start()

    def last(c):
        s = c % slots
        for copy in z_copies(c):
            copy.wait_recv()
        total = work[s, z, y, x_at].astype(F32)
        for k in range(nz - 1):
            total = total + got_z[c, k].astype(F32)
        out[c] = total

    def sent(c):
        for copy in first_copies(c) + second_copies(c) + z_copies(c):
            copy.wait_send()

    def put(c, right):
        if c >= slots:
            sent(c - slots)
        weight_grad(work.at[c % slots], turned, right)

    def step(t, start=True):
        if start and t < chunks:
            begin(t)
        if 0 <= t - 2 < chunks:
            second(t - 2)
        if 0 <= t - 3 < chunks:
            third(t - 3)
        if 0 <= t - 4 < chunks:
            last(t - 4)

    def weight(slot):
        return w[slot].reshape(width, part_width)

    down_grads = [load(grad_down_in.at[c], work.at[c]) for c in range(ff_chunks)]
    mlp_load = load(mlp_in, b1)
    dm_load = load(dm_in, b0)
    down_loads = [
        (load(full.at[chunks - ff_chunks + c], w.at[c]), load(slope_in.at[c], pool.at[c]))
        for c in range(ff_chunks)
    ]
    branch_load = load(branch_in, b4)
    qaug_load = load(qaug_in, qaug)
    for c in range(2):
        down_grads[c].wait()
        step(c)
    for c in range(2, ff_chunks):
        down_grads[c].wait()
    mlp_load.wait()
    transpose_into(turned, b1)
    grad_load = load(grad_in, b1)
    dm_load.wait()
    up_sum[...] = jnp.zeros_like(up_sum)
    up_loads = []
    for c in range(ff_chunks):
        for copy in down_loads[c]:
            copy.wait()

        def back(a, rows):
            gh = dot(b0[rows, :], weight(c)) * pool[c, rows, :].astype(F32)
            up_sum[c] += column_sum(gh)
            pool[c, rows, :] = gh.astype(BF16)

        for_blocks(blocks, pad, back)
        up_loads.append(load(full.at[4 + c], w.at[c]))
        put(ff_chunks + c, pool.at[c])
        if c != 1:
            step(2 + (c + 1) // 2)
    x_load = load(x_in, b0)
    for copy in up_loads:
        copy.wait()
    swaps = []
    for a in range(blocks):
        rows = block_rows(a)
        total = dot_nt(pool[0, rows, :], weight(0))
        for c in range(1, ff_chunks):
            total = total + dot_nt(pool[c, rows, :], weight(c))
        b2[rows, :] = total.astype(BF16)
        copy = remote(b2.at[rows, :], b3.at[rows, :], t_send.at[a], t_recv.at[a], sibling)
        copy.start()
        swaps.append(copy)
    proj_load = load(full.at[3], w.at[3])
    qkv_loads = [load(full.at[j], w.at[j]) for j in range(3)]
    step(5)
    for copy in (x_load, grad_load, branch_load, proj_load):
        copy.wait()
    stats[...] = jnp.zeros_like(stats)
    grad_att = pool.at[3]
    for a in range(blocks):
        rows = block_rows(a)
        s = a // 2
        swaps[a].wait()
        b = b4[rows, :].astype(F32)
        gm = b2[rows, :].astype(F32) + b3[rows, :].astype(F32)
        normed, inverse = normalize(b0[rows, :].astype(F32) + mod[s, 0:1, :] * b)
        stats[s, 1:2, :] += 0.5 * column_sum(gm * normed)
        stats[s, 2:3, :] += 0.5 * column_sum(gm)
        mid = b1[rows, :].astype(F32) + norm_back(gm * (1.0 + mod[s, 3:4, :]), normed, inverse)
        b1[rows, :] = mid.astype(BF16)
        stats[s, 0:1, :] += 0.5 * column_sum(mid * b)
        branch_grad = mid * mod[s, 0:1, :]
        stats[s, 3:4, :] += 0.5 * column_sum(branch_grad)
        low = branch_grad.astype(BF16)
        b4[rows, :] = low
        grad_att[rows, :] = dot(low, weight(3)).astype(BF16)
        if a == 1:
            step(6)
    mid_saves = [load(b1.at[block_rows(s * 2 + core), :], mid_own.at[s]) for s in range(seqs)]
    att = b2.at[:, pl.ds(0, part_width)]
    att_load = load(att_in, att)
    kv_load = load(kv_in, b3)
    transpose_into(turned, b4)
    step(7)
    mixed_load = load(mixed_in, b4)
    att_load.wait()
    put(8, att)
    inverse_load = load(inverse_in, b2)
    kv_load.wait()
    qaug_load.wait()
    qkv_sum[...] = jnp.zeros_like(qkv_sum)

    def group(p, j):
        at = p * 3 + j
        lane = at % 4 * 128
        return at // 4, pl.ds(lane if isinstance(lane, int) else pl.multiple_of(lane, 128), 128)

    def put_group(p, j, rows, values):
        chunk, lanes = group(p, j)
        pool[chunk, rows, lanes] = values.astype(BF16)

    def attend(i, carry):
        p = i // seqs
        s = i % seqs
        start = pl.multiple_of(s * 2 * pad, 16)
        all_rows = pl.ds(start, 2 * pad)
        at = pl.multiple_of(p * 128, 128)
        lanes = pl.ds(at, 128)
        first, unused = lane_code(pad)
        first_all, unused = lane_code(2 * pad)
        k_sides = both_heads(b3[all_rows, lanes], key_spare[all_rows, :])
        v_sides = both_heads(b3[all_rows, pl.ds(at + part_width, 128)], 0.0)
        g_sides = both_heads(pool[3, all_rows, lanes], 0.0)
        grads_k, grads_v, grads_q = [], [], [[], []]
        for side in range(2):
            h = 2 * p + side
            k = k_sides[side]
            v = v_sides[side]
            sum_k = sum_v = None
            for t in range(2):
                rows = pl.ds(pl.multiple_of(start + t * pad, 16), pad)
                q = qaug[h, rows, :]
                g = g_sides[side][t * pad : t * pad + pad]
                prob = jnp.exp2(dot_nt(k, q))
                grad_prob = dot_nt(v, g)
                ds = (prob * (grad_prob - column_sum(prob * grad_prob))).astype(BF16)
                gv = dot(prob.astype(BF16), g)
                gk = dot(ds, q)
                sum_v = gv if t == 0 else sum_v + gv
                sum_k = gk if t == 0 else sum_k + gk
                grads_q[t].append(dot_tn(ds, k))
            grads_k.append(sum_k)
            grads_v.append(sum_v)
        for t in range(2):
            rows = pl.ds(pl.multiple_of(start + t * pad, 16), pad)
            gq = jnp.where(first, grads_q[t][0], grads_q[t][1])
            q = jnp.where(first, qaug[2 * p, rows, :].astype(F32), qaug[2 * p + 1, rows, :].astype(F32))
            qkv_sum[2:3, lanes] += ln2 * column_sum(gq * q)
            put_group(p, 0, rows, gq)
        put_group(p, 1, all_rows, ln2 * jnp.where(first_all, grads_k[0], grads_k[1]))
        gv = jnp.where(first_all, grads_v[0], grads_v[1])
        qkv_sum[1:2, lanes] += column_sum(gv)
        put_group(p, 2, all_rows, gv)
        return carry

    mixed_load.wait()
    transpose_into(turned, b4)
    inverse_load.wait()
    for p in range(pairs):
        lax.fori_loop(p * seqs, (p + 1) * seqs, attend, 0)
        lanes = pl.ds(p * 128, 128)

        def finish_pair(a, rows):
            first, unused = lane_code(pad)
            table = ones[0:128, 0:128]
            scale = key_scale[:, lanes]
            unit = jnp.where(first, qaug[2 * p, rows, :].astype(F32), qaug[2 * p + 1, rows, :].astype(F32))
            unit = unit / scale
            chunk, at = group(p, 0)
            f = pool[chunk, rows, at].astype(F32) * (scale * ln2)
            gq = b2[rows, lanes].astype(F32) * (f - unit * dot((f * unit).astype(BF16), table))
            qkv_sum[0:1, lanes] += column_sum(gq)
            put_group(p, 0, rows, gq)
            unit = b3[rows, lanes].astype(F32)
            chunk, at = group(p, 1)
            f = pool[chunk, rows, at].astype(F32)
            inverse = b2[rows, pl.ds(part_width + p * 128, 128)].astype(F32)
            put_group(p, 1, rows, inverse * (f - unit * dot((f * unit).astype(BF16), table)))

        for_blocks(blocks, pad, finish_pair)
        if p > 0:
            put(8 + p, pool.at[p - 1])
        step(8 + p)
    for copy in qkv_loads:
        copy.wait()
    end_copies = []
    end_saves = []
    for i in range(blocks):
        s = i % seqs
        which = 1 - core if i < seqs else core
        rows = block_rows(s * 2 + which)
        total = None
        for j in range(3):
            places = [group(p, j) for p in range(pairs)]
            low = jnp.concatenate([pool[chunk, rows, at] for chunk, at in places], axis=1)
            term = dot_nt(low, weight(j))
            total = term if j == 0 else total + term
        b0[rows, :] = total.astype(BF16)
        if i < seqs:
            copy = remote(b0.at[rows, :], ga_other.at[s], t_send.at[blocks + s], t_recv.at[blocks + s], sibling)
            copy.start()
            end_copies.append(copy)
        else:
            end_saves.append(load(b0.at[rows, :], ga_own.at[s]))
        if i == 1:
            step(12)
    step(13)
    step(14)
    step(15)
    for copy in end_copies + end_saves + mid_saves:
        copy.wait()
    for c in range(chunks - slots, chunks):
        sent(c)


def backward_pass(grid, sizes, operands, mod, key_spare, key_scale, ones, collective_id):
    nz, ny, nx = grid
    half = nz // 2
    seqs, pad = sizes
    full, slope = operands[0], operands[10]
    chunks = full.shape[0]
    own_rows, part = full.shape[4:]
    ff_chunks = slope.shape[0]
    total = seqs * 2 * pad
    width = nz * ny * nx * own_rows
    heads = part // 64
    wide = ((total, width), BF16)
    chunk = (nz, ny, nx, own_rows, part)
    block = (own_rows, part)
    slots = 8
    outs = [
        ((chunks,) + block, F32),
        ((seqs, pad, width), BF16),
        ((seqs, pad, width), BF16),
        ((seqs, pad, width), BF16),
        ((seqs, 4, width), F32),
        ((ff_chunks, 1, part), F32),
        ((8, part), F32),
    ]
    scratch = [wide] * 5 + [
        ((width, total), BF16),
        ((ff_chunks, total, part), BF16),
        ((heads, total, 128), BF16),
        ((4,) + chunk, BF16),
        ((slots,) + chunk, BF16),
        ((chunks, half, nx) + block, BF16),
        ((chunks, half, ny) + block, BF16),
        ((chunks, half) + block, BF16),
        ((chunks, half) + block, BF16),
        ((chunks, nz - 1) + block, BF16),
    ]
    vmem = pl.BlockSpec(memory_space=pltpu.VMEM)
    hbm = pl.BlockSpec(memory_space=ANY)
    swaps = seqs * 2 + seqs
    return pl.pallas_call(
        functools.partial(backward_kernel, grid, sizes),
        out_shape=[jax.ShapeDtypeStruct(shape, dtype) for shape, dtype in outs],
        in_specs=[hbm] * 13 + [vmem] * 4,
        out_specs=[vmem] + [hbm] * 3 + [vmem] * 3,
        scratch_shapes=[pltpu.VMEM(shape, dtype) for shape, dtype in scratch]
        + [
            pltpu.SemaphoreType.DMA((chunks, 4)),
            pltpu.SemaphoreType.DMA((chunks, 4)),
            pltpu.SemaphoreType.DMA((chunks, nz - 1)),
            pltpu.SemaphoreType.DMA((chunks, nz - 1)),
            pltpu.SemaphoreType.DMA((swaps,)),
            pltpu.SemaphoreType.DMA((swaps,)),
            pltpu.SemaphoreType.DMA((40,)),
        ],
        compiler_params=pltpu.CompilerParams(
            collective_id=collective_id, has_side_effects=True, vmem_limit_bytes=60 * 2**20
        ),
        name="backward_pass",
    )(*operands, mod, key_spare, key_scale, ones)


def finish_kernel(
    grid,
    sizes,
    x_in,
    grad_in,
    branch_in,
    mlp_own,
    mlp_other,
    mid_own,
    ga_own,
    ga_other,
    mod,
    mid_stats,
    up_sum,
    qkv_sum,
    ada,
    output,
    grad_tokens,
    got,
    mod_low,
    back_got,
    rows_in,
    stats,
    message,
    back_message,
    load_sem,
    a_send,
    a_recv,
    c_send,
    c_recv,
):
    nz, ny, nx = grid
    dp = nz * ny * nx
    devices = dp * 2
    seqs, pad = sizes
    chip, core = place()
    me = chip * 2 + core
    length = output.shape[0]
    part_width = qkv_sum.shape[1]
    barrier = pltpu.get_barrier_semaphore()
    for k in range(1, devices):
        peer = (me + k) % devices
        pl.semaphore_signal(barrier, inc=1, device_id=(peer // 2, peer % 2), device_id_type=MESH_ID)

    loads = []
    for s in range(seqs):
        own = pl.ds(pl.multiple_of((s * 2 + core) * pad, 16), pad)
        pieces = [ref.at[own, :] for ref in (x_in, grad_in, branch_in)]
        pieces += [ref.at[s] for ref in (mlp_own, mlp_other, mid_own, ga_own, ga_other)]
        for i, piece in enumerate(pieces):
            copy = pltpu.make_async_copy(piece, rows_in.at[s, i], load_sem.at[s, i])
            copy.start()
            loads.append(copy)
    message[...] = jnp.zeros_like(message)
    back_message[...] = jnp.zeros_like(back_message)
    for s in range(seqs):
        for copy in loads[s * 8 : s * 8 + 8]:
            copy.wait()
        xs, g, unused, own_b, other_b, mid, own_g, other_g = (rows_in[s, i].astype(F32) for i in range(8))
        b = own_b + other_b + mod[s, 7:8, :]
        normed, inverse = normalize(xs)
        gm = own_g + other_g
        gt = mid + norm_back(gm * (1.0 + mod[s, 2:3, :]), normed, inverse)
        grad_tokens[:, s, :] = gt[0:length]
        stats[s, 0:1, :] = mid_stats[s, 0:1, :]
        stats[s, 1:2, :] = column_sum(g * b)
        stats[s, 2:3, :] = column_sum(gm * normed)
        stats[s, 3:4, :] = mid_stats[s, 1:2, :]
        stats[s, 4:5, :] = column_sum(gm)
        stats[s, 5:6, :] = mid_stats[s, 2:3, :]
        stats[s, 6:7, :] = mid_stats[s, 3:4, :]
        stats[s, 7:8, :] = column_sum(g) * mod[s, 1:2, :]

    def iota(shape, dim):
        return lax.broadcasted_iota(jnp.int32, shape, dim)

    def shares(values, span):
        count, lanes = values.shape
        share = span // dp
        mine = (iota((dp, 1, lanes), 2) % span) // share == iota((dp, 1, lanes), 0)
        lane = iota((lanes, 128), 0)
        table = jnp.where(lane // span * share + lane % share == iota((lanes, 128), 1) - 64, 1.0, 0.0)
        split = jnp.where(mine, values, 0.0).reshape(dp * count, lanes).astype(BF16)
        return dot(split, table.astype(BF16)).reshape(dp, count, 128)

    ends = [stats[0, r : r + 1, :] + stats[1, r : r + 1, :] for r in (6, 7)]
    lane = iota((part_width, 128), 0)
    heads_table = jnp.where(lane // 64 == iota((part_width, 128), 1) - 64, 1.0, 0.0).astype(BF16)
    terms = qkv_sum[2:3, :]
    terms_high = terms.astype(BF16)
    terms_low = (terms - terms_high.astype(F32)).astype(BF16)
    both = jnp.concatenate([terms_high.astype(F32), terms_low.astype(F32)], axis=0)
    both = jnp.concatenate([both, jnp.zeros((6, part_width), F32)], axis=0).astype(BF16)
    head_terms = dot(both, heads_table)
    head_sums = head_terms[0:1] + head_terms[1:2]
    head_high = head_sums.astype(BF16).astype(F32)
    vectors = [qkv_sum[0:1, :], qkv_sum[1:2, :]]
    vectors += [end[:, t * part_width : (t + 1) * part_width] for end in ends for t in range(2)]
    vectors += [jnp.zeros((2, part_width), F32)]
    small = shares(jnp.concatenate(vectors, axis=0), 64)
    ups = jnp.concatenate([up_sum[c] for c in range(up_sum.shape[0])] + [jnp.zeros((4, part_width), F32)], axis=0)
    ups = shares(ups, 256)
    six = jnp.concatenate([stats[s, 0:6, :] for s in range(seqs)] + [jnp.zeros((4, stats.shape[2]), F32)], axis=0)
    for d in range(dp):
        at = d // 2 * 128
        cols = six[:, at : at + 128]
        cols = cols if d % 2 == 0 else pltpu.roll(cols, 64, 1)
        right = jnp.concatenate([small[d, 0:6], head_high, head_sums - head_high, ups[d, 0:8]], axis=0)
        message[d] = jnp.where(iota((16, 128), 1) < 64, cols, right).astype(BF16)
    pl.semaphore_wait(barrier, devices - 1)
    copies = []
    for k in range(1, devices):
        peer = (me + k) % devices
        copy = remote(
            message.at[peer // 2], got.at[chip, core], a_send.at[k - 1], a_recv.at[k - 1], (peer // 2, peer % 2)
        )
        copy.start()
        copies.append(copy)
    got[chip, core] = message[chip]
    for s in range(seqs):
        xs, g, branch, own_b, other_b = (rows_in[s, i].astype(F32) for i in range(5))
        b = own_b + other_b + mod[s, 7:8, :]
        output[:, s, :] = (xs + mod[s, 0:1, :] * branch + mod[s, 1:2, :] * b)[0:length]
    for copy in copies:
        copy.wait()
    sums = got[:, 0].astype(F32) + got[:, 1].astype(F32)
    for s in range(seqs):
        low = jnp.concatenate([sums[:, s * 6 + j, 0:64] for j in range(6)], axis=1).astype(BF16)
        mod_low[s] = low
        back = dot(low, ada[...])
        for g in range(part_width // 128):
            back_message[:, s * 4 + g, :] = back[:, g * 128 : g * 128 + 128]
    bias = jnp.sum(sums, axis=0)
    bias = bias[0:6] + bias[6:12]
    back_message[:, 8:14, :] = jnp.broadcast_to(bias, (dp,) + bias.shape)
    copies = []
    for k in range(1, dp):
        to = (chip + k) % dp
        copy = remote(back_message.at[to], back_got.at[chip], c_send.at[k - 1], c_recv.at[k - 1], (to, core))
        copy.start()
        copies.append(copy)
    back_got[chip] = back_message[chip]
    for copy in copies:
        copy.wait()


def finish(grid, sizes, length, operands, collective_id):
    nz, ny, nx = grid
    dp = nz * ny * nx
    seqs, pad = sizes
    width = operands[0].shape[1]
    ada = operands[-1]
    outs = [
        ((length, seqs, width), F32),
        ((length, seqs, width), F32),
        ((dp, 2, 16, 128), BF16),
        ((seqs, dp, ada.shape[0]), BF16),
        ((dp, 16, 128), F32),
    ]
    scratch = [
        ((seqs, 8, pad, width), BF16),
        ((seqs, 8, width), F32),
        ((dp, 16, 128), BF16),
        ((dp, 16, 128), F32),
    ]
    vmem = pl.BlockSpec(memory_space=pltpu.VMEM)
    hbm = pl.BlockSpec(memory_space=ANY)
    return pl.pallas_call(
        functools.partial(finish_kernel, grid, sizes),
        out_shape=[jax.ShapeDtypeStruct(shape, dtype) for shape, dtype in outs],
        in_specs=[hbm] * 8 + [vmem] * 5,
        out_specs=[vmem] * len(outs),
        scratch_shapes=[pltpu.VMEM(shape, dtype) for shape, dtype in scratch]
        + [
            pltpu.SemaphoreType.DMA((seqs, 8)),
            pltpu.SemaphoreType.DMA((2 * dp - 1,)),
            pltpu.SemaphoreType.DMA((2 * dp - 1,)),
            pltpu.SemaphoreType.DMA((dp - 1,)),
            pltpu.SemaphoreType.DMA((dp - 1,)),
        ],
        compiler_params=pltpu.CompilerParams(
            collective_id=collective_id, has_side_effects=True, vmem_limit_bytes=60 * 2**20
        ),
        name="finish",
    )(*operands)


def fast_device(
    grid,
    tokens,
    condition,
    scale_index,
    ada_weight,
    ada_bias,
    qkv_weight,
    query_bias,
    value_bias,
    head_scale,
    proj_weight,
    proj_bias,
    up_weight,
    up_bias,
    down_weight,
    down_bias,
    out_grad,
):
    nz, ny, nx = grid
    dp = nz * ny * nx
    count = dp * 2
    seqs, own_len, width = tokens.shape
    seq_len = own_len * 2
    part = qkv_weight.shape[2]
    heads = head_scale.shape[0]
    head_dim = part // heads
    own_rows = qkv_weight.shape[1]
    ff_chunks = up_weight.shape[1] // part
    chip, core = place()

    shard = jnp.concatenate(
        [
            qkv_weight,
            proj_weight.T[None],
            up_weight.reshape(own_rows, ff_chunks, part).transpose(1, 0, 2),
            down_weight.T.reshape(own_rows, ff_chunks, part).transpose(1, 0, 2),
        ],
        axis=0,
    )
    pad = -(-own_len // 16) * 16
    total = seqs * 2 * pad
    sizes = (seqs, pad)
    halves = condition.reshape(seqs, 2, -1, 128).transpose(1, 0, 2, 3).reshape(2, -1, 128)
    shares = [values.reshape(-1) for values in (ada_bias, query_bias, value_bias, proj_bias, down_bias)]
    shares = jnp.concatenate(shares)
    shares = jnp.pad(shares, (0, -shares.size % 128)).reshape(-1, 128)
    shares = jnp.concatenate([shares, up_bias.reshape(-1, 128)], axis=0)
    small = jnp.concatenate([halves, jnp.broadcast_to(shares, (2,) + shares.shape)], axis=1)
    small = jnp.pad(small, ((0, 0), (0, -small.shape[1] % 16), (0, 0)))
    cols = ada_weight.shape[2]
    ada = ada_weight.transpose(1, 2, 0).reshape(-1, part)
    own_of = lambda values: lax.dynamic_index_in_dim(values, core, 1, keepdims=False)

    level = jnp.pad(
        scale_index.reshape(seqs, 2, own_len), ((0, 0), (0, 0), (0, pad - own_len)), constant_values=100
    ).reshape(total, 1)
    code = jnp.arange(128)[None] % 64
    query_spare = jnp.where(code == level, 1.0, 0.0).astype(BF16)
    key_spare = jnp.where(
        code < SCALES, jnp.where(level > code, MASK, 0.0), jnp.where(code < SCALES + 3, 1.0, 0.0)
    ).astype(BF16)
    key_scale = jnp.repeat(jnp.exp(head_scale) * 1.4426950408889634, head_dim).reshape(1, part)
    head_at = jnp.arange(part) // head_dim
    ones = (head_at[:, None] == head_at[None, :]).astype(BF16)
    (
        full,
        x,
        grad,
        mixed,
        qaug,
        kv,
        inverses,
        att,
        branch,
        mlp,
        slope,
        dm,
        grad_down,
        mlp_part,
        mlp_other,
        mod,
        silu_half,
    ) = forward_pass(
        grid,
        sizes,
        shard,
        tokens.transpose(1, 0, 2),
        out_grad.transpose(1, 0, 2),
        small,
        ada,
        query_spare,
        key_spare,
        key_scale,
        ones,
        0,
    )
    reduced, grad_mid, ga_part, ga_other, mid_stats, up_sum, qkv_sum = backward_pass(
        grid,
        sizes,
        (full, x, grad, mixed, qaug, kv, inverses, att, branch, mlp, slope, dm, grad_down),
        mod,
        key_spare,
        key_scale,
        ones,
        5,
    )
    output, grad_inputs, got, mod_low, back_got = finish(
        grid,
        sizes,
        own_len,
        (x, grad, branch, mlp_part, mlp_other, grad_mid, ga_part, ga_other, mod, mid_stats, up_sum, qkv_sum, ada),
        1,
    )
    grad_ada = jnp.einsum(
        "sdr,sdc->rc", silu_half, mod_low, preferred_element_type=F32
    ).reshape(part, 6, cols)
    same_core = jnp.sum(own_of(got)[:, :, 64:96].astype(F32), axis=0)
    every_core = jnp.sum(got[:, :, :, 64:96].astype(F32), axis=(0, 1))
    owned_ends = [
        lax.dynamic_index_in_dim(every_core, at + core, 0, keepdims=False).reshape(proj_bias.shape) for at in (2, 4)
    ]
    back_sum = jnp.sum(back_got[:, 0:8, :], axis=0)
    grad_silu = back_sum.reshape(seqs, part)
    cond_own = lax.dynamic_slice_in_dim(condition.astype(F32), core * part, part, 1)
    sigmoid = jax.nn.sigmoid(cond_own)
    grad_condition = grad_silu * sigmoid * (1.0 + cond_own * (1.0 - sigmoid))
    ada_rows = lax.dynamic_slice(
        back_got,
        (core * heads, 8, chip * ada_bias.shape[2]),
        (heads, 6, ada_bias.shape[2]),
    )
    grad_ada_bias = ada_rows.transpose(1, 0, 2)

    chunks = reduced.shape[0]
    grad_qkv = reduced[chunks - 3 :].reshape(3, own_rows, 4, 128).transpose(0, 2, 1, 3)
    grad_qkv = grad_qkv.reshape(-1, 3, own_rows, 128)
    wide = lambda values: values.transpose(1, 0, 2).reshape(own_rows, -1)
    return (
        output.transpose(1, 0, 2),
        grad_inputs.transpose(1, 0, 2),
        grad_condition,
        grad_ada,
        grad_ada_bias,
        grad_qkv.transpose(1, 2, 0, 3).reshape(qkv_weight.shape),
        same_core[0].reshape(query_bias.shape),
        same_core[1].reshape(value_bias.shape),
        same_core[6, :heads] + same_core[7, :heads],
        reduced[2 * ff_chunks].T,
        owned_ends[0],
        wide(reduced[ff_chunks : 2 * ff_chunks]),
        same_core[8:12].reshape(up_bias.shape),
        wide(reduced[:ff_chunks]).T,
        owned_ends[1],
    )


def solution(mesh):
    in_specs = (
        P("dp", "tensor", None),
        P("dp", None),
        P("dp", None),
        P("tensor", None, "dp"),
        P(None, "tensor", "dp"),
        P(None, "dp", "tensor"),
        P("tensor", "dp"),
        P("tensor", "dp"),
        P("tensor"),
        P("tensor", "dp"),
        P("tensor", "dp"),
        P("dp", "tensor"),
        P("tensor", "dp"),
        P("tensor", "dp"),
        P("tensor", "dp"),
        P("dp", "tensor", None),
    )
    out_specs = (
        P("dp", "tensor", None),
        P("dp", "tensor", None),
        P("dp", "tensor"),
        P("tensor", None, "dp"),
        P(None, "tensor", "dp"),
        P(None, "dp", "tensor"),
        P("tensor", "dp"),
        P("tensor", "dp"),
        P("tensor"),
        P("tensor", "dp"),
        P("tensor", "dp"),
        P("dp", "tensor"),
        P("tensor", "dp"),
        P("tensor", "dp"),
        P("tensor", "dp"),
    )
    grid = GRIDS.get((mesh.shape["dp"], mesh.shape["tensor"]))
    body = on_device if grid is None else functools.partial(fast_device, grid)
    return jax.shard_map(
        body, mesh=mesh, in_specs=in_specs, out_specs=out_specs, check_vma=False
    )
```

```python
import functools

import jax
import jax.numpy as jnp
from jax import lax
from jax.experimental import pallas as pl
from jax.experimental.pallas import tpu as pltpu
from jax.sharding import PartitionSpec as P

NORM_EPS = 1e-06
HEAD_EPS = 1e-06
GELU_COEF = 0.7978845608028654
GELU_CUBE = 0.044715


def normalize(values):
    centred = values - jnp.mean(values, axis=-1, keepdims=True)
    inverse = lax.rsqrt(jnp.mean(centred * centred, axis=-1, keepdims=True) + NORM_EPS)
    return (centred * inverse, inverse)


def norm_back(grad_normed, normed, inverse):
    return inverse * (
        grad_normed
        - jnp.mean(grad_normed, axis=-1, keepdims=True)
        - normed * jnp.mean(grad_normed * normed, axis=-1, keepdims=True)
    )


def gelu_slope(hidden):
    inner = jnp.tanh(GELU_COEF * (hidden + GELU_CUBE * hidden * hidden * hidden))
    return 0.5 * (1.0 + inner) + 0.5 * hidden * (1.0 - inner * inner) * GELU_COEF * (
        1.0 + 3.0 * GELU_CUBE * hidden * hidden
    )


def masked_scores(query_unit, key_unit, scale_factor, scale_row):
    query_low = (query_unit * scale_factor).astype(jnp.bfloat16)
    key_low = key_unit.astype(jnp.bfloat16)
    scores = jnp.einsum("qhe,khe->hqk", query_low, key_low, preferred_element_type=jnp.float32)
    allowed = scale_row[None, :] <= scale_row[:, None]
    return (jnp.where(allowed[None, :, :], scores, -1e30), query_low, key_low)


def attention_core(mixed_all, qkv_full, query_bias_part, value_bias_part, head_scale, scale_row):
    part_width = qkv_full.shape[2]
    part_heads = head_scale.shape[0]
    head_dim = part_width // part_heads
    seq_len = scale_row.shape[0]
    projected = jnp.einsum("ld,jdc->jlc", mixed_all, qkv_full, preferred_element_type=jnp.float32)
    queries = (projected[0] + query_bias_part.reshape(part_width).astype(jnp.float32)).reshape(
        seq_len, part_heads, head_dim
    )
    keys_raw = projected[1].reshape(seq_len, part_heads, head_dim)
    values_low = (projected[2] + value_bias_part.reshape(part_width).astype(jnp.float32)).astype(
        jnp.bfloat16
    )
    values_low = values_low.reshape(seq_len, part_heads, head_dim)
    query_inverse = lax.rsqrt(jnp.sum(queries * queries, axis=-1, keepdims=True) + HEAD_EPS)
    key_inverse = lax.rsqrt(jnp.sum(keys_raw * keys_raw, axis=-1, keepdims=True) + HEAD_EPS)
    query_unit = queries * query_inverse
    key_unit = keys_raw * key_inverse
    scale_factor = jnp.exp(head_scale)[:, None]
    scores, query_low, key_low = masked_scores(query_unit, key_unit, scale_factor, scale_row)
    row_max = jnp.max(scores, axis=-1, keepdims=True)
    weights_exp = jnp.exp(scores - row_max)
    row_total = jnp.sum(weights_exp, axis=-1, keepdims=True)
    attn_prob = weights_exp / row_total
    log_norm = row_max + jnp.log(row_total)
    attended = jnp.einsum(
        "hqk,khe->qhe",
        attn_prob.astype(jnp.bfloat16),
        values_low,
        preferred_element_type=jnp.float32,
    )
    attended = attended.reshape(seq_len, part_width).astype(jnp.bfloat16)
    return (attended, (query_unit, key_unit, query_inverse, key_inverse, values_low, log_norm))


def forward_step(weights, token_rows, condition_row, scale_row, head_scale):
    (
        ada_full,
        ada_bias_part,
        qkv_full,
        query_bias_part,
        value_bias_part,
        proj_full,
        proj_bias_part,
        up_full,
        up_bias_part,
        down_full,
        down_bias_part,
    ) = weights
    width = token_rows.shape[1]
    part_width = qkv_full.shape[2]
    col_start = lax.axis_index("tensor") * part_width
    cond_rows = lax.dynamic_slice_in_dim(
        condition_row.astype(jnp.float32), col_start, part_width, 0
    )
    silu_rows = jax.nn.silu(cond_rows).astype(jnp.bfloat16)
    mod_terms = jnp.einsum("r,rjc->jc", silu_rows, ada_full, preferred_element_type=jnp.float32)
    own_cols = jnp.concatenate(
        [
            ada_bias_part.reshape(6, part_width),
            proj_bias_part.reshape(1, part_width),
            down_bias_part.reshape(1, part_width),
        ],
        axis=0,
    ).astype(jnp.float32)
    placed = lax.dynamic_update_slice(jnp.zeros((8, width), jnp.float32), own_cols, (0, col_start))
    local_mod = placed + jnp.concatenate([mod_terms, jnp.zeros((2, width), jnp.float32)], axis=0)
    modulation = lax.psum(local_mod, "tensor")
    inputs = token_rows.astype(jnp.float32)
    normed_attn, inverse_attn = normalize(inputs)
    mixed_attn = (normed_attn * (1.0 + modulation[2]) + modulation[4]).astype(jnp.bfloat16)
    mixed_all = lax.all_gather(mixed_attn, "tensor", axis=0, tiled=True)
    attended, attn_kept = attention_core(
        mixed_all, qkv_full, query_bias_part, value_bias_part, head_scale, scale_row
    )
    branch_attn = (
        lax.psum_scatter(
            jnp.dot(attended, proj_full, preferred_element_type=jnp.float32).astype(jnp.bfloat16),
            "tensor",
            scatter_dimension=0,
            tiled=True,
        ).astype(jnp.float32)
        + modulation[6]
    )
    middle = inputs + modulation[0] * branch_attn
    normed_mlp, inverse_mlp = normalize(middle)
    mixed_mlp = (normed_mlp * (1.0 + modulation[3]) + modulation[5]).astype(jnp.bfloat16)
    mlp_all = lax.all_gather(mixed_mlp, "tensor", axis=0, tiled=True)
    hidden = jnp.dot(mlp_all, up_full, preferred_element_type=jnp.float32) + up_bias_part.reshape(
        -1
    ).astype(jnp.float32)
    activated = jax.nn.gelu(hidden, approximate=True).astype(jnp.bfloat16)
    branch_mlp = (
        lax.psum_scatter(
            jnp.dot(activated, down_full, preferred_element_type=jnp.float32).astype(jnp.bfloat16),
            "tensor",
            scatter_dimension=0,
            tiled=True,
        ).astype(jnp.float32)
        + modulation[7]
    )
    output = middle + modulation[1] * branch_mlp
    query_unit, key_unit, query_inverse, key_inverse, values_low, log_norm = attn_kept
    kept = (
        modulation,
        normed_attn,
        inverse_attn,
        mixed_all,
        query_unit,
        key_unit,
        query_inverse,
        key_inverse,
        values_low,
        log_norm,
        attended,
        branch_attn,
        normed_mlp,
        inverse_mlp,
        mlp_all,
        hidden,
        activated,
        branch_mlp,
    )
    return (output, kept)


def backward_step(weights, kept, token_grad, condition_row, scale_row, head_scale):
    (
        ada_full,
        ada_bias_part,
        qkv_full,
        query_bias_part,
        value_bias_part,
        proj_full,
        proj_bias_part,
        up_full,
        up_bias_part,
        down_full,
        down_bias_part,
    ) = weights
    (
        modulation,
        normed_attn,
        inverse_attn,
        mixed_all,
        query_unit,
        key_unit,
        query_inverse,
        key_inverse,
        values_low,
        log_norm,
        attended,
        branch_attn,
        normed_mlp,
        inverse_mlp,
        mlp_all,
        hidden,
        activated,
        branch_mlp,
    ) = kept
    part_width = qkv_full.shape[2]
    part_heads = head_scale.shape[0]
    head_dim = part_width // part_heads
    seq_len = scale_row.shape[0]
    scale_factor = jnp.exp(head_scale)[:, None]
    grad_rows = token_grad.astype(jnp.float32)
    grad_branch_mlp = grad_rows * modulation[1]
    grad_gamma_mlp = jnp.sum(grad_rows * branch_mlp, axis=0)
    grad_down_bias = jnp.sum(grad_branch_mlp, axis=0)
    grad_mlp_all = lax.all_gather(
        grad_branch_mlp.astype(jnp.bfloat16), "tensor", axis=0, tiled=True
    )
    grad_down = jnp.einsum("lf,ld->fd", activated, grad_mlp_all, preferred_element_type=jnp.float32)
    grad_act = jnp.einsum("ld,fd->lf", grad_mlp_all, down_full, preferred_element_type=jnp.float32)
    grad_hidden = grad_act * gelu_slope(hidden)
    grad_up_bias = jnp.sum(grad_hidden, axis=0)
    hidden_low = grad_hidden.astype(jnp.bfloat16)
    grad_up = jnp.einsum("ld,lf->df", mlp_all, hidden_low, preferred_element_type=jnp.float32)
    grad_mixed_mlp = lax.psum_scatter(
        jnp.einsum("lf,df->ld", hidden_low, up_full, preferred_element_type=jnp.float32).astype(
            jnp.bfloat16
        ),
        "tensor",
        scatter_dimension=0,
        tiled=True,
    ).astype(jnp.float32)
    grad_scale_mlp = jnp.sum(grad_mixed_mlp * normed_mlp, axis=0)
    grad_shift_mlp = jnp.sum(grad_mixed_mlp, axis=0)
    grad_middle = grad_rows + norm_back(
        grad_mixed_mlp * (1.0 + modulation[3]), normed_mlp, inverse_mlp
    )
    grad_branch_attn = grad_middle * modulation[0]
    grad_gamma_attn = jnp.sum(grad_middle * branch_attn, axis=0)
    grad_proj_bias = jnp.sum(grad_branch_attn, axis=0)
    grad_attn_all = lax.all_gather(
        grad_branch_attn.astype(jnp.bfloat16), "tensor", axis=0, tiled=True
    )
    grad_proj = jnp.einsum("lc,ld->cd", attended, grad_attn_all, preferred_element_type=jnp.float32)
    grad_attended = jnp.einsum(
        "ld,cd->lc", grad_attn_all, proj_full, preferred_element_type=jnp.float32
    )
    grad_attended = grad_attended.astype(jnp.bfloat16).reshape(seq_len, part_heads, head_dim)
    scores, query_low, key_low = masked_scores(query_unit, key_unit, scale_factor, scale_row)
    attn_prob = jnp.exp(scores - log_norm)
    grad_prob = jnp.einsum(
        "qhe,khe->hqk", grad_attended, values_low, preferred_element_type=jnp.float32
    )
    row_dot = jnp.sum(attn_prob * grad_prob, axis=-1, keepdims=True)
    grad_scores = (attn_prob * (grad_prob - row_dot)).astype(jnp.bfloat16)
    grad_values = jnp.einsum(
        "hqk,qhe->khe",
        attn_prob.astype(jnp.bfloat16),
        grad_attended,
        preferred_element_type=jnp.float32,
    )
    grad_query_scaled = jnp.einsum(
        "hqk,khe->qhe", grad_scores, key_low, preferred_element_type=jnp.float32
    )
    grad_key_unit = jnp.einsum(
        "hqk,qhe->khe", grad_scores, query_low, preferred_element_type=jnp.float32
    )
    grad_head_scale = jnp.sum(grad_query_scaled * query_unit, axis=(0, 2)) * jnp.exp(head_scale)
    grad_query_unit = grad_query_scaled * scale_factor
    grad_queries = query_inverse * (
        grad_query_unit - query_unit * jnp.sum(grad_query_unit * query_unit, axis=-1, keepdims=True)
    )
    grad_keys = key_inverse * (
        grad_key_unit - key_unit * jnp.sum(grad_key_unit * key_unit, axis=-1, keepdims=True)
    )
    grad_query_bias = jnp.sum(grad_queries, axis=0)
    grad_value_bias = jnp.sum(grad_values, axis=0)
    grad_projected = (
        jnp.stack([grad_queries, grad_keys, grad_values])
        .reshape(3, seq_len, part_width)
        .astype(jnp.bfloat16)
    )
    grad_qkv = jnp.einsum(
        "ld,jlc->jdc", mixed_all, grad_projected, preferred_element_type=jnp.float32
    )
    grad_mixed_attn = lax.psum_scatter(
        jnp.einsum(
            "jlc,jdc->ld", grad_projected, qkv_full, preferred_element_type=jnp.float32
        ).astype(jnp.bfloat16),
        "tensor",
        scatter_dimension=0,
        tiled=True,
    ).astype(jnp.float32)
    grad_scale_attn = jnp.sum(grad_mixed_attn * normed_attn, axis=0)
    grad_shift_attn = jnp.sum(grad_mixed_attn, axis=0)
    grad_inputs = grad_middle + norm_back(
        grad_mixed_attn * (1.0 + modulation[2]), normed_attn, inverse_attn
    )
    mod_rows = jnp.stack(
        [
            grad_gamma_attn,
            grad_gamma_mlp,
            grad_scale_attn,
            grad_scale_mlp,
            grad_shift_attn,
            grad_shift_mlp,
            grad_proj_bias,
            grad_down_bias,
        ]
    )
    grad_modulation = lax.psum(mod_rows.astype(jnp.bfloat16), "tensor").astype(jnp.float32)
    col_start = lax.axis_index("tensor") * part_width
    cond_rows = lax.dynamic_slice_in_dim(
        condition_row.astype(jnp.float32), col_start, part_width, 0
    )
    silu_rows = jax.nn.silu(cond_rows).astype(jnp.bfloat16)
    mod_low = grad_modulation[:6].astype(jnp.bfloat16)
    grad_ada = jnp.einsum("r,jc->rjc", silu_rows, mod_low, preferred_element_type=jnp.float32)
    grad_silu = jnp.einsum("jc,rjc->r", mod_low, ada_full, preferred_element_type=jnp.float32)
    sigmoid_rows = jax.nn.sigmoid(cond_rows)
    grad_condition = grad_silu * sigmoid_rows * (1.0 + cond_rows * (1.0 - sigmoid_rows))
    own_cols = lax.dynamic_slice_in_dim(grad_modulation, col_start, part_width, 1)
    increments = (
        grad_ada,
        own_cols[:6].reshape(6, part_heads, head_dim),
        grad_qkv,
        grad_query_bias,
        grad_value_bias,
        grad_head_scale,
        grad_proj,
        own_cols[6].reshape(part_heads, head_dim),
        grad_up,
        grad_up_bias.reshape(part_heads, -1),
        grad_down,
        own_cols[7].reshape(part_heads, head_dim),
    )
    return (increments, grad_inputs, grad_condition)


def on_device(
    tokens,
    condition,
    scale_index,
    ada_weight,
    ada_bias,
    qkv_weight,
    query_bias,
    value_bias,
    head_scale,
    proj_weight,
    proj_bias,
    up_weight,
    up_bias,
    down_weight,
    down_bias,
    out_grad,
):

    def fetch_weights():
        return (
            lax.all_gather(ada_weight, "dp", axis=2, tiled=True),
            lax.all_gather(ada_bias, "dp", axis=2, tiled=True),
            lax.all_gather(qkv_weight, "dp", axis=1, tiled=True),
            lax.all_gather(query_bias, "dp", axis=1, tiled=True),
            lax.all_gather(value_bias, "dp", axis=1, tiled=True),
            lax.all_gather(proj_weight, "dp", axis=1, tiled=True),
            lax.all_gather(proj_bias, "dp", axis=1, tiled=True),
            lax.all_gather(up_weight, "dp", axis=0, tiled=True),
            lax.all_gather(up_bias, "dp", axis=1, tiled=True),
            lax.all_gather(down_weight, "dp", axis=1, tiled=True),
            lax.all_gather(down_bias, "dp", axis=1, tiled=True),
        )

    def forward_scan(carried, step_in):
        token_rows, condition_row, scale_row = step_in
        weights_now = fetch_weights()
        output, kept = forward_step(weights_now, token_rows, condition_row, scale_row, head_scale)
        return (carried, (output, kept))

    unused_carry, (outputs, kept_all) = lax.scan(
        forward_scan, jnp.zeros((), jnp.int32), (tokens, condition, scale_index)
    )
    width = tokens.shape[2]
    part_width = qkv_weight.shape[2]
    part_heads = head_scale.shape[0]
    head_dim = part_width // part_heads
    part_ff = up_weight.shape[1]
    zero_grads = (
        jnp.zeros((part_width, 6, width), jnp.float32),
        jnp.zeros((6, part_heads, head_dim), jnp.float32),
        jnp.zeros((3, width, part_width), jnp.float32),
        jnp.zeros((part_heads, head_dim), jnp.float32),
        jnp.zeros((part_heads, head_dim), jnp.float32),
        jnp.zeros((part_heads,), jnp.float32),
        jnp.zeros((part_width, width), jnp.float32),
        jnp.zeros((part_heads, head_dim), jnp.float32),
        jnp.zeros((width, part_ff), jnp.float32),
        jnp.zeros((part_heads, part_ff // part_heads), jnp.float32),
        jnp.zeros((part_ff, width), jnp.float32),
        jnp.zeros((part_heads, head_dim), jnp.float32),
    )

    def backward_scan(totals, step_in):
        kept, token_grad, condition_row, scale_row = step_in
        weights_now = fetch_weights()
        increments, grad_inputs, grad_condition = backward_step(
            weights_now, kept, token_grad, condition_row, scale_row, head_scale
        )
        totals = tuple((running + increment for running, increment in zip(totals, increments)))
        return (totals, (grad_inputs, grad_condition))

    totals, (grad_tokens, grad_condition) = lax.scan(
        backward_scan, zero_grads, (kept_all, out_grad, condition, scale_index), reverse=True
    )
    scale_total = lax.psum(totals[5], "dp")
    reduced = (
        lax.psum_scatter(
            totals[0].astype(jnp.bfloat16), "dp", scatter_dimension=2, tiled=True
        ).astype(jnp.float32),
        lax.psum_scatter(
            totals[1].astype(jnp.bfloat16), "dp", scatter_dimension=2, tiled=True
        ).astype(jnp.float32),
        lax.psum_scatter(
            totals[2].astype(jnp.bfloat16), "dp", scatter_dimension=1, tiled=True
        ).astype(jnp.float32),
        lax.psum_scatter(
            totals[3].astype(jnp.bfloat16), "dp", scatter_dimension=1, tiled=True
        ).astype(jnp.float32),
        lax.psum_scatter(
            totals[4].astype(jnp.bfloat16), "dp", scatter_dimension=1, tiled=True
        ).astype(jnp.float32),
        lax.psum_scatter(
            totals[6].astype(jnp.bfloat16), "dp", scatter_dimension=1, tiled=True
        ).astype(jnp.float32),
        lax.psum_scatter(
            totals[7].astype(jnp.bfloat16), "dp", scatter_dimension=1, tiled=True
        ).astype(jnp.float32),
        lax.psum_scatter(
            totals[8].astype(jnp.bfloat16), "dp", scatter_dimension=0, tiled=True
        ).astype(jnp.float32),
        lax.psum_scatter(
            totals[9].astype(jnp.bfloat16), "dp", scatter_dimension=1, tiled=True
        ).astype(jnp.float32),
        lax.psum_scatter(
            totals[10].astype(jnp.bfloat16), "dp", scatter_dimension=1, tiled=True
        ).astype(jnp.float32),
        lax.psum_scatter(
            totals[11].astype(jnp.bfloat16), "dp", scatter_dimension=1, tiled=True
        ).astype(jnp.float32),
    )
    return (
        outputs,
        grad_tokens,
        grad_condition,
        reduced[0],
        reduced[1],
        reduced[2],
        reduced[3],
        reduced[4],
        scale_total,
        reduced[5],
        reduced[6],
        reduced[7],
        reduced[8],
        reduced[9],
        reduced[10],
    )


GRIDS = {(16, 2): (4, 2, 2)}
MESH_ID = pl.DeviceIdType.MESH
ANY = pl.ANY
F32 = jnp.float32
BF16 = jnp.bfloat16
SCALES = 10
MASK = -16384.0


def place():
    return (lax.axis_index("dp"), lax.axis_index("tensor"))


def coords(grid):
    chip, core = place()
    nz, ny, nx = grid
    return (chip // (ny * nx), (chip // nx) % ny, chip % nx, core)


def greet_all(count):
    chip, core = place()
    me = chip * 2 + core
    barrier = pltpu.get_barrier_semaphore()
    for k in range(1, count):
        peer = (me + k) % count
        pl.semaphore_signal(barrier, inc=1, device_id=(peer // 2, peer % 2), device_id_type=MESH_ID)
    pl.semaphore_wait(barrier, count - 1)


def remote(src, dst, send_sem, recv_sem, device):
    return pltpu.make_async_remote_copy(
        src_ref=src,
        dst_ref=dst,
        send_sem=send_sem,
        recv_sem=recv_sem,
        device_id=device,
        device_id_type=MESH_ID,
    )


def greet(peers):
    barrier = pltpu.get_barrier_semaphore()
    for peer in peers:
        pl.semaphore_signal(barrier, inc=1, device_id=peer, device_id_type=MESH_ID)
    pl.semaphore_wait(barrier, len(peers))


def forward_kernel(
    grid,
    sizes,
    chunk_counts,
    shard,
    tok,
    grad_in,
    small,
    ada,
    query_spare,
    key_spare,
    key_scale,
    ones,
    full,
    x_out,
    grad_out,
    mixed_out,
    qaug_out,
    kv_out,
    inverse_out,
    att_out,
    branch_out,
    mlp_out,
    slope_out,
    dm_out,
    grad_down_out,
    mlp_own,
    mlp_other,
    mod,
    silu_out,
    x,
    dm,
    mixed,
    other,
    turned,
    qaug,
    kv,
    inverses,
    att,
    w,
    slope,
    act,
    grad_down,
    every,
    mod_send,
    mod_got,
    head_bias,
    up_bias,
    local_sem,
    p_send,
    p_recv,
    t_send,
    t_recv,
    load_sem,
    save_sem,
    a_send,
    a_recv,
):
    nz, ny, nx = grid
    half = nz // 2
    seqs, pad = sizes
    chunks = shard.shape[0]
    ff_chunks = chunk_counts
    dp = nz * ny * nx
    devices = dp * 2
    mod_rows = ada.shape[0] // 128
    z, y, x_at, core = coords(grid)
    width = x.shape[1]
    part_width = att.shape[1]
    pairs = part_width // 128
    blocks = seqs * 2
    length = tok.shape[0]

    def dev(z_to, y_to, x_to):
        return ((z_to * ny + y_to) * nx + x_to, core)

    x_peer = dev(z, y, 1 - x_at)
    y_peer = dev(z, 1 - y, x_at)
    sibling = (place()[0], 1 - core)
    greet_all(devices)

    me = place()[0] * 2 + core
    every[place()[0], core] = small[core]
    mod_send[...] = jnp.zeros_like(mod_send)

    def to_all(round_at, source, target):
        copies = []
        for k in range(1, devices):
            peer = (me + k) % devices
            copy = remote(
                source(peer // 2, peer % 2),
                target.at[place()[0], core],
                a_send.at[round_at, k - 1],
                a_recv.at[round_at, k - 1],
                (peer // 2, peer % 2),
            )
            copy.start()
            copies.append(copy)
        return copies

    small_copies = to_all(0, lambda to, core_to: small.at[core_to], every)

    def own_copy(c):
        return pltpu.make_async_copy(shard.at[c], full.at[c, z, y, x_at], local_sem.at[c])

    low_rows, high_rows = (pl.ds(i * shard.shape[1] // 2, shard.shape[1] // 2) for i in range(2))

    def spread_out(c):
        return c % 3 == 1

    def stage(c, number):
        z_peers = [dev((z + k) % nz, y, x_at) for k in range(1, nz)]
        if not spread_out(c):
            if number == 0:
                moves = [(shard.at[c], full.at[c, z, y, x_at], peer) for peer in z_peers]
            elif number == 1:
                low = full.at[c, pl.ds(0, half), y, x_at]
                high = full.at[c, pl.ds(half, half), y, x_at]
                moves = [(low, low, x_peer), (high, high, y_peer)]
            else:
                low = full.at[c, pl.ds(0, half), y]
                high = full.at[c, pl.ds(half, half), :, x_at]
                moves = [(low, low, y_peer), (high, high, x_peer)]
        elif number == 0:
            moves = [
                (shard.at[c, low_rows], full.at[c, z, y, x_at, low_rows], x_peer),
                (shard.at[c, high_rows], full.at[c, z, y, x_at, high_rows], y_peer),
            ]
        elif number == 1:
            low = full.at[c, z, y, :, low_rows]
            high = full.at[c, z, :, x_at, high_rows]
            moves = [(piece, piece, peer) for peer in z_peers for piece in (low, high)]
        else:
            low = full.at[c, :, y, :, low_rows]
            high = full.at[c, :, :, x_at, high_rows]
            moves = [(low, low, y_peer), (high, high, x_peer)]
        first = (0, 3, 9)[number]
        return [
            remote(src, dst, p_send.at[c, first + i], p_recv.at[c, first + i], peer)
            for i, (src, dst, peer) in enumerate(moves)
        ]

    ahead = 2
    progress = [-ahead]

    def begin_stage(c, number):
        if number == 1:
            own_copy(c).wait()
        for copy in stage(c, number - 1) if number else ():
            copy.wait_recv()
        for copy in stage(c, number):
            copy.start()

    def advance(upto):
        while progress[0] <= upto:
            t = progress[0]
            if 0 <= t + ahead < chunks:
                own_copy(t + ahead).start()
                begin_stage(t + ahead, 0)
            if 0 <= t + 1 < chunks and spread_out(t + 1):
                begin_stage(t + 1, 1)
            if 0 <= t < chunks and not spread_out(t):
                begin_stage(t, 1)
            if 0 <= t - 1 < chunks:
                begin_stage(t - 1, 2)
            progress[0] += 1

    def load(c):
        return pltpu.make_async_copy(full.at[c], w.at[c % 4], load_sem.at[c])

    def begin_load(c):
        for copy in stage(c, 2):
            copy.wait_recv()
        load(c).start()

    def weight(c):
        return w[c % 4].reshape(width, part_width)

    saves = []

    def save(src, dst):
        copy = pltpu.make_async_copy(src, dst, save_sem.at[len(saves)])
        copy.start()
        saves.append(copy)
        return copy

    def block_rows(a):
        return pl.ds(pl.multiple_of(a * pad, 16), pad)

    advance(-2)

    def own_rows(s, which):
        return block_rows(s * 2 + which)

    def conditions():
        for copy in small_copies:
            copy.wait()
        groups = ada.shape[1] // 128
        cond = every[:, 0].astype(F32)
        for s in range(seqs):
            total = None
            for g in range(groups):
                c = cond[:, s * groups + g, :]
                silu = (c / (1.0 + jnp.exp(-c))).astype(BF16)
                silu_out[s, :, g * 128 : g * 128 + 128] = silu
                term = dot_nt(silu, ada[:, g * 128 : g * 128 + 128])
                total = term if g == 0 else total + term
            for i in range(mod_rows):
                mod_send[:, i * seqs + s, :] = total[:, i * 128 : i * 128 + 128]
        return to_all(1, lambda to, core_to: mod_send.at[to], mod_got)

    def iota(shape, dim):
        return lax.broadcasted_iota(jnp.int32, shape, dim)

    def spread(rows, cols, at, unit, span):
        share = span // dp
        row, col = iota((128, cols), 0) - at, iota((128, cols), 1)
        here = (row >= 0) & (row < unit) & (col // span == row // share) & (col % share == row % share)
        placed = dot(rows, jnp.where(here, 1.0, 0.0).astype(BF16)).reshape(dp, -1, cols)
        mine = (iota((dp, 1, cols), 2) % span) // share == iota((dp, 1, cols), 0)
        return jnp.sum(jnp.where(mine, placed, 0.0), axis=0)

    def modulation():
        for copy in mod_copies:
            copy.wait()
        mod_got[place()[0], core] = mod_send[place()[0]]
        first_row = 8
        count = every.shape[2]
        for t in range(2):
            rows = every[:, t].reshape(dp * count, 128)
            at = t * part_width
            quarters = [spread(rows, part_width, q * 32, 32, 64) for q in range(4)]
            for j in range(8):
                vector = j if j < 6 else j + 2
                piece = quarters[vector % 4][first_row + vector // 4 : first_row + vector // 4 + 1]
                for s in range(seqs):
                    mod[s, j : j + 1, at : at + part_width] = piece
        rows = every[:, pl.ds(core, 1)].reshape(dp * count, 128)
        for j in (6, 7):
            piece = spread(rows, part_width, j % 4 * 32, 32, 64)
            head_bias[j : j + 1, :] = piece[first_row + j // 4 : first_row + j // 4 + 1]
        rows = spread(rows, part_width * ff_chunks, 0, 128, 256)
        for c in range(ff_chunks):
            up_bias[c] = rows[first_row + 3 : first_row + 4, c * part_width : (c + 1) * part_width]
        sums = [mod_got[d, 0] + mod_got[d, 1] for d in range(dp)]
        for j in range(6):
            at = j // 2 * seqs
            lanes = j % 2 * 64
            row = jnp.concatenate([total[at : at + seqs, lanes : lanes + 64] for total in sums], axis=1)
            for s in range(seqs):
                mod[s, j : j + 1, :] += row[s : s + 1]

    swaps = []
    for i, (src, dst) in enumerate(((tok, x), (grad_in, dm))):
        for s in range(seqs):
            values = src[:, s, :].astype(F32).astype(BF16)
            start = pl.multiple_of((s * 2 + core) * pad, 16)
            dst[pl.ds(start + length // 16 * 16, pad - length // 16 * 16), :] = jnp.zeros(
                (pad - length // 16 * 16, width), BF16
            )
            dst[pl.ds(start, length), :] = values
            piece = dst.at[own_rows(s, core), :]
            copy = remote(piece, piece, t_send.at[i * seqs + s], t_recv.at[i * seqs + s], sibling)
            copy.start()
            swaps.append(copy)
    advance(-1)
    mod_copies = conditions()
    for copy in swaps[:seqs]:
        copy.wait()
    x_saved = save(x, x_out)
    advance(0)
    for copy in swaps[seqs:]:
        copy.wait()
    grad_saved = save(dm, grad_out)
    advance(1)
    modulation()

    def mix_attn(a, rows):
        s = a // 2
        normed, unused = normalize(x[rows, :].astype(F32))
        mixed[rows, :] = (normed * (1.0 + mod[s, 2:3, :]) + mod[s, 4:5, :]).astype(BF16)

    for_blocks(blocks, pad, mix_attn)
    mixed_saved = save(mixed, mixed_out)
    grad_saved.wait()

    def scale_grad(a, rows):
        dm[rows, :] = (dm[rows, :].astype(F32) * mod[a // 2, 1:2, :]).astype(BF16)

    for_blocks(blocks, pad, scale_grad)
    save(dm, dm_out)
    transpose_into(turned, dm)
    advance(2)
    begin_load(0)
    load(0).wait()

    def project_q(a, rows):
        first, unused = lane_code(pad)
        q_spare = query_spare[rows, :].astype(F32)
        values = dot(mixed[rows, :], weight(0)) + head_bias[6:7, :]
        inv = lax.rsqrt(dot((values * values).astype(BF16), ones[...]) + HEAD_EPS)
        inverses[rows, 0:part_width] = inv.astype(BF16)
        values = values * inv * key_scale[...]
        for p in range(pairs):
            piece = values[:, p * 128 : p * 128 + 128]
            qaug[2 * p, rows, :] = jnp.where(first, piece, q_spare).astype(BF16)
            qaug[2 * p + 1, rows, :] = jnp.where(first, q_spare, piece).astype(BF16)

    for_blocks(blocks, pad, project_q)
    advance(3)
    begin_load(1)
    load(1).wait()

    def project_k(a, rows):
        values = dot(mixed[rows, :], weight(1))
        inv = lax.rsqrt(dot((values * values).astype(BF16), ones[...]) + HEAD_EPS)
        inverses[rows, part_width : 2 * part_width] = inv.astype(BF16)
        kv[rows, 0:part_width] = (values * inv).astype(BF16)

    for_blocks(blocks, pad, project_k)
    inverse_saved = save(inverses, inverse_out)
    advance(4)
    begin_load(2)
    load(2).wait()

    def project_v(a, rows):
        kv[rows, part_width : 2 * part_width] = (
            dot(mixed[rows, :], weight(2)) + head_bias[7:8, :]
        ).astype(BF16)

    for_blocks(blocks, pad, project_v)
    save(kv, kv_out)

    def attend(i, carry):
        p = i // blocks
        block = i % blocks
        rows = block_rows(block)
        all_rows = pl.ds(pl.multiple_of((block // 2) * 2 * pad, 16), 2 * pad)
        at = pl.multiple_of(p * 128, 128)
        first, code = lane_code(pad)
        k_sides = both_heads(kv[all_rows, pl.ds(at, 128)], key_spare[all_rows, :])
        v_sides = both_heads(kv[all_rows, pl.ds(at + part_width, 128)], 1.0)
        outs = []
        for side in range(2):
            h = 2 * p + side
            q = qaug[h, rows, :]
            prob = jnp.exp2(dot_nt(q, k_sides[side])).astype(BF16)
            o = dot(prob, v_sides[side])
            outs.append(o / pltpu.roll(o, 64, 1))
            norm = -jnp.log2(o)
            high = norm.astype(BF16)
            rest = norm - high.astype(F32)
            middle = rest.astype(BF16)
            low = (rest - middle.astype(F32)).astype(BF16)
            spare = jnp.logical_not(first) if side == 0 else first
            q = q.astype(F32)
            for where, piece in enumerate((high, middle, low)):
                q = jnp.where(spare & (code == SCALES + where), piece.astype(F32), q)
            qaug[h, rows, :] = q.astype(BF16)
        att[rows, pl.ds(at, 128)] = jnp.where(first, outs[0], outs[1]).astype(BF16)
        return carry

    count = pairs * blocks
    for quarter in range(4):
        lax.fori_loop(quarter * count // 4, (quarter + 1) * count // 4, attend, 0)
        if quarter == 0:
            advance(5)
        if quarter == 2:
            advance(6)
    begin_load(3)
    save(qaug, qaug_out)
    save(att, att_out)
    load(3).wait()
    inverse_saved.wait()
    part = inverses
    part_copies = []
    for a in range(blocks):
        rows = block_rows(a)
        part[rows, :] = dot_nt(att[rows, :], weight(3)).astype(BF16)
        copy = remote(
            part.at[rows, :], other.at[rows, :], t_send.at[2 * seqs + a], t_recv.at[2 * seqs + a], sibling
        )
        copy.start()
        part_copies.append(copy)
    mixed_saved.wait()
    mlp = mixed
    begin_load(4)
    for a in range(blocks):
        rows = block_rows(a)
        s = a // 2
        part_copies[a].wait()
        b = part[rows, :].astype(F32) + other[rows, :].astype(F32) + mod[s, 6:7, :]
        other[rows, :] = b.astype(BF16)
        normed, unused = normalize(x[rows, :].astype(F32) + mod[s, 0:1, :] * b)
        mlp[rows, :] = (normed * (1.0 + mod[s, 3:4, :]) + mod[s, 5:6, :]).astype(BF16)
    branch_saved = save(other, branch_out)
    save(mlp, mlp_out)
    down_saved = []

    def raise_chunk(c):
        load(4 + c).wait()

        def raise_rows(a, rows):
            h = dot(mlp[rows, :], weight(4 + c)) + up_bias[c]
            square = h * h
            t = jnp.tanh(h * (GELU_COEF + GELU_COEF * GELU_CUBE * square))
            act[c, rows, :] = (0.5 * h * (1.0 + t)).astype(BF16)
            slope[c, rows, :] = (
                0.5 * (1.0 + t)
                + h * (1.0 - t * t) * (0.5 * GELU_COEF + 1.5 * GELU_COEF * GELU_CUBE * square)
            ).astype(BF16)

        for_blocks(blocks, pad, raise_rows)
        save(slope.at[c], slope_out.at[c])

    def down_chunk(c):
        if c >= 2:
            down_saved[c - 2].wait()
        weight_grad(grad_down.at[c % 2], turned, act.at[c])
        down_saved.append(save(grad_down.at[c % 2], grad_down_out.at[c]))

    advance(7)
    begin_load(5)
    raise_chunk(0)
    raise_chunk(1)
    advance(8)
    begin_load(6)
    down_chunk(0)
    raise_chunk(2)
    down_chunk(1)
    advance(9)
    begin_load(7)
    raise_chunk(3)
    advance(10)
    begin_load(8)
    down_chunk(2)
    down_chunk(3)
    advance(11)
    begin_load(9)
    advance(12)
    begin_load(10)
    for copy in (x_saved, branch_saved, load(8), load(9), load(10)):
        copy.wait()

    def lower_most(a, rows):
        total = dot_nt(act[0, rows, :], weight(8))
        for c in range(1, ff_chunks - 1):
            total = total + dot_nt(act[c, rows, :], weight(8 + c))
        high = total.astype(BF16)
        x[rows, :] = high
        other[rows, :] = (total - high.astype(F32)).astype(BF16)

    for_blocks(blocks, pad, lower_most)
    begin_load(11)
    load(11).wait()
    end_copies = []
    for step in range(blocks):
        s = step % seqs
        which = 1 - core if step < seqs else core
        rows = own_rows(s, which)
        total = dot_nt(act[ff_chunks - 1, rows, :], weight(7 + ff_chunks))
        total = total + x[rows, :].astype(F32) + other[rows, :].astype(F32)
        part[rows, :] = total.astype(BF16)
        if step < seqs:
            copy = remote(
                part.at[rows, :],
                mlp_other.at[s],
                t_send.at[2 * seqs + blocks + s],
                t_recv.at[2 * seqs + blocks + s],
                sibling,
            )
            copy.start()
            end_copies.append(copy)
        else:
            save(part.at[rows, :], mlp_own.at[s])
    for copy in end_copies:
        copy.wait()
    done = [mixed_saved, grad_saved, inverse_saved, x_saved, branch_saved] + down_saved[:-2]
    for copy in saves:
        if all(copy is not other_copy for other_copy in done):
            copy.wait()
    for c in range(chunks):
        for number in range(3):
            for copy in stage(c, number):
                copy.wait_send()


def forward_pass(grid, sizes, shard, tok, grad_in, small, ada, query_spare, key_spare, key_scale, ones, collective_id):
    nz, ny, nx = grid
    seqs, pad = sizes
    chunks, own_rows, part = shard.shape
    ff_chunks = (chunks - 4) // 2
    dp = nz * ny * nx
    width = tok.shape[2]
    total = seqs * 2 * pad
    heads = part // 64
    wide = ((total, width), BF16)
    narrow = ((total, part), BF16)
    chunk = (nz, ny, nx, own_rows, part)
    outs = [
        ((chunks,) + chunk, BF16),
        wide,
        wide,
        wide,
        ((heads, total, 128), BF16),
        wide,
        wide,
        narrow,
        wide,
        wide,
        ((ff_chunks, total, part), BF16),
        wide,
        ((ff_chunks,) + chunk, BF16),
        ((seqs, pad, width), BF16),
        ((seqs, pad, width), BF16),
        ((seqs, 8, width), F32),
        ((seqs, dp, part), BF16),
    ]
    scratch = [
        wide,
        wide,
        wide,
        wide,
        ((width, total), BF16),
        ((heads, total, 128), BF16),
        wide,
        wide,
        narrow,
        ((4,) + chunk, BF16),
        ((ff_chunks, total, part), BF16),
        ((ff_chunks, total, part), BF16),
        ((2,) + chunk, BF16),
        ((dp, 2) + small.shape[1:], BF16),
        ((dp, 8, 128), F32),
        ((dp, 2, 8, 128), F32),
        ((8, part), F32),
        ((ff_chunks, 1, part), F32),
    ]
    swaps = 3 * seqs + seqs * 2
    vmem = pl.BlockSpec(memory_space=pltpu.VMEM)
    hbm = pl.BlockSpec(memory_space=ANY)
    return pl.pallas_call(
        functools.partial(forward_kernel, grid, sizes, ff_chunks),
        out_shape=[jax.ShapeDtypeStruct(shape, dtype) for shape, dtype in outs],
        in_specs=[hbm] + [vmem] * 8,
        out_specs=[hbm] * (len(outs) - 2) + [vmem] * 2,
        scratch_shapes=[pltpu.VMEM(shape, dtype) for shape, dtype in scratch]
        + [
            pltpu.SemaphoreType.DMA((chunks,)),
            pltpu.SemaphoreType.DMA((chunks, 14)),
            pltpu.SemaphoreType.DMA((chunks, 14)),
            pltpu.SemaphoreType.DMA((swaps,)),
            pltpu.SemaphoreType.DMA((swaps,)),
            pltpu.SemaphoreType.DMA((chunks,)),
            pltpu.SemaphoreType.DMA((24,)),
            pltpu.SemaphoreType.DMA((2, 2 * dp - 1)),
            pltpu.SemaphoreType.DMA((2, 2 * dp - 1)),
        ],
        compiler_params=pltpu.CompilerParams(
            collective_id=collective_id, has_side_effects=True, vmem_limit_bytes=60 * 2**20
        ),
        name="forward_pass",
    )(shard, tok, grad_in, small, ada, query_spare, key_spare, key_scale, ones)


def dot(a, b):
    return jnp.dot(a, b, preferred_element_type=F32)


def dot_nt(a, b):
    return lax.dot_general(a, b, (((1,), (1,)), ((), ())), preferred_element_type=F32)


def dot_tn(a, b):
    return lax.dot_general(a, b, (((0,), (0,)), ((), ())), preferred_element_type=F32)


def lane_code(rows):
    lane = lax.broadcasted_iota(jnp.int32, (rows, 128), 1)
    return lane < 64, lane & 63


def both_heads(pair, spare):
    first, unused = lane_code(pair.shape[0])
    pair = pair.astype(F32)
    if not isinstance(spare, float):
        spare = spare.astype(F32)
    return (
        jnp.where(first, pair, spare).astype(BF16),
        jnp.where(first, spare, pair).astype(BF16),
    )


def column_sum(values):
    return jnp.sum(values, axis=0, keepdims=True)


def transpose_into(dst, src):
    def step(i, carry):
        at = pl.multiple_of(i * 128, 128)
        dst[:, pl.ds(at, 128)] = src[pl.ds(at, 128), :].T
        return carry

    lax.fori_loop(0, src.shape[0] // 128, step, 0)


def weight_grad(dst, turned, right):
    rows = turned.shape[0] // dst.shape[0]

    def step(i, carry):
        at = pl.ds(pl.multiple_of(i * rows, rows), rows)
        dst[i] = dot(turned[at, :], right[...]).astype(BF16).reshape(dst.shape[1:])
        return carry

    lax.fori_loop(0, dst.shape[0], step, 0)


def for_blocks(count, rows, body):
    def step(a, carry):
        body(a, pl.ds(pl.multiple_of(a * rows, 16), rows))
        return carry

    lax.fori_loop(0, count, step, 0)

def backward_kernel(
    grid,
    sizes,
    full,
    x_in,
    grad_in,
    mixed_in,
    qaug_in,
    kv_in,
    inverse_in,
    att_in,
    branch_in,
    mlp_in,
    slope_in,
    dm_in,
    grad_down_in,
    mod,
    key_spare,
    key_scale,
    ones,
    out_down,
    out_up,
    out_proj,
    out_qkv,
    mid_own,
    ga_own,
    ga_other,
    stats,
    up_sum,
    qkv_sum,
    b0,
    b1,
    b2,
    b3,
    b4,
    turned,
    pool,
    qaug,
    w,
    work,
    got_low,
    got_high,
    next_low,
    next_high,
    got_z,
    p_send,
    p_recv,
    z_send,
    z_recv,
    t_send,
    t_recv,
    load_sem,
):
    nz, ny, nx = grid
    half = nz // 2
    seqs, pad = sizes
    chunks = full.shape[0]
    slots = work.shape[0]
    ff_chunks = slope_in.shape[0]
    z, y, x_at, core = coords(grid)
    width = b0.shape[1]
    part_width = pool.shape[2]
    pairs = part_width // 128
    blocks = seqs * 2
    ln2 = 0.6931471805599453

    def dev(z_to, y_to, x_to):
        return ((z_to * ny + y_to) * nx + x_to, core)

    x_peer = dev(z, y, 1 - x_at)
    y_peer = dev(z, 1 - y, x_at)
    sibling = (place()[0], 1 - core)
    greet([x_peer, y_peer, sibling] + [dev((z + k) % nz, y, x_at) for k in range(1, nz)])

    def block_rows(a):
        return pl.ds(pl.multiple_of(a * pad, 16), pad)

    loads = []

    def load(src, dst):
        copy = pltpu.make_async_copy(src, dst, load_sem.at[len(loads)])
        copy.start()
        loads.append(copy)
        return copy

    def first_copies(c):
        s = c % slots
        return [
            remote(
                work.at[s, pl.ds(0, half), 1 - y], got_low.at[c], p_send.at[c, 0], p_recv.at[c, 0], y_peer
            ),
            remote(
                work.at[s, pl.ds(half, half), :, 1 - x_at],
                got_high.at[c],
                p_send.at[c, 1],
                p_recv.at[c, 1],
                x_peer,
            ),
        ]

    def second_copies(c):
        s = c % slots
        return [
            remote(
                work.at[s, pl.ds(0, half), y, 1 - x_at],
                next_low.at[c],
                p_send.at[c, 2],
                p_recv.at[c, 2],
                x_peer,
            ),
            remote(
                work.at[s, pl.ds(half, half), 1 - y, x_at],
                next_high.at[c],
                p_send.at[c, 3],
                p_recv.at[c, 3],
                y_peer,
            ),
        ]

    def z_copies(c):
        s = c % slots
        return [
            remote(
                work.at[s, (z + k) % nz, y, x_at],
                got_z.at[c, k - 1],
                z_send.at[c, k - 1],
                z_recv.at[c, k - 1],
                dev((z + k) % nz, y, x_at),
            )
            for k in range(1, nz)
        ]

    def add(a, b):
        return (a.astype(F32) + b.astype(F32)).astype(BF16)

    def begin(c):
        for copy in first_copies(c):
            copy.start()

    def second(c):
        s = c % slots
        for copy in first_copies(c):
            copy.wait_recv()
        work[s, 0:half, y] = add(work[s, 0:half, y], got_low[c])
        work[s, half:nz, :, x_at] = add(work[s, half:nz, :, x_at], got_high[c])
        for copy in second_copies(c):
            copy.start()

    def third(c):
        s = c % slots
        for copy in second_copies(c):
            copy.wait_recv()
        work[s, 0:half, y, x_at] = add(work[s, 0:half, y, x_at], next_low[c])
        work[s, half:nz, y, x_at] = add(work[s, half:nz, y, x_at], next_high[c])
        for copy in z_copies(c):
            copy.start()

    def last(c):
        s = c % slots
        for copy in z_copies(c):
            copy.wait_recv()
        total = work[s, z, y, x_at].astype(F32)
        for k in range(nz - 1):
            total = total + got_z[c, k].astype(F32)
        if c < 2 * ff_chunks:
            target = out_down if c < ff_chunks else out_up
            at = c % ff_chunks * part_width
            target[:, at : at + part_width] = total
        elif c == 2 * ff_chunks:
            out_proj[...] = total
        else:
            for i in range(4):
                at = (c - 2 * ff_chunks - 1) * 4 + i
                out_qkv[at % 3, :, at // 3 * 128 : at // 3 * 128 + 128] = total[:, i * 128 : i * 128 + 128]

    def sent(c):
        for copy in first_copies(c) + second_copies(c) + z_copies(c):
            copy.wait_send()

    def put(c, right):
        if c >= slots:
            sent(c - slots)
        weight_grad(work.at[c % slots], turned, right)

    def step(t, start=True):
        if start and t < chunks:
            begin(t)
        if 0 <= t - 2 < chunks:
            second(t - 2)
        if 0 <= t - 3 < chunks:
            third(t - 3)
        if 0 <= t - 4 < chunks:
            last(t - 4)

    def weight(slot):
        return w[slot].reshape(width, part_width)

    down_grads = [load(grad_down_in.at[c], work.at[c]) for c in range(ff_chunks)]
    mlp_load = load(mlp_in, b1)
    dm_load = load(dm_in, b0)
    down_loads = [
        (load(full.at[chunks - ff_chunks + c], w.at[c]), load(slope_in.at[c], pool.at[c]))
        for c in range(ff_chunks)
    ]
    branch_load = load(branch_in, b4)
    qaug_load = load(qaug_in, qaug)
    for c in range(2):
        down_grads[c].wait()
        step(c)
    for c in range(2, ff_chunks):
        down_grads[c].wait()
    mlp_load.wait()
    transpose_into(turned, b1)
    grad_load = load(grad_in, b1)
    dm_load.wait()
    up_sum[...] = jnp.zeros_like(up_sum)
    up_loads = []
    for c in range(ff_chunks):
        for copy in down_loads[c]:
            copy.wait()

        def back(a, rows):
            gh = dot(b0[rows, :], weight(c)) * pool[c, rows, :].astype(F32)
            up_sum[c] += column_sum(gh)
            pool[c, rows, :] = gh.astype(BF16)

        for_blocks(blocks, pad, back)
        up_loads.append(load(full.at[4 + c], w.at[c]))
        put(ff_chunks + c, pool.at[c])
        if c != 1:
            step(2 + (c + 1) // 2)
    x_load = load(x_in, b0)
    for copy in up_loads:
        copy.wait()
    swaps = []
    for a in range(blocks):
        rows = block_rows(a)
        total = dot_nt(pool[0, rows, :], weight(0))
        for c in range(1, ff_chunks):
            total = total + dot_nt(pool[c, rows, :], weight(c))
        b2[rows, :] = total.astype(BF16)
        copy = remote(b2.at[rows, :], b3.at[rows, :], t_send.at[a], t_recv.at[a], sibling)
        copy.start()
        swaps.append(copy)
    proj_load = load(full.at[3], w.at[3])
    qkv_loads = [load(full.at[j], w.at[j]) for j in range(3)]
    step(5)
    for copy in (x_load, grad_load, branch_load, proj_load):
        copy.wait()
    stats[...] = jnp.zeros_like(stats)
    grad_att = pool.at[3]
    for a in range(blocks):
        rows = block_rows(a)
        s = a // 2
        swaps[a].wait()
        b = b4[rows, :].astype(F32)
        gm = b2[rows, :].astype(F32) + b3[rows, :].astype(F32)
        normed, inverse = normalize(b0[rows, :].astype(F32) + mod[s, 0:1, :] * b)
        stats[s, 1:2, :] += 0.5 * column_sum(gm * normed)
        stats[s, 2:3, :] += 0.5 * column_sum(gm)
        mid = b1[rows, :].astype(F32) + norm_back(gm * (1.0 + mod[s, 3:4, :]), normed, inverse)
        b1[rows, :] = mid.astype(BF16)
        stats[s, 0:1, :] += 0.5 * column_sum(mid * b)
        branch_grad = mid * mod[s, 0:1, :]
        stats[s, 3:4, :] += 0.5 * column_sum(branch_grad)
        low = branch_grad.astype(BF16)
        b4[rows, :] = low
        grad_att[rows, :] = dot(low, weight(3)).astype(BF16)
        if a == 1:
            step(6)
    mid_saves = [load(b1.at[block_rows(s * 2 + core), :], mid_own.at[s]) for s in range(seqs)]
    att = b2.at[:, pl.ds(0, part_width)]
    att_load = load(att_in, att)
    kv_load = load(kv_in, b3)
    transpose_into(turned, b4)
    step(7)
    mixed_load = load(mixed_in, b4)
    att_load.wait()
    put(8, att)
    inverse_load = load(inverse_in, b2)
    kv_load.wait()
    qaug_load.wait()
    qkv_sum[...] = jnp.zeros_like(qkv_sum)

    def group(p, j):
        at = p * 3 + j
        lane = at % 4 * 128
        return at // 4, pl.ds(lane if isinstance(lane, int) else pl.multiple_of(lane, 128), 128)

    def put_group(p, j, rows, values):
        chunk, lanes = group(p, j)
        pool[chunk, rows, lanes] = values.astype(BF16)

    def attend(i, carry):
        p = i // seqs
        s = i % seqs
        start = pl.multiple_of(s * 2 * pad, 16)
        all_rows = pl.ds(start, 2 * pad)
        at = pl.multiple_of(p * 128, 128)
        lanes = pl.ds(at, 128)
        first, unused = lane_code(pad)
        first_all, unused = lane_code(2 * pad)
        k_sides = both_heads(b3[all_rows, lanes], key_spare[all_rows, :])
        v_sides = both_heads(b3[all_rows, pl.ds(at + part_width, 128)], 0.0)
        g_sides = both_heads(pool[3, all_rows, lanes], 0.0)
        grads_k, grads_v, grads_q = [], [], [[], []]
        for side in range(2):
            h = 2 * p + side
            k = k_sides[side]
            v = v_sides[side]
            sum_k = sum_v = None
            for t in range(2):
                rows = pl.ds(pl.multiple_of(start + t * pad, 16), pad)
                q = qaug[h, rows, :]
                g = g_sides[side][t * pad : t * pad + pad]
                prob = jnp.exp2(dot_nt(k, q))
                grad_prob = dot_nt(v, g)
                ds = (prob * (grad_prob - column_sum(prob * grad_prob))).astype(BF16)
                gv = dot(prob.astype(BF16), g)
                gk = dot(ds, q)
                sum_v = gv if t == 0 else sum_v + gv
                sum_k = gk if t == 0 else sum_k + gk
                grads_q[t].append(dot_tn(ds, k))
            grads_k.append(sum_k)
            grads_v.append(sum_v)
        for t in range(2):
            rows = pl.ds(pl.multiple_of(start + t * pad, 16), pad)
            gq = jnp.where(first, grads_q[t][0], grads_q[t][1])
            q = jnp.where(first, qaug[2 * p, rows, :].astype(F32), qaug[2 * p + 1, rows, :].astype(F32))
            qkv_sum[2:3, lanes] += ln2 * column_sum(gq * q)
            put_group(p, 0, rows, gq)
        put_group(p, 1, all_rows, ln2 * jnp.where(first_all, grads_k[0], grads_k[1]))
        gv = jnp.where(first_all, grads_v[0], grads_v[1])
        qkv_sum[1:2, lanes] += column_sum(gv)
        put_group(p, 2, all_rows, gv)
        return carry

    mixed_load.wait()
    transpose_into(turned, b4)
    inverse_load.wait()
    for p in range(pairs):
        lax.fori_loop(p * seqs, (p + 1) * seqs, attend, 0)
        lanes = pl.ds(p * 128, 128)

        def finish_pair(a, rows):
            first, unused = lane_code(pad)
            table = ones[0:128, 0:128]
            scale = key_scale[:, lanes]
            unit = jnp.where(first, qaug[2 * p, rows, :].astype(F32), qaug[2 * p + 1, rows, :].astype(F32))
            unit = unit / scale
            chunk, at = group(p, 0)
            f = pool[chunk, rows, at].astype(F32) * (scale * ln2)
            gq = b2[rows, lanes].astype(F32) * (f - unit * dot((f * unit).astype(BF16), table))
            qkv_sum[0:1, lanes] += column_sum(gq)
            put_group(p, 0, rows, gq)
            unit = b3[rows, lanes].astype(F32)
            chunk, at = group(p, 1)
            f = pool[chunk, rows, at].astype(F32)
            inverse = b2[rows, pl.ds(part_width + p * 128, 128)].astype(F32)
            put_group(p, 1, rows, inverse * (f - unit * dot((f * unit).astype(BF16), table)))

        for_blocks(blocks, pad, finish_pair)
        if p > 0:
            put(8 + p, pool.at[p - 1])
        step(8 + p)
    for copy in qkv_loads:
        copy.wait()
    end_copies = []
    end_saves = []
    for i in range(blocks):
        s = i % seqs
        which = 1 - core if i < seqs else core
        rows = block_rows(s * 2 + which)
        total = None
        for j in range(3):
            places = [group(p, j) for p in range(pairs)]
            low = jnp.concatenate([pool[chunk, rows, at] for chunk, at in places], axis=1)
            term = dot_nt(low, weight(j))
            total = term if j == 0 else total + term
        b0[rows, :] = total.astype(BF16)
        if i < seqs:
            copy = remote(b0.at[rows, :], ga_other.at[s], t_send.at[blocks + s], t_recv.at[blocks + s], sibling)
            copy.start()
            end_copies.append(copy)
        else:
            end_saves.append(load(b0.at[rows, :], ga_own.at[s]))
        if i == 1:
            step(12)
    step(13)
    step(14)
    step(15)
    for copy in end_copies + end_saves + mid_saves:
        copy.wait()
    for c in range(chunks - slots, chunks):
        sent(c)


def backward_pass(grid, sizes, operands, mod, key_spare, key_scale, ones, collective_id):
    nz, ny, nx = grid
    half = nz // 2
    seqs, pad = sizes
    full, slope = operands[0], operands[10]
    chunks = full.shape[0]
    own_rows, part = full.shape[4:]
    ff_chunks = slope.shape[0]
    total = seqs * 2 * pad
    width = nz * ny * nx * own_rows
    heads = part // 64
    wide = ((total, width), BF16)
    chunk = (nz, ny, nx, own_rows, part)
    block = (own_rows, part)
    slots = 8
    outs = [
        ((own_rows, ff_chunks * part), F32),
        ((own_rows, ff_chunks * part), F32),
        (block, F32),
        ((3,) + block, F32),
        ((seqs, pad, width), BF16),
        ((seqs, pad, width), BF16),
        ((seqs, pad, width), BF16),
        ((seqs, 4, width), F32),
        ((ff_chunks, 1, part), F32),
        ((8, part), F32),
    ]
    scratch = [wide] * 5 + [
        ((width, total), BF16),
        ((ff_chunks, total, part), BF16),
        ((heads, total, 128), BF16),
        ((4,) + chunk, BF16),
        ((slots,) + chunk, BF16),
        ((chunks, half, nx) + block, BF16),
        ((chunks, half, ny) + block, BF16),
        ((chunks, half) + block, BF16),
        ((chunks, half) + block, BF16),
        ((chunks, nz - 1) + block, BF16),
    ]
    vmem = pl.BlockSpec(memory_space=pltpu.VMEM)
    hbm = pl.BlockSpec(memory_space=ANY)
    swaps = seqs * 2 + seqs
    return pl.pallas_call(
        functools.partial(backward_kernel, grid, sizes),
        out_shape=[jax.ShapeDtypeStruct(shape, dtype) for shape, dtype in outs],
        in_specs=[hbm] * 13 + [vmem] * 4,
        out_specs=[vmem] * 4 + [hbm] * 3 + [vmem] * 3,
        scratch_shapes=[pltpu.VMEM(shape, dtype) for shape, dtype in scratch]
        + [
            pltpu.SemaphoreType.DMA((chunks, 4)),
            pltpu.SemaphoreType.DMA((chunks, 4)),
            pltpu.SemaphoreType.DMA((chunks, nz - 1)),
            pltpu.SemaphoreType.DMA((chunks, nz - 1)),
            pltpu.SemaphoreType.DMA((swaps,)),
            pltpu.SemaphoreType.DMA((swaps,)),
            pltpu.SemaphoreType.DMA((40,)),
        ],
        compiler_params=pltpu.CompilerParams(
            collective_id=collective_id, has_side_effects=True, vmem_limit_bytes=60 * 2**20
        ),
        name="backward_pass",
    )(*operands, mod, key_spare, key_scale, ones)


def finish_kernel(
    grid,
    sizes,
    x_in,
    grad_in,
    branch_in,
    mlp_own,
    mlp_other,
    mid_own,
    ga_own,
    ga_other,
    mod,
    mid_stats,
    up_sum,
    qkv_sum,
    ada,
    output,
    grad_tokens,
    got,
    mod_low,
    back_got,
    rows_in,
    stats,
    message,
    back_message,
    load_sem,
    a_send,
    a_recv,
    c_send,
    c_recv,
):
    nz, ny, nx = grid
    dp = nz * ny * nx
    devices = dp * 2
    seqs, pad = sizes
    chip, core = place()
    me = chip * 2 + core
    length = output.shape[0]
    part_width = qkv_sum.shape[1]
    barrier = pltpu.get_barrier_semaphore()
    for k in range(1, devices):
        peer = (me + k) % devices
        pl.semaphore_signal(barrier, inc=1, device_id=(peer // 2, peer % 2), device_id_type=MESH_ID)

    loads = []
    for s in range(seqs):
        own = pl.ds(pl.multiple_of((s * 2 + core) * pad, 16), pad)
        pieces = [ref.at[own, :] for ref in (x_in, grad_in, branch_in)]
        pieces += [ref.at[s] for ref in (mlp_own, mlp_other, mid_own, ga_own, ga_other)]
        for i, piece in enumerate(pieces):
            copy = pltpu.make_async_copy(piece, rows_in.at[s, i], load_sem.at[s, i])
            copy.start()
            loads.append(copy)
    message[...] = jnp.zeros_like(message)
    back_message[...] = jnp.zeros_like(back_message)
    for s in range(seqs):
        for copy in loads[s * 8 : s * 8 + 8]:
            copy.wait()
        xs, g, unused, own_b, other_b, mid, own_g, other_g = (rows_in[s, i].astype(F32) for i in range(8))
        b = own_b + other_b + mod[s, 7:8, :]
        normed, inverse = normalize(xs)
        gm = own_g + other_g
        gt = mid + norm_back(gm * (1.0 + mod[s, 2:3, :]), normed, inverse)
        grad_tokens[:, s, :] = gt[0:length]
        stats[s, 0:1, :] = mid_stats[s, 0:1, :]
        stats[s, 1:2, :] = column_sum(g * b)
        stats[s, 2:3, :] = column_sum(gm * normed)
        stats[s, 3:4, :] = mid_stats[s, 1:2, :]
        stats[s, 4:5, :] = column_sum(gm)
        stats[s, 5:6, :] = mid_stats[s, 2:3, :]
        stats[s, 6:7, :] = mid_stats[s, 3:4, :]
        stats[s, 7:8, :] = column_sum(g) * mod[s, 1:2, :]

    def iota(shape, dim):
        return lax.broadcasted_iota(jnp.int32, shape, dim)

    def shares(values, span):
        count, lanes = values.shape
        share = span // dp
        mine = (iota((dp, 1, lanes), 2) % span) // share == iota((dp, 1, lanes), 0)
        lane = iota((lanes, 128), 0)
        table = jnp.where(lane // span * share + lane % share == iota((lanes, 128), 1) - 64, 1.0, 0.0)
        split = jnp.where(mine, values, 0.0).reshape(dp * count, lanes).astype(BF16)
        return dot(split, table.astype(BF16)).reshape(dp, count, 128)

    ends = [stats[0, r : r + 1, :] + stats[1, r : r + 1, :] for r in (6, 7)]
    lane = iota((part_width, 128), 0)
    heads_table = jnp.where(lane // 64 == iota((part_width, 128), 1) - 64, 1.0, 0.0).astype(BF16)
    terms = qkv_sum[2:3, :]
    terms_high = terms.astype(BF16)
    terms_low = (terms - terms_high.astype(F32)).astype(BF16)
    both = jnp.concatenate([terms_high.astype(F32), terms_low.astype(F32)], axis=0)
    both = jnp.concatenate([both, jnp.zeros((6, part_width), F32)], axis=0).astype(BF16)
    head_terms = dot(both, heads_table)
    head_sums = head_terms[0:1] + head_terms[1:2]
    head_high = head_sums.astype(BF16).astype(F32)
    vectors = [qkv_sum[0:1, :], qkv_sum[1:2, :]]
    vectors += [end[:, t * part_width : (t + 1) * part_width] for end in ends for t in range(2)]
    vectors += [jnp.zeros((2, part_width), F32)]
    small = shares(jnp.concatenate(vectors, axis=0), 64)
    ups = jnp.concatenate([up_sum[c] for c in range(up_sum.shape[0])] + [jnp.zeros((4, part_width), F32)], axis=0)
    ups = shares(ups, 256)
    six = jnp.concatenate([stats[s, 0:6, :] for s in range(seqs)] + [jnp.zeros((4, stats.shape[2]), F32)], axis=0)
    for d in range(dp):
        at = d // 2 * 128
        cols = six[:, at : at + 128]
        cols = cols if d % 2 == 0 else pltpu.roll(cols, 64, 1)
        right = jnp.concatenate([small[d, 0:6], head_high, head_sums - head_high, ups[d, 0:8]], axis=0)
        message[d] = jnp.where(iota((16, 128), 1) < 64, cols, right).astype(BF16)
    pl.semaphore_wait(barrier, devices - 1)
    copies = []
    for k in range(1, devices):
        peer = (me + k) % devices
        copy = remote(
            message.at[peer // 2], got.at[chip, core], a_send.at[k - 1], a_recv.at[k - 1], (peer // 2, peer % 2)
        )
        copy.start()
        copies.append(copy)
    got[chip, core] = message[chip]
    for s in range(seqs):
        xs, g, branch, own_b, other_b = (rows_in[s, i].astype(F32) for i in range(5))
        b = own_b + other_b + mod[s, 7:8, :]
        output[:, s, :] = (xs + mod[s, 0:1, :] * branch + mod[s, 1:2, :] * b)[0:length]
    for copy in copies:
        copy.wait()
    sums = got[:, 0].astype(F32) + got[:, 1].astype(F32)
    for s in range(seqs):
        low = jnp.concatenate([sums[:, s * 6 + j, 0:64] for j in range(6)], axis=1).astype(BF16)
        mod_low[s] = low
        back = dot(low, ada[...])
        for g in range(part_width // 128):
            back_message[:, s * 4 + g, :] = back[:, g * 128 : g * 128 + 128]
    bias = jnp.sum(sums, axis=0)
    bias = bias[0:6] + bias[6:12]
    back_message[:, 8:14, :] = jnp.broadcast_to(bias, (dp,) + bias.shape)
    copies = []
    for k in range(1, dp):
        to = (chip + k) % dp
        copy = remote(back_message.at[to], back_got.at[chip], c_send.at[k - 1], c_recv.at[k - 1], (to, core))
        copy.start()
        copies.append(copy)
    back_got[chip] = back_message[chip]
    for copy in copies:
        copy.wait()


def finish(grid, sizes, length, operands, collective_id):
    nz, ny, nx = grid
    dp = nz * ny * nx
    seqs, pad = sizes
    width = operands[0].shape[1]
    ada = operands[-1]
    outs = [
        ((length, seqs, width), F32),
        ((length, seqs, width), F32),
        ((dp, 2, 16, 128), BF16),
        ((seqs, dp, ada.shape[0]), BF16),
        ((dp, 16, 128), F32),
    ]
    scratch = [
        ((seqs, 8, pad, width), BF16),
        ((seqs, 8, width), F32),
        ((dp, 16, 128), BF16),
        ((dp, 16, 128), F32),
    ]
    vmem = pl.BlockSpec(memory_space=pltpu.VMEM)
    hbm = pl.BlockSpec(memory_space=ANY)
    return pl.pallas_call(
        functools.partial(finish_kernel, grid, sizes),
        out_shape=[jax.ShapeDtypeStruct(shape, dtype) for shape, dtype in outs],
        in_specs=[hbm] * 8 + [vmem] * 5,
        out_specs=[vmem] * len(outs),
        scratch_shapes=[pltpu.VMEM(shape, dtype) for shape, dtype in scratch]
        + [
            pltpu.SemaphoreType.DMA((seqs, 8)),
            pltpu.SemaphoreType.DMA((2 * dp - 1,)),
            pltpu.SemaphoreType.DMA((2 * dp - 1,)),
            pltpu.SemaphoreType.DMA((dp - 1,)),
            pltpu.SemaphoreType.DMA((dp - 1,)),
        ],
        compiler_params=pltpu.CompilerParams(
            collective_id=collective_id, has_side_effects=True, vmem_limit_bytes=60 * 2**20
        ),
        name="finish",
    )(*operands)


def fast_device(
    grid,
    tokens,
    condition,
    scale_index,
    ada_weight,
    ada_bias,
    qkv_weight,
    query_bias,
    value_bias,
    head_scale,
    proj_weight,
    proj_bias,
    up_weight,
    up_bias,
    down_weight,
    down_bias,
    out_grad,
):
    nz, ny, nx = grid
    dp = nz * ny * nx
    count = dp * 2
    seqs, own_len, width = tokens.shape
    seq_len = own_len * 2
    part = qkv_weight.shape[2]
    heads = head_scale.shape[0]
    head_dim = part // heads
    own_rows = qkv_weight.shape[1]
    ff_chunks = up_weight.shape[1] // part
    chip, core = place()

    shard = jnp.concatenate(
        [
            qkv_weight,
            proj_weight.T[None],
            up_weight.reshape(own_rows, ff_chunks, part).transpose(1, 0, 2),
            down_weight.T.reshape(own_rows, ff_chunks, part).transpose(1, 0, 2),
        ],
        axis=0,
    )
    pad = -(-own_len // 16) * 16
    total = seqs * 2 * pad
    sizes = (seqs, pad)
    halves = condition.reshape(seqs, 2, -1, 128).transpose(1, 0, 2, 3).reshape(2, -1, 128)
    shares = [values.reshape(-1) for values in (ada_bias, query_bias, value_bias, proj_bias, down_bias)]
    shares = jnp.concatenate(shares)
    shares = jnp.pad(shares, (0, -shares.size % 128)).reshape(-1, 128)
    shares = jnp.concatenate([shares, up_bias.reshape(-1, 128)], axis=0)
    small = jnp.concatenate([halves, jnp.broadcast_to(shares, (2,) + shares.shape)], axis=1)
    small = jnp.pad(small, ((0, 0), (0, -small.shape[1] % 16), (0, 0)))
    cols = ada_weight.shape[2]
    ada = ada_weight.transpose(1, 2, 0).reshape(-1, part)
    own_of = lambda values: lax.dynamic_index_in_dim(values, core, 1, keepdims=False)

    level = jnp.pad(
        scale_index.reshape(seqs, 2, own_len), ((0, 0), (0, 0), (0, pad - own_len)), constant_values=100
    ).reshape(total, 1)
    code = jnp.arange(128)[None] % 64
    query_spare = jnp.where(code == level, 1.0, 0.0).astype(BF16)
    key_spare = jnp.where(
        code < SCALES, jnp.where(level > code, MASK, 0.0), jnp.where(code < SCALES + 3, 1.0, 0.0)
    ).astype(BF16)
    key_scale = jnp.repeat(jnp.exp(head_scale) * 1.4426950408889634, head_dim).reshape(1, part)
    head_at = jnp.arange(part) // head_dim
    ones = (head_at[:, None] == head_at[None, :]).astype(BF16)
    (
        full,
        x,
        grad,
        mixed,
        qaug,
        kv,
        inverses,
        att,
        branch,
        mlp,
        slope,
        dm,
        grad_down,
        mlp_part,
        mlp_other,
        mod,
        silu_half,
    ) = forward_pass(
        grid,
        sizes,
        shard,
        tokens.transpose(1, 0, 2),
        out_grad.transpose(1, 0, 2),
        small,
        ada,
        query_spare,
        key_spare,
        key_scale,
        ones,
        0,
    )
    grad_down_rows, grad_up, grad_proj_rows, grad_qkv, grad_mid, ga_part, ga_other, mid_stats, up_sum, qkv_sum = backward_pass(
        grid,
        sizes,
        (full, x, grad, mixed, qaug, kv, inverses, att, branch, mlp, slope, dm, grad_down),
        mod,
        key_spare,
        key_scale,
        ones,
        5,
    )
    output, grad_inputs, got, mod_low, back_got = finish(
        grid,
        sizes,
        own_len,
        (x, grad, branch, mlp_part, mlp_other, grad_mid, ga_part, ga_other, mod, mid_stats, up_sum, qkv_sum, ada),
        1,
    )
    grad_ada = jnp.einsum(
        "sdr,sdc->rc", silu_half, mod_low, preferred_element_type=F32
    ).reshape(part, 6, cols)
    same_core = jnp.sum(own_of(got)[:, :, 64:96].astype(F32), axis=0)
    every_core = jnp.sum(got[:, :, :, 64:96].astype(F32), axis=(0, 1))
    owned_ends = [
        lax.dynamic_index_in_dim(every_core, at + core, 0, keepdims=False).reshape(proj_bias.shape) for at in (2, 4)
    ]
    back_sum = jnp.sum(back_got[:, 0:8, :], axis=0)
    grad_silu = back_sum.reshape(seqs, part)
    cond_own = lax.dynamic_slice_in_dim(condition.astype(F32), core * part, part, 1)
    sigmoid = jax.nn.sigmoid(cond_own)
    grad_condition = grad_silu * sigmoid * (1.0 + cond_own * (1.0 - sigmoid))
    ada_rows = lax.dynamic_slice(
        back_got,
        (core * heads, 8, chip * ada_bias.shape[2]),
        (heads, 6, ada_bias.shape[2]),
    )
    grad_ada_bias = ada_rows.transpose(1, 0, 2)

    return (
        output.transpose(1, 0, 2),
        grad_inputs.transpose(1, 0, 2),
        grad_condition,
        grad_ada,
        grad_ada_bias,
        grad_qkv,
        same_core[0].reshape(query_bias.shape),
        same_core[1].reshape(value_bias.shape),
        same_core[6, :heads] + same_core[7, :heads],
        grad_proj_rows.T,
        owned_ends[0],
        grad_up,
        same_core[8:12].reshape(up_bias.shape),
        grad_down_rows.T,
        owned_ends[1],
    )


def solution(mesh):
    in_specs = (
        P("dp", "tensor", None),
        P("dp", None),
        P("dp", None),
        P("tensor", None, "dp"),
        P(None, "tensor", "dp"),
        P(None, "dp", "tensor"),
        P("tensor", "dp"),
        P("tensor", "dp"),
        P("tensor"),
        P("tensor", "dp"),
        P("tensor", "dp"),
        P("dp", "tensor"),
        P("tensor", "dp"),
        P("tensor", "dp"),
        P("tensor", "dp"),
        P("dp", "tensor", None),
    )
    out_specs = (
        P("dp", "tensor", None),
        P("dp", "tensor", None),
        P("dp", "tensor"),
        P("tensor", None, "dp"),
        P(None, "tensor", "dp"),
        P(None, "dp", "tensor"),
        P("tensor", "dp"),
        P("tensor", "dp"),
        P("tensor"),
        P("tensor", "dp"),
        P("tensor", "dp"),
        P("dp", "tensor"),
        P("tensor", "dp"),
        P("tensor", "dp"),
        P("tensor", "dp"),
    )
    grid = GRIDS.get((mesh.shape["dp"], mesh.shape["tensor"]))
    body = on_device if grid is None else functools.partial(fast_device, grid)
    return jax.shard_map(
        body, mesh=mesh, in_specs=in_specs, out_specs=out_specs, check_vma=False
    )
```
